32 devices in a mesh: ctx: 16 (over z, y, core), fsdp: 2 (over x).
Axes of the slice: x: 2, y: 2, z: 4, core: 2. Of those that a mesh axis runs over, the one named last changes fastest.
Arguments:
- tokens: bfloat16 [2, 4096, 2048], P('fsdp', 'ctx'), may hold values from -6 to 6
- lengths: int32 [2, 2], P('fsdp'), may hold values from 1 to 3072, 4096 in all within a row
- dealing: int32 [2, 16, 256], P('fsdp'), may hold values from 0 to 255, each once within a row
- attn_gain: bfloat16 [2048], P('fsdp'), may hold values from 0.25 to 1.75
- query_weight: bfloat16 [2048, 2048], P('fsdp'), may hold values from -0.125 to 0.125
- kv_weight: bfloat16 [2048, 256], P('fsdp'), may hold values from -0.125 to 0.125
- out_weight: bfloat16 [2048, 2048], P('fsdp'), may hold values from -2 to 2
- mlp_gain: bfloat16 [2048], P('fsdp'), may hold values from 0.25 to 1.75
- gate_weight: bfloat16 [2048, 6144], P('fsdp'), may hold values from -0.125 to 0.125
- up_weight: bfloat16 [2048, 6144], P('fsdp'), may hold values from -0.125 to 0.125
- down_weight: bfloat16 [6144, 2048], P('fsdp'), may hold values from -0.078125 to 0.078125
- cotangent: bfloat16 [2, 4096, 2048], P('fsdp', 'ctx'), may hold values from -6 to 6
Outputs:
- block_output: bfloat16 [2, 4096, 2048], P('fsdp', 'ctx')
- token_grad: float32 [2, 4096, 2048], P('fsdp', 'ctx')
- attn_gain_grad: float32 [2048], P(('ctx', 'fsdp'))
- query_weight_grad: float32 [2048, 2048], P(('ctx', 'fsdp'))
- kv_weight_grad: float32 [2048, 256], P(('ctx', 'fsdp'))
- out_weight_grad: float32 [2048, 2048], P(('ctx', 'fsdp'))
- mlp_gain_grad: float32 [2048], P(('ctx', 'fsdp'))
- gate_weight_grad: float32 [2048, 6144], P(('ctx', 'fsdp'))
- up_weight_grad: float32 [2048, 6144], P(('ctx', 'fsdp'))
- down_weight_grad: float32 [6144, 2048], P(('ctx', 'fsdp'))
The draws below stay inside these ranges and needn't reach their ends.
Inputs may be any that keep to these rules, and one draw needn't show every extreme that they name: In each batch row the 2 lengths sum to 4096 and none exceeds 3072. Each dealing[b, c] holds every number of 0 to 255 once.
All inputs are finite; a program needn't handle non-finite values.
Results may differ from the reference program's by a relative error of at most 0.015.
Values may be sent and summed in bfloat16 or wider, within the bound.
A program may use at most 448 MiB of HBM per device.

```python
import math
import jax
import jax.numpy as jnp
import numpy as np
from jax import lax

D = 2048
H = 16
HD = 128
FF = 6144
WINDOW = 1024
QBLK = 128
TOK_DEV = 256
GROUP = 4096
PIECE = 16
MAXLEN = 3072
NSEQ = 2
N_CTX = 16
N_FSDP = 2


def steps_of(key, extent, split, least, top_value):
    level = 1.0
    for axis_at, parts in split:
        heights = jax.random.uniform(jax.random.fold_in(jax.random.fold_in(key, 6), axis_at), (parts,), jnp.float32, least / len(split), top_value / len(split))
        level = level * jnp.repeat(jnp.exp(heights), extent[axis_at] // parts).reshape((-1,) + (1,) * (len(extent) - 1 - axis_at))
    return level


def split_up(count, total, most, skew):
    weights = [(1 << 20) // math.isqrt(grade ** skew) + 1 for grade in range(2, count + 1)]
    rest, counts = total - most - (count - 1), [1] * (count - 1)
    while rest > 0:
        candidates = [i for i in range(count - 1) if counts[i] < most]
        mass, budget = sum([weights[i] for i in candidates]), rest
        for i in candidates:
            extra = min(most - counts[i], max(1, budget * weights[i] // mass), rest)
            counts[i] = counts[i] + extra
            rest = rest - extra
    return np.array([most] + counts)


def uneven(key, amount, total, bound, skew):
    if amount == 2:
        one = jax.random.randint(key, (), max(1, total - bound), min(bound, total - 1) + 1)
        return jnp.stack([one, total - one])
    sizes = jnp.asarray(split_up(amount, total, bound, skew), jnp.int32)
    pairs = (amount - 1) // 2
    donor, taker = sizes[1:1 + 2 * pairs:2], sizes[2:2 + 2 * pairs:2]
    slack = jnp.minimum(donor - 1, bound - taker)
    passed = jax.random.randint(jax.random.fold_in(key, 1), (pairs,), 0, 1 << 20) % (slack + 1)
    sizes = sizes.at[1:1 + 2 * pairs:2].set(donor - passed).at[2:2 + 2 * pairs:2].set(taker + passed)
    return sizes[jax.random.permutation(jax.random.fold_in(key, 2), amount)]


def centred(rng, shape, deviation, most, shards=(), kind=jnp.bfloat16):
    drawn = deviation * jax.random.normal(rng, shape, jnp.float32)
    if shards:
        drawn = drawn * steps_of(rng, shape, shards, -0.22, 0.18)
    return jnp.clip(drawn, -most, most).astype(kind)


def setup_inputs(seed: int = 0) -> dict:
    splits = jax.random.split(jax.random.key(seed), 13)
    tokens = centred(splits[0], (N_FSDP, GROUP, D), 1.0, 6.0, ((0, 2), (1, 16)))
    lengths = jax.vmap(lambda own: uneven(own, NSEQ, GROUP, MAXLEN, 2))(jax.random.split(splits[1], N_FSDP)).reshape((N_FSDP, NSEQ)).astype(jnp.int32)
    dealing = jax.vmap(lambda own: jax.random.permutation(own, TOK_DEV))(jax.random.split(splits[2], N_FSDP * N_CTX)).reshape((N_FSDP, N_CTX, TOK_DEV)).astype(jnp.int32)
    attn_gain = jnp.clip(1.0 + 0.15 * jax.random.normal(splits[3], (D,), jnp.float32), 0.25, 1.75).astype(jnp.bfloat16)
    query_weight = centred(splits[4], (D, H * HD), D ** -0.5, 0.125, ((0, 2),))
    kv_weight = centred(splits[5], (D, 2 * HD), D ** -0.5, 0.125, ((0, 2),))
    out_weight = centred(splits[6], (H * HD, D), (H * HD * 4 // WINDOW) ** -0.5, 2.0, ((0, 2),))
    mlp_gain = jnp.clip(1.0 + 0.15 * jax.random.normal(splits[7], (D,), jnp.float32), 0.25, 1.75).astype(jnp.bfloat16)
    gate_weight = centred(splits[8], (D, FF), D ** -0.5, 0.125, ((0, 2),))
    up_weight = centred(splits[9], (D, FF), D ** -0.5, 0.125, ((0, 2),))
    down_weight = centred(splits[10], (FF, D), FF ** -0.5, 0.078125, ((0, 2),))
    cotangent = centred(splits[11], (N_FSDP, GROUP, D), 1.0, 6.0, ((0, 2), (1, 16)))
    return {"tokens": tokens, "lengths": lengths, "dealing": dealing, "attn_gain": attn_gain, "query_weight": query_weight, "kv_weight": kv_weight, "out_weight": out_weight, "mlp_gain": mlp_gain, "gate_weight": gate_weight, "up_weight": up_weight, "down_weight": down_weight, "cotangent": cotangent}


epsilon = 1e-06
neg_large = -1e+30

@jax.custom_vjp
def low(v):
    return lax.optimization_barrier(v.astype(jnp.bfloat16)).astype(jnp.float32)

@jax.custom_vjp
def low_back(v):
    return v

def low_keep(v):
    return (low(v), None)

def low_pass(kept, grad):
    return (grad,)

def back_keep(v):
    return (v, None)

def back_low(kept, grad):
    return (low(grad),)
low.defvjp(low_keep, low_pass)
low_back.defvjp(back_keep, back_low)

def precise_dot(left, right):
    return jnp.dot(left, right, precision=lax.Precision.HIGHEST)

def rms_norm(values, gain):
    return values * lax.rsqrt(lax.optimization_barrier(jnp.mean(values * values, axis=-1, keepdims=True)) + epsilon) * gain

def stream_rows(dealing_row):
    stream = jnp.arange(GROUP, dtype=jnp.int32)
    source = stream % TOK_DEV // PIECE
    send_slot = stream // TOK_DEV * PIECE + stream % PIECE
    return (source * TOK_DEV + dealing_row.reshape(-1)[source * TOK_DEV + send_slot]).astype(jnp.int32)

def segment_ids(length_row):
    seg_ends = jnp.cumsum(length_row).astype(jnp.int32)
    stream = jnp.arange(GROUP, dtype=jnp.int32)
    return lax.optimization_barrier(jnp.sum((stream[:, None] >= seg_ends[None, :]).astype(jnp.int32), axis=1))

def attend_row(stream_queries, stream_pairs, segment):
    padded_pairs = jnp.concatenate([jnp.zeros((WINDOW, 2 * HD), stream_pairs.dtype), stream_pairs], 0)
    padded_seg = jnp.concatenate([jnp.full((WINDOW,), -1, jnp.int32), segment.astype(jnp.int32)], 0)
    key_span = WINDOW + QBLK
    distance = jnp.arange(QBLK)[:, None] + WINDOW - jnp.arange(key_span)[None, :]

    def block(offset):
        query_block = lax.dynamic_slice_in_dim(stream_queries, offset, QBLK, 0).reshape(QBLK, H, HD)
        pair_block = lax.dynamic_slice_in_dim(padded_pairs, offset, key_span, 0)
        seg_query = lax.dynamic_slice_in_dim(padded_seg, offset + WINDOW, QBLK, 0)
        seg_key = lax.dynamic_slice_in_dim(padded_seg, offset, key_span, 0)
        allowed = (seg_query[:, None] == seg_key[None, :]) & (distance >= 0) & (distance < WINDOW)
        scores = jnp.einsum('qhd,kd->qhk', query_block, pair_block[:, :HD], precision=lax.Precision.HIGHEST)
        scores = low_back(scores * HD ** (-0.5))
        scores = jnp.where(allowed[:, None, :], scores, neg_large)
        row_max = lax.optimization_barrier(jnp.max(scores, axis=-1, keepdims=True))
        raised = jnp.exp(scores - row_max)
        attn_probs = raised / lax.optimization_barrier(jnp.sum(raised, axis=-1, keepdims=True))
        result = jnp.einsum('qhk,kd->qhd', low(attn_probs), pair_block[:, HD:], precision=lax.Precision.HIGHEST)
        return result.reshape(QBLK, H * HD)
    offsets = jnp.arange(GROUP // QBLK, dtype=jnp.int32) * QBLK
    return lax.map(jax.checkpoint(block), offsets).reshape(GROUP, H * HD)

def forward(inputs, attn_gain, query_weight, kv_weight, out_weight, mlp_gain, gate_weight, up_weight, down_weight, rows, segments):
    flat = inputs.reshape(N_FSDP * GROUP, D)
    normed = low(rms_norm(flat, attn_gain))
    queries = low_back(low(precise_dot(normed, query_weight))).reshape(N_FSDP, GROUP, H * HD)
    pairs = low_back(low(precise_dot(normed, kv_weight))).reshape(N_FSDP, GROUP, 2 * HD)
    contexts = []
    for batch in range(N_FSDP):
        order = rows[batch]
        stream_context = attend_row(queries[batch][order], pairs[batch][order], segments[batch])
        contexts.append(jnp.zeros((GROUP, H * HD), stream_context.dtype).at[order].set(stream_context))
    context = low_back(low(jnp.concatenate(contexts, 0)))
    branch = low_back(precise_dot(context, out_weight))
    resid = flat + branch
    normed_mlp = low(rms_norm(resid, mlp_gain))
    gate = low_back(precise_dot(normed_mlp, gate_weight))
    upward = low_back(precise_dot(normed_mlp, up_weight))
    hidden = low(jax.nn.gelu(gate, approximate=True) * upward)
    return (resid + precise_dot(hidden, down_weight)).reshape(N_FSDP, GROUP, D)

def reference(tokens, lengths, dealing, attn_gain, query_weight, kv_weight, out_weight, mlp_gain, gate_weight, up_weight, down_weight, cotangent):
    rows = jnp.stack([stream_rows(dealing[batch]) for batch in range(N_FSDP)])
    segments = jnp.stack([segment_ids(lengths[batch]) for batch in range(N_FSDP)])
    params = tuple((value.astype(jnp.float32) for value in (tokens, attn_gain, query_weight, kv_weight, out_weight, mlp_gain, gate_weight, up_weight, down_weight)))

    def apply_block(*values):
        return forward(*values, rows, segments)
    output, pullback = jax.vjp(apply_block, *params)
    grads = pullback(cotangent.astype(jnp.float32))
    return (output.astype(jnp.bfloat16), grads[0], grads[1], grads[2], grads[3], grads[4], grads[5], grads[6], grads[7], grads[8])
```

```python
import functools

import jax
import jax.numpy as jnp
from jax import lax
from jax.experimental import pallas as pl
from jax.experimental.pallas import tpu as pltpu
from jax.sharding import Mesh
from jax.sharding import PartitionSpec as P

H = 16
HD = 128
WINDOW = 1024
QBLK = 128
HEADS_STEP = 4
SPAN = WINDOW + QBLK
ROWS = HEADS_STEP * QBLK

epsilon = 1e-06
neg_large = -1e30
scale = HD ** (-0.5)
BF = jnp.bfloat16
F32 = jnp.float32
CTX = ("a", "b", "c")
ALL = ("a", "b", "c", "x")


def mm(left, right):
    return jnp.dot(left, right, preferred_element_type=F32)


def mm_tn(left, right):
    return lax.dot_general(left, right, (((0,), (0,)), ((), ())), preferred_element_type=F32)


def mm_nt(left, right):
    return lax.dot_general(left, right, (((1,), (1,)), ((), ())), preferred_element_type=F32)


def stack_heads(block):
    return jnp.concatenate([block[:, h * HD : (h + 1) * HD] for h in range(HEADS_STEP)], 0)


def unstack_heads(block_t):
    return jnp.concatenate(
        [block_t[:, h * QBLK : (h + 1) * QBLK].T for h in range(HEADS_STEP)], 1
    )


def bias_of(lo_ref, qb):
    key = lax.broadcasted_iota(jnp.int32, (SPAN, QBLK), 0) + qb * QBLK
    query = lax.broadcasted_iota(jnp.int32, (SPAN, QBLK), 1) + (WINDOW + qb * QBLK)
    allowed = (key >= lo_ref[...]) & (key <= query)
    bias = jnp.where(allowed, 0.0, neg_large).astype(F32)
    return jnp.concatenate([bias] * HEADS_STEP, 1)


def attend_kernel(lo_ref, q_ref, kv_ref, o_ref, lse_ref):
    qb = pl.program_id(0)
    rows = pl.ds(pl.multiple_of(qb * QBLK, QBLK), SPAN)
    keys = kv_ref[rows, :HD]
    values = kv_ref[rows, HD:]
    scores = mm_nt(keys, stack_heads(q_ref[...])) * scale + bias_of(lo_ref, qb)
    top = jnp.max(scores, axis=0, keepdims=True)
    raised = jnp.exp(scores - top)
    total = jnp.sum(raised, axis=0, keepdims=True)
    out_t = mm_tn(values, raised.astype(BF)) * (1.0 / total)
    o_ref[...] = unstack_heads(out_t).astype(BF)
    lse_ref[0] = top + jnp.log(total)


def attend_back_kernel(lo_ref, q_ref, kv_ref, do_ref, lse_ref, dq_ref, dkv_ref):
    qb = pl.program_id(0)

    @pl.when((qb == 0) & (pl.program_id(1) == 0))
    def _():
        dkv_ref[...] = jnp.zeros_like(dkv_ref)

    rows = pl.ds(pl.multiple_of(qb * QBLK, QBLK), SPAN)
    keys = kv_ref[rows, :HD]
    values = kv_ref[rows, HD:]
    queries = stack_heads(q_ref[...])
    d_out = stack_heads(do_ref[...])
    scores = mm_nt(keys, queries) * scale + bias_of(lo_ref, qb)
    probs = jnp.exp(scores - lse_ref[0])
    d_probs = mm_nt(values, d_out)
    delta = jnp.sum(probs * d_probs, axis=0, keepdims=True)
    d_scores = (probs * (d_probs - delta)).astype(BF)
    dq_ref[...] = unstack_heads(mm_tn(keys, d_scores) * scale).astype(BF)
    dkv_ref[rows, :HD] += mm(d_scores, queries) * scale
    dkv_ref[rows, HD:] += mm(probs.astype(BF), d_out)


def attend(queries, window, low):
    tok = queries.shape[0]
    groups = H // HEADS_STEP
    blocks = tok // QBLK
    return pl.pallas_call(
        attend_kernel,
        grid=(blocks, groups),
        in_specs=[
            pl.BlockSpec((1, QBLK), lambda i, j: (0, i)),
            pl.BlockSpec((QBLK, HEADS_STEP * HD), lambda i, j: (i, j)),
            pl.BlockSpec((WINDOW + tok, 2 * HD), lambda i, j: (0, 0)),
        ],
        out_specs=[
            pl.BlockSpec((QBLK, HEADS_STEP * HD), lambda i, j: (i, j)),
            pl.BlockSpec((1, 1, ROWS), lambda i, j: (i * groups + j, 0, 0)),
        ],
        out_shape=[
            jax.ShapeDtypeStruct((tok, H * HD), BF),
            jax.ShapeDtypeStruct((blocks * groups, 1, ROWS), F32),
        ],
        compiler_params=pltpu.CompilerParams(vmem_limit_bytes=48 * 1024 * 1024),
        cost_estimate=pl.CostEstimate(
            flops=4 * tok * H * HD * SPAN, bytes_accessed=4 * 1024 * 1024, transcendentals=0
        ),
        name="attend",
    )(low, queries, window)


def attend_back(queries, window, low, d_context, lse):
    tok = queries.shape[0]
    groups = H // HEADS_STEP
    blocks = tok // QBLK
    return pl.pallas_call(
        attend_back_kernel,
        grid=(blocks, groups),
        in_specs=[
            pl.BlockSpec((1, QBLK), lambda i, j: (0, i)),
            pl.BlockSpec((QBLK, HEADS_STEP * HD), lambda i, j: (i, j)),
            pl.BlockSpec((WINDOW + tok, 2 * HD), lambda i, j: (0, 0)),
            pl.BlockSpec((QBLK, HEADS_STEP * HD), lambda i, j: (i, j)),
            pl.BlockSpec((1, 1, ROWS), lambda i, j: (i * groups + j, 0, 0)),
        ],
        out_specs=[
            pl.BlockSpec((QBLK, HEADS_STEP * HD), lambda i, j: (i, j)),
            pl.BlockSpec((WINDOW + tok, 2 * HD), lambda i, j: (0, 0)),
        ],
        out_shape=[
            jax.ShapeDtypeStruct((tok, H * HD), BF),
            jax.ShapeDtypeStruct((WINDOW + tok, 2 * HD), F32),
        ],
        compiler_params=pltpu.CompilerParams(vmem_limit_bytes=48 * 1024 * 1024),
        cost_estimate=pl.CostEstimate(
            flops=10 * tok * H * HD * SPAN, bytes_accessed=6 * 1024 * 1024, transcendentals=0
        ),
        name="attend_back",
    )(low, queries, window, d_context, lse)


def ring_order(size_a, size_b):
    if size_b == 1:
        return [a for a in range(size_a)]
    order = [(a, 0) for a in range(size_a)]
    forward = True
    for a in reversed(range(size_a)):
        columns = range(1, size_b) if forward else reversed(range(1, size_b))
        order += [(a, b) for b in columns]
        forward = not forward
    return [a * size_b + b for a, b in order]


def norm_stats(values):
    inv = lax.rsqrt(jnp.mean(values * values, axis=-1, keepdims=True) + epsilon)
    return values * inv, inv


def norm_back(unit, inv, gain, grad):
    scaled = grad * gain
    inner = jnp.mean(scaled * unit, axis=-1, keepdims=True)
    return inv * (scaled - unit * inner), jnp.sum(grad * unit, axis=0)


def on_device(
    sizes,
    tokens,
    lengths,
    dealing,
    attn_gain,
    query_weight,
    kv_weight,
    out_weight,
    mlp_gain,
    gate_weight,
    up_weight,
    down_weight,
    cotangent,
):
    size_a, size_b, size_x = sizes
    chips = size_a * size_b
    n_ctx = chips * 2
    ranks = 2 * size_x
    ia, ib, ic, ix = (lax.axis_index(name) for name in ALL)
    chip = ia * size_b + ib
    own = chip * 2 + ic
    flat = own * size_x + ix
    rank = ix * 2 + ic
    tok = tokens.shape[1]
    width = tokens.shape[2]
    piece = tok // n_ctx
    halo = WINDOW // tok
    swap = [(0, 1), (1, 0)]

    def pick(array, index, axis=0):
        return lax.dynamic_index_in_dim(array, index, axis, keepdims=False)

    def put(array, part, index, axis=0):
        return lax.dynamic_update_index_in_dim(array, part, index, axis)

    def to_core(array):
        return lax.ppermute(array, "c", swap)

    def to_x(array, step):
        return lax.ppermute(array, "x", [(i, (i + step) % size_x) for i in range(size_x)])

    def shift_ctx(array, step):
        pairs = [(i, i + step) for i in range(n_ctx) if 0 <= i + step < n_ctx]
        return lax.ppermute(array, CTX, pairs)

    def from_x(step):
        return (ix + size_x - step) % size_x

    def whole_weight(shard):
        rows, cols = shard.shape
        halves = shard.reshape(2, rows // 2, cols)
        full = jnp.zeros((size_x, 2, rows // 2, cols), shard.dtype)
        full = lax.dynamic_update_slice(full, halves[None], (ix, 0, 0, 0))
        mine = pick(halves, ic)
        for step in range(1, size_x):
            got = to_x(mine, step)
            other = to_core(got)
            full = lax.dynamic_update_slice(full, got[None, None], (from_x(step), ic, 0, 0))
            full = lax.dynamic_update_slice(full, other[None, None], (from_x(step), 1 - ic, 0, 0))
        return full.reshape(size_x * rows, cols)

    def rank_columns(shard):
        rows, cols = shard.shape
        part = cols // ranks
        own_part = lax.dynamic_slice(shard, (0, rank * part), (rows, part))
        full = jnp.zeros((size_x, rows, part), shard.dtype)
        full = put(full, own_part, ix)
        for step in range(1, size_x):
            target = ((ix + step) % size_x) * 2 + ic
            got = to_x(lax.dynamic_slice(shard, (0, target * part), (rows, part)), step)
            full = put(full, got, from_x(step))
        return full.reshape(size_x * rows, part)

    def group_rows(array):
        parts = [array, to_core(array)]
        for step in range(1, size_x):
            got = to_x(array, step)
            parts += [got, to_core(got)]
        return jnp.concatenate(parts, 0)

    def group_columns(array):
        part = array.shape[1] // ranks
        view = array.reshape(tok, size_x, 2, part)
        kept = pick(view, ic, 2)
        got = to_core(pick(view, 1 - ic, 2))
        both = jnp.stack([kept, got])
        parts = [pick(both, ix, 2).reshape(2 * tok, part)]
        for step in range(1, size_x):
            sent = pick(both, (ix + step) % size_x, 2).reshape(2 * tok, part)
            parts.append(to_x(sent, step))
        return jnp.concatenate(parts, 0)

    def group_sum(part_of):
        total = None
        for step in list(range(1, size_x)) + [0]:
            both = part_of(step)
            summed = both[:tok] + to_core(both[tok:].astype(BF)).astype(F32)
            if step:
                summed = to_x(summed.astype(BF), size_x - step).astype(F32)
            total = summed if total is None else total + summed
        return total

    order = ring_order(size_a, size_b)
    place = [order.index(g) for g in range(chips)]
    position = jnp.asarray(place, jnp.int32)[chip]
    onward = [(order[p], order[(p + 1) % chips]) for p in range(chips)]
    backward = [(order[p], order[(p - 1) % chips]) for p in range(chips)]

    def ring_sum(chunks, slots):
        rows = chunks.shape[1]
        chunk_at = jnp.asarray([slots[g] for g in order], jnp.int32)
        half = rows // 2
        held_f = held_b = None
        for step in range(1, chips + 1):
            at_f = chunk_at[(position + 2 * chips - step) % chips]
            at_b = chunk_at[(position + step) % chips]
            part_f = lax.dynamic_slice(
                chunks, (at_f, 0, 0), (1, half, chunks.shape[2])
            )[0].astype(F32)
            part_b = lax.dynamic_slice(
                chunks, (at_b, half, 0), (1, rows - half, chunks.shape[2])
            )[0].astype(F32)
            if step > 1:
                part_f = part_f + held_f.astype(F32)
                part_b = part_b + held_b.astype(F32)
            if step == chips:
                return jnp.concatenate([part_f, part_b], 0)
            held_f = lax.ppermute(part_f.astype(BF), ("a", "b"), onward)
            held_b = lax.ppermute(part_b.astype(BF), ("a", "b"), backward)

    if (size_a, size_b, size_x) == (4, 2, 2):
        slot = [(g % 2) * 4 + ((g // 2) % 2) * 2 + (g // 2) // 2 for g in range(chips)]
    else:
        slot = list(range(chips))
    keep_pairs = []
    for g in range(chips):
        for c in range(2):
            for x in range(size_x):
                keep_pairs.append(((g * 2 + c) * size_x + x, (x * 2 + c) * chips + slot[g]))

    def sum_rows(grad):
        chunks = grad.astype(BF).reshape(chips, grad.shape[0] // chips, grad.shape[1])
        summed = ring_sum(chunks, slot)
        return lax.ppermute(summed.astype(BF), ALL, keep_pairs).astype(F32)

    def sum_columns(grad):
        rows, part = grad.shape
        chunks = grad.astype(BF).reshape(chips, rows // chips, part)
        summed = ring_sum(chunks, list(range(chips))).astype(BF).reshape(2, size_x, rows // (chips * ranks), part)
        both = jnp.zeros((2,) + summed.shape[1:], BF)
        both = put(both, pick(summed, ic), ic)
        both = put(both, to_core(pick(summed, 1 - ic)), 1 - ic)
        full = jnp.zeros((size_x, 2) + summed.shape[2:], BF)
        full = put(full, pick(both, ix, 1), ix)
        for step in range(1, size_x):
            full = put(full, to_x(pick(both, (ix + step) % size_x, 1), step), from_x(step))
        return full.transpose(2, 0, 1, 3).reshape(-1, ranks * part).astype(F32)

    def sum_gain(grad):
        for name, size in (("c", 2), ("x", size_x), ("b", size_b), ("a", size_a)):
            step = 1
            while step < size:
                grad = grad + lax.ppermute(grad, name, [(i, i ^ step) for i in range(size)])
                step *= 2
        part = grad.shape[0] // (n_ctx * size_x)
        return lax.dynamic_slice(grad, (flat * part,), (part,))

    own_deal = pick(dealing[0], own)
    deal = (own_deal[:, None] == jnp.arange(tok, dtype=jnp.int32)[None, :]).astype(BF)

    def to_stream(array):
        return lax.all_to_all(
            mm(deal, array).astype(BF), CTX, split_axis=0, concat_axis=0, tiled=True
        )

    def from_stream(array):
        dealt = lax.all_to_all(array, CTX, split_axis=0, concat_axis=0, tiled=True)
        return mm_tn(deal, dealt)

    gains = whole_weight(jnp.stack([attn_gain, mlp_gain], 1).reshape(-1, 2)).astype(F32)
    gain_one = gains[:, 0]
    gain_two = gains[:, 1]
    inputs_low = to_stream(tokens[0])
    w_query = whole_weight(query_weight)
    w_kv = whole_weight(kv_weight)
    w_out = whole_weight(out_weight)
    cot = to_stream(cotangent[0])
    w_gate = rank_columns(gate_weight)
    w_up = rank_columns(up_weight)
    down_part = down_weight.shape[0] // 2
    w_down = lax.dynamic_slice(down_weight, (ic * down_part, 0), (down_part, width))

    inputs = inputs_low.astype(F32)
    unit_one, inv_one = norm_stats(inputs)
    normed = (unit_one * gain_one).astype(BF)
    pairs = mm(normed, w_kv).astype(BF)
    window = jnp.concatenate([shift_ctx(pairs, halo - j) for j in range(halo)] + [pairs], 0)
    queries = mm(normed, w_query).astype(BF)
    stream = own * tok + jnp.arange(tok, dtype=jnp.int32)
    ends = jnp.cumsum(lengths[0])
    starts = jnp.max(jnp.where(stream[:, None] >= ends[None, :], ends[None, :], 0), axis=1)
    low = jnp.maximum(starts, stream - (WINDOW - 1)) - (own * tok - WINDOW)
    low = low.astype(jnp.int32)[None, :]
    context, lse = attend(queries, window, low)
    resid = inputs + mm(context, w_out)

    unit_two, inv_two = norm_stats(resid)
    normed_mlp = group_rows((unit_two * gain_two).astype(BF))
    cot_rows = group_rows(cot)
    gate = mm(normed_mlp, w_gate)
    upward = mm(normed_mlp, w_up)
    d_hidden = mm_nt(cot_rows, w_down)
    act, pull = jax.vjp(lambda v: jax.nn.gelu(v, approximate=True), gate)
    hidden = (act * upward).astype(BF)
    d_gate = pull(d_hidden * upward)[0].astype(BF)
    d_upward = (d_hidden * act).astype(BF)

    def rows_of(array, step):
        return array[2 * step * tok : 2 * (step + 1) * tok]

    d_normed_mlp = group_sum(
        lambda step: mm_nt(rows_of(d_gate, step), w_gate) + mm_nt(rows_of(d_upward, step), w_up)
    )
    down_grad = sum_rows(mm_tn(hidden, cot_rows))
    gate_grad = sum_columns(mm_tn(normed_mlp, d_gate))
    up_grad = sum_columns(mm_tn(normed_mlp, d_upward))
    branch_mlp = group_sum(lambda step: mm(rows_of(hidden, step), w_down))
    block_output = from_stream((resid + branch_mlp).astype(BF)).astype(BF)
    d_resid_part, mlp_gain_grad = norm_back(unit_two, inv_two, gain_two, d_normed_mlp)
    mlp_gain_grad = sum_gain(mlp_gain_grad)
    d_resid = cot.astype(F32) + d_resid_part
    d_branch = d_resid.astype(BF)

    d_context = mm_nt(d_branch, w_out).astype(BF)
    out_grad = sum_rows(mm_tn(group_columns(context), group_rows(d_branch)))
    d_queries, d_window = attend_back(queries, window, low, d_context, lse)
    d_pairs = d_window[halo * tok :]
    for j in range(halo):
        part = d_window[j * tok : (j + 1) * tok].astype(BF)
        d_pairs = d_pairs + shift_ctx(part, j - halo).astype(F32)
    d_pairs = d_pairs.astype(BF)
    normed_rows = group_rows(normed)
    query_grad = sum_columns(mm_tn(normed_rows, group_columns(d_queries)))
    kv_part = width // ranks
    normed_part = lax.dynamic_slice(normed_rows, (0, rank * kv_part), (ranks * tok, kv_part))
    kv_grad = sum_rows(mm_tn(normed_part, group_rows(d_pairs)))
    d_normed = mm_nt(d_queries, w_query) + mm_nt(d_pairs, w_kv)
    d_inputs, attn_gain_grad = norm_back(unit_one, inv_one, gain_one, d_normed)
    attn_gain_grad = sum_gain(attn_gain_grad)
    token_grad = from_stream((d_resid + d_inputs).astype(BF))
    return (
        block_output[None],
        token_grad[None],
        attn_gain_grad,
        query_grad,
        kv_grad,
        out_grad,
        mlp_gain_grad,
        gate_grad,
        up_grad,
        down_grad,
    )


def solution(mesh):
    n_ctx, size_x = mesh.shape["ctx"], mesh.shape["fsdp"]
    chips = n_ctx // 2
    size_a = 4 if chips % 4 == 0 else chips
    size_b = chips // size_a
    fine = Mesh(mesh.devices.reshape(size_a, size_b, 2, size_x), ALL)
    rows = P("x", CTX, None)
    split = P("x", None)
    every = P(ALL)
    matrix = P(ALL, None)
    return jax.shard_map(
        functools.partial(on_device, (size_a, size_b, size_x)),
        mesh=fine,
        in_specs=(
            rows,
            split,
            P("x", None, None),
            P("x"),
            split,
            split,
            split,
            P("x"),
            split,
            split,
            split,
            rows,
        ),
        out_specs=(rows, rows, every, matrix, matrix, matrix, every, matrix, matrix, matrix),
        check_vma=False,
    )
```

```python
import functools

import jax
import jax.numpy as jnp
from jax import lax
from jax.experimental import pallas as pl
from jax.experimental.pallas import tpu as pltpu
from jax.sharding import Mesh
from jax.sharding import PartitionSpec as P

H = 16
HD = 128
WINDOW = 1024
QBLK = 128
HEADS_STEP = 4
SPAN = WINDOW + QBLK
ROWS = HEADS_STEP * QBLK

epsilon = 1e-06
neg_large = -1e30
scale = HD ** (-0.5)
BF = jnp.bfloat16
F32 = jnp.float32
CTX = ("a", "b", "c")
ALL = ("a", "b", "c", "x")
MESH = pl.DeviceIdType.MESH


def mm(left, right):
    return jnp.dot(left, right, preferred_element_type=F32)


def mm_tn(left, right):
    return lax.dot_general(left, right, (((0,), (0,)), ((), ())), preferred_element_type=F32)


def mm_nt(left, right):
    return lax.dot_general(left, right, (((1,), (1,)), ((), ())), preferred_element_type=F32)


def stack_heads(block):
    return jnp.concatenate([block[:, h * HD : (h + 1) * HD] for h in range(HEADS_STEP)], 0)


def unstack_heads(block_t):
    return jnp.concatenate(
        [block_t[:, h * QBLK : (h + 1) * QBLK].T for h in range(HEADS_STEP)], 1
    )


def bias_of(lo_ref, qb):
    key = lax.broadcasted_iota(jnp.int32, (SPAN, QBLK), 0) + qb * QBLK
    query = lax.broadcasted_iota(jnp.int32, (SPAN, QBLK), 1) + (WINDOW + qb * QBLK)
    allowed = (key >= lo_ref[...]) & (key <= query)
    bias = jnp.where(allowed, 0.0, neg_large).astype(F32)
    return jnp.concatenate([bias] * HEADS_STEP, 1)


def attend_kernel(lo_ref, q_ref, kv_ref, o_ref, lse_ref):
    qb = pl.program_id(0)
    rows = pl.ds(pl.multiple_of(qb * QBLK, QBLK), SPAN)
    keys = kv_ref[rows, :HD]
    values = kv_ref[rows, HD:]
    scores = mm_nt(keys, stack_heads(q_ref[...])) * scale + bias_of(lo_ref, qb)
    top = jnp.max(scores, axis=0, keepdims=True)
    raised = jnp.exp(scores - top)
    total = jnp.sum(raised, axis=0, keepdims=True)
    out_t = mm_tn(values, raised.astype(BF)) * (1.0 / total)
    o_ref[...] = unstack_heads(out_t).astype(BF)
    lse_ref[0] = top + jnp.log(total)


def attend_back_kernel(lo_ref, q_ref, kv_ref, do_ref, lse_ref, dq_ref, dkv_ref):
    qb = pl.program_id(0)

    @pl.when((qb == 0) & (pl.program_id(1) == 0))
    def _():
        dkv_ref[...] = jnp.zeros_like(dkv_ref)

    rows = pl.ds(pl.multiple_of(qb * QBLK, QBLK), SPAN)
    keys = kv_ref[rows, :HD]
    values = kv_ref[rows, HD:]
    queries = stack_heads(q_ref[...])
    d_out = stack_heads(do_ref[...])
    scores = mm_nt(keys, queries) * scale + bias_of(lo_ref, qb)
    probs = jnp.exp(scores - lse_ref[0])
    d_probs = mm_nt(values, d_out)
    delta = jnp.sum(probs * d_probs, axis=0, keepdims=True)
    d_scores = (probs * (d_probs - delta)).astype(BF)
    dq_ref[...] = unstack_heads(mm_tn(keys, d_scores) * scale).astype(BF)
    dkv_ref[rows, :HD] += mm(d_scores, queries) * scale
    dkv_ref[rows, HD:] += mm(probs.astype(BF), d_out)


def attend(queries, window, low):
    tok = queries.shape[0]
    groups = H // HEADS_STEP
    blocks = tok // QBLK
    return pl.pallas_call(
        attend_kernel,
        grid=(blocks, groups),
        in_specs=[
            pl.BlockSpec((1, QBLK), lambda i, j: (0, i)),
            pl.BlockSpec((QBLK, HEADS_STEP * HD), lambda i, j: (i, j)),
            pl.BlockSpec((WINDOW + tok, 2 * HD), lambda i, j: (0, 0)),
        ],
        out_specs=[
            pl.BlockSpec((QBLK, HEADS_STEP * HD), lambda i, j: (i, j)),
            pl.BlockSpec((1, 1, ROWS), lambda i, j: (i * groups + j, 0, 0)),
        ],
        out_shape=[
            jax.ShapeDtypeStruct((tok, H * HD), BF),
            jax.ShapeDtypeStruct((blocks * groups, 1, ROWS), F32),
        ],
        compiler_params=pltpu.CompilerParams(vmem_limit_bytes=48 * 1024 * 1024),
        cost_estimate=pl.CostEstimate(
            flops=4 * tok * H * HD * SPAN, bytes_accessed=4 * 1024 * 1024, transcendentals=0
        ),
        name="attend",
    )(low, queries, window)


def attend_back(queries, window, low, d_context, lse):
    tok = queries.shape[0]
    groups = H // HEADS_STEP
    blocks = tok // QBLK
    return pl.pallas_call(
        attend_back_kernel,
        grid=(blocks, groups),
        in_specs=[
            pl.BlockSpec((1, QBLK), lambda i, j: (0, i)),
            pl.BlockSpec((QBLK, HEADS_STEP * HD), lambda i, j: (i, j)),
            pl.BlockSpec((WINDOW + tok, 2 * HD), lambda i, j: (0, 0)),
            pl.BlockSpec((QBLK, HEADS_STEP * HD), lambda i, j: (i, j)),
            pl.BlockSpec((1, 1, ROWS), lambda i, j: (i * groups + j, 0, 0)),
        ],
        out_specs=[
            pl.BlockSpec((QBLK, HEADS_STEP * HD), lambda i, j: (i, j)),
            pl.BlockSpec((WINDOW + tok, 2 * HD), lambda i, j: (0, 0)),
        ],
        out_shape=[
            jax.ShapeDtypeStruct((tok, H * HD), BF),
            jax.ShapeDtypeStruct((WINDOW + tok, 2 * HD), F32),
        ],
        compiler_params=pltpu.CompilerParams(vmem_limit_bytes=48 * 1024 * 1024),
        cost_estimate=pl.CostEstimate(
            flops=10 * tok * H * HD * SPAN, bytes_accessed=6 * 1024 * 1024, transcendentals=0
        ),
        name="attend_back",
    )(low, queries, window, d_context, lse)


def snake(pos, size_a, size_b):
    if size_b == 1:
        return pos, pos * 0
    down = pos // size_a
    first = 1 - (down + 7) // 8
    q = (pos - size_a) * (1 - first)
    a_up = size_a - 1 - q // (size_b - 1)
    k = q % (size_b - 1)
    odd = a_up % 2
    b_up = odd * (1 + k) + (1 - odd) * (size_b - 1 - k)
    return first * pos + (1 - first) * a_up, (1 - first) * b_up


def snake_place(a, b, size_a, size_b):
    if size_b == 1:
        return a
    moved = (b + size_b - 1) // size_b
    odd = a % 2
    along = odd * (b - 1) + (1 - odd) * (size_b - 1 - b)
    return (1 - moved) * a + moved * (size_a + (size_a - 1 - a) * (size_b - 1) + along)


def kept_slot(a, b, size_a, size_b):
    half = size_a * size_b // 2
    return (1 - b % 2) * half + a * (size_b // 2) + b // 2


class Job:
    def __init__(self, phase, left, right, rows, cols, by_rank):
        self.phase, self.left, self.right = phase, left, right
        self.rows, self.cols, self.by_rank = rows, cols, by_rank


def grads_kernel(sizes, jobs, n_left, n_right, *refs):
    size_a, size_b, size_x = sizes
    chips = size_a * size_b
    ranks = 2 * size_x
    count = len(jobs)
    lefts_in, refs = refs[:n_left], refs[n_left:]
    rights_in, refs = refs[:n_right], refs[n_right:]
    outs, refs = refs[:count], refs[count:]
    lefts, refs = refs[:n_left], refs[n_left:]
    rights, refs = refs[:n_right], refs[n_right:]
    recv, refs = refs[:count], refs[count:]
    send, refs = refs[:count], refs[count:]
    done, refs = refs[:count], refs[count:]
    load_sem, send_sem, recv_sem, done_send, done_recv, own_sem = refs
    ia, ib, ic, ix = (lax.axis_index(name) for name in ALL)
    rank = ix * 2 + ic
    place = snake_place(ia, ib, size_a, size_b)

    def on_ring(step):
        return snake((place + 2 * chips + step) % chips, size_a, size_b)

    def member(k):
        return (ic + k // size_x) % 2, (ix + k % size_x) % size_x

    kept = rank * chips + kept_slot(ia, ib, size_a, size_b)
    kept_chip = kept // ranks
    kept_id = (kept_chip // size_b, kept_chip % size_b, (kept // size_x) % 2, kept % size_x)
    flat = ((ia * size_b + ib) * 2 + ic) * size_x + ix
    from_rank = flat // chips
    from_slot = flat % chips
    half = chips // 2
    from_id = (
        (from_slot % half) // (size_b // 2),
        ((from_slot % half) % (size_b // 2)) * 2 + 1 - from_slot // half,
        from_rank % 2,
        from_rank // 2,
    )

    loads = []
    for i, (src, dst) in enumerate(zip(lefts_in + rights_in, lefts + rights)):
        loads.append(pltpu.make_async_copy(src, dst, load_sem.at[i]))
    for copy in loads:
        copy.start()

    barrier = pltpu.get_barrier_semaphore()
    greeted = [on_ring(1) + (ic, ix), on_ring(-1) + (ic, ix), from_id]
    greeted += [(ia, ib) + member(k) for k in range(1, ranks)]
    for device in greeted:
        pl.semaphore_signal(barrier, inc=1, device_id=device, device_id_type=MESH)
    pl.semaphore_wait(barrier, len(greeted))

    def ring_copy(j, way, step, parity):
        neighbour = on_ring(1 - 2 * way) + (ic, ix)
        return pltpu.make_async_remote_copy(
            src_ref=send[j].at[way, parity],
            dst_ref=recv[j].at[way, step],
            send_sem=send_sem.at[j, way, parity],
            recv_sem=recv_sem.at[j, way, step],
            device_id=neighbour,
            device_id_type=MESH,
        )

    def product(j, way, step):
        job = jobs[j]
        a, b = on_ring(step * (2 * way - 1))
        part = job.rows // chips
        if job.by_rank:
            start = kept_slot(a, b, size_a, size_b) * part
            if lefts[job.left].shape[0] != job.rows:
                start = start + rank * job.rows
        else:
            start = (a * size_b + b) * part
        cols = job.cols // 2
        left = lefts[job.left][pl.ds(pl.multiple_of(start, part), part), :]
        return jnp.dot(
            left, rights[job.right][:, way * cols : (way + 1) * cols], preferred_element_type=F32
        )

    def deliver(j):
        job = jobs[j]
        if job.by_rank:
            return [
                pltpu.make_async_remote_copy(
                    src_ref=done[j],
                    dst_ref=outs[j],
                    send_sem=done_send.at[j, 0],
                    recv_sem=done_recv.at[j, 0],
                    device_id=kept_id,
                    device_id_type=MESH,
                )
            ]
        part = job.rows // (chips * ranks)
        copies = []
        for k in range(1, ranks):
            c, x = member(k)
            start = pl.multiple_of((c * size_x + x) * part, part)
            copies.append(
                pltpu.make_async_remote_copy(
                    src_ref=done[j].at[pl.ds(start, part), :],
                    dst_ref=outs[j].at[rank],
                    send_sem=done_send.at[j, k],
                    recv_sem=done_recv.at[j, k],
                    device_id=(ia, ib, c, x),
                    device_id_type=MESH,
                )
            )
        start = pl.multiple_of((ic * size_x + ix) * part, part)
        copies.append(
            pltpu.make_async_copy(done[j].at[pl.ds(start, part), :], outs[j].at[rank], own_sem.at[j])
        )
        return copies

    loaded = set()
    for phase in range(1 + max(job.phase for job in jobs)):
        mine = [j for j in range(count) if jobs[j].phase == phase]
        for j in mine:
            for i in (jobs[j].left, n_left + jobs[j].right):
                if i not in loaded:
                    loaded.add(i)
                    loads[i].wait()
            for way in range(2):
                send[j][way, 0] = product(j, way, 1).astype(BF)
                ring_copy(j, way, 0, 0).start()

        def step_of(step, carry):
            parity = step % 2
            for j in mine:
                for way in range(2):
                    part = product(j, way, step + 1)
                    ring_copy(j, way, step - 1, 1 - parity).wait_recv()
                    part = part + recv[j][way, step - 1].astype(F32)

                    @pl.when(step >= 2)
                    def _():
                        ring_copy(j, way, step - 2, parity).wait_send()

                    send[j][way, parity] = part.astype(BF)
                    ring_copy(j, way, step, parity).start()
            return carry

        lax.fori_loop(1, chips - 1, step_of, 0)
        last = chips - 2
        for j in mine:
            cols = jobs[j].cols // 2
            for way in range(2):
                part = product(j, way, chips)
                ring_copy(j, way, last, last % 2).wait_recv()
                part = part + recv[j][way, last].astype(F32)
                done[j][:, way * cols : (way + 1) * cols] = part.astype(BF)
            for copy in deliver(j):
                copy.start()
            for way in range(2):
                ring_copy(j, way, last - 1, (last - 1) % 2).wait_send()
                ring_copy(j, way, last, last % 2).wait_send()
    for j in range(count):
        for copy in deliver(j):
            copy.wait()


def sum_grads(sizes, jobs, lefts, rights):
    size_a, size_b, size_x = sizes
    chips = size_a * size_b
    ranks = 2 * size_x
    outs, recv, send, done = [], [], [], []
    flops = 0
    for job in jobs:
        part = job.rows // chips
        if job.by_rank:
            outs.append(jax.ShapeDtypeStruct((part, job.cols), BF))
        else:
            outs.append(jax.ShapeDtypeStruct((ranks, part // ranks, job.cols), BF))
        recv.append(pltpu.VMEM((2, chips - 1, part, job.cols // 2), BF))
        send.append(pltpu.VMEM((2, 2, part, job.cols // 2), BF))
        done.append(pltpu.VMEM((part, job.cols), BF))
        flops += 2 * job.rows * job.cols * rights[job.right].shape[0]
    count = len(jobs)
    sem = pltpu.SemaphoreType.DMA
    return pl.pallas_call(
        functools.partial(grads_kernel, sizes, jobs, len(lefts), len(rights)),
        in_specs=[pl.BlockSpec(memory_space=pl.ANY)] * (len(lefts) + len(rights)),
        out_specs=[pl.BlockSpec(memory_space=pl.ANY)] * count,
        out_shape=outs,
        scratch_shapes=[pltpu.VMEM(a.shape, BF) for a in lefts + rights]
        + recv
        + send
        + done
        + [
            sem((len(lefts) + len(rights),)),
            sem((count, 2, 2)),
            sem((count, 2, chips - 1)),
            sem((count, ranks)),
            sem((count, ranks)),
            sem((count,)),
        ],
        compiler_params=pltpu.CompilerParams(
            collective_id=0, has_side_effects=True, vmem_limit_bytes=60 * 1024 * 1024
        ),
        cost_estimate=pl.CostEstimate(
            flops=flops, bytes_accessed=400 * 1024 * 1024, transcendentals=0
        ),
        name="sum_grads",
    )(*lefts, *rights)


def norm_stats(values):
    inv = lax.rsqrt(jnp.mean(values * values, axis=-1, keepdims=True) + epsilon)
    return values * inv, inv


def norm_back(unit, inv, gain, grad):
    scaled = grad * gain
    inner = jnp.mean(scaled * unit, axis=-1, keepdims=True)
    return inv * (scaled - unit * inner), jnp.sum(grad * unit, axis=0)


def on_device(
    sizes,
    tokens,
    lengths,
    dealing,
    attn_gain,
    query_weight,
    kv_weight,
    out_weight,
    mlp_gain,
    gate_weight,
    up_weight,
    down_weight,
    cotangent,
):
    size_a, size_b, size_x = sizes
    chips = size_a * size_b
    n_ctx = chips * 2
    ranks = 2 * size_x
    ia, ib, ic, ix = (lax.axis_index(name) for name in ALL)
    chip = ia * size_b + ib
    own = chip * 2 + ic
    flat = own * size_x + ix
    rank = ix * 2 + ic
    tok = tokens.shape[1]
    width = tokens.shape[2]
    piece = tok // n_ctx
    halo = WINDOW // tok
    swap = [(0, 1), (1, 0)]

    def pick(array, index, axis=0):
        return lax.dynamic_index_in_dim(array, index, axis, keepdims=False)

    def put(array, part, index, axis=0):
        return lax.dynamic_update_index_in_dim(array, part, index, axis)

    def to_core(array):
        return lax.ppermute(array, "c", swap)

    def to_x(array, step):
        return lax.ppermute(array, "x", [(i, (i + step) % size_x) for i in range(size_x)])

    def shift_ctx(array, step):
        pairs = [(i, i + step) for i in range(n_ctx) if 0 <= i + step < n_ctx]
        return lax.ppermute(array, CTX, pairs)

    def from_x(step):
        return (ix + size_x - step) % size_x

    def whole_weight(shard):
        rows, cols = shard.shape
        halves = shard.reshape(2, rows // 2, cols)
        full = jnp.zeros((size_x, 2, rows // 2, cols), shard.dtype)
        full = lax.dynamic_update_slice(full, halves[None], (ix, 0, 0, 0))
        mine = pick(halves, ic)
        for step in range(1, size_x):
            got = to_x(mine, step)
            other = to_core(got)
            full = lax.dynamic_update_slice(full, got[None, None], (from_x(step), ic, 0, 0))
            full = lax.dynamic_update_slice(full, other[None, None], (from_x(step), 1 - ic, 0, 0))
        return full.reshape(size_x * rows, cols)

    def rank_columns(shard):
        rows, cols = shard.shape
        part = cols // ranks
        own_part = lax.dynamic_slice(shard, (0, rank * part), (rows, part))
        full = jnp.zeros((size_x, rows, part), shard.dtype)
        full = put(full, own_part, ix)
        for step in range(1, size_x):
            target = ((ix + step) % size_x) * 2 + ic
            got = to_x(lax.dynamic_slice(shard, (0, target * part), (rows, part)), step)
            full = put(full, got, from_x(step))
        return full.reshape(size_x * rows, part)

    def group_rows(array):
        parts = [array, to_core(array)]
        for step in range(1, size_x):
            got = to_x(array, step)
            parts += [got, to_core(got)]
        return jnp.concatenate(parts, 0)

    def group_columns(array):
        part = array.shape[1] // ranks
        view = array.reshape(tok, size_x, 2, part)
        kept = pick(view, ic, 2)
        got = to_core(pick(view, 1 - ic, 2))
        both = jnp.stack([kept, got])
        parts = [pick(both, ix, 2).reshape(2 * tok, part)]
        for step in range(1, size_x):
            sent = pick(both, (ix + step) % size_x, 2).reshape(2 * tok, part)
            parts.append(to_x(sent, step))
        return jnp.concatenate(parts, 0)

    def group_sum(part_of):
        total = None
        for step in list(range(1, size_x)) + [0]:
            both = part_of(step)
            summed = both[:tok] + to_core(both[tok:].astype(BF)).astype(F32)
            if step:
                summed = to_x(summed.astype(BF), size_x - step).astype(F32)
            total = summed if total is None else total + summed
        return total

    def sum_rows(grad):
        summed = lax.psum_scatter(
            grad.astype(BF), ("a", "b"), scatter_dimension=0, tiled=True
        )
        keep_pairs = []
        for g in range(chips):
            for c in range(2):
                for x in range(size_x):
                    keep_pairs.append(((g * 2 + c) * size_x + x, (x * 2 + c) * chips + g))
        return lax.ppermute(summed, ALL, keep_pairs).astype(F32)

    def sum_gain(grad):
        for name, size in (("c", 2), ("x", size_x), ("b", size_b), ("a", size_a)):
            step = 1
            while step < size:
                grad = grad + lax.ppermute(grad, name, [(i, i ^ step) for i in range(size)])
                step *= 2
        part = grad.shape[0] // (n_ctx * size_x)
        return lax.dynamic_slice(grad, (flat * part,), (part,))

    own_deal = pick(dealing[0], own)
    deal = (own_deal[:, None] == jnp.arange(tok, dtype=jnp.int32)[None, :]).astype(BF)

    def to_stream(array):
        return lax.all_to_all(
            mm(deal, array).astype(BF), CTX, split_axis=0, concat_axis=0, tiled=True
        )

    def from_stream(array):
        dealt = lax.all_to_all(array, CTX, split_axis=0, concat_axis=0, tiled=True)
        return mm_tn(deal, dealt)

    gains = whole_weight(jnp.stack([attn_gain, mlp_gain], 1).reshape(-1, 2)).astype(F32)
    gain_one = gains[:, 0]
    gain_two = gains[:, 1]
    inputs_low = to_stream(tokens[0])
    w_query = whole_weight(query_weight)
    w_kv = whole_weight(kv_weight)
    w_out = whole_weight(out_weight)
    cot = to_stream(cotangent[0])
    w_gate = rank_columns(gate_weight)
    w_up = rank_columns(up_weight)
    down_part = down_weight.shape[0] // 2
    w_down = lax.dynamic_slice(down_weight, (ic * down_part, 0), (down_part, width))

    inputs = inputs_low.astype(F32)
    unit_one, inv_one = norm_stats(inputs)
    normed = (unit_one * gain_one).astype(BF)
    pairs = mm(normed, w_kv).astype(BF)
    window = jnp.concatenate([shift_ctx(pairs, halo - j) for j in range(halo)] + [pairs], 0)
    queries = mm(normed, w_query).astype(BF)
    stream = own * tok + jnp.arange(tok, dtype=jnp.int32)
    ends = jnp.cumsum(lengths[0])
    starts = jnp.max(jnp.where(stream[:, None] >= ends[None, :], ends[None, :], 0), axis=1)
    low = jnp.maximum(starts, stream - (WINDOW - 1)) - (own * tok - WINDOW)
    low = low.astype(jnp.int32)[None, :]
    context, lse = attend(queries, window, low)
    resid = inputs + mm(context, w_out)

    unit_two, inv_two = norm_stats(resid)
    normed_mlp = group_rows((unit_two * gain_two).astype(BF))
    cot_rows = group_rows(cot)
    gate = mm(normed_mlp, w_gate)
    upward = mm(normed_mlp, w_up)
    d_hidden = mm_nt(cot_rows, w_down)
    act, pull = jax.vjp(lambda v: jax.nn.gelu(v, approximate=True), gate)
    hidden = (act * upward).astype(BF)
    d_gate = pull(d_hidden * upward)[0].astype(BF)
    d_upward = (d_hidden * act).astype(BF)

    def rows_of(array, step):
        return array[2 * step * tok : 2 * (step + 1) * tok]

    d_normed_mlp = group_sum(
        lambda step: mm_nt(rows_of(d_gate, step), w_gate) + mm_nt(rows_of(d_upward, step), w_up)
    )
    down_grad = sum_rows(mm_tn(hidden, cot_rows))
    branch_mlp = group_sum(lambda step: mm(rows_of(hidden, step), w_down))
    block_output = from_stream((resid + branch_mlp).astype(BF)).astype(BF)
    d_resid_part, mlp_gain_grad = norm_back(unit_two, inv_two, gain_two, d_normed_mlp)
    mlp_gain_grad = sum_gain(mlp_gain_grad)
    d_resid = cot.astype(F32) + d_resid_part
    d_branch = d_resid.astype(BF)

    d_context = mm_nt(d_branch, w_out).astype(BF)
    context_cols = group_columns(context)
    branch_rows = group_rows(d_branch)
    d_queries, d_window = attend_back(queries, window, low, d_context, lse)
    d_pairs = d_window[halo * tok :]
    for j in range(halo):
        part = d_window[j * tok : (j + 1) * tok].astype(BF)
        d_pairs = d_pairs + shift_ctx(part, j - halo).astype(F32)
    d_pairs = d_pairs.astype(BF)
    jobs = [
        Job(0, 0, 0, width, d_gate.shape[1], False),
        Job(0, 0, 1, width, d_upward.shape[1], False),
        Job(1, 1, 2, width, width // ranks, False),
        Job(1, 2, 3, width // ranks, width, True),
        Job(1, 1, 4, width // ranks, 2 * HD, True),
    ]
    sums = sum_grads(
        sizes,
        jobs,
        [normed_mlp.T, group_rows(normed).T, context_cols.T],
        [d_gate, d_upward, group_columns(d_queries), branch_rows, group_rows(d_pairs)],
    )
    gate_grad, up_grad, query_grad = (
        v.transpose(1, 0, 2).reshape(v.shape[1], -1).astype(F32) for v in sums[:3]
    )
    out_grad, kv_grad = (v.astype(F32) for v in sums[3:])
    d_normed = mm_nt(d_queries, w_query) + mm_nt(d_pairs, w_kv)
    d_inputs, attn_gain_grad = norm_back(unit_one, inv_one, gain_one, d_normed)
    attn_gain_grad = sum_gain(attn_gain_grad)
    token_grad = from_stream((d_resid + d_inputs).astype(BF))
    return (
        block_output[None],
        token_grad[None],
        attn_gain_grad,
        query_grad,
        kv_grad,
        out_grad,
        mlp_gain_grad,
        gate_grad,
        up_grad,
        down_grad,
    )


def solution(mesh):
    n_ctx, size_x = mesh.shape["ctx"], mesh.shape["fsdp"]
    chips = n_ctx // 2
    size_a = 4 if chips % 4 == 0 else chips
    size_b = chips // size_a
    fine = Mesh(mesh.devices.reshape(size_a, size_b, 2, size_x), ALL)
    rows = P("x", CTX, None)
    split = P("x", None)
    every = P(ALL)
    matrix = P(ALL, None)
    return jax.shard_map(
        functools.partial(on_device, (size_a, size_b, size_x)),
        mesh=fine,
        in_specs=(
            rows,
            split,
            P("x", None, None),
            P("x"),
            split,
            split,
            split,
            P("x"),
            split,
            split,
            split,
            rows,
        ),
        out_specs=(rows, rows, every, matrix, matrix, matrix, every, matrix, matrix, matrix),
        check_vma=False,
    )
```

```python
import functools

import jax
import jax.numpy as jnp
from jax import lax
from jax.experimental import pallas as pl
from jax.experimental.pallas import tpu as pltpu
from jax.sharding import Mesh
from jax.sharding import PartitionSpec as P

H = 16
HD = 128
WINDOW = 1024
QBLK = 128
HEADS_STEP = 4
SPAN = WINDOW + QBLK
ROWS = HEADS_STEP * QBLK

epsilon = 1e-06
neg_large = -1e30
scale = HD ** (-0.5)
BF = jnp.bfloat16
F32 = jnp.float32
CTX = ("a", "b", "c")
ALL = ("a", "b", "c", "x")
MESH = pl.DeviceIdType.MESH


def mm(left, right):
    return jnp.dot(left, right, preferred_element_type=F32)


def mm_tn(left, right):
    return lax.dot_general(left, right, (((0,), (0,)), ((), ())), preferred_element_type=F32)


def mm_nt(left, right):
    return lax.dot_general(left, right, (((1,), (1,)), ((), ())), preferred_element_type=F32)


def stack_heads(block):
    return jnp.concatenate([block[:, h * HD : (h + 1) * HD] for h in range(HEADS_STEP)], 0)


def unstack_heads(block_t):
    return jnp.concatenate(
        [block_t[:, h * QBLK : (h + 1) * QBLK].T for h in range(HEADS_STEP)], 1
    )


def bias_of(lo_ref, qb):
    key = lax.broadcasted_iota(jnp.int32, (SPAN, QBLK), 0) + qb * QBLK
    query = lax.broadcasted_iota(jnp.int32, (SPAN, QBLK), 1) + (WINDOW + qb * QBLK)
    allowed = (key >= lo_ref[...]) & (key <= query)
    bias = jnp.where(allowed, 0.0, neg_large).astype(F32)
    return jnp.concatenate([bias] * HEADS_STEP, 1)


def attend_kernel(lo_ref, q_ref, kv_ref, o_ref, lse_ref):
    qb = pl.program_id(0)
    rows = pl.ds(pl.multiple_of(qb * QBLK, QBLK), SPAN)
    keys = kv_ref[rows, :HD]
    values = kv_ref[rows, HD:]
    scores = mm_nt(keys, stack_heads(q_ref[...])) * scale + bias_of(lo_ref, qb)
    top = jnp.max(scores, axis=0, keepdims=True)
    raised = jnp.exp(scores - top)
    total = jnp.sum(raised, axis=0, keepdims=True)
    out_t = mm_tn(values, raised.astype(BF)) * (1.0 / total)
    o_ref[...] = unstack_heads(out_t).astype(BF)
    lse_ref[0] = top + jnp.log(total)


def attend_back_kernel(lo_ref, q_ref, kv_ref, do_ref, lse_ref, dq_ref, dkv_ref):
    qb = pl.program_id(0)

    @pl.when((qb == 0) & (pl.program_id(1) == 0))
    def _():
        dkv_ref[...] = jnp.zeros_like(dkv_ref)

    rows = pl.ds(pl.multiple_of(qb * QBLK, QBLK), SPAN)
    keys = kv_ref[rows, :HD]
    values = kv_ref[rows, HD:]
    queries = stack_heads(q_ref[...])
    d_out = stack_heads(do_ref[...])
    scores = mm_nt(keys, queries) * scale + bias_of(lo_ref, qb)
    probs = jnp.exp(scores - lse_ref[0])
    d_probs = mm_nt(values, d_out)
    delta = jnp.sum(probs * d_probs, axis=0, keepdims=True)
    d_scores = (probs * (d_probs - delta)).astype(BF)
    dq_ref[...] = unstack_heads(mm_tn(keys, d_scores) * scale).astype(BF)
    dkv_ref[rows, :HD] += mm(d_scores, queries) * scale
    dkv_ref[rows, HD:] += mm(probs.astype(BF), d_out)


def attend(queries, window, low):
    tok = queries.shape[0]
    groups = H // HEADS_STEP
    blocks = tok // QBLK
    return pl.pallas_call(
        attend_kernel,
        grid=(blocks, groups),
        in_specs=[
            pl.BlockSpec((1, QBLK), lambda i, j: (0, i)),
            pl.BlockSpec((QBLK, HEADS_STEP * HD), lambda i, j: (i, j)),
            pl.BlockSpec((WINDOW + tok, 2 * HD), lambda i, j: (0, 0)),
        ],
        out_specs=[
            pl.BlockSpec((QBLK, HEADS_STEP * HD), lambda i, j: (i, j)),
            pl.BlockSpec((1, 1, ROWS), lambda i, j: (i * groups + j, 0, 0)),
        ],
        out_shape=[
            jax.ShapeDtypeStruct((tok, H * HD), BF),
            jax.ShapeDtypeStruct((blocks * groups, 1, ROWS), F32),
        ],
        compiler_params=pltpu.CompilerParams(vmem_limit_bytes=48 * 1024 * 1024),
        cost_estimate=pl.CostEstimate(
            flops=4 * tok * H * HD * SPAN, bytes_accessed=4 * 1024 * 1024, transcendentals=0
        ),
        name="attend",
    )(low, queries, window)


def attend_back(queries, window, low, d_context, lse):
    tok = queries.shape[0]
    groups = H // HEADS_STEP
    blocks = tok // QBLK
    return pl.pallas_call(
        attend_back_kernel,
        grid=(blocks, groups),
        in_specs=[
            pl.BlockSpec((1, QBLK), lambda i, j: (0, i)),
            pl.BlockSpec((QBLK, HEADS_STEP * HD), lambda i, j: (i, j)),
            pl.BlockSpec((WINDOW + tok, 2 * HD), lambda i, j: (0, 0)),
            pl.BlockSpec((QBLK, HEADS_STEP * HD), lambda i, j: (i, j)),
            pl.BlockSpec((1, 1, ROWS), lambda i, j: (i * groups + j, 0, 0)),
        ],
        out_specs=[
            pl.BlockSpec((QBLK, HEADS_STEP * HD), lambda i, j: (i, j)),
            pl.BlockSpec((WINDOW + tok, 2 * HD), lambda i, j: (0, 0)),
        ],
        out_shape=[
            jax.ShapeDtypeStruct((tok, H * HD), BF),
            jax.ShapeDtypeStruct((WINDOW + tok, 2 * HD), F32),
        ],
        compiler_params=pltpu.CompilerParams(vmem_limit_bytes=48 * 1024 * 1024),
        cost_estimate=pl.CostEstimate(
            flops=10 * tok * H * HD * SPAN, bytes_accessed=6 * 1024 * 1024, transcendentals=0
        ),
        name="attend_back",
    )(low, queries, window, d_context, lse)


def snake(pos, size_a, size_b):
    if size_b == 1:
        return pos, pos * 0
    down = pos // size_a
    first = 1 - (down + 7) // 8
    q = (pos - size_a) * (1 - first)
    a_up = size_a - 1 - q // (size_b - 1)
    k = q % (size_b - 1)
    odd = a_up % 2
    b_up = odd * (1 + k) + (1 - odd) * (size_b - 1 - k)
    return first * pos + (1 - first) * a_up, (1 - first) * b_up


def snake_place(a, b, size_a, size_b):
    if size_b == 1:
        return a
    moved = (b + size_b - 1) // size_b
    odd = a % 2
    along = odd * (b - 1) + (1 - odd) * (size_b - 1 - b)
    return (1 - moved) * a + moved * (size_a + (size_a - 1 - a) * (size_b - 1) + along)


def kept_slot(a, b, size_a, size_b):
    half = size_a * size_b // 2
    return (1 - b % 2) * half + a * (size_b // 2) + b // 2


class Piece:
    def __init__(self, at, rows, square, shared, part, parts):
        self.at, self.rows, self.square, self.shared = at, rows, square, shared
        self.part, self.parts = part, parts
        self.relays = [0, 1, 2, 3] if square else []
        if shared:
            self.relays += [4, 5, 6, 7, 8] if square else [4]


def fetch_kernel(sizes, pieces, n_in, n_dealt, *refs):
    size_a, size_b, size_x = sizes
    n_ctx = size_a * size_b * 2
    ins, refs = refs[:n_in], refs[n_in:]
    outs, refs = refs[:n_in], refs[n_in:]
    n_weights = n_in - n_dealt - 1
    stages, refs = refs[:n_weights], refs[n_weights:]
    keep_sem, own_sem, deal_send, deal_recv, gain_send, gain_recv = refs[:6]
    x_send, x_recv, relay_send, relay_recv = refs[6:]
    ia, ib, ic, ix = (lax.axis_index(name) for name in ALL)
    own = (ia * size_b + ib) * 2 + ic
    rank = ix * 2 + ic
    pa, pb = ia % 2, ib % 2
    other_a, other_b = ia + 1 - 2 * pa, ib + 1 - 2 * pb
    corner = pa * 2 + pb
    corner_a, corner_b, corner_d = (1 - pa) * 2 + pb, pa * 2 + 1 - pb, 3 - corner

    barrier = pltpu.get_barrier_semaphore()
    greeted = []
    for k in range(1, n_ctx):
        e = (own + k) % n_ctx
        greeted.append((e // 2 // size_b, e // 2 % size_b, e % 2, ix))
    for s in range(1, size_x):
        greeted.append((ia, ib, ic, (ix + s) % size_x))
    for device in greeted:
        pl.semaphore_signal(barrier, inc=1, device_id=device, device_id_type=MESH)
    pl.semaphore_wait(barrier, len(greeted))

    def remote(src, dst, send, recv, device):
        return pltpu.make_async_remote_copy(
            src_ref=src,
            dst_ref=dst,
            send_sem=send,
            recv_sem=recv,
            device_id=device,
            device_id_type=MESH,
        )

    def x_copy(i, s):
        p = pieces[i]
        shard, full = ins[p.at], outs[p.at]
        target = (ix + s) % size_x
        height = shard.shape[0]
        rows, start = region(p, corner, ic)
        if p.shared:
            src = shard.at[pl.ds(start, rows), :]
        else:
            cols = full.shape[1]
            at = pl.multiple_of((target * 2 + ic) * cols, cols)
            src = shard.at[pl.ds(start, rows), pl.ds(at, cols)]
        dst = full.at[pl.ds(pl.multiple_of(ix * height + start, rows), rows), :]
        return remote(src, dst, x_send.at[i, s], x_recv.at[i, s], (ia, ib, ic, target))

    def region(p, which, core):
        owner = which if p.square else 0
        owners = 4 if p.square else 1
        if p.shared:
            owner, owners = owner * 2 + core, owners * 2
        rows = p.rows // (owners * p.parts)
        return rows, pl.multiple_of((owner * p.parts + p.part) * rows, rows)

    def landed(i, s, which, core, half=None):
        p = pieces[i]
        rows, start = region(p, which, core)
        start = start + (ix + size_x - s) % size_x * p.rows
        if half is not None:
            rows = rows // 2
            start = start + half * rows
        return outs[p.at].at[pl.ds(pl.multiple_of(start, rows), rows), :]

    def relay(i, s, kind, incoming=False):
        sem = (relay_send.at[i, s, kind], relay_recv.at[i, s, kind])
        if kind < 4:
            device = (other_a, ib, ic, ix) if kind in (1, 2) else (ia, other_b, ic, ix)
            sent = (
                landed(i, s, corner, ic),
                landed(i, s, corner, ic),
                landed(i, s, corner_b, ic, 0),
                landed(i, s, corner_a, ic, 1),
            )[kind]
            came = (
                landed(i, s, corner_b, ic),
                landed(i, s, corner_a, ic),
                landed(i, s, corner_d, ic, 0),
                landed(i, s, corner_d, ic, 1),
            )[kind]
        else:
            device = (ia, ib, 1 - ic, ix)
            which, half = ((corner, None), (corner_b, None), (corner_a, None), (corner_d, 0), (corner_d, 1))[
                kind - 4
            ]
            sent = landed(i, s, which, ic, half)
            came = landed(i, s, which, 1 - ic, half)
        ref = came if incoming else sent
        return remote(ref, ref, *sem, device)

    rows = ins[0].shape[0] // n_ctx

    def deal_copy(t, k):
        e = (own + k) % n_ctx
        src = ins[t].at[pl.ds(pl.multiple_of(e * rows, rows), rows), :]
        dst = outs[t].at[pl.ds(pl.multiple_of(own * rows, rows), rows), :]
        if k == 0:
            return pltpu.make_async_copy(src, dst, own_sem.at[t])
        device = (e // 2 // size_b, e // 2 % size_b, e % 2, ix)
        return remote(src, dst, deal_send.at[t, k], deal_recv.at[t, k], device)

    g = n_in - 1

    def gain_copy(s):
        if s == 0:
            return pltpu.make_async_copy(ins[g], outs[g].at[ix], own_sem.at[g])
        device = (ia, ib, ic, (ix + s) % size_x)
        return remote(ins[g], outs[g].at[ix], gain_send.at[s], gain_recv.at[s], device)

    def keep_copy(w, out):
        shard, full = ins[w], outs[w]
        stage = stages[w - n_dealt]
        height = shard.shape[0]
        sem = keep_sem.at[w, out]
        if out:
            dst = full.at[pl.ds(pl.multiple_of(ix * height, height), height), :]
            return pltpu.make_async_copy(stage, dst, sem)
        src = shard
        if full.shape[1] != shard.shape[1]:
            cols = full.shape[1]
            src = shard.at[:, pl.ds(pl.multiple_of(rank * cols, cols), cols)]
        return pltpu.make_async_copy(src, stage, sem)

    ahead = 4
    order = [(i, s) for i in range(len(pieces)) for s in range(1, size_x)]
    for k in range(n_ctx):
        deal_copy(0, k).start()
    for s in range(size_x):
        gain_copy(s).start()
    for i, s in order[:ahead]:
        x_copy(i, s).start()
    for t in range(1, n_dealt):
        for k in range(n_ctx):
            deal_copy(t, k).start()
    for w in range(n_dealt, n_dealt + n_weights):
        keep_copy(w, 0).start()

    for n in range(len(order) + 2):
        if n < n_weights:
            keep_copy(n_dealt + n, 0).wait()
            keep_copy(n_dealt + n, 1).start()
        if n < len(order):
            i, s = order[n]
            x_copy(i, s).wait_recv()
            for kind in (0, 1, 4):
                if kind in pieces[i].relays:
                    relay(i, s, kind).start()
            if n + ahead < len(order):
                x_copy(i, s).wait_send()
                x_copy(*order[n + ahead]).start()
        if 1 <= n <= len(order) and pieces[order[n - 1][0]].square:
            i, s = order[n - 1]
            relay(i, s, 0, True).wait_recv()
            relay(i, s, 2).start()
            relay(i, s, 1, True).wait_recv()
            relay(i, s, 3).start()
            if pieces[i].shared:
                relay(i, s, 5).start()
                relay(i, s, 6).start()
        if n >= 2 and pieces[order[n - 2][0]].square:
            i, s = order[n - 2]
            relay(i, s, 2, True).wait_recv()
            relay(i, s, 3, True).wait_recv()
            if pieces[i].shared:
                relay(i, s, 7).start()
                relay(i, s, 8).start()

    for n, (i, s) in enumerate(order):
        if n + ahead >= len(order):
            x_copy(i, s).wait_send()
        for kind in pieces[i].relays:
            relay(i, s, kind).wait_send()
            if kind >= 4:
                relay(i, s, kind, True).wait_recv()
    for t in range(n_dealt):
        for k in range(n_ctx):
            deal_copy(t, k).wait()
    for s in range(size_x):
        gain_copy(s).wait()
    for w in range(n_dealt, n_dealt + n_weights):
        keep_copy(w, 1).wait()


def fetch(sizes, dealt, shared, split, gains):
    size_a, size_b, size_x = sizes
    n_ctx = size_a * size_b * 2
    ins = dealt + shared + split + [gains]
    outs = [jax.ShapeDtypeStruct(a.shape, BF) for a in dealt]
    outs += [jax.ShapeDtypeStruct((size_x * a.shape[0], a.shape[1]), BF) for a in shared]
    outs += [
        jax.ShapeDtypeStruct((size_x * a.shape[0], a.shape[1] // (2 * size_x)), BF) for a in split
    ]
    outs.append(jax.ShapeDtypeStruct((size_x,) + gains.shape, BF))
    pieces = []
    first = len(dealt)
    pieces.append(Piece(first, shared[0].shape[0], True, True, 0, 1))
    for part in range(2):
        for n, a in enumerate(split):
            pieces.append(Piece(first + len(shared) + n, a.shape[0], True, False, part, 2))
    for n, a in enumerate(shared[1:]):
        pieces.append(Piece(first + 1 + n, a.shape[0], False, True, 0, 1))
    count = len(pieces)
    sem = pltpu.SemaphoreType.DMA
    return pl.pallas_call(
        functools.partial(fetch_kernel, sizes, pieces, len(ins), len(dealt)),
        in_specs=[pl.BlockSpec(memory_space=pl.ANY)] * len(ins),
        out_specs=[pl.BlockSpec(memory_space=pl.ANY)] * len(outs),
        out_shape=outs,
        scratch_shapes=[
            pltpu.VMEM((a.shape[0], o.shape[1]), BF)
            for a, o in zip(ins[len(dealt) : -1], outs[len(dealt) : -1])
        ]
        + [
            sem((len(ins), 2)),
            sem((len(ins),)),
            sem((len(dealt), n_ctx)),
            sem((len(dealt), n_ctx)),
            sem((size_x,)),
            sem((size_x,)),
            sem((count, size_x)),
            sem((count, size_x)),
            sem((count, size_x, 9)),
            sem((count, size_x, 9)),
        ],
        compiler_params=pltpu.CompilerParams(
            collective_id=1, has_side_effects=True, vmem_limit_bytes=48 * 1024 * 1024
        ),
        cost_estimate=pl.CostEstimate(
            flops=0, bytes_accessed=300 * 1024 * 1024, transcendentals=0
        ),
        name="fetch",
    )(*ins)


class Job:
    def __init__(self, phase, left, right, rows, cols, by_rank):
        self.phase, self.left, self.right = phase, left, right
        self.rows, self.cols, self.by_rank = rows, cols, by_rank


def grads_kernel(sizes, jobs, n_left, n_right, *refs):
    size_a, size_b, size_x = sizes
    chips = size_a * size_b
    ranks = 2 * size_x
    count = len(jobs)
    lefts_in, refs = refs[:n_left], refs[n_left:]
    rights_in, refs = refs[:n_right], refs[n_right:]
    outs, refs = refs[:count], refs[count:]
    lefts, refs = refs[:n_left], refs[n_left:]
    rights, refs = refs[:n_right], refs[n_right:]
    recv, refs = refs[:count], refs[count:]
    send, refs = refs[:count], refs[count:]
    done, refs = refs[:count], refs[count:]
    load_sem, send_sem, recv_sem, done_send, done_recv, own_sem = refs
    ia, ib, ic, ix = (lax.axis_index(name) for name in ALL)
    rank = ix * 2 + ic
    place = snake_place(ia, ib, size_a, size_b)

    def on_ring(step):
        return snake((place + 2 * chips + step) % chips, size_a, size_b)

    def member(k):
        return (ic + k // size_x) % 2, (ix + k % size_x) % size_x

    kept = rank * chips + kept_slot(ia, ib, size_a, size_b)
    kept_chip = kept // ranks
    kept_id = (kept_chip // size_b, kept_chip % size_b, (kept // size_x) % 2, kept % size_x)
    flat = ((ia * size_b + ib) * 2 + ic) * size_x + ix
    from_rank = flat // chips
    from_slot = flat % chips
    half = chips // 2
    from_id = (
        (from_slot % half) // (size_b // 2),
        ((from_slot % half) % (size_b // 2)) * 2 + 1 - from_slot // half,
        from_rank % 2,
        from_rank // 2,
    )

    loads = []
    for i, (src, dst) in enumerate(zip(lefts_in + rights_in, lefts + rights)):
        loads.append(pltpu.make_async_copy(src, dst, load_sem.at[i]))
    for copy in loads:
        copy.start()

    barrier = pltpu.get_barrier_semaphore()
    greeted = [on_ring(1) + (ic, ix), on_ring(-1) + (ic, ix), from_id]
    greeted += [(ia, ib) + member(k) for k in range(1, ranks)]
    for device in greeted:
        pl.semaphore_signal(barrier, inc=1, device_id=device, device_id_type=MESH)
    pl.semaphore_wait(barrier, len(greeted))

    def ring_copy(j, way, step, parity):
        neighbour = on_ring(1 - 2 * way) + (ic, ix)
        return pltpu.make_async_remote_copy(
            src_ref=send[j].at[way, parity],
            dst_ref=recv[j].at[way, step],
            send_sem=send_sem.at[j, way, parity],
            recv_sem=recv_sem.at[j, way, step],
            device_id=neighbour,
            device_id_type=MESH,
        )

    def product(j, way, step):
        job = jobs[j]
        a, b = on_ring(step * (2 * way - 1))
        part = job.rows // chips
        if job.by_rank:
            start = kept_slot(a, b, size_a, size_b) * part
            if lefts[job.left].shape[0] != job.rows:
                start = start + rank * job.rows
        else:
            start = (a * size_b + b) * part
        cols = job.cols // 2
        left = lefts[job.left][pl.ds(pl.multiple_of(start, part), part), :]
        return jnp.dot(
            left, rights[job.right][:, way * cols : (way + 1) * cols], preferred_element_type=F32
        )

    def deliver(j):
        job = jobs[j]
        if job.by_rank:
            return [
                pltpu.make_async_remote_copy(
                    src_ref=done[j],
                    dst_ref=outs[j],
                    send_sem=done_send.at[j, 0],
                    recv_sem=done_recv.at[j, 0],
                    device_id=kept_id,
                    device_id_type=MESH,
                )
            ]
        part = job.rows // (chips * ranks)
        copies = []
        for k in range(1, ranks):
            c, x = member(k)
            start = pl.multiple_of((c * size_x + x) * part, part)
            copies.append(
                pltpu.make_async_remote_copy(
                    src_ref=done[j].at[pl.ds(start, part), :],
                    dst_ref=outs[j].at[rank],
                    send_sem=done_send.at[j, k],
                    recv_sem=done_recv.at[j, k],
                    device_id=(ia, ib, c, x),
                    device_id_type=MESH,
                )
            )
        start = pl.multiple_of((ic * size_x + ix) * part, part)
        copies.append(
            pltpu.make_async_copy(done[j].at[pl.ds(start, part), :], outs[j].at[rank], own_sem.at[j])
        )
        return copies

    loaded = set()
    for phase in range(1 + max(job.phase for job in jobs)):
        mine = [j for j in range(count) if jobs[j].phase == phase]
        for j in mine:
            for i in (jobs[j].left, n_left + jobs[j].right):
                if i not in loaded:
                    loaded.add(i)
                    loads[i].wait()
            for way in range(2):
                send[j][way, 0] = product(j, way, 1).astype(BF)
                ring_copy(j, way, 0, 0).start()

        def step_of(step, carry):
            parity = step % 2
            for j in mine:
                for way in range(2):
                    part = product(j, way, step + 1)
                    ring_copy(j, way, step - 1, 1 - parity).wait_recv()
                    part = part + recv[j][way, step - 1].astype(F32)

                    @pl.when(step >= 2)
                    def _():
                        ring_copy(j, way, step - 2, parity).wait_send()

                    send[j][way, parity] = part.astype(BF)
                    ring_copy(j, way, step, parity).start()
            return carry

        lax.fori_loop(1, chips - 1, step_of, 0)
        last = chips - 2
        for j in mine:
            cols = jobs[j].cols // 2
            for way in range(2):
                part = product(j, way, chips)
                ring_copy(j, way, last, last % 2).wait_recv()
                part = part + recv[j][way, last].astype(F32)
                done[j][:, way * cols : (way + 1) * cols] = part.astype(BF)
            for copy in deliver(j):
                copy.start()
            for way in range(2):
                ring_copy(j, way, last - 1, (last - 1) % 2).wait_send()
                ring_copy(j, way, last, last % 2).wait_send()
    for j in range(count):
        for copy in deliver(j):
            copy.wait()


def sum_grads(sizes, jobs, lefts, rights):
    size_a, size_b, size_x = sizes
    chips = size_a * size_b
    ranks = 2 * size_x
    outs, recv, send, done = [], [], [], []
    flops = 0
    for job in jobs:
        part = job.rows // chips
        if job.by_rank:
            outs.append(jax.ShapeDtypeStruct((part, job.cols), BF))
        else:
            outs.append(jax.ShapeDtypeStruct((ranks, part // ranks, job.cols), BF))
        recv.append(pltpu.VMEM((2, chips - 1, part, job.cols // 2), BF))
        send.append(pltpu.VMEM((2, 2, part, job.cols // 2), BF))
        done.append(pltpu.VMEM((part, job.cols), BF))
        flops += 2 * job.rows * job.cols * rights[job.right].shape[0]
    count = len(jobs)
    sem = pltpu.SemaphoreType.DMA
    return pl.pallas_call(
        functools.partial(grads_kernel, sizes, jobs, len(lefts), len(rights)),
        in_specs=[pl.BlockSpec(memory_space=pl.ANY)] * (len(lefts) + len(rights)),
        out_specs=[pl.BlockSpec(memory_space=pl.ANY)] * count,
        out_shape=outs,
        scratch_shapes=[pltpu.VMEM(a.shape, BF) for a in lefts + rights]
        + recv
        + send
        + done
        + [
            sem((len(lefts) + len(rights),)),
            sem((count, 2, 2)),
            sem((count, 2, chips - 1)),
            sem((count, ranks)),
            sem((count, ranks)),
            sem((count,)),
        ],
        compiler_params=pltpu.CompilerParams(
            collective_id=0, has_side_effects=True, vmem_limit_bytes=60 * 1024 * 1024
        ),
        cost_estimate=pl.CostEstimate(
            flops=flops, bytes_accessed=400 * 1024 * 1024, transcendentals=0
        ),
        name="sum_grads",
    )(*lefts, *rights)


def norm_stats(values):
    inv = lax.rsqrt(jnp.mean(values * values, axis=-1, keepdims=True) + epsilon)
    return values * inv, inv


def norm_back(unit, inv, gain, grad):
    scaled = grad * gain
    inner = jnp.mean(scaled * unit, axis=-1, keepdims=True)
    return inv * (scaled - unit * inner), jnp.sum(grad * unit, axis=0)


def on_device(
    sizes,
    tokens,
    lengths,
    dealing,
    attn_gain,
    query_weight,
    kv_weight,
    out_weight,
    mlp_gain,
    gate_weight,
    up_weight,
    down_weight,
    cotangent,
):
    size_a, size_b, size_x = sizes
    chips = size_a * size_b
    n_ctx = chips * 2
    ranks = 2 * size_x
    ia, ib, ic, ix = (lax.axis_index(name) for name in ALL)
    chip = ia * size_b + ib
    own = chip * 2 + ic
    flat = own * size_x + ix
    rank = ix * 2 + ic
    tok = tokens.shape[1]
    width = tokens.shape[2]
    piece = tok // n_ctx
    halo = WINDOW // tok
    swap = [(0, 1), (1, 0)]

    def pick(array, index, axis=0):
        return lax.dynamic_index_in_dim(array, index, axis, keepdims=False)

    def put(array, part, index, axis=0):
        return lax.dynamic_update_index_in_dim(array, part, index, axis)

    def to_core(array):
        return lax.ppermute(array, "c", swap)

    def to_x(array, step):
        return lax.ppermute(array, "x", [(i, (i + step) % size_x) for i in range(size_x)])

    def shift_ctx(array, step):
        pairs = [(i, i + step) for i in range(n_ctx) if 0 <= i + step < n_ctx]
        return lax.ppermute(array, CTX, pairs)

    def from_x(step):
        return (ix + size_x - step) % size_x

    def group_rows(array):
        parts = [array, to_core(array)]
        for step in range(1, size_x):
            got = to_x(array, step)
            parts += [got, to_core(got)]
        return jnp.concatenate(parts, 0)

    def group_columns(array):
        part = array.shape[1] // ranks
        view = array.reshape(tok, size_x, 2, part)
        kept = pick(view, ic, 2)
        got = to_core(pick(view, 1 - ic, 2))
        both = jnp.stack([kept, got])
        parts = [pick(both, ix, 2).reshape(2 * tok, part)]
        for step in range(1, size_x):
            sent = pick(both, (ix + step) % size_x, 2).reshape(2 * tok, part)
            parts.append(to_x(sent, step))
        return jnp.concatenate(parts, 0)

    def group_sum(part_of):
        total = None
        for step in list(range(1, size_x)) + [0]:
            both = part_of(step)
            summed = both[:tok] + to_core(both[tok:].astype(BF)).astype(F32)
            if step:
                summed = to_x(summed.astype(BF), size_x - step).astype(F32)
            total = summed if total is None else total + summed
        return total

    def sum_rows(grad):
        summed = lax.psum_scatter(
            grad.astype(BF), ("a", "b"), scatter_dimension=0, tiled=True
        )
        keep_pairs = []
        for g in range(chips):
            for c in range(2):
                for x in range(size_x):
                    keep_pairs.append(((g * 2 + c) * size_x + x, (x * 2 + c) * chips + g))
        return lax.ppermute(summed, ALL, keep_pairs).astype(F32)

    def sum_gain(grad):
        for name, size in (("c", 2), ("x", size_x), ("b", size_b), ("a", size_a)):
            step = 1
            while step < size:
                grad = grad + lax.ppermute(grad, name, [(i, i ^ step) for i in range(size)])
                step *= 2
        part = grad.shape[0] // (n_ctx * size_x)
        return lax.dynamic_slice(grad, (flat * part,), (part,))

    own_deal = pick(dealing[0], own)
    deal = (own_deal[:, None] == jnp.arange(tok, dtype=jnp.int32)[None, :]).astype(BF)

    def from_stream(array):
        dealt = lax.all_to_all(array, CTX, split_axis=0, concat_axis=0, tiled=True)
        return mm_tn(deal, dealt)

    gains = jnp.stack([attn_gain, mlp_gain]).reshape(-1, 128)
    inputs_low, cot, w_query, w_kv, w_out, w_gate, w_up, gains = fetch(
        sizes,
        [mm(deal, tokens[0]).astype(BF), mm(deal, cotangent[0]).astype(BF)],
        [query_weight, kv_weight, out_weight],
        [gate_weight, up_weight],
        gains,
    )
    gains = gains.reshape(size_x, 2, -1).astype(F32)
    gain_one = gains[:, 0].reshape(-1)
    gain_two = gains[:, 1].reshape(-1)
    down_part = down_weight.shape[0] // 2
    w_down = lax.dynamic_slice(down_weight, (ic * down_part, 0), (down_part, width))

    inputs = inputs_low.astype(F32)
    unit_one, inv_one = norm_stats(inputs)
    normed = (unit_one * gain_one).astype(BF)
    pairs = mm(normed, w_kv).astype(BF)
    window = jnp.concatenate([shift_ctx(pairs, halo - j) for j in range(halo)] + [pairs], 0)
    queries = mm(normed, w_query).astype(BF)
    stream = own * tok + jnp.arange(tok, dtype=jnp.int32)
    ends = jnp.cumsum(lengths[0])
    starts = jnp.max(jnp.where(stream[:, None] >= ends[None, :], ends[None, :], 0), axis=1)
    low = jnp.maximum(starts, stream - (WINDOW - 1)) - (own * tok - WINDOW)
    low = low.astype(jnp.int32)[None, :]
    context, lse = attend(queries, window, low)
    resid = inputs + mm(context, w_out)

    unit_two, inv_two = norm_stats(resid)
    normed_mlp = group_rows((unit_two * gain_two).astype(BF))
    cot_rows = group_rows(cot)
    gate = mm(normed_mlp, w_gate)
    upward = mm(normed_mlp, w_up)
    d_hidden = mm_nt(cot_rows, w_down)
    act, pull = jax.vjp(lambda v: jax.nn.gelu(v, approximate=True), gate)
    hidden = (act * upward).astype(BF)
    d_gate = pull(d_hidden * upward)[0].astype(BF)
    d_upward = (d_hidden * act).astype(BF)

    def rows_of(array, step):
        return array[2 * step * tok : 2 * (step + 1) * tok]

    d_normed_mlp = group_sum(
        lambda step: mm_nt(rows_of(d_gate, step), w_gate) + mm_nt(rows_of(d_upward, step), w_up)
    )
    down_grad = sum_rows(mm_tn(hidden, cot_rows))
    branch_mlp = group_sum(lambda step: mm(rows_of(hidden, step), w_down))
    block_output = from_stream((resid + branch_mlp).astype(BF)).astype(BF)
    d_resid_part, mlp_gain_grad = norm_back(unit_two, inv_two, gain_two, d_normed_mlp)
    mlp_gain_grad = sum_gain(mlp_gain_grad)
    d_resid = cot.astype(F32) + d_resid_part
    d_branch = d_resid.astype(BF)

    d_context = mm_nt(d_branch, w_out).astype(BF)
    context_cols = group_columns(context)
    branch_rows = group_rows(d_branch)
    d_queries, d_window = attend_back(queries, window, low, d_context, lse)
    d_pairs = d_window[halo * tok :]
    for j in range(halo):
        part = d_window[j * tok : (j + 1) * tok].astype(BF)
        d_pairs = d_pairs + shift_ctx(part, j - halo).astype(F32)
    d_pairs = d_pairs.astype(BF)
    jobs = [
        Job(0, 0, 0, width, d_gate.shape[1], False),
        Job(0, 0, 1, width, d_upward.shape[1], False),
        Job(1, 1, 2, width, width // ranks, False),
        Job(1, 2, 3, width // ranks, width, True),
        Job(1, 1, 4, width // ranks, 2 * HD, True),
    ]
    sums = sum_grads(
        sizes,
        jobs,
        [normed_mlp.T, group_rows(normed).T, context_cols.T],
        [d_gate, d_upward, group_columns(d_queries), branch_rows, group_rows(d_pairs)],
    )
    gate_grad, up_grad, query_grad = (
        v.transpose(1, 0, 2).reshape(v.shape[1], -1).astype(F32) for v in sums[:3]
    )
    out_grad, kv_grad = (v.astype(F32) for v in sums[3:])
    d_normed = mm_nt(d_queries, w_query) + mm_nt(d_pairs, w_kv)
    d_inputs, attn_gain_grad = norm_back(unit_one, inv_one, gain_one, d_normed)
    attn_gain_grad = sum_gain(attn_gain_grad)
    token_grad = from_stream((d_resid + d_inputs).astype(BF))
    return (
        block_output[None],
        token_grad[None],
        attn_gain_grad,
        query_grad,
        kv_grad,
        out_grad,
        mlp_gain_grad,
        gate_grad,
        up_grad,
        down_grad,
    )


def solution(mesh):
    n_ctx, size_x = mesh.shape["ctx"], mesh.shape["fsdp"]
    chips = n_ctx // 2
    size_a = 4 if chips % 4 == 0 else chips
    size_b = chips // size_a
    fine = Mesh(mesh.devices.reshape(size_a, size_b, 2, size_x), ALL)
    rows = P("x", CTX, None)
    split = P("x", None)
    every = P(ALL)
    matrix = P(ALL, None)
    return jax.shard_map(
        functools.partial(on_device, (size_a, size_b, size_x)),
        mesh=fine,
        in_specs=(
            rows,
            split,
            P("x", None, None),
            P("x"),
            split,
            split,
            split,
            P("x"),
            split,
            split,
            split,
            rows,
        ),
        out_specs=(rows, rows, every, matrix, matrix, matrix, every, matrix, matrix, matrix),
        check_vma=False,
    )
```

```python
import functools

import jax
import jax.numpy as jnp
from jax import lax
from jax.experimental import pallas as pl
from jax.experimental.pallas import tpu as pltpu
from jax.sharding import Mesh
from jax.sharding import PartitionSpec as P

H = 16
HD = 128
WINDOW = 1024
QBLK = 128
HEADS_STEP = 4
SPAN = WINDOW + QBLK
ROWS = HEADS_STEP * QBLK

epsilon = 1e-06
neg_large = -1e30
scale = HD ** (-0.5)
BF = jnp.bfloat16
F32 = jnp.float32
CTX = ("a", "b", "c")
ALL = ("a", "b", "c", "x")
MESH = pl.DeviceIdType.MESH


def mm(left, right):
    return jnp.dot(left, right, preferred_element_type=F32)


def mm_tn(left, right):
    return lax.dot_general(left, right, (((0,), (0,)), ((), ())), preferred_element_type=F32)


def mm_nt(left, right):
    return lax.dot_general(left, right, (((1,), (1,)), ((), ())), preferred_element_type=F32)


def stack_heads(block):
    return jnp.concatenate([block[:, h * HD : (h + 1) * HD] for h in range(HEADS_STEP)], 0)


def unstack_heads(block_t):
    return jnp.concatenate(
        [block_t[:, h * QBLK : (h + 1) * QBLK].T for h in range(HEADS_STEP)], 1
    )


def bias_of(lo_ref, qb):
    key = lax.broadcasted_iota(jnp.int32, (SPAN, QBLK), 0) + qb * QBLK
    query = lax.broadcasted_iota(jnp.int32, (SPAN, QBLK), 1) + (WINDOW + qb * QBLK)
    allowed = (key >= lo_ref[...]) & (key <= query)
    bias = jnp.where(allowed, 0.0, neg_large).astype(F32)
    return jnp.concatenate([bias] * HEADS_STEP, 1)


def attend_kernel(lo_ref, q_ref, kv_ref, o_ref, lse_ref):
    qb = pl.program_id(0)
    rows = pl.ds(pl.multiple_of(qb * QBLK, QBLK), SPAN)
    keys = kv_ref[rows, :HD]
    values = kv_ref[rows, HD:]
    scores = mm_nt(keys, stack_heads(q_ref[...])) * scale + bias_of(lo_ref, qb)
    top = jnp.max(scores, axis=0, keepdims=True)
    raised = jnp.exp(scores - top)
    total = jnp.sum(raised, axis=0, keepdims=True)
    out_t = mm_tn(values, raised.astype(BF)) * (1.0 / total)
    o_ref[...] = unstack_heads(out_t).astype(BF)
    lse_ref[0] = top + jnp.log(total)


def attend_back_kernel(lo_ref, q_ref, kv_ref, do_ref, lse_ref, dq_ref, dkv_ref):
    qb = pl.program_id(0)

    @pl.when((qb == 0) & (pl.program_id(1) == 0))
    def _():
        dkv_ref[...] = jnp.zeros_like(dkv_ref)

    rows = pl.ds(pl.multiple_of(qb * QBLK, QBLK), SPAN)
    keys = kv_ref[rows, :HD]
    values = kv_ref[rows, HD:]
    queries = stack_heads(q_ref[...])
    d_out = stack_heads(do_ref[...])
    scores = mm_nt(keys, queries) * scale + bias_of(lo_ref, qb)
    probs = jnp.exp(scores - lse_ref[0])
    d_probs = mm_nt(values, d_out)
    delta = jnp.sum(probs * d_probs, axis=0, keepdims=True)
    d_scores = (probs * (d_probs - delta)).astype(BF)
    dq_ref[...] = unstack_heads(mm_tn(keys, d_scores) * scale).astype(BF)
    dkv_ref[rows, :HD] += mm(d_scores, queries) * scale
    dkv_ref[rows, HD:] += mm(probs.astype(BF), d_out)


def attend(queries, window, low):
    tok = queries.shape[0]
    groups = H // HEADS_STEP
    blocks = tok // QBLK
    return pl.pallas_call(
        attend_kernel,
        grid=(blocks, groups),
        in_specs=[
            pl.BlockSpec((1, QBLK), lambda i, j: (0, i)),
            pl.BlockSpec((QBLK, HEADS_STEP * HD), lambda i, j: (i, j)),
            pl.BlockSpec((WINDOW + tok, 2 * HD), lambda i, j: (0, 0)),
        ],
        out_specs=[
            pl.BlockSpec((QBLK, HEADS_STEP * HD), lambda i, j: (i, j)),
            pl.BlockSpec((1, 1, ROWS), lambda i, j: (i * groups + j, 0, 0)),
        ],
        out_shape=[
            jax.ShapeDtypeStruct((tok, H * HD), BF),
            jax.ShapeDtypeStruct((blocks * groups, 1, ROWS), F32),
        ],
        compiler_params=pltpu.CompilerParams(vmem_limit_bytes=48 * 1024 * 1024),
        cost_estimate=pl.CostEstimate(
            flops=4 * tok * H * HD * SPAN, bytes_accessed=4 * 1024 * 1024, transcendentals=0
        ),
        name="attend",
    )(low, queries, window)


def attend_back(queries, window, low, d_context, lse):
    tok = queries.shape[0]
    groups = H // HEADS_STEP
    blocks = tok // QBLK
    return pl.pallas_call(
        attend_back_kernel,
        grid=(blocks, groups),
        in_specs=[
            pl.BlockSpec((1, QBLK), lambda i, j: (0, i)),
            pl.BlockSpec((QBLK, HEADS_STEP * HD), lambda i, j: (i, j)),
            pl.BlockSpec((WINDOW + tok, 2 * HD), lambda i, j: (0, 0)),
            pl.BlockSpec((QBLK, HEADS_STEP * HD), lambda i, j: (i, j)),
            pl.BlockSpec((1, 1, ROWS), lambda i, j: (i * groups + j, 0, 0)),
        ],
        out_specs=[
            pl.BlockSpec((QBLK, HEADS_STEP * HD), lambda i, j: (i, j)),
            pl.BlockSpec((WINDOW + tok, 2 * HD), lambda i, j: (0, 0)),
        ],
        out_shape=[
            jax.ShapeDtypeStruct((tok, H * HD), BF),
            jax.ShapeDtypeStruct((WINDOW + tok, 2 * HD), F32),
        ],
        compiler_params=pltpu.CompilerParams(vmem_limit_bytes=48 * 1024 * 1024),
        cost_estimate=pl.CostEstimate(
            flops=10 * tok * H * HD * SPAN, bytes_accessed=6 * 1024 * 1024, transcendentals=0
        ),
        name="attend_back",
    )(low, queries, window, d_context, lse)


def snake(pos, size_a, size_b):
    if size_b == 1:
        return pos, pos * 0
    down = pos // size_a
    first = 1 - (down + 7) // 8
    q = (pos - size_a) * (1 - first)
    a_up = size_a - 1 - q // (size_b - 1)
    k = q % (size_b - 1)
    odd = a_up % 2
    b_up = odd * (1 + k) + (1 - odd) * (size_b - 1 - k)
    return first * pos + (1 - first) * a_up, (1 - first) * b_up


def snake_place(a, b, size_a, size_b):
    if size_b == 1:
        return a
    moved = (b + size_b - 1) // size_b
    odd = a % 2
    along = odd * (b - 1) + (1 - odd) * (size_b - 1 - b)
    return (1 - moved) * a + moved * (size_a + (size_a - 1 - a) * (size_b - 1) + along)


def kept_slot(a, b, size_a, size_b):
    half = size_a * size_b // 2
    return (1 - b % 2) * half + a * (size_b // 2) + b // 2


class Piece:
    def __init__(self, at, rows, square, shared, part, parts):
        self.at, self.rows, self.square, self.shared = at, rows, square, shared
        self.part, self.parts = part, parts
        self.relays = [0, 1, 2, 3] if square else []
        if shared:
            self.relays += [4, 5, 6, 7, 8] if square else [4]


def fetch_kernel(sizes, pieces, n_in, n_dealt, *refs):
    size_a, size_b, size_x = sizes
    n_ctx = size_a * size_b * 2
    ins, refs = refs[:n_in], refs[n_in:]
    outs, refs = refs[:n_in], refs[n_in:]
    n_weights = n_in - n_dealt - 1
    stages, refs = refs[:n_weights], refs[n_weights:]
    keep_sem, own_sem, deal_send, deal_recv, gain_send, gain_recv = refs[:6]
    x_send, x_recv, relay_send, relay_recv = refs[6:]
    ia, ib, ic, ix = (lax.axis_index(name) for name in ALL)
    own = (ia * size_b + ib) * 2 + ic
    rank = ix * 2 + ic
    pa, pb = ia % 2, ib % 2
    other_a, other_b = ia + 1 - 2 * pa, ib + 1 - 2 * pb
    corner = pa * 2 + pb
    corner_a, corner_b, corner_d = (1 - pa) * 2 + pb, pa * 2 + 1 - pb, 3 - corner

    barrier = pltpu.get_barrier_semaphore()
    greeted = []
    for k in range(1, n_ctx):
        e = (own + k) % n_ctx
        greeted.append((e // 2 // size_b, e // 2 % size_b, e % 2, ix))
    for s in range(1, size_x):
        greeted.append((ia, ib, ic, (ix + s) % size_x))
    for device in greeted:
        pl.semaphore_signal(barrier, inc=1, device_id=device, device_id_type=MESH)
    pl.semaphore_wait(barrier, len(greeted))

    def remote(src, dst, send, recv, device):
        return pltpu.make_async_remote_copy(
            src_ref=src,
            dst_ref=dst,
            send_sem=send,
            recv_sem=recv,
            device_id=device,
            device_id_type=MESH,
        )

    def x_copy(i, s):
        p = pieces[i]
        shard, full = ins[p.at], outs[p.at]
        target = (ix + s) % size_x
        height = shard.shape[0]
        rows, start = region(p, corner, ic)
        if p.shared:
            src = shard.at[pl.ds(start, rows), :]
        else:
            cols = full.shape[1]
            at = pl.multiple_of((target * 2 + ic) * cols, cols)
            src = shard.at[pl.ds(start, rows), pl.ds(at, cols)]
        dst = full.at[pl.ds(pl.multiple_of(ix * height + start, rows), rows), :]
        return remote(src, dst, x_send.at[i, s], x_recv.at[i, s], (ia, ib, ic, target))

    def region(p, which, core):
        owner = which if p.square else 0
        owners = 4 if p.square else 1
        if p.shared:
            owner, owners = owner * 2 + core, owners * 2
        rows = p.rows // (owners * p.parts)
        return rows, pl.multiple_of((owner * p.parts + p.part) * rows, rows)

    def landed(i, s, which, core, half=None):
        p = pieces[i]
        rows, start = region(p, which, core)
        start = start + (ix + size_x - s) % size_x * p.rows
        if half is not None:
            rows = rows // 2
            start = start + half * rows
        return outs[p.at].at[pl.ds(pl.multiple_of(start, rows), rows), :]

    def relay(i, s, kind, incoming=False):
        sem = (relay_send.at[i, s, kind], relay_recv.at[i, s, kind])
        if kind < 4:
            device = (other_a, ib, ic, ix) if kind in (1, 2) else (ia, other_b, ic, ix)
            sent = (
                landed(i, s, corner, ic),
                landed(i, s, corner, ic),
                landed(i, s, corner_b, ic, 0),
                landed(i, s, corner_a, ic, 1),
            )[kind]
            came = (
                landed(i, s, corner_b, ic),
                landed(i, s, corner_a, ic),
                landed(i, s, corner_d, ic, 0),
                landed(i, s, corner_d, ic, 1),
            )[kind]
        else:
            device = (ia, ib, 1 - ic, ix)
            which, half = ((corner, None), (corner_b, None), (corner_a, None), (corner_d, 0), (corner_d, 1))[
                kind - 4
            ]
            sent = landed(i, s, which, ic, half)
            came = landed(i, s, which, 1 - ic, half)
        ref = came if incoming else sent
        return remote(ref, ref, *sem, device)

    rows = ins[0].shape[0] // n_ctx

    def deal_copy(t, k):
        e = (own + k) % n_ctx
        src = ins[t].at[pl.ds(pl.multiple_of(e * rows, rows), rows), :]
        dst = outs[t].at[pl.ds(pl.multiple_of(own * rows, rows), rows), :]
        if k == 0:
            return pltpu.make_async_copy(src, dst, own_sem.at[t])
        device = (e // 2 // size_b, e // 2 % size_b, e % 2, ix)
        return remote(src, dst, deal_send.at[t, k], deal_recv.at[t, k], device)

    g = n_in - 1

    def gain_copy(s):
        if s == 0:
            return pltpu.make_async_copy(ins[g], outs[g].at[ix], own_sem.at[g])
        device = (ia, ib, ic, (ix + s) % size_x)
        return remote(ins[g], outs[g].at[ix], gain_send.at[s], gain_recv.at[s], device)

    def keep_copy(w, out):
        shard, full = ins[w], outs[w]
        stage = stages[w - n_dealt]
        height = shard.shape[0]
        sem = keep_sem.at[w, out]
        if out:
            dst = full.at[pl.ds(pl.multiple_of(ix * height, height), height), :]
            return pltpu.make_async_copy(stage, dst, sem)
        src = shard
        if full.shape[1] != shard.shape[1]:
            cols = full.shape[1]
            src = shard.at[:, pl.ds(pl.multiple_of(rank * cols, cols), cols)]
        return pltpu.make_async_copy(src, stage, sem)

    ahead = 4
    order = [(i, s) for i in range(len(pieces)) for s in range(1, size_x)]
    for k in range(n_ctx):
        deal_copy(0, k).start()
    for s in range(size_x):
        gain_copy(s).start()
    for i, s in order[:ahead]:
        x_copy(i, s).start()
    for t in range(1, n_dealt):
        for k in range(n_ctx):
            deal_copy(t, k).start()
    for w in range(n_dealt, n_dealt + n_weights):
        keep_copy(w, 0).start()

    for n in range(len(order) + 2):
        if n < n_weights:
            keep_copy(n_dealt + n, 0).wait()
            keep_copy(n_dealt + n, 1).start()
        if n < len(order):
            i, s = order[n]
            x_copy(i, s).wait_recv()
            for kind in (0, 1, 4):
                if kind in pieces[i].relays:
                    relay(i, s, kind).start()
            if n + ahead < len(order):
                x_copy(i, s).wait_send()
                x_copy(*order[n + ahead]).start()
        if 1 <= n <= len(order) and pieces[order[n - 1][0]].square:
            i, s = order[n - 1]
            relay(i, s, 0, True).wait_recv()
            relay(i, s, 2).start()
            relay(i, s, 1, True).wait_recv()
            relay(i, s, 3).start()
            if pieces[i].shared:
                relay(i, s, 5).start()
                relay(i, s, 6).start()
        if n >= 2 and pieces[order[n - 2][0]].square:
            i, s = order[n - 2]
            relay(i, s, 2, True).wait_recv()
            relay(i, s, 3, True).wait_recv()
            if pieces[i].shared:
                relay(i, s, 7).start()
                relay(i, s, 8).start()

    for n, (i, s) in enumerate(order):
        if n + ahead >= len(order):
            x_copy(i, s).wait_send()
        for kind in pieces[i].relays:
            relay(i, s, kind).wait_send()
            if kind >= 4:
                relay(i, s, kind, True).wait_recv()
    for t in range(n_dealt):
        for k in range(n_ctx):
            deal_copy(t, k).wait()
    for s in range(size_x):
        gain_copy(s).wait()
    for w in range(n_dealt, n_dealt + n_weights):
        keep_copy(w, 1).wait()


def fetch(sizes, dealt, shared, split, gains):
    size_a, size_b, size_x = sizes
    n_ctx = size_a * size_b * 2
    ins = dealt + shared + split + [gains]
    outs = [jax.ShapeDtypeStruct(a.shape, BF) for a in dealt]
    outs += [jax.ShapeDtypeStruct((size_x * a.shape[0], a.shape[1]), BF) for a in shared]
    outs += [
        jax.ShapeDtypeStruct((size_x * a.shape[0], a.shape[1] // (2 * size_x)), BF) for a in split
    ]
    outs.append(jax.ShapeDtypeStruct((size_x,) + gains.shape, BF))
    pieces = []
    first = len(dealt)
    pieces.append(Piece(first, shared[0].shape[0], True, True, 0, 1))
    for part in range(2):
        for n, a in enumerate(split):
            pieces.append(Piece(first + len(shared) + n, a.shape[0], True, False, part, 2))
    for n, a in enumerate(shared[1:]):
        pieces.append(Piece(first + 1 + n, a.shape[0], False, True, 0, 1))
    count = len(pieces)
    sem = pltpu.SemaphoreType.DMA
    return pl.pallas_call(
        functools.partial(fetch_kernel, sizes, pieces, len(ins), len(dealt)),
        in_specs=[pl.BlockSpec(memory_space=pl.ANY)] * len(ins),
        out_specs=[pl.BlockSpec(memory_space=pl.ANY)] * len(outs),
        out_shape=outs,
        scratch_shapes=[
            pltpu.VMEM((a.shape[0], o.shape[1]), BF)
            for a, o in zip(ins[len(dealt) : -1], outs[len(dealt) : -1])
        ]
        + [
            sem((len(ins), 2)),
            sem((len(ins),)),
            sem((len(dealt), n_ctx)),
            sem((len(dealt), n_ctx)),
            sem((size_x,)),
            sem((size_x,)),
            sem((count, size_x)),
            sem((count, size_x)),
            sem((count, size_x, 9)),
            sem((count, size_x, 9)),
        ],
        compiler_params=pltpu.CompilerParams(
            collective_id=1, has_side_effects=True, vmem_limit_bytes=48 * 1024 * 1024
        ),
        cost_estimate=pl.CostEstimate(
            flops=0, bytes_accessed=300 * 1024 * 1024, transcendentals=0
        ),
        name="fetch",
    )(*ins)


class Job:
    def __init__(self, phase, left, right, rows, cols, by_rank):
        self.phase, self.left, self.right = phase, left, right
        self.rows, self.cols, self.by_rank = rows, cols, by_rank


def grads_kernel(sizes, jobs, *refs):
    size_a, size_b, size_x = sizes
    chips = size_a * size_b
    n_ctx = 2 * chips
    ranks = 2 * size_x
    count = len(jobs)
    ins, refs = refs[:11], refs[11:]
    outs, refs = refs[:count], refs[count:]
    dealt, refs = refs[:2], refs[2:]
    gain_out, refs = refs[0], refs[1:]
    held, refs = refs[:8], refs[8:]
    gain_ctx, gain_x, refs = refs[0], refs[1], refs[2:]
    recv, refs = refs[:count], refs[count:]
    send, refs = refs[:count], refs[count:]
    done, refs = refs[:count], refs[count:]
    load_sem, group_send, group_recv, deal_send, deal_recv = refs[:5]
    gain_send, gain_recv, send_sem, recv_sem, done_send, done_recv, own_sem = refs[5:]
    ia, ib, ic, ix = (lax.axis_index(name) for name in ALL)
    own = (ia * size_b + ib) * 2 + ic
    rank = ix * 2 + ic
    place = snake_place(ia, ib, size_a, size_b)

    def on_ring(step):
        return snake((place + 2 * chips + step) % chips, size_a, size_b)

    def member(k):
        return (ic + k // size_x) % 2, (ix + k % size_x) % size_x

    def ctx_device(k):
        e = (own + k) % n_ctx
        return e // 2 // size_b, e // 2 % size_b, e % 2, ix

    kept = rank * chips + kept_slot(ia, ib, size_a, size_b)
    kept_chip = kept // ranks
    kept_id = (kept_chip // size_b, kept_chip % size_b, (kept // size_x) % 2, kept % size_x)
    flat = own * size_x + ix
    from_rank = flat // chips
    from_slot = flat % chips
    half = chips // 2
    from_id = (
        (from_slot % half) // (size_b // 2),
        ((from_slot % half) % (size_b // 2)) * 2 + 1 - from_slot // half,
        from_rank % 2,
        from_rank // 2,
    )

    def remote(src, dst, sent, came, device):
        return pltpu.make_async_remote_copy(
            src_ref=src,
            dst_ref=dst,
            send_sem=sent,
            recv_sem=came,
            device_id=device,
            device_id_type=MESH,
        )

    loads = [pltpu.make_async_copy(ins[i], held[i], load_sem.at[i]) for i in range(3)]
    for copy in loads:
        copy.start()

    barrier = pltpu.get_barrier_semaphore()
    greeted = [ctx_device(k) for k in range(1, n_ctx)] + [from_id]
    greeted += [(ia, ib) + member(k) for k in range(ranks) if k % size_x]
    for device in greeted:
        pl.semaphore_signal(barrier, inc=1, device_id=device, device_id_type=MESH)
    pl.semaphore_wait(barrier, len(greeted))

    def group_copy(i, k):
        c, x = member(k)
        src, dst = ins[i], held[i].at[k]
        target = x * 2 + c
        if i == 4:
            rows = held[i].shape[1]
            src = src.at[pl.ds(pl.multiple_of(target * rows, rows), rows), :]
        if i == 6:
            cols = held[i].shape[2]
            src = src.at[:, pl.ds(pl.multiple_of(target * cols, cols), cols)]
        if k == 0:
            return pltpu.make_async_copy(src, dst, load_sem.at[i])
        return remote(src, dst, group_send.at[i, k], group_recv.at[i, k], (ia, ib, c, x))

    def deal_copy(t, k):
        e = (own + k) % n_ctx
        rows = ins[8 + t].shape[0] // n_ctx
        src = ins[8 + t].at[pl.ds(pl.multiple_of(e * rows, rows), rows), :]
        dst = dealt[t].at[pl.ds(pl.multiple_of(own * rows, rows), rows), :]
        if k == 0:
            return pltpu.make_async_copy(src, dst, load_sem.at[8 + t])
        return remote(src, dst, deal_send.at[t, k], deal_recv.at[t, k], ctx_device(k))

    def gain_copy(k):
        src, dst = ins[10].at[(own + k) % n_ctx], gain_ctx.at[k]
        if k == 0:
            return pltpu.make_async_copy(src, dst, load_sem.at[10])
        return remote(src, dst, deal_send.at[2, k], deal_recv.at[2, k], ctx_device(k))

    def gain_copy_x(s):
        device = (ia, ib, ic, (ix + s) % size_x)
        return remote(gain_x.at[0], gain_x.at[s], gain_send.at[s], gain_recv.at[s], device)

    def ring_copy(j, way, step, parity):
        neighbour = on_ring(1 - 2 * way) + (ic, ix)
        return remote(
            send[j].at[way, parity],
            recv[j].at[way, step],
            send_sem.at[j, way, parity],
            recv_sem.at[j, way, step],
            neighbour,
        )

    def product(j, way, step):
        job = jobs[j]
        a, b = on_ring(step * (2 * way - 1))
        part = job.rows // chips
        cols = slice(way * job.cols // 2, (way + 1) * job.cols // 2)
        left, right = held[job.left], held[job.right]
        if job.phase == 0:
            start = pl.multiple_of((a * size_b + b) * part, part)
            return mm_tn(left[:, pl.ds(start, part)], right[:, cols])
        if job.by_rank:
            start = kept_slot(a, b, size_a, size_b) * part
            if left.shape[1] != job.rows:
                start = start + rank * job.rows
        else:
            start = (a * size_b + b) * part
        rows = pl.ds(pl.multiple_of(start, part), part)
        total = mm(left[0, rows, :], right[0, :, cols])
        for k in range(1, ranks):
            total = total + mm(left[k, rows, :], right[k, :, cols])
        return total

    def deliver(j):
        job = jobs[j]
        if job.by_rank:
            return [remote(done[j], outs[j], done_send.at[j, 0], done_recv.at[j, 0], kept_id)]
        part = job.rows // (chips * ranks)
        copies = []
        for k in range(ranks):
            c, x = member(k)
            start = pl.multiple_of((c * size_x + x) * part, part)
            src, dst = done[j].at[pl.ds(start, part), :], outs[j].at[rank]
            if k == 0:
                copies.append(pltpu.make_async_copy(src, dst, own_sem.at[j]))
            else:
                copies.append(
                    remote(src, dst, done_send.at[j, k], done_recv.at[j, k], (ia, ib, c, x))
                )
        return copies

    for copy in loads:
        copy.wait()
    for phase in range(2):
        mine = [j for j in range(count) if jobs[j].phase == phase]
        for j in mine:
            for way in range(2):
                send[j][way, 0] = product(j, way, 1).astype(BF)
                ring_copy(j, way, 0, 0).start()
        if phase == 0:
            for k in range(n_ctx):
                gain_copy(k).start()
            for i in range(3, 8):
                for k in range(ranks):
                    group_copy(i, k).start()
            for t in range(2):
                for k in range(n_ctx):
                    deal_copy(t, k).start()

        def step_of(step, carry):
            parity = step % 2
            for j in mine:
                for way in range(2):
                    part = product(j, way, step + 1)
                    ring_copy(j, way, step - 1, 1 - parity).wait_recv()
                    part = part + recv[j][way, step - 1].astype(F32)

                    @pl.when(step >= 2)
                    def _():
                        ring_copy(j, way, step - 2, parity).wait_send()

                    send[j][way, parity] = part.astype(BF)
                    ring_copy(j, way, step, parity).start()
            return carry

        lax.fori_loop(1, chips - 1, step_of, 0)
        if phase == 0:
            for k in range(n_ctx):
                gain_copy(k).wait()
            gain_x[0] = jnp.sum(gain_ctx[...], axis=0)
            for s in range(1, size_x):
                gain_copy_x(s).start()
        last = chips - 2
        for j in mine:
            cols = jobs[j].cols // 2
            for way in range(2):
                part = product(j, way, chips)
                ring_copy(j, way, last, last % 2).wait_recv()
                part = part + recv[j][way, last].astype(F32)
                done[j][:, way * cols : (way + 1) * cols] = part.astype(BF)
            for copy in deliver(j):
                copy.start()
            for way in range(2):
                ring_copy(j, way, last - 1, (last - 1) % 2).wait_send()
                ring_copy(j, way, last, last % 2).wait_send()
        if phase == 0:
            for i in range(3, 8):
                for k in range(ranks):
                    group_copy(i, k).wait()
    for s in range(1, size_x):
        gain_copy_x(s).wait()
    gain_out[...] = jnp.sum(gain_x[...], axis=0)
    for t in range(2):
        for k in range(n_ctx):
            deal_copy(t, k).wait()
    for j in range(count):
        for copy in deliver(j):
            copy.wait()


def sum_grads(sizes, ins):
    size_a, size_b, size_x = sizes
    chips = size_a * size_b
    ranks = 2 * size_x
    normed_mlp, d_gate, d_upward = ins[:3]
    width = normed_mlp.shape[1]
    tok = ins[5].shape[0]
    part_width = width // ranks
    jobs = [
        Job(0, 0, 1, width, d_gate.shape[1], False),
        Job(0, 0, 2, width, d_upward.shape[1], False),
        Job(1, 3, 6, width, part_width, False),
        Job(1, 4, 5, part_width, width, True),
        Job(1, 3, 7, part_width, 2 * HD, True),
    ]
    held = [pltpu.VMEM(a.shape, BF) for a in ins[:3]]
    held += [
        pltpu.VMEM((ranks,) + shape, BF)
        for shape in (
            (width, tok),
            (part_width, tok),
            (tok, width),
            (tok, part_width),
            (tok, 2 * HD),
        )
    ]
    outs, recv, send, done = [], [], [], []
    flops = 0
    for job in jobs:
        part = job.rows // chips
        if job.by_rank:
            outs.append(jax.ShapeDtypeStruct((part, job.cols), BF))
        else:
            outs.append(jax.ShapeDtypeStruct((ranks, part // ranks, job.cols), BF))
        recv.append(pltpu.VMEM((2, chips - 1, part, job.cols // 2), BF))
        send.append(pltpu.VMEM((2, 2, part, job.cols // 2), BF))
        done.append(pltpu.VMEM((part, job.cols), BF))
        flops += 2 * job.rows * job.cols * normed_mlp.shape[0]
    count = len(jobs)
    outs += [jax.ShapeDtypeStruct((tok, width), BF)] * 2
    gain_shape = ins[10].shape[1:]
    outs.append(jax.ShapeDtypeStruct(gain_shape, F32))
    sem = pltpu.SemaphoreType.DMA
    return pl.pallas_call(
        functools.partial(grads_kernel, sizes, jobs),
        in_specs=[pl.BlockSpec(memory_space=pl.ANY)] * len(ins),
        out_specs=[pl.BlockSpec(memory_space=pl.ANY)] * (count + 2)
        + [pl.BlockSpec(memory_space=pltpu.VMEM)],
        out_shape=outs,
        scratch_shapes=held
        + [pltpu.VMEM((2 * chips,) + gain_shape, F32), pltpu.VMEM((size_x,) + gain_shape, F32)]
        + recv
        + send
        + done
        + [
            sem((len(ins),)),
            sem((8, ranks)),
            sem((8, ranks)),
            sem((3, 2 * chips)),
            sem((3, 2 * chips)),
            sem((size_x,)),
            sem((size_x,)),
            sem((count, 2, 2)),
            sem((count, 2, chips - 1)),
            sem((count, ranks)),
            sem((count, ranks)),
            sem((count,)),
        ],
        compiler_params=pltpu.CompilerParams(
            collective_id=0, has_side_effects=True, vmem_limit_bytes=60 * 1024 * 1024
        ),
        cost_estimate=pl.CostEstimate(
            flops=flops, bytes_accessed=400 * 1024 * 1024, transcendentals=0
        ),
        name="sum_grads",
    )(*ins)


def norm_stats(values):
    inv = lax.rsqrt(jnp.mean(values * values, axis=-1, keepdims=True) + epsilon)
    return values * inv, inv


def norm_back(unit, inv, gain, grad):
    scaled = grad * gain
    inner = jnp.mean(scaled * unit, axis=-1, keepdims=True)
    return inv * (scaled - unit * inner), jnp.sum(grad * unit, axis=0)


def on_device(
    sizes,
    tokens,
    lengths,
    dealing,
    attn_gain,
    query_weight,
    kv_weight,
    out_weight,
    mlp_gain,
    gate_weight,
    up_weight,
    down_weight,
    cotangent,
):
    size_a, size_b, size_x = sizes
    chips = size_a * size_b
    n_ctx = chips * 2
    ranks = 2 * size_x
    ia, ib, ic, ix = (lax.axis_index(name) for name in ALL)
    chip = ia * size_b + ib
    own = chip * 2 + ic
    flat = own * size_x + ix
    rank = ix * 2 + ic
    tok = tokens.shape[1]
    width = tokens.shape[2]
    piece = tok // n_ctx
    halo = WINDOW // tok
    swap = [(0, 1), (1, 0)]

    def pick(array, index, axis=0):
        return lax.dynamic_index_in_dim(array, index, axis, keepdims=False)

    def put(array, part, index, axis=0):
        return lax.dynamic_update_index_in_dim(array, part, index, axis)

    def to_core(array):
        return lax.ppermute(array, "c", swap)

    def to_x(array, step):
        return lax.ppermute(array, "x", [(i, (i + step) % size_x) for i in range(size_x)])

    def shift_ctx(array, step):
        pairs = [(i, i + step) for i in range(n_ctx) if 0 <= i + step < n_ctx]
        return lax.ppermute(array, CTX, pairs)

    def from_x(step):
        return (ix + size_x - step) % size_x

    def group_rows(array):
        parts = [array, to_core(array)]
        for step in range(1, size_x):
            got = to_x(array, step)
            parts += [got, to_core(got)]
        return jnp.concatenate(parts, 0)

    def group_sum(part_of):
        total = None
        for step in list(range(1, size_x)) + [0]:
            both = part_of(step)
            summed = both[:tok] + to_core(both[tok:].astype(BF)).astype(F32)
            if step:
                summed = to_x(summed.astype(BF), size_x - step).astype(F32)
            total = summed if total is None else total + summed
        return total

    def sum_rows(grad):
        summed = lax.psum_scatter(
            grad.astype(BF), ("a", "b"), scatter_dimension=0, tiled=True
        )
        keep_pairs = []
        for g in range(chips):
            for c in range(2):
                for x in range(size_x):
                    keep_pairs.append(((g * 2 + c) * size_x + x, (x * 2 + c) * chips + g))
        return lax.ppermute(summed, ALL, keep_pairs).astype(F32)

    own_deal = pick(dealing[0], own)
    deal = (own_deal[:, None] == jnp.arange(tok, dtype=jnp.int32)[None, :]).astype(BF)

    gains = jnp.stack([attn_gain, mlp_gain]).reshape(-1, 128)
    inputs_low, cot, w_query, w_kv, w_out, w_gate, w_up, gains = fetch(
        sizes,
        [mm(deal, tokens[0]).astype(BF), mm(deal, cotangent[0]).astype(BF)],
        [query_weight, kv_weight, out_weight],
        [gate_weight, up_weight],
        gains,
    )
    gains = gains.reshape(size_x, 2, -1).astype(F32)
    gain_one = gains[:, 0].reshape(-1)
    gain_two = gains[:, 1].reshape(-1)
    down_part = down_weight.shape[0] // 2
    w_down = lax.dynamic_slice(down_weight, (ic * down_part, 0), (down_part, width))

    inputs = inputs_low.astype(F32)
    unit_one, inv_one = norm_stats(inputs)
    normed = (unit_one * gain_one).astype(BF)
    pairs = mm(normed, w_kv).astype(BF)
    window = jnp.concatenate([shift_ctx(pairs, halo - j) for j in range(halo)] + [pairs], 0)
    queries = mm(normed, w_query).astype(BF)
    stream = own * tok + jnp.arange(tok, dtype=jnp.int32)
    ends = jnp.cumsum(lengths[0])
    starts = jnp.max(jnp.where(stream[:, None] >= ends[None, :], ends[None, :], 0), axis=1)
    low = jnp.maximum(starts, stream - (WINDOW - 1)) - (own * tok - WINDOW)
    low = low.astype(jnp.int32)[None, :]
    context, lse = attend(queries, window, low)
    resid = inputs + mm(context, w_out)

    unit_two, inv_two = norm_stats(resid)
    normed_mlp = group_rows((unit_two * gain_two).astype(BF))
    cot_rows = group_rows(cot)
    gate = mm(normed_mlp, w_gate)
    upward = mm(normed_mlp, w_up)
    d_hidden = mm_nt(cot_rows, w_down)
    act, pull = jax.vjp(lambda v: jax.nn.gelu(v, approximate=True), gate)
    hidden = (act * upward).astype(BF)
    d_gate = pull(d_hidden * upward)[0].astype(BF)
    d_upward = (d_hidden * act).astype(BF)

    def rows_of(array, step):
        return array[2 * step * tok : 2 * (step + 1) * tok]

    d_normed_mlp = group_sum(
        lambda step: mm_nt(rows_of(d_gate, step), w_gate) + mm_nt(rows_of(d_upward, step), w_up)
    )
    down_grad = sum_rows(mm_tn(hidden, cot_rows))
    branch_mlp = group_sum(lambda step: mm(rows_of(hidden, step), w_down))
    block_output = (resid + branch_mlp).astype(BF)
    d_resid_part, mlp_gain_grad = norm_back(unit_two, inv_two, gain_two, d_normed_mlp)
    d_resid = cot.astype(F32) + d_resid_part
    d_branch = d_resid.astype(BF)

    d_context = mm_nt(d_branch, w_out).astype(BF)
    d_queries, d_window = attend_back(queries, window, low, d_context, lse)
    d_pairs = d_window[halo * tok :]
    for j in range(halo):
        part = d_window[j * tok : (j + 1) * tok].astype(BF)
        d_pairs = d_pairs + shift_ctx(part, j - halo).astype(F32)
    d_pairs = d_pairs.astype(BF)
    d_normed = mm_nt(d_queries, w_query) + mm_nt(d_pairs, w_kv)
    d_inputs, attn_gain_grad = norm_back(unit_one, inv_one, gain_one, d_normed)
    gain_part = width // (n_ctx * size_x)
    gain_grads = jnp.stack([attn_gain_grad, mlp_gain_grad]).reshape(2, n_ctx, size_x, gain_part)
    gain_grads = gain_grads.transpose(1, 2, 0, 3).reshape(n_ctx, -1)
    gain_grads = jnp.pad(gain_grads, ((0, 0), (0, 1024 - gain_grads.shape[1])))
    sums = sum_grads(
        sizes,
        [
            normed_mlp,
            d_gate,
            d_upward,
            normed.T,
            context.T,
            d_branch,
            d_queries,
            d_pairs,
            block_output,
            (d_resid + d_inputs).astype(BF),
            gain_grads.reshape(n_ctx, 8, 128),
        ],
    )
    gate_grad, up_grad, query_grad = (
        v.transpose(1, 0, 2).reshape(v.shape[1], -1).astype(F32) for v in sums[:3]
    )
    out_grad, kv_grad = (v.astype(F32) for v in sums[3:5])
    block_output = mm_tn(deal, sums[5]).astype(BF)
    token_grad = mm_tn(deal, sums[6])
    gain_grads = lax.dynamic_slice(sums[7].reshape(-1), (ix * 2 * gain_part,), (2 * gain_part,))
    attn_gain_grad, mlp_gain_grad = gain_grads[:gain_part], gain_grads[gain_part:]
    return (
        block_output[None],
        token_grad[None],
        attn_gain_grad,
        query_grad,
        kv_grad,
        out_grad,
        mlp_gain_grad,
        gate_grad,
        up_grad,
        down_grad,
    )


def solution(mesh):
    n_ctx, size_x = mesh.shape["ctx"], mesh.shape["fsdp"]
    chips = n_ctx // 2
    size_a = 4 if chips % 4 == 0 else chips
    size_b = chips // size_a
    fine = Mesh(mesh.devices.reshape(size_a, size_b, 2, size_x), ALL)
    rows = P("x", CTX, None)
    split = P("x", None)
    every = P(ALL)
    matrix = P(ALL, None)
    return jax.shard_map(
        functools.partial(on_device, (size_a, size_b, size_x)),
        mesh=fine,
        in_specs=(
            rows,
            split,
            P("x", None, None),
            P("x"),
            split,
            split,
            split,
            P("x"),
            split,
            split,
            split,
            rows,
        ),
        out_specs=(rows, rows, every, matrix, matrix, matrix, every, matrix, matrix, matrix),
        check_vma=False,
    )
```

```python
import functools

import jax
import jax.numpy as jnp
import numpy as np
from jax import lax
from jax.experimental import pallas as pl
from jax.experimental.pallas import tpu as pltpu
from jax.sharding import Mesh
from jax.sharding import PartitionSpec as P

H = 16
HD = 128
WINDOW = 1024
QBLK = 128
HEADS_STEP = 4
SPAN = WINDOW + QBLK
ROWS = HEADS_STEP * QBLK

epsilon = 1e-06
neg_large = -1e30
scale = HD ** (-0.5)
root = (2.0 / np.pi) ** 0.5
cubic = 0.044715
BF = jnp.bfloat16
F32 = jnp.float32
CTX = ("a", "b", "c")
ALL = ("a", "b", "c", "x")
MESH = pl.DeviceIdType.MESH


def mm(left, right):
    return jnp.dot(left, right, preferred_element_type=F32)


def mm_tn(left, right):
    return lax.dot_general(left, right, (((0,), (0,)), ((), ())), preferred_element_type=F32)


def mm_nt(left, right):
    return lax.dot_general(left, right, (((1,), (1,)), ((), ())), preferred_element_type=F32)


def stack_heads(block):
    return jnp.concatenate([block[:, h * HD : (h + 1) * HD] for h in range(HEADS_STEP)], 0)


def unstack_heads(block_t):
    return jnp.concatenate(
        [block_t[:, h * QBLK : (h + 1) * QBLK].T for h in range(HEADS_STEP)], 1
    )


def bias_of(lo_ref, qb):
    key = lax.broadcasted_iota(jnp.int32, (SPAN, QBLK), 0) + qb * QBLK
    query = lax.broadcasted_iota(jnp.int32, (SPAN, QBLK), 1) + (WINDOW + qb * QBLK)
    allowed = (key >= lo_ref[...]) & (key <= query)
    bias = jnp.where(allowed, 0.0, neg_large).astype(F32)
    return jnp.concatenate([bias] * HEADS_STEP, 1)


def attend_kernel(lo_ref, q_ref, kv_ref, o_ref, lse_ref):
    qb = pl.program_id(0)
    rows = pl.ds(pl.multiple_of(qb * QBLK, QBLK), SPAN)
    keys = kv_ref[rows, :HD]
    values = kv_ref[rows, HD:]
    scores = mm_nt(keys, stack_heads(q_ref[...])) * scale + bias_of(lo_ref, qb)
    top = jnp.max(scores, axis=0, keepdims=True)
    raised = jnp.exp(scores - top)
    total = jnp.sum(raised, axis=0, keepdims=True)
    out_t = mm_tn(values, raised.astype(BF)) * (1.0 / total)
    o_ref[...] = unstack_heads(out_t).astype(BF)
    lse_ref[0] = top + jnp.log(total)


def attend_back_kernel(lo_ref, q_ref, kv_ref, do_ref, lse_ref, dq_ref, dkv_ref):
    qb = pl.program_id(0)

    @pl.when((qb == 0) & (pl.program_id(1) == 0))
    def _():
        dkv_ref[...] = jnp.zeros_like(dkv_ref)

    rows = pl.ds(pl.multiple_of(qb * QBLK, QBLK), SPAN)
    keys = kv_ref[rows, :HD]
    values = kv_ref[rows, HD:]
    queries = stack_heads(q_ref[...])
    d_out = stack_heads(do_ref[...])
    scores = mm_nt(keys, queries) * scale + bias_of(lo_ref, qb)
    probs = jnp.exp(scores - lse_ref[0])
    d_probs = mm_nt(values, d_out)
    delta = jnp.sum(probs * d_probs, axis=0, keepdims=True)
    d_scores = (probs * (d_probs - delta)).astype(BF)
    dq_ref[...] = unstack_heads(mm_tn(keys, d_scores) * scale).astype(BF)
    dkv_ref[rows, :HD] += mm(d_scores, queries) * scale
    dkv_ref[rows, HD:] += mm(probs.astype(BF), d_out)


def attend(queries, window, low):
    tok = queries.shape[0]
    groups = H // HEADS_STEP
    blocks = tok // QBLK
    return pl.pallas_call(
        attend_kernel,
        grid=(blocks, groups),
        in_specs=[
            pl.BlockSpec((1, QBLK), lambda i, j: (0, i)),
            pl.BlockSpec((QBLK, HEADS_STEP * HD), lambda i, j: (i, j)),
            pl.BlockSpec((WINDOW + tok, 2 * HD), lambda i, j: (0, 0)),
        ],
        out_specs=[
            pl.BlockSpec((QBLK, HEADS_STEP * HD), lambda i, j: (i, j)),
            pl.BlockSpec((1, 1, ROWS), lambda i, j: (i * groups + j, 0, 0)),
        ],
        out_shape=[
            jax.ShapeDtypeStruct((tok, H * HD), BF),
            jax.ShapeDtypeStruct((blocks * groups, 1, ROWS), F32),
        ],
        compiler_params=pltpu.CompilerParams(vmem_limit_bytes=48 * 1024 * 1024),
        cost_estimate=pl.CostEstimate(
            flops=4 * tok * H * HD * SPAN, bytes_accessed=4 * 1024 * 1024, transcendentals=0
        ),
        name="attend",
    )(low, queries, window)


def attend_back(queries, window, low, d_context, lse):
    tok = queries.shape[0]
    groups = H // HEADS_STEP
    blocks = tok // QBLK
    return pl.pallas_call(
        attend_back_kernel,
        grid=(blocks, groups),
        in_specs=[
            pl.BlockSpec((1, QBLK), lambda i, j: (0, i)),
            pl.BlockSpec((QBLK, HEADS_STEP * HD), lambda i, j: (i, j)),
            pl.BlockSpec((WINDOW + tok, 2 * HD), lambda i, j: (0, 0)),
            pl.BlockSpec((QBLK, HEADS_STEP * HD), lambda i, j: (i, j)),
            pl.BlockSpec((1, 1, ROWS), lambda i, j: (i * groups + j, 0, 0)),
        ],
        out_specs=[
            pl.BlockSpec((QBLK, HEADS_STEP * HD), lambda i, j: (i, j)),
            pl.BlockSpec((WINDOW + tok, 2 * HD), lambda i, j: (0, 0)),
        ],
        out_shape=[
            jax.ShapeDtypeStruct((tok, H * HD), BF),
            jax.ShapeDtypeStruct((WINDOW + tok, 2 * HD), F32),
        ],
        compiler_params=pltpu.CompilerParams(vmem_limit_bytes=48 * 1024 * 1024),
        cost_estimate=pl.CostEstimate(
            flops=10 * tok * H * HD * SPAN, bytes_accessed=6 * 1024 * 1024, transcendentals=0
        ),
        name="attend_back",
    )(low, queries, window, d_context, lse)


def snake(pos, size_a, size_b):
    if size_b == 1:
        return pos, pos * 0
    down = pos // size_a
    first = 1 - (down + 7) // 8
    q = (pos - size_a) * (1 - first)
    a_up = size_a - 1 - q // (size_b - 1)
    k = q % (size_b - 1)
    odd = a_up % 2
    b_up = odd * (1 + k) + (1 - odd) * (size_b - 1 - k)
    return first * pos + (1 - first) * a_up, (1 - first) * b_up


def snake_place(a, b, size_a, size_b):
    if size_b == 1:
        return a
    moved = (b + size_b - 1) // size_b
    odd = a % 2
    along = odd * (b - 1) + (1 - odd) * (size_b - 1 - b)
    return (1 - moved) * a + moved * (size_a + (size_a - 1 - a) * (size_b - 1) + along)


def kept_slot(a, b, size_a, size_b):
    half = size_a * size_b // 2
    return (1 - b % 2) * half + a * (size_b // 2) + b // 2


class Piece:
    def __init__(self, at, rows, square, shared, part, parts):
        self.at, self.rows, self.square, self.shared = at, rows, square, shared
        self.part, self.parts = part, parts
        self.relays = [0, 1, 2, 3] if square else []
        if shared:
            self.relays += [4, 5, 6, 7, 8] if square else [4]


def fetch_kernel(sizes, pieces, n_in, n_dealt, *refs):
    size_a, size_b, size_x = sizes
    n_ctx = size_a * size_b * 2
    ins, refs = refs[:n_in], refs[n_in:]
    outs, refs = refs[:n_in], refs[n_in:]
    n_weights = n_in - n_dealt - 1
    stages, refs = refs[:n_weights], refs[n_weights:]
    keep_sem, own_sem, deal_send, deal_recv, gain_send, gain_recv = refs[:6]
    x_send, x_recv, relay_send, relay_recv = refs[6:]
    ia, ib, ic, ix = (lax.axis_index(name) for name in ALL)
    own = (ia * size_b + ib) * 2 + ic
    rank = ix * 2 + ic
    pa, pb = ia % 2, ib % 2
    other_a, other_b = ia + 1 - 2 * pa, ib + 1 - 2 * pb
    corner = pa * 2 + pb
    corner_a, corner_b, corner_d = (1 - pa) * 2 + pb, pa * 2 + 1 - pb, 3 - corner

    barrier = pltpu.get_barrier_semaphore()
    greeted = []
    for k in range(1, n_ctx):
        e = (own + k) % n_ctx
        greeted.append((e // 2 // size_b, e // 2 % size_b, e % 2, ix))
    for s in range(1, size_x):
        greeted.append((ia, ib, ic, (ix + s) % size_x))
    for device in greeted:
        pl.semaphore_signal(barrier, inc=1, device_id=device, device_id_type=MESH)
    pl.semaphore_wait(barrier, len(greeted))

    def remote(src, dst, send, recv, device):
        return pltpu.make_async_remote_copy(
            src_ref=src,
            dst_ref=dst,
            send_sem=send,
            recv_sem=recv,
            device_id=device,
            device_id_type=MESH,
        )

    def x_copy(i, s):
        p = pieces[i]
        shard, full = ins[p.at], outs[p.at]
        target = (ix + s) % size_x
        height = shard.shape[0]
        rows, start = region(p, corner, ic)
        if p.shared:
            src = shard.at[pl.ds(start, rows), :]
        else:
            cols = full.shape[1]
            at = pl.multiple_of((target * 2 + ic) * cols, cols)
            src = shard.at[pl.ds(start, rows), pl.ds(at, cols)]
        dst = full.at[pl.ds(pl.multiple_of(ix * height + start, rows), rows), :]
        return remote(src, dst, x_send.at[i, s], x_recv.at[i, s], (ia, ib, ic, target))

    def region(p, which, core):
        owner = which if p.square else 0
        owners = 4 if p.square else 1
        if p.shared:
            owner, owners = owner * 2 + core, owners * 2
        rows = p.rows // (owners * p.parts)
        return rows, pl.multiple_of((owner * p.parts + p.part) * rows, rows)

    def landed(i, s, which, core, half=None):
        p = pieces[i]
        rows, start = region(p, which, core)
        start = start + (ix + size_x - s) % size_x * p.rows
        if half is not None:
            rows = rows // 2
            start = start + half * rows
        return outs[p.at].at[pl.ds(pl.multiple_of(start, rows), rows), :]

    def relay(i, s, kind, incoming=False):
        sem = (relay_send.at[i, s, kind], relay_recv.at[i, s, kind])
        if kind < 4:
            device = (other_a, ib, ic, ix) if kind in (1, 2) else (ia, other_b, ic, ix)
            sent = (
                landed(i, s, corner, ic),
                landed(i, s, corner, ic),
                landed(i, s, corner_b, ic, 0),
                landed(i, s, corner_a, ic, 1),
            )[kind]
            came = (
                landed(i, s, corner_b, ic),
                landed(i, s, corner_a, ic),
                landed(i, s, corner_d, ic, 0),
                landed(i, s, corner_d, ic, 1),
            )[kind]
        else:
            device = (ia, ib, 1 - ic, ix)
            which, half = ((corner, None), (corner_b, None), (corner_a, None), (corner_d, 0), (corner_d, 1))[
                kind - 4
            ]
            sent = landed(i, s, which, ic, half)
            came = landed(i, s, which, 1 - ic, half)
        ref = came if incoming else sent
        return remote(ref, ref, *sem, device)

    rows = ins[0].shape[0] // n_ctx

    def deal_copy(t, k):
        e = (own + k) % n_ctx
        src = ins[t].at[pl.ds(pl.multiple_of(e * rows, rows), rows), :]
        dst = outs[t].at[pl.ds(pl.multiple_of(own * rows, rows), rows), :]
        if k == 0:
            return pltpu.make_async_copy(src, dst, own_sem.at[t])
        device = (e // 2 // size_b, e // 2 % size_b, e % 2, ix)
        return remote(src, dst, deal_send.at[t, k], deal_recv.at[t, k], device)

    g = n_in - 1

    def gain_copy(s):
        if s == 0:
            return pltpu.make_async_copy(ins[g], outs[g].at[ix], own_sem.at[g])
        device = (ia, ib, ic, (ix + s) % size_x)
        return remote(ins[g], outs[g].at[ix], gain_send.at[s], gain_recv.at[s], device)

    def keep_copy(w, out):
        shard, full = ins[w], outs[w]
        stage = stages[w - n_dealt]
        height = shard.shape[0]
        sem = keep_sem.at[w, out]
        if out:
            dst = full.at[pl.ds(pl.multiple_of(ix * height, height), height), :]
            return pltpu.make_async_copy(stage, dst, sem)
        src = shard
        if full.shape[1] != shard.shape[1]:
            cols = full.shape[1]
            src = shard.at[:, pl.ds(pl.multiple_of(rank * cols, cols), cols)]
        return pltpu.make_async_copy(src, stage, sem)

    ahead = 4
    order = [(i, s) for i in range(len(pieces)) for s in range(1, size_x)]
    for k in range(n_ctx):
        deal_copy(0, k).start()
    for s in range(size_x):
        gain_copy(s).start()
    for i, s in order[:ahead]:
        x_copy(i, s).start()
    for t in range(1, n_dealt):
        for k in range(n_ctx):
            deal_copy(t, k).start()
    for w in range(n_dealt, n_dealt + n_weights):
        keep_copy(w, 0).start()

    for n in range(len(order) + 2):
        if n < n_weights:
            keep_copy(n_dealt + n, 0).wait()
            keep_copy(n_dealt + n, 1).start()
        if n < len(order):
            i, s = order[n]
            x_copy(i, s).wait_recv()
            for kind in (0, 1, 4):
                if kind in pieces[i].relays:
                    relay(i, s, kind).start()
            if n + ahead < len(order):
                x_copy(i, s).wait_send()
                x_copy(*order[n + ahead]).start()
        if 1 <= n <= len(order) and pieces[order[n - 1][0]].square:
            i, s = order[n - 1]
            relay(i, s, 0, True).wait_recv()
            relay(i, s, 2).start()
            relay(i, s, 1, True).wait_recv()
            relay(i, s, 3).start()
            if pieces[i].shared:
                relay(i, s, 5).start()
                relay(i, s, 6).start()
        if n >= 2 and pieces[order[n - 2][0]].square:
            i, s = order[n - 2]
            relay(i, s, 2, True).wait_recv()
            relay(i, s, 3, True).wait_recv()
            if pieces[i].shared:
                relay(i, s, 7).start()
                relay(i, s, 8).start()

    for n, (i, s) in enumerate(order):
        if n + ahead >= len(order):
            x_copy(i, s).wait_send()
        for kind in pieces[i].relays:
            relay(i, s, kind).wait_send()
            if kind >= 4:
                relay(i, s, kind, True).wait_recv()
    for t in range(n_dealt):
        for k in range(n_ctx):
            deal_copy(t, k).wait()
    for s in range(size_x):
        gain_copy(s).wait()
    for w in range(n_dealt, n_dealt + n_weights):
        keep_copy(w, 1).wait()


def fetch(sizes, dealt, shared, split, gains):
    size_a, size_b, size_x = sizes
    n_ctx = size_a * size_b * 2
    ins = dealt + shared + split + [gains]
    outs = [jax.ShapeDtypeStruct(a.shape, BF) for a in dealt]
    outs += [jax.ShapeDtypeStruct((size_x * a.shape[0], a.shape[1]), BF) for a in shared]
    outs += [
        jax.ShapeDtypeStruct((size_x * a.shape[0], a.shape[1] // (2 * size_x)), BF) for a in split
    ]
    outs.append(jax.ShapeDtypeStruct((size_x,) + gains.shape, BF))
    pieces = []
    first = len(dealt)
    pieces.append(Piece(first, shared[0].shape[0], True, True, 0, 1))
    for part in range(2):
        for n, a in enumerate(split):
            pieces.append(Piece(first + len(shared) + n, a.shape[0], True, False, part, 2))
    for n, a in enumerate(shared[1:]):
        pieces.append(Piece(first + 1 + n, a.shape[0], False, True, 0, 1))
    count = len(pieces)
    sem = pltpu.SemaphoreType.DMA
    return pl.pallas_call(
        functools.partial(fetch_kernel, sizes, pieces, len(ins), len(dealt)),
        in_specs=[pl.BlockSpec(memory_space=pl.ANY)] * len(ins),
        out_specs=[pl.BlockSpec(memory_space=pl.ANY)] * len(outs),
        out_shape=outs,
        scratch_shapes=[
            pltpu.VMEM((a.shape[0], o.shape[1]), BF)
            for a, o in zip(ins[len(dealt) : -1], outs[len(dealt) : -1])
        ]
        + [
            sem((len(ins), 2)),
            sem((len(ins),)),
            sem((len(dealt), n_ctx)),
            sem((len(dealt), n_ctx)),
            sem((size_x,)),
            sem((size_x,)),
            sem((count, size_x)),
            sem((count, size_x)),
            sem((count, size_x, 9)),
            sem((count, size_x, 9)),
        ],
        compiler_params=pltpu.CompilerParams(
            collective_id=1, has_side_effects=True, vmem_limit_bytes=48 * 1024 * 1024
        ),
        cost_estimate=pl.CostEstimate(
            flops=0, bytes_accessed=300 * 1024 * 1024, transcendentals=0
        ),
        name="fetch",
    )(*ins)


def mlp_kernel(sizes, own_ref, *refs):
    size_a, size_b, size_x = sizes
    ranks = 2 * size_x
    cots_in, refs = refs[:ranks], refs[ranks:]
    weights_in, refs = refs[:3], refs[3:]
    grad_ref, rows_out, dg_out, du_out, part_out, down_out, refs = *refs[:6], refs[6:]
    rows, cot, w_gate, w_up, w_down, hid, dg, du = refs[:8]
    to_core, in_core, to_x, in_x, total, part_stage, down_stage = refs[8:15]
    load_sem, ag_send, ag_recv, core_send, core_recv, x_send, x_recv, out_sem, stage_sem = refs[15:]
    ia, ib, ic, ix = (lax.axis_index(name) for name in ALL)
    hidden_units = w_down.shape[0]
    tok, width = own_ref.shape
    tiles, _, tile = total.shape
    unit = hid.shape[2] // (hid.shape[2] // 512 if hid.shape[2] % 512 == 0 else hid.shape[2] // 256)

    loads = [
        pltpu.make_async_copy(own_ref, rows.at[0], load_sem.at[0]),
        pltpu.make_async_copy(weights_in[0], w_gate, load_sem.at[1]),
        pltpu.make_async_copy(weights_in[1], w_up, load_sem.at[2]),
        pltpu.make_async_copy(
            weights_in[2].at[pl.ds(pl.multiple_of(ic * hidden_units, hidden_units), hidden_units), :],
            w_down,
            load_sem.at[3],
        ),
    ]
    for b in range(ranks):
        loads.append(pltpu.make_async_copy(cots_in[b], cot.at[b], load_sem.at[4 + b]))
    for copy in loads:
        copy.start()

    partner = (ia, ib, 1 - ic, ix)

    def across(step):
        return ia, ib, ic, (ix + size_x + step) % size_x

    barrier = pltpu.get_barrier_semaphore()
    greeted = [partner] + [across(s) for s in range(1, size_x)]
    for device in greeted:
        pl.semaphore_signal(barrier, inc=1, device_id=device, device_id_type=MESH)
    pl.semaphore_wait(barrier, len(greeted))

    def remote(src, dst, sent, came, device):
        return pltpu.make_async_remote_copy(
            src_ref=src,
            dst_ref=dst,
            send_sem=sent,
            recv_sem=came,
            device_id=device,
            device_id_type=MESH,
        )

    def gather(b):
        if b == 1:
            return remote(own_ref, rows.at[1], ag_send.at[1], ag_recv.at[1], partner)
        if b % 2:
            return remote(rows.at[b - 1], rows.at[b], ag_send.at[b], ag_recv.at[b], partner)
        return remote(own_ref, rows.at[b], ag_send.at[b], ag_recv.at[b], across(b // 2))

    def core_copy(s):
        return remote(to_core.at[s], in_core.at[s], core_send.at[s], core_recv.at[s], partner)

    def x_copy(s, t):
        return remote(
            to_x.at[s, t], in_x.at[s, t], x_send.at[s, t], x_recv.at[s, t], across(-s)
        )

    def results(b):
        to = pl.ds(b * tok, tok)
        return [
            pltpu.make_async_copy(rows.at[b], rows_out.at[to, :], out_sem.at[0, b]),
            pltpu.make_async_copy(dg.at[b], dg_out.at[to, :], out_sem.at[1, b]),
            pltpu.make_async_copy(du.at[b], du_out.at[to, :], out_sem.at[2, b]),
        ]

    def forward(b):
        def step(t, carry):
            units = pl.ds(pl.multiple_of(t * unit, unit), unit)
            gate = mm(rows[b], w_gate[:, units])
            upward = mm(rows[b], w_up[:, units])
            d_hidden = mm_nt(cot[b], w_down[units, :])
            square = gate * gate
            bent = jnp.tanh(root * gate * (1.0 + cubic * square))
            half = 0.5 * (1.0 + bent)
            act = gate * half
            slope = half + 0.5 * gate * (1.0 - bent * bent) * root * (1.0 + 3.0 * cubic * square)
            hid[b, :, units] = (act * upward).astype(BF)
            dg[b, :, units] = (d_hidden * upward * slope).astype(BF)
            du[b, :, units] = (d_hidden * act).astype(BF)
            return carry

        lax.fori_loop(0, hid.shape[2] // unit, step, 0)
        for copy in results(b):
            copy.start()

    def backward(b):
        s, other = b // 2, b % 2
        if not other:
            core_copy(s).wait_recv()

        def step(t, carry):
            at = pl.ds(pl.multiple_of(t * tile, tile), tile)
            value = mm_nt(dg[b], w_gate[at, :]) + mm_nt(du[b], w_up[at, :])
            if other:
                to_core[s, t] = value.astype(BF)
                return carry
            value = value + in_core[s, t].astype(F32)
            if s:
                to_x[s, t] = value.astype(BF)
                x_copy(s, t).start()
            else:
                total[t] = value
            return carry

        lax.fori_loop(0, tiles, step, 0)
        if other:
            core_copy(s).start()

    def part_copy(b):
        return pltpu.make_async_copy(part_stage.at[b % 2], part_out.at[b], stage_sem.at[b % 2])

    def branch(b):
        if b >= 2:
            part_copy(b - 2).wait()

        def step(t, carry):
            at = pl.ds(pl.multiple_of(t * tile, tile), tile)
            part_stage[b % 2, :, at] = mm(hid[b], w_down[:, at]).astype(BF)
            return carry

        lax.fori_loop(0, tiles, step, 0)
        part_copy(b).start()

    depth = down_stage.shape[1]
    strips = hidden_units // depth

    def down_copy(t, slot):
        to = pl.ds(pl.multiple_of(t * depth, depth), depth)
        return pltpu.make_async_copy(down_stage.at[slot], down_out.at[to, :], stage_sem.at[2 + slot])

    def down_step(t, carry):
        slot = t % 2

        @pl.when(t >= 2)
        def _():
            down_copy(t - 2, slot).wait()

        units = pl.ds(pl.multiple_of(t * depth, depth), depth)
        value = mm_tn(hid[0, :, units], cot[0])
        for b in range(1, ranks):
            value = value + mm_tn(hid[b, :, units], cot[b])
        down_stage[slot] = value.astype(BF)
        down_copy(t, slot).start()
        return carry

    gather(1).start()
    for s in range(1, size_x):
        gather(2 * s).start()
    for copy in loads:
        copy.wait()
    forward(0)
    gather(1).wait_recv()
    forward(1)
    backward(1)
    for s in range(1, size_x):
        gather(2 * s).wait_recv()
        gather(2 * s + 1).start()
        forward(2 * s)
        gather(2 * s + 1).wait_recv()
        forward(2 * s + 1)
        backward(2 * s + 1)
        backward(2 * s)
    backward(0)
    lax.fori_loop(0, strips, down_step, 0)
    for b in range(ranks):
        branch(b)
    for s in range(1, size_x):
        for t in range(tiles):
            x_copy(s, t).wait()
    for t in range(tiles):
        value = total[t]
        for s in range(1, size_x):
            value = value + in_x[s, t].astype(F32)
        grad_ref[:, t * tile : (t + 1) * tile] = value
    for b in range(1, ranks):
        gather(b).wait_send()
    for s in range(size_x):
        core_copy(s).wait_send()
    for b in range(ranks):
        for copy in results(b):
            copy.wait()
    part_copy(ranks - 2).wait()
    part_copy(ranks - 1).wait()
    down_copy(strips - 2, (strips - 2) % 2).wait()
    down_copy(strips - 1, (strips - 1) % 2).wait()


def feed_forward(sizes, normed, cots, w_gate, w_up, down_weight):
    ranks = 2 * sizes[2]
    size_x = sizes[2]
    tok, width = normed.shape
    units = w_gate.shape[1]
    tile = 512
    tiles = width // tile
    sem = pltpu.SemaphoreType.DMA
    hbm = pl.BlockSpec(memory_space=pl.ANY)
    return pl.pallas_call(
        functools.partial(mlp_kernel, sizes),
        in_specs=[hbm] * (4 + ranks),
        out_specs=[pl.BlockSpec(memory_space=pltpu.VMEM)] + [hbm] * 5,
        out_shape=[
            jax.ShapeDtypeStruct((tok, width), F32),
            jax.ShapeDtypeStruct((ranks * tok, width), BF),
            jax.ShapeDtypeStruct((ranks * tok, units), BF),
            jax.ShapeDtypeStruct((ranks * tok, units), BF),
            jax.ShapeDtypeStruct((ranks, tok, width), BF),
            jax.ShapeDtypeStruct((units, width), BF),
        ],
        scratch_shapes=[
            pltpu.VMEM((ranks, tok, width), BF),
            pltpu.VMEM((ranks, tok, width), BF),
            pltpu.VMEM((width, units), BF),
            pltpu.VMEM((width, units), BF),
            pltpu.VMEM((units, width), BF),
            pltpu.VMEM((ranks, tok, units), BF),
            pltpu.VMEM((ranks, tok, units), BF),
            pltpu.VMEM((ranks, tok, units), BF),
            pltpu.VMEM((size_x, tiles, tok, tile), BF),
            pltpu.VMEM((size_x, tiles, tok, tile), BF),
            pltpu.VMEM((size_x, tiles, tok, tile), BF),
            pltpu.VMEM((size_x, tiles, tok, tile), BF),
            pltpu.VMEM((tiles, tok, tile), F32),
            pltpu.VMEM((2, tok, width), BF),
            pltpu.VMEM((2, 256, width), BF),
            sem((4 + ranks,)),
            sem((ranks,)),
            sem((ranks,)),
            sem((size_x,)),
            sem((size_x,)),
            sem((size_x, tiles)),
            sem((size_x, tiles)),
            sem((3, ranks)),
            sem((4,)),
        ],
        compiler_params=pltpu.CompilerParams(
            collective_id=2, has_side_effects=True, vmem_limit_bytes=62 * 1024 * 1024
        ),
        cost_estimate=pl.CostEstimate(
            flops=14 * ranks * tok * width * units,
            bytes_accessed=60 * 1024 * 1024,
            transcendentals=0,
        ),
        name="feed_forward",
    )(normed, *cots, w_gate, w_up, down_weight)


class Job:
    def __init__(self, phase, left, right, rows, cols, by_rank):
        self.phase, self.left, self.right = phase, left, right
        self.rows, self.cols, self.by_rank = rows, cols, by_rank


def grads_kernel(sizes, jobs, *refs):
    size_a, size_b, size_x = sizes
    chips = size_a * size_b
    n_ctx = 2 * chips
    ranks = 2 * size_x
    count = len(jobs)
    ins, refs = refs[:12], refs[12:]
    outs, refs = refs[:count], refs[count:]
    dealt, refs = refs[:2], refs[2:]
    gain_out, refs = refs[0], refs[1:]
    held, refs = refs[:8], refs[8:]
    gain_ctx, gain_x, parts_in, resid_in, block_out, refs = *refs[:5], refs[5:]
    recv, refs = refs[:count], refs[count:]
    send, refs = refs[:count], refs[count:]
    done, refs = refs[:count], refs[count:]
    load_sem, group_send, group_recv, deal_send, deal_recv = refs[:5]
    gain_send, gain_recv, send_sem, recv_sem, done_send, done_recv, own_sem = refs[5:]
    ia, ib, ic, ix = (lax.axis_index(name) for name in ALL)
    own = (ia * size_b + ib) * 2 + ic
    rank = ix * 2 + ic
    place = snake_place(ia, ib, size_a, size_b)

    def on_ring(step):
        return snake((place + 2 * chips + step) % chips, size_a, size_b)

    def member(k):
        return (ic + k // size_x) % 2, (ix + k % size_x) % size_x

    def ctx_device(k):
        e = (own + k) % n_ctx
        return e // 2 // size_b, e // 2 % size_b, e % 2, ix

    kept = rank * chips + kept_slot(ia, ib, size_a, size_b)
    kept_chip = kept // ranks
    kept_id = (kept_chip // size_b, kept_chip % size_b, (kept // size_x) % 2, kept % size_x)
    flat = own * size_x + ix
    from_rank = flat // chips
    from_slot = flat % chips
    half = chips // 2
    from_id = (
        (from_slot % half) // (size_b // 2),
        ((from_slot % half) % (size_b // 2)) * 2 + 1 - from_slot // half,
        from_rank % 2,
        from_rank // 2,
    )

    def remote(src, dst, sent, came, device):
        return pltpu.make_async_remote_copy(
            src_ref=src,
            dst_ref=dst,
            send_sem=sent,
            recv_sem=came,
            device_id=device,
            device_id_type=MESH,
        )

    loads = [pltpu.make_async_copy(ins[i], held[i], load_sem.at[i]) for i in range(3)]
    for copy in loads:
        copy.start()

    barrier = pltpu.get_barrier_semaphore()
    greeted = [ctx_device(k) for k in range(1, n_ctx)] + [from_id]
    greeted += [(ia, ib) + member(k) for k in range(ranks) if k % size_x]
    for device in greeted:
        pl.semaphore_signal(barrier, inc=1, device_id=device, device_id_type=MESH)
    pl.semaphore_wait(barrier, len(greeted))

    def group_copy(i, k):
        c, x = member(k)
        src, dst = ins[i], held[i].at[k]
        target = x * 2 + c
        if i == 4:
            rows = held[i].shape[1]
            src = src.at[pl.ds(pl.multiple_of(target * rows, rows), rows), :]
        if i == 6:
            cols = held[i].shape[2]
            src = src.at[:, pl.ds(pl.multiple_of(target * cols, cols), cols)]
        if k == 0:
            return pltpu.make_async_copy(src, dst, load_sem.at[i])
        return remote(src, dst, group_send.at[i, k], group_recv.at[i, k], (ia, ib, c, x))

    def deal_copy(t, k):
        e = (own + k) % n_ctx
        source = block_out if t == 0 else ins[9]
        rows = source.shape[0] // n_ctx
        src = source.at[pl.ds(pl.multiple_of(e * rows, rows), rows), :]
        dst = dealt[t].at[pl.ds(pl.multiple_of(own * rows, rows), rows), :]
        if k == 0:
            return pltpu.make_async_copy(src, dst, load_sem.at[8 + t])
        return remote(src, dst, deal_send.at[t, k], deal_recv.at[t, k], ctx_device(k))

    def part_copy(b):
        src, dst = ins[8].at[b], parts_in.at[b]
        if b == 0:
            return pltpu.make_async_copy(src, dst, own_sem.at[count])
        device = (ia, ib, (ic + b) % 2, (ix + size_x - b // 2) % size_x)
        return remote(src, dst, group_send.at[0, b], group_recv.at[0, b], device)

    resid_copy = pltpu.make_async_copy(ins[11], resid_in, load_sem.at[11])

    def gain_copy(k):
        src, dst = ins[10].at[(own + k) % n_ctx], gain_ctx.at[k]
        if k == 0:
            return pltpu.make_async_copy(src, dst, load_sem.at[10])
        return remote(src, dst, deal_send.at[2, k], deal_recv.at[2, k], ctx_device(k))

    def gain_copy_x(s):
        device = (ia, ib, ic, (ix + s) % size_x)
        return remote(gain_x.at[0], gain_x.at[s], gain_send.at[s], gain_recv.at[s], device)

    def ring_copy(j, way, step, parity):
        neighbour = on_ring(1 - 2 * way) + (ic, ix)
        return remote(
            send[j].at[way, parity],
            recv[j].at[way, step],
            send_sem.at[j, way, parity],
            recv_sem.at[j, way, step],
            neighbour,
        )

    def product(j, way, step):
        job = jobs[j]
        a, b = on_ring(step * (2 * way - 1))
        part = job.rows // chips
        cols = slice(way * job.cols // 2, (way + 1) * job.cols // 2)
        left, right = held[job.left], held[job.right]
        if job.phase == 0:
            start = pl.multiple_of((a * size_b + b) * part, part)
            return mm_tn(left[:, pl.ds(start, part)], right[:, cols])
        if job.by_rank:
            start = kept_slot(a, b, size_a, size_b) * part
            if left.shape[1] != job.rows:
                start = start + rank * job.rows
        else:
            start = (a * size_b + b) * part
        rows = pl.ds(pl.multiple_of(start, part), part)
        total = mm(left[0, rows, :], right[0, :, cols])
        for k in range(1, ranks):
            total = total + mm(left[k, rows, :], right[k, :, cols])
        return total

    def deliver(j):
        job = jobs[j]
        if job.by_rank:
            return [remote(done[j], outs[j], done_send.at[j, 0], done_recv.at[j, 0], kept_id)]
        part = job.rows // (chips * ranks)
        copies = []
        for k in range(ranks):
            c, x = member(k)
            start = pl.multiple_of((c * size_x + x) * part, part)
            src, dst = done[j].at[pl.ds(start, part), :], outs[j].at[rank]
            if k == 0:
                copies.append(pltpu.make_async_copy(src, dst, own_sem.at[j]))
            else:
                copies.append(
                    remote(src, dst, done_send.at[j, k], done_recv.at[j, k], (ia, ib, c, x))
                )
        return copies

    for copy in loads:
        copy.wait()
    for phase in range(2):
        mine = [j for j in range(count) if jobs[j].phase == phase]
        for j in mine:
            for way in range(2):
                send[j][way, 0] = product(j, way, 1).astype(BF)
                ring_copy(j, way, 0, 0).start()
        if phase == 0:
            for k in range(n_ctx):
                gain_copy(k).start()
            for i in range(3, 8):
                for k in range(ranks):
                    group_copy(i, k).start()
            for b in range(ranks):
                part_copy(b).start()
            resid_copy.start()
            for k in range(n_ctx):
                deal_copy(1, k).start()

        def step_of(step, carry):
            parity = step % 2
            for j in mine:
                for way in range(2):
                    part = product(j, way, step + 1)
                    ring_copy(j, way, step - 1, 1 - parity).wait_recv()
                    part = part + recv[j][way, step - 1].astype(F32)

                    @pl.when(step >= 2)
                    def _():
                        ring_copy(j, way, step - 2, parity).wait_send()

                    send[j][way, parity] = part.astype(BF)
                    ring_copy(j, way, step, parity).start()
            return carry

        lax.fori_loop(1, chips - 1, step_of, 0)
        if phase == 0:
            for k in range(n_ctx):
                gain_copy(k).wait()
            gain_x[0] = jnp.sum(gain_ctx[...], axis=0)
            for s in range(1, size_x):
                gain_copy_x(s).start()
            resid_copy.wait()
            for b in range(ranks):
                part_copy(b).wait()
            summed = resid_in[...]
            for b in range(ranks):
                summed = summed + parts_in[b].astype(F32)
            block_out[...] = summed.astype(BF)
            for k in range(n_ctx):
                deal_copy(0, k).start()
        last = chips - 2
        for j in mine:
            cols = jobs[j].cols // 2
            for way in range(2):
                part = product(j, way, chips)
                ring_copy(j, way, last, last % 2).wait_recv()
                part = part + recv[j][way, last].astype(F32)
                done[j][:, way * cols : (way + 1) * cols] = part.astype(BF)
            for copy in deliver(j):
                copy.start()
            for way in range(2):
                ring_copy(j, way, last - 1, (last - 1) % 2).wait_send()
                ring_copy(j, way, last, last % 2).wait_send()
        if phase == 0:
            for i in range(3, 8):
                for k in range(ranks):
                    group_copy(i, k).wait()
    for s in range(1, size_x):
        gain_copy_x(s).wait()
    gain_out[...] = jnp.sum(gain_x[...], axis=0)
    for t in range(2):
        for k in range(n_ctx):
            deal_copy(t, k).wait()
    for j in range(count):
        for copy in deliver(j):
            copy.wait()


def sum_grads(sizes, ins):
    size_a, size_b, size_x = sizes
    chips = size_a * size_b
    ranks = 2 * size_x
    normed_mlp, d_gate, d_upward = ins[:3]
    width = normed_mlp.shape[1]
    tok = ins[5].shape[0]
    part_width = width // ranks
    jobs = [
        Job(0, 0, 1, width, d_gate.shape[1], False),
        Job(0, 0, 2, width, d_upward.shape[1], False),
        Job(1, 3, 6, width, part_width, False),
        Job(1, 4, 5, part_width, width, True),
        Job(1, 3, 7, part_width, 2 * HD, True),
    ]
    held = [pltpu.VMEM(a.shape, BF) for a in ins[:3]]
    held += [
        pltpu.VMEM((ranks,) + shape, BF)
        for shape in (
            (width, tok),
            (part_width, tok),
            (tok, width),
            (tok, part_width),
            (tok, 2 * HD),
        )
    ]
    outs, recv, send, done = [], [], [], []
    flops = 0
    for job in jobs:
        part = job.rows // chips
        if job.by_rank:
            outs.append(jax.ShapeDtypeStruct((part, job.cols), BF))
        else:
            outs.append(jax.ShapeDtypeStruct((ranks, part // ranks, job.cols), BF))
        recv.append(pltpu.VMEM((2, chips - 1, part, job.cols // 2), BF))
        send.append(pltpu.VMEM((2, 2, part, job.cols // 2), BF))
        done.append(pltpu.VMEM((part, job.cols), BF))
        flops += 2 * job.rows * job.cols * normed_mlp.shape[0]
    count = len(jobs)
    outs += [jax.ShapeDtypeStruct((tok, width), BF)] * 2
    gain_shape = ins[10].shape[1:]
    outs.append(jax.ShapeDtypeStruct(gain_shape, F32))
    sem = pltpu.SemaphoreType.DMA
    return pl.pallas_call(
        functools.partial(grads_kernel, sizes, jobs),
        in_specs=[pl.BlockSpec(memory_space=pl.ANY)] * len(ins),
        out_specs=[pl.BlockSpec(memory_space=pl.ANY)] * (count + 2)
        + [pl.BlockSpec(memory_space=pltpu.VMEM)],
        out_shape=outs,
        scratch_shapes=held
        + [
            pltpu.VMEM((2 * chips,) + gain_shape, F32),
            pltpu.VMEM((size_x,) + gain_shape, F32),
            pltpu.VMEM((ranks, tok, width), BF),
            pltpu.VMEM((tok, width), F32),
            pltpu.VMEM((tok, width), BF),
        ]
        + recv
        + send
        + done
        + [
            sem((len(ins),)),
            sem((8, ranks)),
            sem((8, ranks)),
            sem((3, 2 * chips)),
            sem((3, 2 * chips)),
            sem((size_x,)),
            sem((size_x,)),
            sem((count, 2, 2)),
            sem((count, 2, chips - 1)),
            sem((count, ranks)),
            sem((count, ranks)),
            sem((count + 1,)),
        ],
        compiler_params=pltpu.CompilerParams(
            collective_id=0, has_side_effects=True, vmem_limit_bytes=60 * 1024 * 1024
        ),
        cost_estimate=pl.CostEstimate(
            flops=flops, bytes_accessed=400 * 1024 * 1024, transcendentals=0
        ),
        name="sum_grads",
    )(*ins)


def norm_stats(values):
    inv = lax.rsqrt(jnp.mean(values * values, axis=-1, keepdims=True) + epsilon)
    return values * inv, inv


def norm_back(unit, inv, gain, grad):
    scaled = grad * gain
    inner = jnp.mean(scaled * unit, axis=-1, keepdims=True)
    return inv * (scaled - unit * inner), jnp.sum(grad * unit, axis=0)


def on_device(
    sizes,
    tokens,
    lengths,
    dealing,
    attn_gain,
    query_weight,
    kv_weight,
    out_weight,
    mlp_gain,
    gate_weight,
    up_weight,
    down_weight,
    cotangent,
):
    size_a, size_b, size_x = sizes
    chips = size_a * size_b
    n_ctx = chips * 2
    ranks = 2 * size_x
    ia, ib, ic, ix = (lax.axis_index(name) for name in ALL)
    chip = ia * size_b + ib
    own = chip * 2 + ic
    flat = own * size_x + ix
    rank = ix * 2 + ic
    tok = tokens.shape[1]
    width = tokens.shape[2]
    piece = tok // n_ctx
    halo = WINDOW // tok
    swap = [(0, 1), (1, 0)]

    def pick(array, index, axis=0):
        return lax.dynamic_index_in_dim(array, index, axis, keepdims=False)

    def put(array, part, index, axis=0):
        return lax.dynamic_update_index_in_dim(array, part, index, axis)

    def to_core(array):
        return lax.ppermute(array, "c", swap)

    def to_x(array, step):
        return lax.ppermute(array, "x", [(i, (i + step) % size_x) for i in range(size_x)])

    def shift_ctx(array, step):
        pairs = [(i, i + step) for i in range(n_ctx) if 0 <= i + step < n_ctx]
        return lax.ppermute(array, CTX, pairs)

    def from_x(step):
        return (ix + size_x - step) % size_x

    def group_rows(array):
        parts = [array, to_core(array)]
        for step in range(1, size_x):
            got = to_x(array, step)
            parts += [got, to_core(got)]
        return parts

    def sum_rows(grad):
        summed = lax.psum_scatter(
            grad.astype(BF), ("a", "b"), scatter_dimension=0, tiled=True
        )
        keep_pairs = []
        for g in range(chips):
            for c in range(2):
                for x in range(size_x):
                    keep_pairs.append(((g * 2 + c) * size_x + x, (x * 2 + c) * chips + g))
        return lax.ppermute(summed, ALL, keep_pairs).astype(F32)

    own_deal = pick(dealing[0], own)
    deal = (own_deal[:, None] == jnp.arange(tok, dtype=jnp.int32)[None, :]).astype(BF)

    gains = jnp.stack([attn_gain, mlp_gain]).reshape(-1, 128)
    inputs_low, cot, w_query, w_kv, w_out, w_gate, w_up, gains = fetch(
        sizes,
        [mm(deal, tokens[0]).astype(BF), mm(deal, cotangent[0]).astype(BF)],
        [query_weight, kv_weight, out_weight],
        [gate_weight, up_weight],
        gains,
    )
    gains = gains.reshape(size_x, 2, -1).astype(F32)
    gain_one = gains[:, 0].reshape(-1)
    gain_two = gains[:, 1].reshape(-1)

    cot_parts = group_rows(cot)

    inputs = inputs_low.astype(F32)
    unit_one, inv_one = norm_stats(inputs)
    normed = (unit_one * gain_one).astype(BF)
    pairs = mm(normed, w_kv).astype(BF)
    window = jnp.concatenate([shift_ctx(pairs, halo - j) for j in range(halo)] + [pairs], 0)
    queries = mm(normed, w_query).astype(BF)
    stream = own * tok + jnp.arange(tok, dtype=jnp.int32)
    ends = jnp.cumsum(lengths[0])
    starts = jnp.max(jnp.where(stream[:, None] >= ends[None, :], ends[None, :], 0), axis=1)
    low = jnp.maximum(starts, stream - (WINDOW - 1)) - (own * tok - WINDOW)
    low = low.astype(jnp.int32)[None, :]
    context, lse = attend(queries, window, low)
    resid = inputs + mm(context, w_out)

    unit_two, inv_two = norm_stats(resid)
    d_normed_mlp, mlp_rows, d_gate, d_upward, mlp_parts, down_grad = feed_forward(
        sizes, (unit_two * gain_two).astype(BF), cot_parts, w_gate, w_up, down_weight
    )
    down_grad = sum_rows(down_grad)
    d_resid_part, mlp_gain_grad = norm_back(unit_two, inv_two, gain_two, d_normed_mlp)
    d_resid = cot.astype(F32) + d_resid_part
    d_branch = d_resid.astype(BF)

    d_context = mm_nt(d_branch, w_out).astype(BF)
    d_queries, d_window = attend_back(queries, window, low, d_context, lse)
    d_pairs = d_window[halo * tok :]
    for j in range(halo):
        part = d_window[j * tok : (j + 1) * tok].astype(BF)
        d_pairs = d_pairs + shift_ctx(part, j - halo).astype(F32)
    d_pairs = d_pairs.astype(BF)
    d_normed = mm_nt(d_queries, w_query) + mm_nt(d_pairs, w_kv)
    d_inputs, attn_gain_grad = norm_back(unit_one, inv_one, gain_one, d_normed)
    gain_part = width // (n_ctx * size_x)
    gain_grads = jnp.stack([attn_gain_grad, mlp_gain_grad]).reshape(2, n_ctx, size_x, gain_part)
    gain_grads = gain_grads.transpose(1, 2, 0, 3).reshape(n_ctx, -1)
    gain_grads = jnp.pad(gain_grads, ((0, 0), (0, 1024 - gain_grads.shape[1])))
    sums = sum_grads(
        sizes,
        [
            mlp_rows,
            d_gate,
            d_upward,
            normed.T,
            context.T,
            d_branch,
            d_queries,
            d_pairs,
            mlp_parts,
            (d_resid + d_inputs).astype(BF),
            gain_grads.reshape(n_ctx, 8, 128),
            resid,
        ],
    )
    gate_grad, up_grad, query_grad = (
        v.transpose(1, 0, 2).reshape(v.shape[1], -1).astype(F32) for v in sums[:3]
    )
    out_grad, kv_grad = (v.astype(F32) for v in sums[3:5])
    block_output = mm_tn(deal, sums[5]).astype(BF)
    token_grad = mm_tn(deal, sums[6])
    gain_grads = lax.dynamic_slice(sums[7].reshape(-1), (ix * 2 * gain_part,), (2 * gain_part,))
    attn_gain_grad, mlp_gain_grad = gain_grads[:gain_part], gain_grads[gain_part:]
    return (
        block_output[None],
        token_grad[None],
        attn_gain_grad,
        query_grad,
        kv_grad,
        out_grad,
        mlp_gain_grad,
        gate_grad,
        up_grad,
        down_grad,
    )


def solution(mesh):
    n_ctx, size_x = mesh.shape["ctx"], mesh.shape["fsdp"]
    chips = n_ctx // 2
    size_a = 4 if chips % 4 == 0 else chips
    size_b = chips // size_a
    fine = Mesh(mesh.devices.reshape(size_a, size_b, 2, size_x), ALL)
    rows = P("x", CTX, None)
    split = P("x", None)
    every = P(ALL)
    matrix = P(ALL, None)
    return jax.shard_map(
        functools.partial(on_device, (size_a, size_b, size_x)),
        mesh=fine,
        in_specs=(
            rows,
            split,
            P("x", None, None),
            P("x"),
            split,
            split,
            split,
            P("x"),
            split,
            split,
            split,
            rows,
        ),
        out_specs=(rows, rows, every, matrix, matrix, matrix, every, matrix, matrix, matrix),
        check_vma=False,
    )
```

```python
import functools

import jax
import jax.numpy as jnp
import numpy as np
from jax import lax
from jax.experimental import pallas as pl
from jax.experimental.pallas import tpu as pltpu
from jax.sharding import Mesh
from jax.sharding import PartitionSpec as P

H = 16
HD = 128
WINDOW = 1024
QBLK = 128
HEADS_STEP = 4
SPAN = WINDOW + QBLK
ROWS = HEADS_STEP * QBLK

epsilon = 1e-06
neg_large = -1e30
scale = HD ** (-0.5)
root = (2.0 / np.pi) ** 0.5
cubic = 0.044715
BF = jnp.bfloat16
F32 = jnp.float32
CTX = ("a", "b", "c")
ALL = ("a", "b", "c", "x")
MESH = pl.DeviceIdType.MESH


def mm(left, right):
    return jnp.dot(left, right, preferred_element_type=F32)


def mm_tn(left, right):
    return lax.dot_general(left, right, (((0,), (0,)), ((), ())), preferred_element_type=F32)


def mm_nt(left, right):
    return lax.dot_general(left, right, (((1,), (1,)), ((), ())), preferred_element_type=F32)


def stack_heads(block):
    return jnp.concatenate([block[:, h * HD : (h + 1) * HD] for h in range(HEADS_STEP)], 0)


def unstack_heads(block_t):
    return jnp.concatenate(
        [block_t[:, h * QBLK : (h + 1) * QBLK].T for h in range(HEADS_STEP)], 1
    )


def bias_of(lo, qb):
    key = lax.broadcasted_iota(jnp.int32, (SPAN, QBLK), 0) + qb * QBLK
    query = lax.broadcasted_iota(jnp.int32, (SPAN, QBLK), 1) + (WINDOW + qb * QBLK)
    allowed = (key >= lo) & (key <= query)
    bias = jnp.where(allowed, 0.0, neg_large).astype(F32)
    return jnp.concatenate([bias] * HEADS_STEP, 1)


def attend_block(bias, queries, keys, values):
    scores = mm_nt(keys, queries) * scale + bias
    top = jnp.max(scores, axis=0, keepdims=True)
    raised = jnp.exp(scores - top)
    total = jnp.sum(raised, axis=0, keepdims=True)
    return mm_tn(values, raised.astype(BF)) * (1.0 / total), top + jnp.log(total)


def attend_back_kernel(lo_ref, q_ref, kv_ref, do_ref, lse_ref, dq_ref, dkv_ref):
    qb = pl.program_id(0)

    @pl.when((qb == 0) & (pl.program_id(1) == 0))
    def _():
        dkv_ref[...] = jnp.zeros_like(dkv_ref)

    rows = pl.ds(pl.multiple_of(qb * QBLK, QBLK), SPAN)
    keys = kv_ref[rows, :HD]
    values = kv_ref[rows, HD:]
    queries = stack_heads(q_ref[...])
    d_out = stack_heads(do_ref[...])
    scores = mm_nt(keys, queries) * scale + bias_of(lo_ref[...], qb)
    probs = jnp.exp(scores - lse_ref[0])
    d_probs = mm_nt(values, d_out)
    delta = jnp.sum(probs * d_probs, axis=0, keepdims=True)
    d_scores = (probs * (d_probs - delta)).astype(BF)
    dq_ref[...] = unstack_heads(mm_tn(keys, d_scores) * scale).astype(BF)
    dkv_ref[rows, :HD] += mm(d_scores, queries) * scale
    dkv_ref[rows, HD:] += mm(probs.astype(BF), d_out)


def attend_back(queries, window, low, d_context, lse):
    tok = queries.shape[0]
    groups = H // HEADS_STEP
    blocks = tok // QBLK
    return pl.pallas_call(
        attend_back_kernel,
        grid=(blocks, groups),
        in_specs=[
            pl.BlockSpec((1, QBLK), lambda i, j: (0, i)),
            pl.BlockSpec((QBLK, HEADS_STEP * HD), lambda i, j: (i, j)),
            pl.BlockSpec((WINDOW + tok, 2 * HD), lambda i, j: (0, 0)),
            pl.BlockSpec((QBLK, HEADS_STEP * HD), lambda i, j: (i, j)),
            pl.BlockSpec((1, 1, ROWS), lambda i, j: (i * groups + j, 0, 0)),
        ],
        out_specs=[
            pl.BlockSpec((QBLK, HEADS_STEP * HD), lambda i, j: (i, j)),
            pl.BlockSpec((WINDOW + tok, 2 * HD), lambda i, j: (0, 0)),
        ],
        out_shape=[
            jax.ShapeDtypeStruct((tok, H * HD), BF),
            jax.ShapeDtypeStruct((WINDOW + tok, 2 * HD), F32),
        ],
        compiler_params=pltpu.CompilerParams(vmem_limit_bytes=48 * 1024 * 1024),
        cost_estimate=pl.CostEstimate(
            flops=10 * tok * H * HD * SPAN, bytes_accessed=6 * 1024 * 1024, transcendentals=0
        ),
        name="attend_back",
    )(low, queries, window, d_context, lse)


def snake(pos, size_a, size_b):
    if size_b == 1:
        return pos, pos * 0
    down = pos // size_a
    first = 1 - (down + 7) // 8
    q = (pos - size_a) * (1 - first)
    a_up = size_a - 1 - q // (size_b - 1)
    k = q % (size_b - 1)
    odd = a_up % 2
    b_up = odd * (1 + k) + (1 - odd) * (size_b - 1 - k)
    return first * pos + (1 - first) * a_up, (1 - first) * b_up


def snake_place(a, b, size_a, size_b):
    if size_b == 1:
        return a
    moved = (b + size_b - 1) // size_b
    odd = a % 2
    along = odd * (b - 1) + (1 - odd) * (size_b - 1 - b)
    return (1 - moved) * a + moved * (size_a + (size_a - 1 - a) * (size_b - 1) + along)


def kept_slot(a, b, size_a, size_b):
    half = size_a * size_b // 2
    return (1 - b % 2) * half + a * (size_b // 2) + b // 2


class Piece:
    def __init__(self, at, rows, square, shared, part, parts):
        self.at, self.rows, self.square, self.shared = at, rows, square, shared
        self.part, self.parts = part, parts
        self.relays = [0, 1, 2, 3] if square else []
        if shared:
            self.relays += [4, 5, 6, 7, 8] if square else [4]


def fetch_kernel(sizes, pieces, n_in, n_dealt, *refs):
    size_a, size_b, size_x = sizes
    n_ctx = size_a * size_b * 2
    ins, low_ref, refs = refs[:n_in], refs[n_in], refs[n_in + 1 :]
    outs, refs = refs[:n_in], refs[n_in:]
    normed_ref, query_ref, window_out, context_ref, lse_ref, cot_rows, refs = *refs[:6], refs[6:]
    tok_in, w_query, w_kv, gain_in, window, refs = *refs[:5], refs[5:]
    load_sem, halo_send, halo_recv, cot_send, cot_recv, refs = *refs[:5], refs[5:]
    n_weights = n_in - n_dealt - 1
    stages, refs = refs[:n_weights], refs[n_weights:]
    keep_sem, own_sem, deal_send, deal_recv, gain_send, gain_recv = refs[:6]
    x_send, x_recv, relay_send, relay_recv = refs[6:]
    ia, ib, ic, ix = (lax.axis_index(name) for name in ALL)
    own = (ia * size_b + ib) * 2 + ic
    rank = ix * 2 + ic
    pa, pb = ia % 2, ib % 2
    other_a, other_b = ia + 1 - 2 * pa, ib + 1 - 2 * pb
    corner = pa * 2 + pb
    corner_a, corner_b, corner_d = (1 - pa) * 2 + pb, pa * 2 + 1 - pb, 3 - corner

    barrier = pltpu.get_barrier_semaphore()
    greeted = []
    for k in range(1, n_ctx):
        e = (own + k) % n_ctx
        greeted.append((e // 2 // size_b, e // 2 % size_b, e % 2, ix))
    for s in range(1, size_x):
        greeted.append((ia, ib, ic, (ix + s) % size_x))
    for device in greeted:
        pl.semaphore_signal(barrier, inc=1, device_id=device, device_id_type=MESH)
    pl.semaphore_wait(barrier, len(greeted))

    def remote(src, dst, send, recv, device):
        return pltpu.make_async_remote_copy(
            src_ref=src,
            dst_ref=dst,
            send_sem=send,
            recv_sem=recv,
            device_id=device,
            device_id_type=MESH,
        )

    def x_copy(i, s):
        p = pieces[i]
        shard, full = ins[p.at], outs[p.at]
        target = (ix + s) % size_x
        height = shard.shape[0]
        rows, start = region(p, corner, ic)
        if p.shared:
            src = shard.at[pl.ds(start, rows), :]
        else:
            cols = full.shape[1]
            at = pl.multiple_of((target * 2 + ic) * cols, cols)
            src = shard.at[pl.ds(start, rows), pl.ds(at, cols)]
        dst = full.at[pl.ds(pl.multiple_of(ix * height + start, rows), rows), :]
        return remote(src, dst, x_send.at[i, s], x_recv.at[i, s], (ia, ib, ic, target))

    def region(p, which, core):
        owner = which if p.square else 0
        owners = 4 if p.square else 1
        if p.shared:
            owner, owners = owner * 2 + core, owners * 2
        rows = p.rows // (owners * p.parts)
        return rows, pl.multiple_of((owner * p.parts + p.part) * rows, rows)

    def landed(i, s, which, core, half=None):
        p = pieces[i]
        rows, start = region(p, which, core)
        start = start + (ix + size_x - s) % size_x * p.rows
        if half is not None:
            rows = rows // 2
            start = start + half * rows
        return outs[p.at].at[pl.ds(pl.multiple_of(start, rows), rows), :]

    def relay(i, s, kind, incoming=False):
        sem = (relay_send.at[i, s, kind], relay_recv.at[i, s, kind])
        if kind < 4:
            device = (other_a, ib, ic, ix) if kind in (1, 2) else (ia, other_b, ic, ix)
            sent = (
                landed(i, s, corner, ic),
                landed(i, s, corner, ic),
                landed(i, s, corner_b, ic, 0),
                landed(i, s, corner_a, ic, 1),
            )[kind]
            came = (
                landed(i, s, corner_b, ic),
                landed(i, s, corner_a, ic),
                landed(i, s, corner_d, ic, 0),
                landed(i, s, corner_d, ic, 1),
            )[kind]
        else:
            device = (ia, ib, 1 - ic, ix)
            which, half = ((corner, None), (corner_b, None), (corner_a, None), (corner_d, 0), (corner_d, 1))[
                kind - 4
            ]
            sent = landed(i, s, which, ic, half)
            came = landed(i, s, which, 1 - ic, half)
        ref = came if incoming else sent
        return remote(ref, ref, *sem, device)

    rows = ins[0].shape[0] // n_ctx

    def deal_copy(t, k):
        e = (own + k) % n_ctx
        src = ins[t].at[pl.ds(pl.multiple_of(e * rows, rows), rows), :]
        dst = outs[t].at[pl.ds(pl.multiple_of(own * rows, rows), rows), :]
        if k == 0:
            return pltpu.make_async_copy(src, dst, own_sem.at[t])
        device = (e // 2 // size_b, e // 2 % size_b, e % 2, ix)
        return remote(src, dst, deal_send.at[t, k], deal_recv.at[t, k], device)

    g = n_in - 1

    def gain_copy(s):
        if s == 0:
            return pltpu.make_async_copy(ins[g], outs[g].at[ix], own_sem.at[g])
        device = (ia, ib, ic, (ix + s) % size_x)
        return remote(ins[g], outs[g].at[ix], gain_send.at[s], gain_recv.at[s], device)

    def keep_copy(w, out):
        shard, full = ins[w], outs[w]
        stage = stages[w - n_dealt]
        height = shard.shape[0]
        sem = keep_sem.at[w, out]
        if out:
            dst = full.at[pl.ds(pl.multiple_of(ix * height, height), height), :]
            return pltpu.make_async_copy(stage, dst, sem)
        src = shard
        if full.shape[1] != shard.shape[1]:
            cols = full.shape[1]
            src = shard.at[:, pl.ds(pl.multiple_of(rank * cols, cols), cols)]
        return pltpu.make_async_copy(src, stage, sem)

    tok = tok_in.shape[0]
    halo = WINDOW // tok
    at_query, at_kv = n_dealt, n_dealt + 1

    def load(src, dst, n):
        copy = pltpu.make_async_copy(src, dst, load_sem.at[n])
        copy.start()
        copy.wait()

    def core_parts_in(i):
        for s in range(1, size_x):
            for kind in pieces[i].relays:
                if kind >= 4:
                    relay(i, s, kind, True).wait_recv()
        keep_copy(pieces[i].at, 1).wait()

    def halo_copy(k):
        e = own + k
        device = (e // 2 // size_b, e // 2 % size_b, e % 2, ix)
        src = window.at[pl.ds(WINDOW, tok), :]
        dst = window.at[pl.ds((halo - k) * tok, tok), :]
        return remote(src, dst, halo_send.at[k - 1], halo_recv.at[k - 1], device)

    def normalise():
        for k in range(n_ctx):
            deal_copy(0, k).wait()
        for s in range(size_x):
            gain_copy(s).wait()
        load(outs[0], tok_in, 0)
        load(outs[g], gain_in, 1)
        gain = []
        for x in range(size_x):
            values = gain_in[x].astype(F32)
            gain += [values[r : r + 1, :] for r in range(values.shape[0] // 2)]
        values = tok_in[...].astype(F32)
        unit, _ = norm_stats(values)
        normed_ref[...] = (unit * jnp.concatenate(gain, 1)).astype(BF)

    def keys_values():
        core_parts_in(1)
        load(outs[at_kv], w_kv, 2)
        window[WINDOW:, :] = mm(normed_ref[...], w_kv[...]).astype(BF)
        for k in range(1, halo + 1):

            @pl.when(own + k < n_ctx)
            def _():
                halo_copy(k).start()

            @pl.when(own < k)
            def _():
                window[(halo - k) * tok : (halo - k + 1) * tok, :] = jnp.zeros((tok, 2 * HD), BF)

    def project():
        core_parts_in(0)
        load(outs[at_query], w_query, 3)

        def step(t, carry):
            cols = pl.ds(pl.multiple_of(t * 512, 512), 512)
            query_ref[:, cols] = mm(normed_ref[...], w_query[:, cols]).astype(BF)
            return carry

        lax.fori_loop(0, H * HD // 512, step, 0)

    def halo_in():
        for k in range(1, halo + 1):

            @pl.when(own >= k)
            def _():
                halo_copy(k).wait_recv()

    def cot_copy(b):
        sems = (cot_send.at[b], cot_recv.at[b])
        if b % 2:
            src = outs[1] if b == 1 else cot_rows.at[b - 2]
            return remote(src, cot_rows.at[b - 1], *sems, (ia, ib, 1 - ic, ix))
        device = (ia, ib, ic, (ix + b // 2) % size_x)
        return remote(outs[1], cot_rows.at[b - 1], *sems, device)

    def spread_cotangent():
        for k in range(n_ctx):
            deal_copy(1, k).wait()
        for s in range(1, size_x):
            cot_copy(2 * s).start()
        cot_copy(1).start()

    def attend(qb):
        low = low_ref[:, qb * QBLK : (qb + 1) * QBLK]
        bias = bias_of(low, qb)
        keys = window[qb * QBLK : qb * QBLK + SPAN, :HD]
        values = window[qb * QBLK : qb * QBLK + SPAN, HD:]
        rows = slice(qb * QBLK, (qb + 1) * QBLK)

        def step(t, carry):
            width = HEADS_STEP * HD
            cols = pl.ds(pl.multiple_of(t * width, width), width)
            out_t, lse = attend_block(bias, stack_heads(query_ref[rows, cols]), keys, values)
            context_ref[rows, cols] = unstack_heads(out_t).astype(BF)
            lse_ref[qb * (H // HEADS_STEP) + t] = lse
            return carry

        lax.fori_loop(0, H // HEADS_STEP, step, 0)

    blocks = tok // QBLK
    tasks = {2 * size_x - 1: [normalise, keys_values], 2 * size_x: [spread_cotangent, project]}
    for qb in range(blocks):
        task = functools.partial(attend, qb)
        tasks[2 * size_x + 1 + qb] = [halo_in, task] if qb == 0 else [task]

    ahead = 4
    order = [(i, s) for i in range(len(pieces)) for s in range(1, size_x)]
    for k in range(n_ctx):
        deal_copy(0, k).start()
    for s in range(size_x):
        gain_copy(s).start()
    for i, s in order[:ahead]:
        x_copy(i, s).start()
    for t in range(1, n_dealt):
        for k in range(n_ctx):
            deal_copy(t, k).start()
    for w in range(n_dealt, n_dealt + n_weights):
        keep_copy(w, 0).start()

    for n in range(len(order) + 2):
        if n < n_weights:
            keep_copy(n_dealt + n, 0).wait()
            keep_copy(n_dealt + n, 1).start()
        if n < len(order):
            i, s = order[n]
            x_copy(i, s).wait_recv()
            for kind in (0, 1, 4):
                if kind in pieces[i].relays:
                    relay(i, s, kind).start()
            if n + ahead < len(order):
                x_copy(i, s).wait_send()
                x_copy(*order[n + ahead]).start()
        if 1 <= n <= len(order) and pieces[order[n - 1][0]].square:
            i, s = order[n - 1]
            relay(i, s, 0, True).wait_recv()
            relay(i, s, 2).start()
            relay(i, s, 1, True).wait_recv()
            relay(i, s, 3).start()
            if pieces[i].shared:
                relay(i, s, 5).start()
                relay(i, s, 6).start()
        if n >= 2 and pieces[order[n - 2][0]].square:
            i, s = order[n - 2]
            relay(i, s, 2, True).wait_recv()
            relay(i, s, 3, True).wait_recv()
            if pieces[i].shared:
                relay(i, s, 7).start()
                relay(i, s, 8).start()
        for task in tasks.get(n, []):
            task()

    for s in range(1, size_x):
        cot_copy(2 * s).wait_recv()
        cot_copy(2 * s + 1).start()
    window_out[...] = window[...]
    for k in range(1, halo + 1):

        @pl.when(own + k < n_ctx)
        def _():
            halo_copy(k).wait_send()

    for n, (i, s) in enumerate(order):
        if n + ahead >= len(order):
            x_copy(i, s).wait_send()
        for kind in pieces[i].relays:
            relay(i, s, kind).wait_send()
            if kind >= 4 and i > 1:
                relay(i, s, kind, True).wait_recv()
    for b in range(1, 2 * size_x):
        cot_copy(b).wait_send()
        if b % 2:
            cot_copy(b).wait_recv()
    for w in range(n_dealt + 2, n_dealt + n_weights):
        keep_copy(w, 1).wait()


def fetch(sizes, dealt, shared, split, gains, low):
    size_a, size_b, size_x = sizes
    n_ctx = size_a * size_b * 2
    ins = dealt + shared + split + [gains]
    outs = [jax.ShapeDtypeStruct(a.shape, BF) for a in dealt]
    outs += [jax.ShapeDtypeStruct((size_x * a.shape[0], a.shape[1]), BF) for a in shared]
    outs += [
        jax.ShapeDtypeStruct((size_x * a.shape[0], a.shape[1] // (2 * size_x)), BF) for a in split
    ]
    outs.append(jax.ShapeDtypeStruct((size_x,) + gains.shape, BF))
    pieces = []
    first = len(dealt)
    pieces.append(Piece(first, shared[0].shape[0], True, True, 0, 1))
    pieces.append(Piece(first + 1, shared[1].shape[0], False, True, 0, 1))
    for part in range(2):
        for n, a in enumerate(split):
            pieces.append(Piece(first + len(shared) + n, a.shape[0], True, False, part, 2))
    pieces.append(Piece(first + 2, shared[2].shape[0], False, True, 0, 1))
    count = len(pieces)
    tok, width = dealt[0].shape
    sem = pltpu.SemaphoreType.DMA
    vmem = pl.BlockSpec(memory_space=pltpu.VMEM)
    return pl.pallas_call(
        functools.partial(fetch_kernel, sizes, pieces, len(ins), len(dealt)),
        in_specs=[pl.BlockSpec(memory_space=pl.ANY)] * len(ins) + [vmem],
        out_specs=[pl.BlockSpec(memory_space=pl.ANY)] * len(outs) + [vmem] * 5 + [pl.BlockSpec(memory_space=pl.ANY)],
        out_shape=outs
        + [
            jax.ShapeDtypeStruct((tok, width), BF),
            jax.ShapeDtypeStruct((tok, H * HD), BF),
            jax.ShapeDtypeStruct((WINDOW + tok, 2 * HD), BF),
            jax.ShapeDtypeStruct((tok, H * HD), BF),
            jax.ShapeDtypeStruct((tok // QBLK * (H // HEADS_STEP), 1, ROWS), F32),
            jax.ShapeDtypeStruct((2 * size_x - 1, tok, width), BF),
        ],
        scratch_shapes=[
            pltpu.VMEM((tok, width), BF),
            pltpu.VMEM((width, H * HD), BF),
            pltpu.VMEM((width, 2 * HD), BF),
            pltpu.VMEM((size_x,) + gains.shape, BF),
            pltpu.VMEM((WINDOW + tok, 2 * HD), BF),
            sem((4,)),
            sem((WINDOW // tok,)),
            sem((WINDOW // tok,)),
            sem((2 * size_x,)),
            sem((2 * size_x,)),
        ]
        + [
            pltpu.VMEM((a.shape[0], o.shape[1]), BF)
            for a, o in zip(ins[len(dealt) : -1], outs[len(dealt) : -1])
        ]
        + [
            sem((len(ins), 2)),
            sem((len(ins),)),
            sem((len(dealt), n_ctx)),
            sem((len(dealt), n_ctx)),
            sem((size_x,)),
            sem((size_x,)),
            sem((count, size_x)),
            sem((count, size_x)),
            sem((count, size_x, 9)),
            sem((count, size_x, 9)),
        ],
        compiler_params=pltpu.CompilerParams(
            collective_id=1, has_side_effects=True, vmem_limit_bytes=60 * 1024 * 1024
        ),
        cost_estimate=pl.CostEstimate(
            flops=0, bytes_accessed=300 * 1024 * 1024, transcendentals=0
        ),
        name="fetch",
    )(*ins, low)


def mlp_kernel(sizes, own_ref, *refs):
    size_a, size_b, size_x = sizes
    ranks = 2 * size_x
    cots_in, refs = refs[:2], refs[2:]
    weights_in, refs = refs[:3], refs[3:]
    grad_ref, rows_out, dg_out, du_out, part_out, down_out, refs = *refs[:6], refs[6:]
    rows, cot, w_gate, w_up, w_down, hid, dg, du = refs[:8]
    to_core, in_core, to_x, in_x, total, part_stage, down_stage = refs[8:15]
    load_sem, ag_send, ag_recv, core_send, core_recv, x_send, x_recv, out_sem, stage_sem = refs[15:]
    ia, ib, ic, ix = (lax.axis_index(name) for name in ALL)
    hidden_units = w_down.shape[0]
    tok, width = own_ref.shape
    tiles, _, tile = total.shape
    unit = hid.shape[2] // (hid.shape[2] // 512 if hid.shape[2] % 512 == 0 else hid.shape[2] // 256)

    loads = [
        pltpu.make_async_copy(own_ref, rows.at[0], load_sem.at[0]),
        pltpu.make_async_copy(weights_in[0], w_gate, load_sem.at[1]),
        pltpu.make_async_copy(weights_in[1], w_up, load_sem.at[2]),
        pltpu.make_async_copy(
            weights_in[2].at[pl.ds(pl.multiple_of(ic * hidden_units, hidden_units), hidden_units), :],
            w_down,
            load_sem.at[3],
        ),
    ]
    loads.append(pltpu.make_async_copy(cots_in[0], cot.at[0], load_sem.at[4]))
    loads.append(pltpu.make_async_copy(cots_in[1], cot.at[pl.ds(1, ranks - 1)], load_sem.at[5]))
    for copy in loads:
        copy.start()

    partner = (ia, ib, 1 - ic, ix)

    def across(step):
        return ia, ib, ic, (ix + size_x + step) % size_x

    barrier = pltpu.get_barrier_semaphore()
    greeted = [partner] + [across(s) for s in range(1, size_x)]
    for device in greeted:
        pl.semaphore_signal(barrier, inc=1, device_id=device, device_id_type=MESH)
    pl.semaphore_wait(barrier, len(greeted))

    def remote(src, dst, sent, came, device):
        return pltpu.make_async_remote_copy(
            src_ref=src,
            dst_ref=dst,
            send_sem=sent,
            recv_sem=came,
            device_id=device,
            device_id_type=MESH,
        )

    def gather(b):
        if b == 1:
            return remote(own_ref, rows.at[1], ag_send.at[1], ag_recv.at[1], partner)
        if b % 2:
            return remote(rows.at[b - 1], rows.at[b], ag_send.at[b], ag_recv.at[b], partner)
        return remote(own_ref, rows.at[b], ag_send.at[b], ag_recv.at[b], across(b // 2))

    def core_copy(s):
        return remote(to_core.at[s], in_core.at[s], core_send.at[s], core_recv.at[s], partner)

    def x_copy(s, t):
        return remote(
            to_x.at[s, t], in_x.at[s, t], x_send.at[s, t], x_recv.at[s, t], across(-s)
        )

    def results(b):
        to = pl.ds(b * tok, tok)
        return [
            pltpu.make_async_copy(rows.at[b], rows_out.at[to, :], out_sem.at[0, b]),
            pltpu.make_async_copy(dg.at[b], dg_out.at[to, :], out_sem.at[1, b]),
            pltpu.make_async_copy(du.at[b], du_out.at[to, :], out_sem.at[2, b]),
        ]

    def forward(b):
        def step(t, carry):
            units = pl.ds(pl.multiple_of(t * unit, unit), unit)
            gate = mm(rows[b], w_gate[:, units])
            upward = mm(rows[b], w_up[:, units])
            d_hidden = mm_nt(cot[b], w_down[units, :])
            square = gate * gate
            bent = jnp.tanh(root * gate * (1.0 + cubic * square))
            half = 0.5 * (1.0 + bent)
            act = gate * half
            slope = half + 0.5 * gate * (1.0 - bent * bent) * root * (1.0 + 3.0 * cubic * square)
            hid[b, :, units] = (act * upward).astype(BF)
            dg[b, :, units] = (d_hidden * upward * slope).astype(BF)
            du[b, :, units] = (d_hidden * act).astype(BF)
            return carry

        lax.fori_loop(0, hid.shape[2] // unit, step, 0)
        for copy in results(b):
            copy.start()

    def backward(b):
        s, other = b // 2, b % 2
        if not other:
            core_copy(s).wait_recv()

        def step(t, carry):
            at = pl.ds(pl.multiple_of(t * tile, tile), tile)
            value = mm_nt(dg[b], w_gate[at, :]) + mm_nt(du[b], w_up[at, :])
            if other:
                to_core[s, t] = value.astype(BF)
                return carry
            value = value + in_core[s, t].astype(F32)
            if s:
                to_x[s, t] = value.astype(BF)
                x_copy(s, t).start()
            else:
                total[t] = value
            return carry

        lax.fori_loop(0, tiles, step, 0)
        if other:
            core_copy(s).start()

    def part_copy(b):
        return pltpu.make_async_copy(part_stage.at[b % 2], part_out.at[b], stage_sem.at[b % 2])

    def branch(b):
        if b >= 2:
            part_copy(b - 2).wait()

        def step(t, carry):
            at = pl.ds(pl.multiple_of(t * tile, tile), tile)
            part_stage[b % 2, :, at] = mm(hid[b], w_down[:, at]).astype(BF)
            return carry

        lax.fori_loop(0, tiles, step, 0)
        part_copy(b).start()

    depth = down_stage.shape[1]
    strips = hidden_units // depth

    def down_copy(t, slot):
        to = pl.ds(pl.multiple_of(t * depth, depth), depth)
        return pltpu.make_async_copy(down_stage.at[slot], down_out.at[to, :], stage_sem.at[2 + slot])

    def down_step(t, carry):
        slot = t % 2

        @pl.when(t >= 2)
        def _():
            down_copy(t - 2, slot).wait()

        units = pl.ds(pl.multiple_of(t * depth, depth), depth)
        value = mm_tn(hid[0, :, units], cot[0])
        for b in range(1, ranks):
            value = value + mm_tn(hid[b, :, units], cot[b])
        down_stage[slot] = value.astype(BF)
        down_copy(t, slot).start()
        return carry

    gather(1).start()
    for s in range(1, size_x):
        gather(2 * s).start()
    for copy in loads:
        copy.wait()
    forward(0)
    gather(1).wait_recv()
    forward(1)
    backward(1)
    for s in range(1, size_x):
        gather(2 * s).wait_recv()
        gather(2 * s + 1).start()
        forward(2 * s)
        gather(2 * s + 1).wait_recv()
        forward(2 * s + 1)
        backward(2 * s + 1)
        backward(2 * s)
    backward(0)
    lax.fori_loop(0, strips, down_step, 0)
    for b in range(ranks):
        branch(b)
    for s in range(1, size_x):
        for t in range(tiles):
            x_copy(s, t).wait()
    for t in range(tiles):
        value = total[t]
        for s in range(1, size_x):
            value = value + in_x[s, t].astype(F32)
        grad_ref[:, t * tile : (t + 1) * tile] = value
    for b in range(1, ranks):
        gather(b).wait_send()
    for s in range(size_x):
        core_copy(s).wait_send()
    for b in range(ranks):
        for copy in results(b):
            copy.wait()
    part_copy(ranks - 2).wait()
    part_copy(ranks - 1).wait()
    down_copy(strips - 2, (strips - 2) % 2).wait()
    down_copy(strips - 1, (strips - 1) % 2).wait()


def feed_forward(sizes, normed, cot, cot_rows, w_gate, w_up, down_weight):
    ranks = 2 * sizes[2]
    size_x = sizes[2]
    tok, width = normed.shape
    units = w_gate.shape[1]
    tile = 512
    tiles = width // tile
    sem = pltpu.SemaphoreType.DMA
    hbm = pl.BlockSpec(memory_space=pl.ANY)
    return pl.pallas_call(
        functools.partial(mlp_kernel, sizes),
        in_specs=[hbm] * 6,
        out_specs=[pl.BlockSpec(memory_space=pltpu.VMEM)] + [hbm] * 5,
        out_shape=[
            jax.ShapeDtypeStruct((tok, width), F32),
            jax.ShapeDtypeStruct((ranks * tok, width), BF),
            jax.ShapeDtypeStruct((ranks * tok, units), BF),
            jax.ShapeDtypeStruct((ranks * tok, units), BF),
            jax.ShapeDtypeStruct((ranks, tok, width), BF),
            jax.ShapeDtypeStruct((units, width), BF),
        ],
        scratch_shapes=[
            pltpu.VMEM((ranks, tok, width), BF),
            pltpu.VMEM((ranks, tok, width), BF),
            pltpu.VMEM((width, units), BF),
            pltpu.VMEM((width, units), BF),
            pltpu.VMEM((units, width), BF),
            pltpu.VMEM((ranks, tok, units), BF),
            pltpu.VMEM((ranks, tok, units), BF),
            pltpu.VMEM((ranks, tok, units), BF),
            pltpu.VMEM((size_x, tiles, tok, tile), BF),
            pltpu.VMEM((size_x, tiles, tok, tile), BF),
            pltpu.VMEM((size_x, tiles, tok, tile), BF),
            pltpu.VMEM((size_x, tiles, tok, tile), BF),
            pltpu.VMEM((tiles, tok, tile), F32),
            pltpu.VMEM((2, tok, width), BF),
            pltpu.VMEM((2, 256, width), BF),
            sem((6,)),
            sem((ranks,)),
            sem((ranks,)),
            sem((size_x,)),
            sem((size_x,)),
            sem((size_x, tiles)),
            sem((size_x, tiles)),
            sem((3, ranks)),
            sem((4,)),
        ],
        compiler_params=pltpu.CompilerParams(
            collective_id=2, has_side_effects=True, vmem_limit_bytes=62 * 1024 * 1024
        ),
        cost_estimate=pl.CostEstimate(
            flops=14 * ranks * tok * width * units,
            bytes_accessed=60 * 1024 * 1024,
            transcendentals=0,
        ),
        name="feed_forward",
    )(normed, cot, cot_rows, w_gate, w_up, down_weight)


class Job:
    def __init__(self, phase, left, right, rows, cols, by_rank):
        self.phase, self.left, self.right = phase, left, right
        self.rows, self.cols, self.by_rank = rows, cols, by_rank


def grads_kernel(sizes, jobs, *refs):
    size_a, size_b, size_x = sizes
    chips = size_a * size_b
    n_ctx = 2 * chips
    ranks = 2 * size_x
    count = len(jobs)
    ins, refs = refs[:12], refs[12:]
    outs, refs = refs[:count], refs[count:]
    dealt, refs = refs[:2], refs[2:]
    gain_out, refs = refs[0], refs[1:]
    held, refs = refs[:8], refs[8:]
    gain_ctx, gain_x, parts_in, resid_in, block_out, refs = *refs[:5], refs[5:]
    recv, refs = refs[:count], refs[count:]
    send, refs = refs[:count], refs[count:]
    done, refs = refs[:count], refs[count:]
    load_sem, group_send, group_recv, deal_send, deal_recv = refs[:5]
    gain_send, gain_recv, send_sem, recv_sem, done_send, done_recv, own_sem = refs[5:]
    ia, ib, ic, ix = (lax.axis_index(name) for name in ALL)
    own = (ia * size_b + ib) * 2 + ic
    rank = ix * 2 + ic
    place = snake_place(ia, ib, size_a, size_b)

    def on_ring(step):
        return snake((place + 2 * chips + step) % chips, size_a, size_b)

    def member(k):
        return (ic + k // size_x) % 2, (ix + k % size_x) % size_x

    def ctx_device(k):
        e = (own + k) % n_ctx
        return e // 2 // size_b, e // 2 % size_b, e % 2, ix

    kept = rank * chips + kept_slot(ia, ib, size_a, size_b)
    kept_chip = kept // ranks
    kept_id = (kept_chip // size_b, kept_chip % size_b, (kept // size_x) % 2, kept % size_x)
    flat = own * size_x + ix
    from_rank = flat // chips
    from_slot = flat % chips
    half = chips // 2
    from_id = (
        (from_slot % half) // (size_b // 2),
        ((from_slot % half) % (size_b // 2)) * 2 + 1 - from_slot // half,
        from_rank % 2,
        from_rank // 2,
    )

    def remote(src, dst, sent, came, device):
        return pltpu.make_async_remote_copy(
            src_ref=src,
            dst_ref=dst,
            send_sem=sent,
            recv_sem=came,
            device_id=device,
            device_id_type=MESH,
        )

    loads = [pltpu.make_async_copy(ins[i], held[i], load_sem.at[i]) for i in range(3)]
    for copy in loads:
        copy.start()

    barrier = pltpu.get_barrier_semaphore()
    greeted = [ctx_device(k) for k in range(1, n_ctx)] + [from_id]
    greeted += [(ia, ib) + member(k) for k in range(ranks) if k % size_x]
    for device in greeted:
        pl.semaphore_signal(barrier, inc=1, device_id=device, device_id_type=MESH)
    pl.semaphore_wait(barrier, len(greeted))

    def group_copy(i, k):
        c, x = member(k)
        src, dst = ins[i], held[i].at[k]
        target = x * 2 + c
        if i == 4:
            rows = held[i].shape[1]
            src = src.at[pl.ds(pl.multiple_of(target * rows, rows), rows), :]
        if i == 6:
            cols = held[i].shape[2]
            src = src.at[:, pl.ds(pl.multiple_of(target * cols, cols), cols)]
        if k == 0:
            return pltpu.make_async_copy(src, dst, load_sem.at[i])
        return remote(src, dst, group_send.at[i, k], group_recv.at[i, k], (ia, ib, c, x))

    def deal_copy(t, k):
        e = (own + k) % n_ctx
        source = block_out if t == 0 else ins[9]
        rows = source.shape[0] // n_ctx
        src = source.at[pl.ds(pl.multiple_of(e * rows, rows), rows), :]
        dst = dealt[t].at[pl.ds(pl.multiple_of(own * rows, rows), rows), :]
        if k == 0:
            return pltpu.make_async_copy(src, dst, load_sem.at[8 + t])
        return remote(src, dst, deal_send.at[t, k], deal_recv.at[t, k], ctx_device(k))

    def part_copy(b):
        src, dst = ins[8].at[b], parts_in.at[b]
        if b == 0:
            return pltpu.make_async_copy(src, dst, own_sem.at[count])
        device = (ia, ib, (ic + b) % 2, (ix + size_x - b // 2) % size_x)
        return remote(src, dst, group_send.at[0, b], group_recv.at[0, b], device)

    resid_copy = pltpu.make_async_copy(ins[11], resid_in, load_sem.at[11])

    def gain_copy(k):
        src, dst = ins[10].at[(own + k) % n_ctx], gain_ctx.at[k]
        if k == 0:
            return pltpu.make_async_copy(src, dst, load_sem.at[10])
        return remote(src, dst, deal_send.at[2, k], deal_recv.at[2, k], ctx_device(k))

    def gain_copy_x(s):
        device = (ia, ib, ic, (ix + s) % size_x)
        return remote(gain_x.at[0], gain_x.at[s], gain_send.at[s], gain_recv.at[s], device)

    def ring_copy(j, way, step, parity):
        neighbour = on_ring(1 - 2 * way) + (ic, ix)
        return remote(
            send[j].at[way, parity],
            recv[j].at[way, step],
            send_sem.at[j, way, parity],
            recv_sem.at[j, way, step],
            neighbour,
        )

    def product(j, way, step):
        job = jobs[j]
        a, b = on_ring(step * (2 * way - 1))
        part = job.rows // chips
        cols = slice(way * job.cols // 2, (way + 1) * job.cols // 2)
        left, right = held[job.left], held[job.right]
        if job.phase == 0:
            start = pl.multiple_of((a * size_b + b) * part, part)
            return mm_tn(left[:, pl.ds(start, part)], right[:, cols])
        if job.by_rank:
            start = kept_slot(a, b, size_a, size_b) * part
            if left.shape[1] != job.rows:
                start = start + rank * job.rows
        else:
            start = (a * size_b + b) * part
        rows = pl.ds(pl.multiple_of(start, part), part)
        total = mm(left[0, rows, :], right[0, :, cols])
        for k in range(1, ranks):
            total = total + mm(left[k, rows, :], right[k, :, cols])
        return total

    def deliver(j):
        job = jobs[j]
        if job.by_rank:
            return [remote(done[j], outs[j], done_send.at[j, 0], done_recv.at[j, 0], kept_id)]
        part = job.rows // (chips * ranks)
        copies = []
        for k in range(ranks):
            c, x = member(k)
            start = pl.multiple_of((c * size_x + x) * part, part)
            src, dst = done[j].at[pl.ds(start, part), :], outs[j].at[rank]
            if k == 0:
                copies.append(pltpu.make_async_copy(src, dst, own_sem.at[j]))
            else:
                copies.append(
                    remote(src, dst, done_send.at[j, k], done_recv.at[j, k], (ia, ib, c, x))
                )
        return copies

    for copy in loads:
        copy.wait()
    for phase in range(2):
        mine = [j for j in range(count) if jobs[j].phase == phase]
        for j in mine:
            for way in range(2):
                send[j][way, 0] = product(j, way, 1).astype(BF)
                ring_copy(j, way, 0, 0).start()
        if phase == 0:
            for k in range(n_ctx):
                gain_copy(k).start()
            for i in range(3, 8):
                for k in range(ranks):
                    group_copy(i, k).start()
            for b in range(ranks):
                part_copy(b).start()
            resid_copy.start()
            for k in range(n_ctx):
                deal_copy(1, k).start()

        def step_of(step, carry):
            parity = step % 2
            for j in mine:
                for way in range(2):
                    part = product(j, way, step + 1)
                    ring_copy(j, way, step - 1, 1 - parity).wait_recv()
                    part = part + recv[j][way, step - 1].astype(F32)

                    @pl.when(step >= 2)
                    def _():
                        ring_copy(j, way, step - 2, parity).wait_send()

                    send[j][way, parity] = part.astype(BF)
                    ring_copy(j, way, step, parity).start()
            return carry

        lax.fori_loop(1, chips - 1, step_of, 0)
        if phase == 0:
            for k in range(n_ctx):
                gain_copy(k).wait()
            gain_x[0] = jnp.sum(gain_ctx[...], axis=0)
            for s in range(1, size_x):
                gain_copy_x(s).start()
            resid_copy.wait()
            for b in range(ranks):
                part_copy(b).wait()
            summed = resid_in[...]
            for b in range(ranks):
                summed = summed + parts_in[b].astype(F32)
            block_out[...] = summed.astype(BF)
            for k in range(n_ctx):
                deal_copy(0, k).start()
        last = chips - 2
        for j in mine:
            cols = jobs[j].cols // 2
            for way in range(2):
                part = product(j, way, chips)
                ring_copy(j, way, last, last % 2).wait_recv()
                part = part + recv[j][way, last].astype(F32)
                done[j][:, way * cols : (way + 1) * cols] = part.astype(BF)
            for copy in deliver(j):
                copy.start()
            for way in range(2):
                ring_copy(j, way, last - 1, (last - 1) % 2).wait_send()
                ring_copy(j, way, last, last % 2).wait_send()
        if phase == 0:
            for i in range(3, 8):
                for k in range(ranks):
                    group_copy(i, k).wait()
    for s in range(1, size_x):
        gain_copy_x(s).wait()
    gain_out[...] = jnp.sum(gain_x[...], axis=0)
    for t in range(2):
        for k in range(n_ctx):
            deal_copy(t, k).wait()
    for j in range(count):
        for copy in deliver(j):
            copy.wait()


def sum_grads(sizes, ins):
    size_a, size_b, size_x = sizes
    chips = size_a * size_b
    ranks = 2 * size_x
    normed_mlp, d_gate, d_upward = ins[:3]
    width = normed_mlp.shape[1]
    tok = ins[5].shape[0]
    part_width = width // ranks
    jobs = [
        Job(0, 0, 1, width, d_gate.shape[1], False),
        Job(0, 0, 2, width, d_upward.shape[1], False),
        Job(1, 3, 6, width, part_width, False),
        Job(1, 4, 5, part_width, width, True),
        Job(1, 3, 7, part_width, 2 * HD, True),
    ]
    held = [pltpu.VMEM(a.shape, BF) for a in ins[:3]]
    held += [
        pltpu.VMEM((ranks,) + shape, BF)
        for shape in (
            (width, tok),
            (part_width, tok),
            (tok, width),
            (tok, part_width),
            (tok, 2 * HD),
        )
    ]
    outs, recv, send, done = [], [], [], []
    flops = 0
    for job in jobs:
        part = job.rows // chips
        if job.by_rank:
            outs.append(jax.ShapeDtypeStruct((part, job.cols), BF))
        else:
            outs.append(jax.ShapeDtypeStruct((ranks, part // ranks, job.cols), BF))
        recv.append(pltpu.VMEM((2, chips - 1, part, job.cols // 2), BF))
        send.append(pltpu.VMEM((2, 2, part, job.cols // 2), BF))
        done.append(pltpu.VMEM((part, job.cols), BF))
        flops += 2 * job.rows * job.cols * normed_mlp.shape[0]
    count = len(jobs)
    outs += [jax.ShapeDtypeStruct((tok, width), BF)] * 2
    gain_shape = ins[10].shape[1:]
    outs.append(jax.ShapeDtypeStruct(gain_shape, F32))
    sem = pltpu.SemaphoreType.DMA
    return pl.pallas_call(
        functools.partial(grads_kernel, sizes, jobs),
        in_specs=[pl.BlockSpec(memory_space=pl.ANY)] * len(ins),
        out_specs=[pl.BlockSpec(memory_space=pl.ANY)] * (count + 2)
        + [pl.BlockSpec(memory_space=pltpu.VMEM)],
        out_shape=outs,
        scratch_shapes=held
        + [
            pltpu.VMEM((2 * chips,) + gain_shape, F32),
            pltpu.VMEM((size_x,) + gain_shape, F32),
            pltpu.VMEM((ranks, tok, width), BF),
            pltpu.VMEM((tok, width), F32),
            pltpu.VMEM((tok, width), BF),
        ]
        + recv
        + send
        + done
        + [
            sem((len(ins),)),
            sem((8, ranks)),
            sem((8, ranks)),
            sem((3, 2 * chips)),
            sem((3, 2 * chips)),
            sem((size_x,)),
            sem((size_x,)),
            sem((count, 2, 2)),
            sem((count, 2, chips - 1)),
            sem((count, ranks)),
            sem((count, ranks)),
            sem((count + 1,)),
        ],
        compiler_params=pltpu.CompilerParams(
            collective_id=0, has_side_effects=True, vmem_limit_bytes=60 * 1024 * 1024
        ),
        cost_estimate=pl.CostEstimate(
            flops=flops, bytes_accessed=400 * 1024 * 1024, transcendentals=0
        ),
        name="sum_grads",
    )(*ins)


def norm_stats(values):
    inv = lax.rsqrt(jnp.mean(values * values, axis=-1, keepdims=True) + epsilon)
    return values * inv, inv


def norm_back(unit, inv, gain, grad):
    scaled = grad * gain
    inner = jnp.mean(scaled * unit, axis=-1, keepdims=True)
    return inv * (scaled - unit * inner), jnp.sum(grad * unit, axis=0)


def on_device(
    sizes,
    tokens,
    lengths,
    dealing,
    attn_gain,
    query_weight,
    kv_weight,
    out_weight,
    mlp_gain,
    gate_weight,
    up_weight,
    down_weight,
    cotangent,
):
    size_a, size_b, size_x = sizes
    chips = size_a * size_b
    n_ctx = chips * 2
    ranks = 2 * size_x
    ia, ib, ic, ix = (lax.axis_index(name) for name in ALL)
    chip = ia * size_b + ib
    own = chip * 2 + ic
    flat = own * size_x + ix
    rank = ix * 2 + ic
    tok = tokens.shape[1]
    width = tokens.shape[2]
    piece = tok // n_ctx
    halo = WINDOW // tok

    def pick(array, index, axis=0):
        return lax.dynamic_index_in_dim(array, index, axis, keepdims=False)

    def shift_ctx(array, step):
        pairs = [(i, i + step) for i in range(n_ctx) if 0 <= i + step < n_ctx]
        return lax.ppermute(array, CTX, pairs)

    def from_x(step):
        return (ix + size_x - step) % size_x

    def sum_rows(grad):
        summed = lax.psum_scatter(
            grad.astype(BF), ("a", "b"), scatter_dimension=0, tiled=True
        )
        keep_pairs = []
        for g in range(chips):
            for c in range(2):
                for x in range(size_x):
                    keep_pairs.append(((g * 2 + c) * size_x + x, (x * 2 + c) * chips + g))
        return lax.ppermute(summed, ALL, keep_pairs).astype(F32)

    own_deal = pick(dealing[0], own)
    deal = (own_deal[:, None] == jnp.arange(tok, dtype=jnp.int32)[None, :]).astype(BF)

    gains = jnp.stack([attn_gain, mlp_gain]).reshape(-1, 128)
    stream = own * tok + jnp.arange(tok, dtype=jnp.int32)
    ends = jnp.cumsum(lengths[0])
    starts = jnp.max(jnp.where(stream[:, None] >= ends[None, :], ends[None, :], 0), axis=1)
    low = jnp.maximum(starts, stream - (WINDOW - 1)) - (own * tok - WINDOW)
    low = low.astype(jnp.int32)[None, :]
    inputs_low, cot, w_query, w_kv, w_out, w_gate, w_up, gains, *attended = fetch(
        sizes,
        [mm(deal, tokens[0]).astype(BF), mm(deal, cotangent[0]).astype(BF)],
        [query_weight, kv_weight, out_weight],
        [gate_weight, up_weight],
        gains,
        low,
    )
    normed, queries, window, context, lse, cot_rows = attended
    gains = gains.reshape(size_x, 2, -1).astype(F32)
    gain_one = gains[:, 0].reshape(-1)
    gain_two = gains[:, 1].reshape(-1)


    inputs = inputs_low.astype(F32)
    unit_one, inv_one = norm_stats(inputs)
    resid = inputs + mm(context, w_out)

    unit_two, inv_two = norm_stats(resid)
    d_normed_mlp, mlp_rows, d_gate, d_upward, mlp_parts, down_grad = feed_forward(
        sizes, (unit_two * gain_two).astype(BF), cot, cot_rows, w_gate, w_up, down_weight
    )
    down_grad = sum_rows(down_grad)
    d_resid_part, mlp_gain_grad = norm_back(unit_two, inv_two, gain_two, d_normed_mlp)
    d_resid = cot.astype(F32) + d_resid_part
    d_branch = d_resid.astype(BF)

    d_context = mm_nt(d_branch, w_out).astype(BF)
    d_queries, d_window = attend_back(queries, window, low, d_context, lse)
    d_pairs = d_window[halo * tok :]
    for j in range(halo):
        part = d_window[j * tok : (j + 1) * tok].astype(BF)
        d_pairs = d_pairs + shift_ctx(part, j - halo).astype(F32)
    d_pairs = d_pairs.astype(BF)
    d_normed = mm_nt(d_queries, w_query) + mm_nt(d_pairs, w_kv)
    d_inputs, attn_gain_grad = norm_back(unit_one, inv_one, gain_one, d_normed)
    gain_part = width // (n_ctx * size_x)
    gain_grads = jnp.stack([attn_gain_grad, mlp_gain_grad]).reshape(2, n_ctx, size_x, gain_part)
    gain_grads = gain_grads.transpose(1, 2, 0, 3).reshape(n_ctx, -1)
    gain_grads = jnp.pad(gain_grads, ((0, 0), (0, 1024 - gain_grads.shape[1])))
    sums = sum_grads(
        sizes,
        [
            mlp_rows,
            d_gate,
            d_upward,
            normed.T,
            context.T,
            d_branch,
            d_queries,
            d_pairs,
            mlp_parts,
            (d_resid + d_inputs).astype(BF),
            gain_grads.reshape(n_ctx, 8, 128),
            resid,
        ],
    )
    gate_grad, up_grad, query_grad = (
        v.transpose(1, 0, 2).reshape(v.shape[1], -1).astype(F32) for v in sums[:3]
    )
    out_grad, kv_grad = (v.astype(F32) for v in sums[3:5])
    block_output = mm_tn(deal, sums[5]).astype(BF)
    token_grad = mm_tn(deal, sums[6])
    gain_grads = lax.dynamic_slice(sums[7].reshape(-1), (ix * 2 * gain_part,), (2 * gain_part,))
    attn_gain_grad, mlp_gain_grad = gain_grads[:gain_part], gain_grads[gain_part:]
    return (
        block_output[None],
        token_grad[None],
        attn_gain_grad,
        query_grad,
        kv_grad,
        out_grad,
        mlp_gain_grad,
        gate_grad,
        up_grad,
        down_grad,
    )


def solution(mesh):
    n_ctx, size_x = mesh.shape["ctx"], mesh.shape["fsdp"]
    chips = n_ctx // 2
    size_a = 4 if chips % 4 == 0 else chips
    size_b = chips // size_a
    fine = Mesh(mesh.devices.reshape(size_a, size_b, 2, size_x), ALL)
    rows = P("x", CTX, None)
    split = P("x", None)
    every = P(ALL)
    matrix = P(ALL, None)
    return jax.shard_map(
        functools.partial(on_device, (size_a, size_b, size_x)),
        mesh=fine,
        in_specs=(
            rows,
            split,
            P("x", None, None),
            P("x"),
            split,
            split,
            split,
            P("x"),
            split,
            split,
            split,
            rows,
        ),
        out_specs=(rows, rows, every, matrix, matrix, matrix, every, matrix, matrix, matrix),
        check_vma=False,
    )
```

```python
import functools

import jax
import jax.numpy as jnp
import numpy as np
from jax import lax
from jax.experimental import pallas as pl
from jax.experimental.pallas import tpu as pltpu
from jax.sharding import Mesh
from jax.sharding import PartitionSpec as P

H = 16
HD = 128
WINDOW = 1024
QBLK = 128
HEADS_STEP = 4
SPAN = WINDOW + QBLK
ROWS = HEADS_STEP * QBLK

epsilon = 1e-06
neg_large = -1e30
scale = HD ** (-0.5)
root = (2.0 / np.pi) ** 0.5
cubic = 0.044715
BF = jnp.bfloat16
F32 = jnp.float32
CTX = ("a", "b", "c")
ALL = ("a", "b", "c", "x")
MESH = pl.DeviceIdType.MESH


def mm(left, right):
    return jnp.dot(left, right, preferred_element_type=F32)


def mm_tn(left, right):
    return lax.dot_general(left, right, (((0,), (0,)), ((), ())), preferred_element_type=F32)


def mm_nt(left, right):
    return lax.dot_general(left, right, (((1,), (1,)), ((), ())), preferred_element_type=F32)


def stack_heads(block):
    return jnp.concatenate([block[:, h * HD : (h + 1) * HD] for h in range(HEADS_STEP)], 0)


def unstack_heads(block_t):
    return jnp.concatenate(
        [block_t[:, h * QBLK : (h + 1) * QBLK].T for h in range(HEADS_STEP)], 1
    )


def bias_of(lo, qb):
    key = lax.broadcasted_iota(jnp.int32, (SPAN, QBLK), 0) + qb * QBLK
    query = lax.broadcasted_iota(jnp.int32, (SPAN, QBLK), 1) + (WINDOW + qb * QBLK)
    allowed = (key >= lo) & (key <= query)
    bias = jnp.where(allowed, 0.0, neg_large).astype(F32)
    return jnp.concatenate([bias] * HEADS_STEP, 1)


def attend_block(bias, queries, keys, values):
    scores = mm_nt(keys, queries) * scale + bias
    top = jnp.max(scores, axis=0, keepdims=True)
    raised = jnp.exp(scores - top)
    total = jnp.sum(raised, axis=0, keepdims=True)
    return mm_tn(values, raised.astype(BF)) * (1.0 / total), top + jnp.log(total)


def snake(pos, size_a, size_b):
    if size_b == 1:
        return pos, pos * 0
    down = pos // size_a
    first = 1 - (down + 7) // 8
    q = (pos - size_a) * (1 - first)
    a_up = size_a - 1 - q // (size_b - 1)
    k = q % (size_b - 1)
    odd = a_up % 2
    b_up = odd * (1 + k) + (1 - odd) * (size_b - 1 - k)
    return first * pos + (1 - first) * a_up, (1 - first) * b_up


def snake_place(a, b, size_a, size_b):
    if size_b == 1:
        return a
    moved = (b + size_b - 1) // size_b
    odd = a % 2
    along = odd * (b - 1) + (1 - odd) * (size_b - 1 - b)
    return (1 - moved) * a + moved * (size_a + (size_a - 1 - a) * (size_b - 1) + along)


def kept_slot(a, b, size_a, size_b):
    half = size_a * size_b // 2
    return (1 - b % 2) * half + a * (size_b // 2) + b // 2


def back_kernel(sizes, low_ref, q_ref, kv_ref, branch_ref, lse_ref, down_in, *refs):
    size_a, size_b, size_x = sizes
    weights_in, refs = refs[:3], refs[3:]
    dq_ref, pairs_ref, sum_ref, normed_ref, refs = *refs[:4], refs[4:]
    w_out, w_query, w_kv, do_ref, refs = *refs[:4], refs[4:]
    dkv, down, recv, send, halo_out, halo_in = refs[:6]
    load_sem, send_sem, recv_sem, halo_send, halo_recv = refs[6:]
    chips = size_a * size_b
    n_ctx = chips * 2
    ia, ib, ic, ix = (lax.axis_index(name) for name in ALL)
    own = (ia * size_b + ib) * 2 + ic
    place = snake_place(ia, ib, size_a, size_b)
    tok = q_ref.shape[0]
    halo = WINDOW // tok
    groups = H // HEADS_STEP
    blocks = tok // QBLK * groups
    part = down.shape[0] // chips
    quarter = down.shape[1] // 4
    chains = [(way, sub) for way in range(2) for sub in range(2)]
    last = chips - 2

    loading = pltpu.make_async_copy(down_in, down, load_sem.at[0])
    loading.start()
    weights = [
        pltpu.make_async_copy(src, dst, load_sem.at[1 + n])
        for n, (src, dst) in enumerate(zip(weights_in, (w_out, w_query, w_kv)))
    ]
    for copy in weights:
        copy.start()
    dkv[...] = jnp.zeros_like(dkv)

    def on_ring(step):
        return snake((place + 2 * chips + step) % chips, size_a, size_b)

    def ctx_device(step):
        e = (own + n_ctx + step) % n_ctx
        return e // 2 // size_b, e // 2 % size_b, e % 2, ix

    barrier = pltpu.get_barrier_semaphore()
    for k in range(1, n_ctx):
        pl.semaphore_signal(barrier, inc=1, device_id=ctx_device(k), device_id_type=MESH)
    pl.semaphore_wait(barrier, n_ctx - 1)

    def remote(src, dst, sent, came, device):
        return pltpu.make_async_remote_copy(
            src_ref=src,
            dst_ref=dst,
            send_sem=sent,
            recv_sem=came,
            device_id=device,
            device_id_type=MESH,
        )

    def ring_copy(way, sub, step, parity):
        return remote(
            send.at[way, sub, parity],
            recv.at[way, sub, step],
            send_sem.at[way, sub, parity],
            recv_sem.at[way, sub, step],
            on_ring(1 - 2 * way) + (ic, ix),
        )

    def columns(way, sub):
        return slice((2 * way + sub) * quarter, (2 * way + sub + 1) * quarter)

    def chunk(way, sub, step):
        a, b = on_ring(step * (2 * way - 1))
        rows = pl.ds(pl.multiple_of(kept_slot(a, b, size_a, size_b) * part, part), part)
        return down[rows, columns(way, sub)]

    def advance(step):
        parity = step % 2
        for way, sub in chains:
            value = chunk(way, sub, step + 1).astype(F32)
            ring_copy(way, sub, step - 1, 1 - parity).wait_recv()
            value = value + recv[way, sub, step - 1].astype(F32)

            @pl.when(step >= 2)
            def _():
                ring_copy(way, sub, step - 2, parity).wait_send()

            send[way, sub, parity] = value.astype(BF)
            ring_copy(way, sub, step, parity).start()

    def attend_step(t):
        qb, hg = t // groups, t % groups
        width = HEADS_STEP * HD
        block = pl.ds(pl.multiple_of(qb * QBLK, QBLK), QBLK)
        cols = pl.ds(pl.multiple_of(hg * width, width), width)
        rows = pl.ds(pl.multiple_of(qb * QBLK, QBLK), SPAN)
        keys = kv_ref[rows, :HD]
        values = kv_ref[rows, HD:]
        queries = stack_heads(q_ref[block, cols])
        d_out = stack_heads(do_ref[block, cols])
        scores = mm_nt(keys, queries) * scale + bias_of(low_ref[qb], qb)
        probs = jnp.exp(scores - lse_ref[t])
        d_probs = mm_nt(values, d_out)
        delta = jnp.sum(probs * d_probs, axis=0, keepdims=True)
        d_scores = (probs * (d_probs - delta)).astype(BF)
        dq_ref[block, cols] = unstack_heads(mm_tn(keys, d_scores) * scale).astype(BF)
        dkv[rows, :HD] += mm(d_scores, queries) * scale
        dkv[rows, HD:] += mm(probs.astype(BF), d_out)

    def halo_copy(k):
        sems = (halo_send.at[k - 1], halo_recv.at[k - 1])
        return remote(halo_out.at[k - 1], halo_in.at[k - 1], *sems, ctx_device(-k))

    def both(step, carry):
        advance(step)
        attend_step(2 * step - 2)
        attend_step(2 * step - 1)
        return carry

    def alone(step, carry):
        advance(step)
        return carry

    tile = 512

    def context_step(t, carry):
        at = pl.ds(pl.multiple_of(t * tile, tile), tile)
        do_ref[:, at] = mm_nt(branch_ref[...], w_out[at, :]).astype(BF)
        return carry

    def normed_step(t, carry):
        at = pl.ds(pl.multiple_of(t * tile, tile), tile)
        normed_ref[:, at] = mm_nt(dq_ref[...], w_query[at, :]) + mm_nt(pairs_ref[...], w_kv[at, :])
        return carry

    loading.wait()
    for way, sub in chains:
        send[way, sub, 0] = chunk(way, sub, 1)
        ring_copy(way, sub, 0, 0).start()
    weights[0].wait()
    lax.fori_loop(0, w_out.shape[0] // tile, context_step, 0)
    busy = blocks // 2
    lax.fori_loop(1, busy + 1, both, 0)
    for k in range(1, halo + 1):

        @pl.when(own >= k)
        def _():
            halo_out[k - 1] = dkv[(halo - k) * tok : (halo - k + 1) * tok, :].astype(BF)
            halo_copy(k).start()

    lax.fori_loop(busy + 1, busy + 2, alone, 0)
    for k in range(1, halo + 1):

        @pl.when(own + k < n_ctx)
        def _():
            halo_copy(k).wait_recv()
            dkv[WINDOW:, :] += halo_in[k - 1].astype(F32)

    pairs_ref[...] = dkv[WINDOW:, :].astype(BF)
    for copy in weights[1:]:
        copy.wait()
    lax.fori_loop(0, w_query.shape[0] // tile, normed_step, 0)
    lax.fori_loop(busy + 2, last + 1, alone, 0)
    for way, sub in chains:
        value = chunk(way, sub, chips).astype(F32)
        ring_copy(way, sub, last, last % 2).wait_recv()
        value = value + recv[way, sub, last].astype(F32)
        sum_ref[:, columns(way, sub)] = value.astype(BF)
    for way, sub in chains:
        ring_copy(way, sub, last - 1, (last - 1) % 2).wait_send()
        ring_copy(way, sub, last, last % 2).wait_send()
    for k in range(1, halo + 1):

        @pl.when(own >= k)
        def _():
            halo_copy(k).wait_send()


def attend_back(sizes, queries, window, low, d_branch, lse, down, w_out, w_query, w_kv):
    chips = sizes[0] * sizes[1]
    tok = queries.shape[0]
    halo = WINDOW // tok
    part, width = down.shape[0] // chips, down.shape[1]
    sem = pltpu.SemaphoreType.DMA
    vmem = pl.BlockSpec(memory_space=pltpu.VMEM)
    return pl.pallas_call(
        functools.partial(back_kernel, sizes),
        in_specs=[vmem] * 5 + [pl.BlockSpec(memory_space=pl.ANY)] * 4,
        out_specs=[vmem] * 4,
        out_shape=[
            jax.ShapeDtypeStruct((tok, H * HD), BF),
            jax.ShapeDtypeStruct((tok, 2 * HD), BF),
            jax.ShapeDtypeStruct((part, width), BF),
            jax.ShapeDtypeStruct((tok, width), F32),
        ],
        scratch_shapes=[
            pltpu.VMEM(w_out.shape, BF),
            pltpu.VMEM(w_query.shape, BF),
            pltpu.VMEM(w_kv.shape, BF),
            pltpu.VMEM((tok, H * HD), BF),
            pltpu.VMEM((WINDOW + tok, 2 * HD), F32),
            pltpu.VMEM(down.shape, BF),
            pltpu.VMEM((2, 2, chips - 1, part, width // 4), BF),
            pltpu.VMEM((2, 2, 2, part, width // 4), BF),
            pltpu.VMEM((halo, tok, 2 * HD), BF),
            pltpu.VMEM((halo, tok, 2 * HD), BF),
            sem((4,)),
            sem((2, 2, 2)),
            sem((2, 2, chips - 1)),
            sem((halo,)),
            sem((halo,)),
        ],
        compiler_params=pltpu.CompilerParams(
            collective_id=3, has_side_effects=True, vmem_limit_bytes=60 * 1024 * 1024
        ),
        cost_estimate=pl.CostEstimate(
            flops=10 * tok * H * HD * SPAN, bytes_accessed=100 * 1024 * 1024, transcendentals=0
        ),
        name="attend_back",
    )(low.reshape(tok // QBLK, 1, QBLK), queries, window, d_branch, lse, down, w_out, w_query, w_kv)


class Piece:
    def __init__(self, at, rows, square, shared, part, parts):
        self.at, self.rows, self.square, self.shared = at, rows, square, shared
        self.part, self.parts = part, parts
        self.relays = [0, 1, 2, 3] if square else []
        if shared:
            self.relays += [4, 5, 6, 7, 8] if square else [4]


def fetch_kernel(sizes, pieces, n_in, n_dealt, *refs):
    size_a, size_b, size_x = sizes
    n_ctx = size_a * size_b * 2
    ins, low_ref, refs = refs[:n_in], refs[n_in], refs[n_in + 1 :]
    outs, refs = refs[:n_in], refs[n_in:]
    normed_ref, query_ref, window_out, context_ref, lse_ref, cot_rows, refs = *refs[:6], refs[6:]
    tok_in, w_query, w_kv, gain_in, window, refs = *refs[:5], refs[5:]
    load_sem, halo_send, halo_recv, cot_send, cot_recv, refs = *refs[:5], refs[5:]
    n_weights = n_in - n_dealt - 1
    stages, refs = refs[:n_weights], refs[n_weights:]
    keep_sem, own_sem, deal_send, deal_recv, gain_send, gain_recv = refs[:6]
    x_send, x_recv, relay_send, relay_recv = refs[6:]
    ia, ib, ic, ix = (lax.axis_index(name) for name in ALL)
    own = (ia * size_b + ib) * 2 + ic
    rank = ix * 2 + ic
    pa, pb = ia % 2, ib % 2
    other_a, other_b = ia + 1 - 2 * pa, ib + 1 - 2 * pb
    corner = pa * 2 + pb
    corner_a, corner_b, corner_d = (1 - pa) * 2 + pb, pa * 2 + 1 - pb, 3 - corner

    barrier = pltpu.get_barrier_semaphore()
    greeted = []
    for k in range(1, n_ctx):
        e = (own + k) % n_ctx
        greeted.append((e // 2 // size_b, e // 2 % size_b, e % 2, ix))
    for s in range(1, size_x):
        greeted.append((ia, ib, ic, (ix + s) % size_x))
    for device in greeted:
        pl.semaphore_signal(barrier, inc=1, device_id=device, device_id_type=MESH)
    pl.semaphore_wait(barrier, len(greeted))

    def remote(src, dst, send, recv, device):
        return pltpu.make_async_remote_copy(
            src_ref=src,
            dst_ref=dst,
            send_sem=send,
            recv_sem=recv,
            device_id=device,
            device_id_type=MESH,
        )

    def x_copy(i, s):
        p = pieces[i]
        shard, full = ins[p.at], outs[p.at]
        target = (ix + s) % size_x
        height = shard.shape[0]
        rows, start = region(p, corner, ic)
        if p.shared:
            src = shard.at[pl.ds(start, rows), :]
        else:
            cols = full.shape[1]
            at = pl.multiple_of((target * 2 + ic) * cols, cols)
            src = shard.at[pl.ds(start, rows), pl.ds(at, cols)]
        dst = full.at[pl.ds(pl.multiple_of(ix * height + start, rows), rows), :]
        return remote(src, dst, x_send.at[i, s], x_recv.at[i, s], (ia, ib, ic, target))

    def region(p, which, core):
        owner = which if p.square else 0
        owners = 4 if p.square else 1
        if p.shared:
            owner, owners = owner * 2 + core, owners * 2
        rows = p.rows // (owners * p.parts)
        return rows, pl.multiple_of((owner * p.parts + p.part) * rows, rows)

    def landed(i, s, which, core, half=None):
        p = pieces[i]
        rows, start = region(p, which, core)
        start = start + (ix + size_x - s) % size_x * p.rows
        if half is not None:
            rows = rows // 2
            start = start + half * rows
        return outs[p.at].at[pl.ds(pl.multiple_of(start, rows), rows), :]

    def relay(i, s, kind, incoming=False):
        sem = (relay_send.at[i, s, kind], relay_recv.at[i, s, kind])
        if kind < 4:
            device = (other_a, ib, ic, ix) if kind in (1, 2) else (ia, other_b, ic, ix)
            sent = (
                landed(i, s, corner, ic),
                landed(i, s, corner, ic),
                landed(i, s, corner_b, ic, 0),
                landed(i, s, corner_a, ic, 1),
            )[kind]
            came = (
                landed(i, s, corner_b, ic),
                landed(i, s, corner_a, ic),
                landed(i, s, corner_d, ic, 0),
                landed(i, s, corner_d, ic, 1),
            )[kind]
        else:
            device = (ia, ib, 1 - ic, ix)
            which, half = ((corner, None), (corner_b, None), (corner_a, None), (corner_d, 0), (corner_d, 1))[
                kind - 4
            ]
            sent = landed(i, s, which, ic, half)
            came = landed(i, s, which, 1 - ic, half)
        ref = came if incoming else sent
        return remote(ref, ref, *sem, device)

    rows = ins[0].shape[0] // n_ctx

    def deal_copy(t, k):
        e = (own + k) % n_ctx
        src = ins[t].at[pl.ds(pl.multiple_of(e * rows, rows), rows), :]
        dst = outs[t].at[pl.ds(pl.multiple_of(own * rows, rows), rows), :]
        if k == 0:
            return pltpu.make_async_copy(src, dst, own_sem.at[t])
        device = (e // 2 // size_b, e // 2 % size_b, e % 2, ix)
        return remote(src, dst, deal_send.at[t, k], deal_recv.at[t, k], device)

    g = n_in - 1

    def gain_copy(s):
        if s == 0:
            return pltpu.make_async_copy(ins[g], outs[g].at[ix], own_sem.at[g])
        device = (ia, ib, ic, (ix + s) % size_x)
        return remote(ins[g], outs[g].at[ix], gain_send.at[s], gain_recv.at[s], device)

    def keep_copy(w, out):
        shard, full = ins[w], outs[w]
        stage = stages[w - n_dealt]
        height = shard.shape[0]
        sem = keep_sem.at[w, out]
        if out:
            dst = full.at[pl.ds(pl.multiple_of(ix * height, height), height), :]
            return pltpu.make_async_copy(stage, dst, sem)
        src = shard
        if full.shape[1] != shard.shape[1]:
            cols = full.shape[1]
            src = shard.at[:, pl.ds(pl.multiple_of(rank * cols, cols), cols)]
        return pltpu.make_async_copy(src, stage, sem)

    tok = tok_in.shape[0]
    halo = WINDOW // tok
    at_query, at_kv = n_dealt, n_dealt + 1

    def load(src, dst, n):
        copy = pltpu.make_async_copy(src, dst, load_sem.at[n])
        copy.start()
        copy.wait()

    def core_parts_in(i):
        for s in range(1, size_x):
            for kind in pieces[i].relays:
                if kind >= 4:
                    relay(i, s, kind, True).wait_recv()
        keep_copy(pieces[i].at, 1).wait()

    def halo_copy(k):
        e = own + k
        device = (e // 2 // size_b, e // 2 % size_b, e % 2, ix)
        src = window.at[pl.ds(WINDOW, tok), :]
        dst = window.at[pl.ds((halo - k) * tok, tok), :]
        return remote(src, dst, halo_send.at[k - 1], halo_recv.at[k - 1], device)

    def normalise():
        for k in range(n_ctx):
            deal_copy(0, k).wait()
        for s in range(size_x):
            gain_copy(s).wait()
        load(outs[0], tok_in, 0)
        load(outs[g], gain_in, 1)
        gain = []
        for x in range(size_x):
            values = gain_in[x].astype(F32)
            gain += [values[r : r + 1, :] for r in range(values.shape[0] // 2)]
        values = tok_in[...].astype(F32)
        unit, _ = norm_stats(values)
        normed_ref[...] = (unit * jnp.concatenate(gain, 1)).astype(BF)

    def keys_values():
        core_parts_in(1)
        load(outs[at_kv], w_kv, 2)
        window[WINDOW:, :] = mm(normed_ref[...], w_kv[...]).astype(BF)
        for k in range(1, halo + 1):

            @pl.when(own + k < n_ctx)
            def _():
                halo_copy(k).start()

            @pl.when(own < k)
            def _():
                window[(halo - k) * tok : (halo - k + 1) * tok, :] = jnp.zeros((tok, 2 * HD), BF)

    def project():
        core_parts_in(0)
        load(outs[at_query], w_query, 3)

        def step(t, carry):
            cols = pl.ds(pl.multiple_of(t * 512, 512), 512)
            query_ref[:, cols] = mm(normed_ref[...], w_query[:, cols]).astype(BF)
            return carry

        lax.fori_loop(0, H * HD // 512, step, 0)

    def halo_in():
        for k in range(1, halo + 1):

            @pl.when(own >= k)
            def _():
                halo_copy(k).wait_recv()

    def cot_copy(b):
        sems = (cot_send.at[b], cot_recv.at[b])
        if b % 2:
            src = outs[1] if b == 1 else cot_rows.at[b - 2]
            return remote(src, cot_rows.at[b - 1], *sems, (ia, ib, 1 - ic, ix))
        device = (ia, ib, ic, (ix + b // 2) % size_x)
        return remote(outs[1], cot_rows.at[b - 1], *sems, device)

    def spread_cotangent():
        for k in range(n_ctx):
            deal_copy(1, k).wait()
        for s in range(1, size_x):
            cot_copy(2 * s).start()
        cot_copy(1).start()

    def attend(qb):
        low = low_ref[:, qb * QBLK : (qb + 1) * QBLK]
        bias = bias_of(low, qb)
        keys = window[qb * QBLK : qb * QBLK + SPAN, :HD]
        values = window[qb * QBLK : qb * QBLK + SPAN, HD:]
        rows = slice(qb * QBLK, (qb + 1) * QBLK)

        def step(t, carry):
            width = HEADS_STEP * HD
            cols = pl.ds(pl.multiple_of(t * width, width), width)
            out_t, lse = attend_block(bias, stack_heads(query_ref[rows, cols]), keys, values)
            context_ref[rows, cols] = unstack_heads(out_t).astype(BF)
            lse_ref[qb * (H // HEADS_STEP) + t] = lse
            return carry

        lax.fori_loop(0, H // HEADS_STEP, step, 0)

    blocks = tok // QBLK
    tasks = {2 * size_x - 1: [normalise, keys_values], 2 * size_x: [spread_cotangent, project]}
    for qb in range(blocks):
        task = functools.partial(attend, qb)
        tasks[2 * size_x + 1 + qb] = [halo_in, task] if qb == 0 else [task]

    ahead = 4
    order = [(i, s) for i in range(len(pieces)) for s in range(1, size_x)]
    for k in range(n_ctx):
        deal_copy(0, k).start()
    for s in range(size_x):
        gain_copy(s).start()
    for i, s in order[:ahead]:
        x_copy(i, s).start()
    for t in range(1, n_dealt):
        for k in range(n_ctx):
            deal_copy(t, k).start()
    for w in range(n_dealt, n_dealt + n_weights):
        keep_copy(w, 0).start()

    for n in range(len(order) + 2):
        if n < n_weights:
            keep_copy(n_dealt + n, 0).wait()
            keep_copy(n_dealt + n, 1).start()
        if n < len(order):
            i, s = order[n]
            x_copy(i, s).wait_recv()
            for kind in (0, 1, 4):
                if kind in pieces[i].relays:
                    relay(i, s, kind).start()
            if n + ahead < len(order):
                x_copy(i, s).wait_send()
                x_copy(*order[n + ahead]).start()
        if 1 <= n <= len(order) and pieces[order[n - 1][0]].square:
            i, s = order[n - 1]
            relay(i, s, 0, True).wait_recv()
            relay(i, s, 2).start()
            relay(i, s, 1, True).wait_recv()
            relay(i, s, 3).start()
            if pieces[i].shared:
                relay(i, s, 5).start()
                relay(i, s, 6).start()
        if n >= 2 and pieces[order[n - 2][0]].square:
            i, s = order[n - 2]
            relay(i, s, 2, True).wait_recv()
            relay(i, s, 3, True).wait_recv()
            if pieces[i].shared:
                relay(i, s, 7).start()
                relay(i, s, 8).start()
        for task in tasks.get(n, []):
            task()

    for s in range(1, size_x):
        cot_copy(2 * s).wait_recv()
        cot_copy(2 * s + 1).start()
    window_out[...] = window[...]
    for k in range(1, halo + 1):

        @pl.when(own + k < n_ctx)
        def _():
            halo_copy(k).wait_send()

    for n, (i, s) in enumerate(order):
        if n + ahead >= len(order):
            x_copy(i, s).wait_send()
        for kind in pieces[i].relays:
            relay(i, s, kind).wait_send()
            if kind >= 4 and i > 1:
                relay(i, s, kind, True).wait_recv()
    for b in range(1, 2 * size_x):
        cot_copy(b).wait_send()
        if b % 2:
            cot_copy(b).wait_recv()
    for w in range(n_dealt + 2, n_dealt + n_weights):
        keep_copy(w, 1).wait()


def fetch(sizes, dealt, shared, split, gains, low):
    size_a, size_b, size_x = sizes
    n_ctx = size_a * size_b * 2
    ins = dealt + shared + split + [gains]
    outs = [jax.ShapeDtypeStruct(a.shape, BF) for a in dealt]
    outs += [jax.ShapeDtypeStruct((size_x * a.shape[0], a.shape[1]), BF) for a in shared]
    outs += [
        jax.ShapeDtypeStruct((size_x * a.shape[0], a.shape[1] // (2 * size_x)), BF) for a in split
    ]
    outs.append(jax.ShapeDtypeStruct((size_x,) + gains.shape, BF))
    pieces = []
    first = len(dealt)
    pieces.append(Piece(first, shared[0].shape[0], True, True, 0, 1))
    pieces.append(Piece(first + 1, shared[1].shape[0], False, True, 0, 1))
    for part in range(2):
        for n, a in enumerate(split):
            pieces.append(Piece(first + len(shared) + n, a.shape[0], True, False, part, 2))
    pieces.append(Piece(first + 2, shared[2].shape[0], False, True, 0, 1))
    count = len(pieces)
    tok, width = dealt[0].shape
    sem = pltpu.SemaphoreType.DMA
    vmem = pl.BlockSpec(memory_space=pltpu.VMEM)
    return pl.pallas_call(
        functools.partial(fetch_kernel, sizes, pieces, len(ins), len(dealt)),
        in_specs=[pl.BlockSpec(memory_space=pl.ANY)] * len(ins) + [vmem],
        out_specs=[pl.BlockSpec(memory_space=pl.ANY)] * len(outs) + [vmem] * 5 + [pl.BlockSpec(memory_space=pl.ANY)],
        out_shape=outs
        + [
            jax.ShapeDtypeStruct((tok, width), BF),
            jax.ShapeDtypeStruct((tok, H * HD), BF),
            jax.ShapeDtypeStruct((WINDOW + tok, 2 * HD), BF),
            jax.ShapeDtypeStruct((tok, H * HD), BF),
            jax.ShapeDtypeStruct((tok // QBLK * (H // HEADS_STEP), 1, ROWS), F32),
            jax.ShapeDtypeStruct((2 * size_x - 1, tok, width), BF),
        ],
        scratch_shapes=[
            pltpu.VMEM((tok, width), BF),
            pltpu.VMEM((width, H * HD), BF),
            pltpu.VMEM((width, 2 * HD), BF),
            pltpu.VMEM((size_x,) + gains.shape, BF),
            pltpu.VMEM((WINDOW + tok, 2 * HD), BF),
            sem((4,)),
            sem((WINDOW // tok,)),
            sem((WINDOW // tok,)),
            sem((2 * size_x,)),
            sem((2 * size_x,)),
        ]
        + [
            pltpu.VMEM((a.shape[0], o.shape[1]), BF)
            for a, o in zip(ins[len(dealt) : -1], outs[len(dealt) : -1])
        ]
        + [
            sem((len(ins), 2)),
            sem((len(ins),)),
            sem((len(dealt), n_ctx)),
            sem((len(dealt), n_ctx)),
            sem((size_x,)),
            sem((size_x,)),
            sem((count, size_x)),
            sem((count, size_x)),
            sem((count, size_x, 9)),
            sem((count, size_x, 9)),
        ],
        compiler_params=pltpu.CompilerParams(
            collective_id=1, has_side_effects=True, vmem_limit_bytes=60 * 1024 * 1024
        ),
        cost_estimate=pl.CostEstimate(
            flops=0, bytes_accessed=300 * 1024 * 1024, transcendentals=0
        ),
        name="fetch",
    )(*ins, low)


def mlp_kernel(sizes, own_ref, *refs):
    size_a, size_b, size_x = sizes
    ranks = 2 * size_x
    cots_in, refs = refs[:2], refs[2:]
    weights_in, refs = refs[:3], refs[3:]
    grad_ref, rows_out, dg_out, du_out, part_out, down_out, refs = *refs[:6], refs[6:]
    rows, cot, w_gate, w_up, w_down, hid, dg, du = refs[:8]
    to_core, in_core, to_x, in_x, total, part_stage, down_stage = refs[8:15]
    load_sem, ag_send, ag_recv, core_send, core_recv, x_send, x_recv, out_sem, stage_sem = refs[15:]
    ia, ib, ic, ix = (lax.axis_index(name) for name in ALL)
    hidden_units = w_down.shape[0]
    tok, width = own_ref.shape
    tiles, _, tile = total.shape
    unit = hid.shape[2] // (hid.shape[2] // 512 if hid.shape[2] % 512 == 0 else hid.shape[2] // 256)

    loads = [
        pltpu.make_async_copy(own_ref, rows.at[0], load_sem.at[0]),
        pltpu.make_async_copy(weights_in[0], w_gate, load_sem.at[1]),
        pltpu.make_async_copy(weights_in[1], w_up, load_sem.at[2]),
        pltpu.make_async_copy(
            weights_in[2].at[pl.ds(pl.multiple_of(ic * hidden_units, hidden_units), hidden_units), :],
            w_down,
            load_sem.at[3],
        ),
    ]
    loads.append(pltpu.make_async_copy(cots_in[0], cot.at[0], load_sem.at[4]))
    loads.append(pltpu.make_async_copy(cots_in[1], cot.at[pl.ds(1, ranks - 1)], load_sem.at[5]))
    for copy in loads:
        copy.start()

    partner = (ia, ib, 1 - ic, ix)

    def across(step):
        return ia, ib, ic, (ix + size_x + step) % size_x

    barrier = pltpu.get_barrier_semaphore()
    greeted = [partner] + [across(s) for s in range(1, size_x)]
    for device in greeted:
        pl.semaphore_signal(barrier, inc=1, device_id=device, device_id_type=MESH)
    pl.semaphore_wait(barrier, len(greeted))

    def remote(src, dst, sent, came, device):
        return pltpu.make_async_remote_copy(
            src_ref=src,
            dst_ref=dst,
            send_sem=sent,
            recv_sem=came,
            device_id=device,
            device_id_type=MESH,
        )

    def gather(b):
        if b == 1:
            return remote(own_ref, rows.at[1], ag_send.at[1], ag_recv.at[1], partner)
        if b % 2:
            return remote(rows.at[b - 1], rows.at[b], ag_send.at[b], ag_recv.at[b], partner)
        return remote(own_ref, rows.at[b], ag_send.at[b], ag_recv.at[b], across(b // 2))

    def core_copy(s):
        return remote(to_core.at[s], in_core.at[s], core_send.at[s], core_recv.at[s], partner)

    def x_copy(s, t):
        return remote(
            to_x.at[s, t], in_x.at[s, t], x_send.at[s, t], x_recv.at[s, t], across(-s)
        )

    def results(b):
        to = pl.ds(b * tok, tok)
        return [
            pltpu.make_async_copy(rows.at[b], rows_out.at[to, :], out_sem.at[0, b]),
            pltpu.make_async_copy(dg.at[b], dg_out.at[to, :], out_sem.at[1, b]),
            pltpu.make_async_copy(du.at[b], du_out.at[to, :], out_sem.at[2, b]),
        ]

    def forward(b):
        def step(t, carry):
            units = pl.ds(pl.multiple_of(t * unit, unit), unit)
            gate = mm(rows[b], w_gate[:, units])
            upward = mm(rows[b], w_up[:, units])
            d_hidden = mm_nt(cot[b], w_down[units, :])
            square = gate * gate
            bent = jnp.tanh(root * gate * (1.0 + cubic * square))
            half = 0.5 * (1.0 + bent)
            act = gate * half
            slope = half + 0.5 * gate * (1.0 - bent * bent) * root * (1.0 + 3.0 * cubic * square)
            hid[b, :, units] = (act * upward).astype(BF)
            dg[b, :, units] = (d_hidden * upward * slope).astype(BF)
            du[b, :, units] = (d_hidden * act).astype(BF)
            return carry

        lax.fori_loop(0, hid.shape[2] // unit, step, 0)
        for copy in results(b):
            copy.start()

    def backward(b):
        s, other = b // 2, b % 2
        if not other:
            core_copy(s).wait_recv()

        def step(t, carry):
            at = pl.ds(pl.multiple_of(t * tile, tile), tile)
            value = mm_nt(dg[b], w_gate[at, :]) + mm_nt(du[b], w_up[at, :])
            if other:
                to_core[s, t] = value.astype(BF)
                return carry
            value = value + in_core[s, t].astype(F32)
            if s:
                to_x[s, t] = value.astype(BF)
                x_copy(s, t).start()
            else:
                total[t] = value
            return carry

        lax.fori_loop(0, tiles, step, 0)
        if other:
            core_copy(s).start()

    def part_copy(b):
        return pltpu.make_async_copy(part_stage.at[b % 2], part_out.at[b], stage_sem.at[b % 2])

    def branch(b):
        if b >= 2:
            part_copy(b - 2).wait()

        def step(t, carry):
            at = pl.ds(pl.multiple_of(t * tile, tile), tile)
            part_stage[b % 2, :, at] = mm(hid[b], w_down[:, at]).astype(BF)
            return carry

        lax.fori_loop(0, tiles, step, 0)
        part_copy(b).start()

    depth = down_stage.shape[1]
    strips = hidden_units // depth

    def down_copy(t, slot):
        to = pl.ds(pl.multiple_of(t * depth, depth), depth)
        return pltpu.make_async_copy(down_stage.at[slot], down_out.at[to, :], stage_sem.at[2 + slot])

    def down_step(t, carry):
        slot = t % 2

        @pl.when(t >= 2)
        def _():
            down_copy(t - 2, slot).wait()

        units = pl.ds(pl.multiple_of(t * depth, depth), depth)
        value = mm_tn(hid[0, :, units], cot[0])
        for b in range(1, ranks):
            value = value + mm_tn(hid[b, :, units], cot[b])
        down_stage[slot] = value.astype(BF)
        down_copy(t, slot).start()
        return carry

    gather(1).start()
    for s in range(1, size_x):
        gather(2 * s).start()
    for copy in loads:
        copy.wait()
    forward(0)
    gather(1).wait_recv()
    forward(1)
    backward(1)
    for s in range(1, size_x):
        gather(2 * s).wait_recv()
        gather(2 * s + 1).start()
        forward(2 * s)
        gather(2 * s + 1).wait_recv()
        forward(2 * s + 1)
        backward(2 * s + 1)
        backward(2 * s)
    backward(0)
    lax.fori_loop(0, strips, down_step, 0)
    for b in range(ranks):
        branch(b)
    for s in range(1, size_x):
        for t in range(tiles):
            x_copy(s, t).wait()
    for t in range(tiles):
        value = total[t]
        for s in range(1, size_x):
            value = value + in_x[s, t].astype(F32)
        grad_ref[:, t * tile : (t + 1) * tile] = value
    for b in range(1, ranks):
        gather(b).wait_send()
    for s in range(size_x):
        core_copy(s).wait_send()
    for b in range(ranks):
        for copy in results(b):
            copy.wait()
    part_copy(ranks - 2).wait()
    part_copy(ranks - 1).wait()
    down_copy(strips - 2, (strips - 2) % 2).wait()
    down_copy(strips - 1, (strips - 1) % 2).wait()


def feed_forward(sizes, normed, cot, cot_rows, w_gate, w_up, down_weight):
    ranks = 2 * sizes[2]
    size_x = sizes[2]
    tok, width = normed.shape
    units = w_gate.shape[1]
    tile = 512
    tiles = width // tile
    sem = pltpu.SemaphoreType.DMA
    hbm = pl.BlockSpec(memory_space=pl.ANY)
    return pl.pallas_call(
        functools.partial(mlp_kernel, sizes),
        in_specs=[hbm] * 6,
        out_specs=[pl.BlockSpec(memory_space=pltpu.VMEM)] + [hbm] * 5,
        out_shape=[
            jax.ShapeDtypeStruct((tok, width), F32),
            jax.ShapeDtypeStruct((ranks * tok, width), BF),
            jax.ShapeDtypeStruct((ranks * tok, units), BF),
            jax.ShapeDtypeStruct((ranks * tok, units), BF),
            jax.ShapeDtypeStruct((ranks, tok, width), BF),
            jax.ShapeDtypeStruct((units, width), BF),
        ],
        scratch_shapes=[
            pltpu.VMEM((ranks, tok, width), BF),
            pltpu.VMEM((ranks, tok, width), BF),
            pltpu.VMEM((width, units), BF),
            pltpu.VMEM((width, units), BF),
            pltpu.VMEM((units, width), BF),
            pltpu.VMEM((ranks, tok, units), BF),
            pltpu.VMEM((ranks, tok, units), BF),
            pltpu.VMEM((ranks, tok, units), BF),
            pltpu.VMEM((size_x, tiles, tok, tile), BF),
            pltpu.VMEM((size_x, tiles, tok, tile), BF),
            pltpu.VMEM((size_x, tiles, tok, tile), BF),
            pltpu.VMEM((size_x, tiles, tok, tile), BF),
            pltpu.VMEM((tiles, tok, tile), F32),
            pltpu.VMEM((2, tok, width), BF),
            pltpu.VMEM((2, 256, width), BF),
            sem((6,)),
            sem((ranks,)),
            sem((ranks,)),
            sem((size_x,)),
            sem((size_x,)),
            sem((size_x, tiles)),
            sem((size_x, tiles)),
            sem((3, ranks)),
            sem((4,)),
        ],
        compiler_params=pltpu.CompilerParams(
            collective_id=2, has_side_effects=True, vmem_limit_bytes=62 * 1024 * 1024
        ),
        cost_estimate=pl.CostEstimate(
            flops=14 * ranks * tok * width * units,
            bytes_accessed=60 * 1024 * 1024,
            transcendentals=0,
        ),
        name="feed_forward",
    )(normed, cot, cot_rows, w_gate, w_up, down_weight)


class Job:
    def __init__(self, phase, left, right, rows, cols, by_rank):
        self.phase, self.left, self.right = phase, left, right
        self.rows, self.cols, self.by_rank = rows, cols, by_rank


def grads_kernel(sizes, jobs, *refs):
    size_a, size_b, size_x = sizes
    chips = size_a * size_b
    n_ctx = 2 * chips
    ranks = 2 * size_x
    count = len(jobs)
    ins, refs = refs[:13], refs[13:]
    outs, refs = refs[:count], refs[count:]
    down_out, refs = refs[0], refs[1:]
    dealt, refs = refs[:2], refs[2:]
    gain_out, refs = refs[0], refs[1:]
    held, refs = refs[:8], refs[8:]
    gain_ctx, gain_x, resid_in, part_own, part_core, part_x, refs = *refs[:6], refs[6:]
    recv, refs = refs[:count], refs[count:]
    send, refs = refs[:count], refs[count:]
    done, refs = refs[:count], refs[count:]
    load_sem, group_send, group_recv, deal_send, deal_recv, part_sem = refs[:6]
    gain_send, gain_recv, send_sem, recv_sem, done_send, done_recv, own_sem = refs[6:]
    ia, ib, ic, ix = (lax.axis_index(name) for name in ALL)
    own = (ia * size_b + ib) * 2 + ic
    rank = ix * 2 + ic
    place = snake_place(ia, ib, size_a, size_b)

    def on_ring(step):
        return snake((place + 2 * chips + step) % chips, size_a, size_b)

    def member(k):
        return (ic + k) % 2, (ix + k // 2) % size_x

    def ctx_device(k):
        e = (own + k) % n_ctx
        return e // 2 // size_b, e // 2 % size_b, e % 2, ix

    kept = rank * chips + kept_slot(ia, ib, size_a, size_b)
    kept_chip = kept // ranks
    kept_id = (kept_chip // size_b, kept_chip % size_b, (kept // size_x) % 2, kept % size_x)
    flat = own * size_x + ix
    from_rank = flat // chips
    from_slot = flat % chips
    half = chips // 2
    from_id = (
        (from_slot % half) // (size_b // 2),
        ((from_slot % half) % (size_b // 2)) * 2 + 1 - from_slot // half,
        from_rank % 2,
        from_rank // 2,
    )

    def remote(src, dst, sent, came, device):
        return pltpu.make_async_remote_copy(
            src_ref=src,
            dst_ref=dst,
            send_sem=sent,
            recv_sem=came,
            device_id=device,
            device_id_type=MESH,
        )

    loads = [pltpu.make_async_copy(ins[i], held[i], load_sem.at[i]) for i in range(3)]
    for copy in loads:
        copy.start()

    barrier = pltpu.get_barrier_semaphore()
    greeted = [ctx_device(k) for k in range(1, n_ctx)] + [from_id]
    greeted += [(ia, ib) + member(k) for k in range(2, ranks)]
    for device in greeted:
        pl.semaphore_signal(barrier, inc=1, device_id=device, device_id_type=MESH)
    pl.semaphore_wait(barrier, len(greeted))

    passed_on = (3, 5)

    def group_copy(i, k):
        c, x = member(k)
        src, dst = ins[i], held[i].at[k]
        target = x * 2 + c
        if i == 4:
            rows = held[i].shape[1]
            src = src.at[pl.ds(pl.multiple_of(target * rows, rows), rows), :]
        if i == 6:
            cols = held[i].shape[2]
            src = src.at[:, pl.ds(pl.multiple_of(target * cols, cols), cols)]
        if k == 0:
            return pltpu.make_async_copy(src, dst, load_sem.at[i])
        if k % 2 and k > 1 and i in passed_on:
            src, x = held[i].at[k - 1], ix
        return remote(src, dst, group_send.at[i, k], group_recv.at[i, k], (ia, ib, c, x))

    def deal_copy(t, k):
        e = (own + k) % n_ctx
        source = part_own.at[0] if t == 0 else ins[9]
        rows = source.shape[0] // n_ctx
        src = source.at[pl.ds(pl.multiple_of(e * rows, rows), rows), :]
        dst = dealt[t].at[pl.ds(pl.multiple_of(own * rows, rows), rows), :]
        if k == 0:
            return pltpu.make_async_copy(src, dst, load_sem.at[8 + t])
        return remote(src, dst, deal_send.at[t, k], deal_recv.at[t, k], ctx_device(k))

    def part_load(step):
        return pltpu.make_async_copy(ins[8].at[2 * step], part_own.at[step], part_sem.at[step])

    def part_core_copy(step):
        device = (ia, ib, 1 - ic, ix)
        src, dst = ins[8].at[2 * step + 1], part_core.at[step]
        return remote(src, dst, group_send.at[0, step], group_recv.at[0, step], device)

    def part_x_copy(step):
        device = (ia, ib, ic, (ix + size_x - step) % size_x)
        src, dst = part_own.at[step], part_x.at[step - 1]
        return remote(src, dst, group_send.at[1, step], group_recv.at[1, step], device)

    down_copy = remote(ins[12], down_out, done_send.at[count, 0], done_recv.at[count, 0], kept_id)
    resid_copy = pltpu.make_async_copy(ins[11], resid_in, load_sem.at[11])

    def gain_copy(k):
        src, dst = ins[10].at[(own + k) % n_ctx], gain_ctx.at[k]
        if k == 0:
            return pltpu.make_async_copy(src, dst, load_sem.at[10])
        return remote(src, dst, deal_send.at[2, k], deal_recv.at[2, k], ctx_device(k))

    def gain_copy_x(s):
        device = (ia, ib, ic, (ix + s) % size_x)
        return remote(gain_x.at[0], gain_x.at[s], gain_send.at[s], gain_recv.at[s], device)

    def ring_copy(j, way, step, parity):
        neighbour = on_ring(1 - 2 * way) + (ic, ix)
        return remote(
            send[j].at[way, parity],
            recv[j].at[way, step],
            send_sem.at[j, way, parity],
            recv_sem.at[j, way, step],
            neighbour,
        )

    def product(j, way, step):
        job = jobs[j]
        a, b = on_ring(step * (2 * way - 1))
        part = job.rows // chips
        cols = slice(way * job.cols // 2, (way + 1) * job.cols // 2)
        left, right = held[job.left], held[job.right]
        if job.phase == 0:
            start = pl.multiple_of((a * size_b + b) * part, part)
            return mm_tn(left[:, pl.ds(start, part)], right[:, cols])
        if job.by_rank:
            start = kept_slot(a, b, size_a, size_b) * part
            if left.shape[1] != job.rows:
                start = start + rank * job.rows
        else:
            start = (a * size_b + b) * part
        rows = pl.ds(pl.multiple_of(start, part), part)
        total = mm(left[0, rows, :], right[0, :, cols])
        for k in range(1, ranks):
            total = total + mm(left[k, rows, :], right[k, :, cols])
        return total

    def deliver(j):
        job = jobs[j]
        if job.by_rank:
            return [remote(done[j], outs[j], done_send.at[j, 0], done_recv.at[j, 0], kept_id)]
        part = job.rows // (chips * ranks)
        copies = []
        for k in range(ranks):
            c, x = member(k)
            start = pl.multiple_of((c * size_x + x) * part, part)
            src, dst = done[j].at[pl.ds(start, part), :], outs[j].at[rank]
            if k == 0:
                copies.append(pltpu.make_async_copy(src, dst, own_sem.at[j]))
            else:
                copies.append(
                    remote(src, dst, done_send.at[j, k], done_recv.at[j, k], (ia, ib, c, x))
                )
        return copies

    def begin(j):
        for way in range(2):
            send[j][way, 0] = product(j, way, 1).astype(BF)
            ring_copy(j, way, 0, 0).start()

    def advance(j, step):
        parity = step % 2
        for way in range(2):
            part = product(j, way, step + 1)
            ring_copy(j, way, step - 1, 1 - parity).wait_recv()
            part = part + recv[j][way, step - 1].astype(F32)

            @pl.when(step >= 2)
            def _():
                ring_copy(j, way, step - 2, parity).wait_send()

            send[j][way, parity] = part.astype(BF)
            ring_copy(j, way, step, parity).start()

    last = chips - 2

    def finish(j):
        cols = jobs[j].cols // 2
        for way in range(2):
            part = product(j, way, chips)
            ring_copy(j, way, last, last % 2).wait_recv()
            part = part + recv[j][way, last].astype(F32)
            done[j][:, way * cols : (way + 1) * cols] = part.astype(BF)
        for copy in deliver(j):
            copy.start()
        for way in range(2):
            ring_copy(j, way, last - 1, (last - 1) % 2).wait_send()
            ring_copy(j, way, last, last % 2).wait_send()

    early = [j for j in range(count) if jobs[j].phase == 0]
    late = [j for j in range(count) if jobs[j].phase == 1]
    lag = 3

    def early_step(step, carry):
        for j in early:
            advance(j, step)
        return carry

    def both_step(step, carry):
        for j in late:
            advance(j, step - lag)
        for j in early:
            advance(j, step)
        return carry

    def late_step(step, carry):
        for j in late:
            advance(j, step)
        return carry

    for copy in loads:
        copy.wait()
    for j in early:
        begin(j)
    for step in range(size_x):
        part_load(step).start()
        part_core_copy(step).start()
    for i in (6, 7, 5, 4, 3):
        for k in range(ranks):
            if not (k % 2 and k > 1 and i in passed_on):
                group_copy(i, k).start()
    resid_copy.start()
    for k in range(n_ctx):
        gain_copy(k).start()
    for k in range(n_ctx):
        deal_copy(1, k).start()
    down_copy.start()
    lax.fori_loop(1, 2, early_step, 0)
    for step in range(size_x):
        part_load(step).wait()
        part_core_copy(step).wait()
    for step in range(1, size_x):
        summed = part_own[step].astype(F32) + part_core[step].astype(F32)
        part_own[step] = summed.astype(BF)
        part_x_copy(step).start()
    lax.fori_loop(2, lag, early_step, 0)
    for i in reversed(passed_on):
        for k in range(2, ranks, 2):
            group_copy(i, k).wait_recv()
            group_copy(i, k + 1).start()
    for k in range(n_ctx):
        gain_copy(k).wait()
    gain_x[0] = jnp.sum(gain_ctx[...], axis=0)
    for s in range(1, size_x):
        gain_copy_x(s).start()
    lax.fori_loop(lag, lag + 1, early_step, 0)
    for i in range(3, 8):
        for k in range(ranks):
            if k and k % 2 == 0 and i in passed_on:
                group_copy(i, k).wait_send()
            else:
                group_copy(i, k).wait()
    for j in late:
        begin(j)
    resid_copy.wait()
    summed = resid_in[...] + part_own[0].astype(F32) + part_core[0].astype(F32)
    for step in range(1, size_x):
        part_x_copy(step).wait()
        summed = summed + part_x[step - 1].astype(F32)
    part_own[0] = summed.astype(BF)
    for k in range(n_ctx):
        deal_copy(0, k).start()
    lax.fori_loop(lag + 1, last + 1, both_step, 0)
    for j in early:
        finish(j)
    lax.fori_loop(last + 1 - lag, last + 1, late_step, 0)
    for j in late:
        finish(j)
    for s in range(1, size_x):
        gain_copy_x(s).wait()
    gain_out[...] = jnp.sum(gain_x[...], axis=0)
    for t in range(2):
        for k in range(n_ctx):
            deal_copy(t, k).wait()
    down_copy.wait()
    for j in range(count):
        for copy in deliver(j):
            copy.wait()


def sum_grads(sizes, ins):
    size_a, size_b, size_x = sizes
    chips = size_a * size_b
    ranks = 2 * size_x
    normed_mlp, d_gate, d_upward = ins[:3]
    width = normed_mlp.shape[1]
    tok = ins[5].shape[0]
    part_width = width // ranks
    jobs = [
        Job(0, 0, 1, width, d_gate.shape[1], False),
        Job(0, 0, 2, width, d_upward.shape[1], False),
        Job(1, 3, 6, width, part_width, False),
        Job(1, 4, 5, part_width, width, True),
        Job(1, 3, 7, part_width, 2 * HD, True),
    ]
    held = [pltpu.VMEM(a.shape, BF) for a in ins[:3]]
    held += [
        pltpu.VMEM((ranks,) + shape, BF)
        for shape in (
            (width, tok),
            (part_width, tok),
            (tok, width),
            (tok, part_width),
            (tok, 2 * HD),
        )
    ]
    outs, recv, send, done = [], [], [], []
    flops = 0
    for job in jobs:
        part = job.rows // chips
        if job.by_rank:
            outs.append(jax.ShapeDtypeStruct((part, job.cols), BF))
        else:
            outs.append(jax.ShapeDtypeStruct((ranks, part // ranks, job.cols), BF))
        recv.append(pltpu.VMEM((2, chips - 1, part, job.cols // 2), BF))
        send.append(pltpu.VMEM((2, 2, part, job.cols // 2), BF))
        done.append(pltpu.VMEM((part, job.cols), BF))
        flops += 2 * job.rows * job.cols * normed_mlp.shape[0]
    count = len(jobs)
    outs.append(jax.ShapeDtypeStruct(ins[12].shape, BF))
    outs += [jax.ShapeDtypeStruct((tok, width), BF)] * 2
    gain_shape = ins[10].shape[1:]
    outs.append(jax.ShapeDtypeStruct(gain_shape, F32))
    sem = pltpu.SemaphoreType.DMA
    return pl.pallas_call(
        functools.partial(grads_kernel, sizes, jobs),
        in_specs=[pl.BlockSpec(memory_space=pl.ANY)] * len(ins),
        out_specs=[pl.BlockSpec(memory_space=pl.ANY)] * (count + 3)
        + [pl.BlockSpec(memory_space=pltpu.VMEM)],
        out_shape=outs,
        scratch_shapes=held
        + [
            pltpu.VMEM((2 * chips,) + gain_shape, F32),
            pltpu.VMEM((size_x,) + gain_shape, F32),
            pltpu.VMEM((tok, width), F32),
            pltpu.VMEM((size_x, tok, width), BF),
            pltpu.VMEM((size_x, tok, width), BF),
            pltpu.VMEM((size_x - 1, tok, width), BF),
        ]
        + recv
        + send
        + done
        + [
            sem((len(ins),)),
            sem((8, ranks)),
            sem((8, ranks)),
            sem((3, 2 * chips)),
            sem((3, 2 * chips)),
            sem((size_x,)),
            sem((size_x,)),
            sem((size_x,)),
            sem((count, 2, 2)),
            sem((count, 2, chips - 1)),
            sem((count + 1, ranks)),
            sem((count + 1, ranks)),
            sem((count,)),
        ],
        compiler_params=pltpu.CompilerParams(
            collective_id=0, has_side_effects=True, vmem_limit_bytes=63 * 1024 * 1024
        ),
        cost_estimate=pl.CostEstimate(
            flops=flops, bytes_accessed=400 * 1024 * 1024, transcendentals=0
        ),
        name="sum_grads",
    )(*ins)


def norm_stats(values):
    inv = lax.rsqrt(jnp.mean(values * values, axis=-1, keepdims=True) + epsilon)
    return values * inv, inv


def norm_back(unit, inv, gain, grad):
    scaled = grad * gain
    inner = jnp.mean(scaled * unit, axis=-1, keepdims=True)
    return inv * (scaled - unit * inner), jnp.sum(grad * unit, axis=0)


def on_device(
    sizes,
    tokens,
    lengths,
    dealing,
    attn_gain,
    query_weight,
    kv_weight,
    out_weight,
    mlp_gain,
    gate_weight,
    up_weight,
    down_weight,
    cotangent,
):
    size_a, size_b, size_x = sizes
    chips = size_a * size_b
    n_ctx = chips * 2
    ranks = 2 * size_x
    ia, ib, ic, ix = (lax.axis_index(name) for name in ALL)
    chip = ia * size_b + ib
    own = chip * 2 + ic
    flat = own * size_x + ix
    rank = ix * 2 + ic
    tok = tokens.shape[1]
    width = tokens.shape[2]
    piece = tok // n_ctx
    halo = WINDOW // tok

    def pick(array, index, axis=0):
        return lax.dynamic_index_in_dim(array, index, axis, keepdims=False)

    own_deal = pick(dealing[0], own)
    deal = (own_deal[:, None] == jnp.arange(tok, dtype=jnp.int32)[None, :]).astype(BF)

    gains = jnp.stack([attn_gain, mlp_gain]).reshape(-1, 128)
    stream = own * tok + jnp.arange(tok, dtype=jnp.int32)
    ends = jnp.cumsum(lengths[0])
    starts = jnp.max(jnp.where(stream[:, None] >= ends[None, :], ends[None, :], 0), axis=1)
    low = jnp.maximum(starts, stream - (WINDOW - 1)) - (own * tok - WINDOW)
    low = low.astype(jnp.int32)[None, :]
    inputs_low, cot, w_query, w_kv, w_out, w_gate, w_up, gains, *attended = fetch(
        sizes,
        [mm(deal, tokens[0]).astype(BF), mm(deal, cotangent[0]).astype(BF)],
        [query_weight, kv_weight, out_weight],
        [gate_weight, up_weight],
        gains,
        low,
    )
    normed, queries, window, context, lse, cot_rows = attended
    gains = gains.reshape(size_x, 2, -1).astype(F32)
    gain_one = gains[:, 0].reshape(-1)
    gain_two = gains[:, 1].reshape(-1)


    inputs = inputs_low.astype(F32)
    unit_one, inv_one = norm_stats(inputs)
    resid = inputs + mm(context, w_out)

    unit_two, inv_two = norm_stats(resid)
    d_normed_mlp, mlp_rows, d_gate, d_upward, mlp_parts, down_grad = feed_forward(
        sizes, (unit_two * gain_two).astype(BF), cot, cot_rows, w_gate, w_up, down_weight
    )
    d_resid_part, mlp_gain_grad = norm_back(unit_two, inv_two, gain_two, d_normed_mlp)
    d_resid = cot.astype(F32) + d_resid_part
    d_branch = d_resid.astype(BF)

    d_queries, d_pairs, down_sum, d_normed = attend_back(
        sizes, queries, window, low, d_branch, lse, down_grad, w_out, w_query, w_kv
    )
    d_inputs, attn_gain_grad = norm_back(unit_one, inv_one, gain_one, d_normed)
    gain_part = width // (n_ctx * size_x)
    gain_grads = jnp.stack([attn_gain_grad, mlp_gain_grad]).reshape(2, n_ctx, size_x, gain_part)
    gain_grads = gain_grads.transpose(1, 2, 0, 3).reshape(n_ctx, -1)
    gain_grads = jnp.pad(gain_grads, ((0, 0), (0, 1024 - gain_grads.shape[1])))
    sums = sum_grads(
        sizes,
        [
            mlp_rows,
            d_gate,
            d_upward,
            normed.T,
            context.T,
            d_branch,
            d_queries,
            d_pairs,
            mlp_parts,
            (d_resid + d_inputs).astype(BF),
            gain_grads.reshape(n_ctx, 8, 128),
            resid,
            down_sum,
        ],
    )
    gate_grad, up_grad, query_grad = (
        v.transpose(1, 0, 2).reshape(v.shape[1], -1).astype(F32) for v in sums[:3]
    )
    out_grad, kv_grad, down_grad = (v.astype(F32) for v in sums[3:6])
    block_output = mm_tn(deal, sums[6]).astype(BF)
    token_grad = mm_tn(deal, sums[7])
    gain_grads = lax.dynamic_slice(sums[8].reshape(-1), (ix * 2 * gain_part,), (2 * gain_part,))
    attn_gain_grad, mlp_gain_grad = gain_grads[:gain_part], gain_grads[gain_part:]
    return (
        block_output[None],
        token_grad[None],
        attn_gain_grad,
        query_grad,
        kv_grad,
        out_grad,
        mlp_gain_grad,
        gate_grad,
        up_grad,
        down_grad,
    )


def solution(mesh):
    n_ctx, size_x = mesh.shape["ctx"], mesh.shape["fsdp"]
    chips = n_ctx // 2
    size_a = 4 if chips % 4 == 0 else chips
    size_b = chips // size_a
    fine = Mesh(mesh.devices.reshape(size_a, size_b, 2, size_x), ALL)
    rows = P("x", CTX, None)
    split = P("x", None)
    every = P(ALL)
    matrix = P(ALL, None)
    return jax.shard_map(
        functools.partial(on_device, (size_a, size_b, size_x)),
        mesh=fine,
        in_specs=(
            rows,
            split,
            P("x", None, None),
            P("x"),
            split,
            split,
            split,
            P("x"),
            split,
            split,
            split,
            rows,
        ),
        out_specs=(rows, rows, every, matrix, matrix, matrix, every, matrix, matrix, matrix),
        check_vma=False,
    )
```

```python
import functools

import jax
import jax.numpy as jnp
import numpy as np
from jax import lax
from jax.experimental import pallas as pl
from jax.experimental.pallas import tpu as pltpu
from jax.sharding import Mesh
from jax.sharding import PartitionSpec as P

H = 16
HD = 128
WINDOW = 1024
QBLK = 128
HEADS_STEP = 4
SPAN = WINDOW + QBLK
ROWS = HEADS_STEP * QBLK

epsilon = 1e-06
neg_large = -1e30
scale = HD ** (-0.5)
root = (2.0 / np.pi) ** 0.5
cubic = 0.044715
BF = jnp.bfloat16
F32 = jnp.float32
CTX = ("a", "b", "c")
ALL = ("a", "b", "c", "x")
MESH = pl.DeviceIdType.MESH


def mm(left, right):
    return jnp.dot(left, right, preferred_element_type=F32)


def mm_tn(left, right):
    return lax.dot_general(left, right, (((0,), (0,)), ((), ())), preferred_element_type=F32)


def mm_nt(left, right):
    return lax.dot_general(left, right, (((1,), (1,)), ((), ())), preferred_element_type=F32)


def stack_heads(block):
    return jnp.concatenate([block[:, h * HD : (h + 1) * HD] for h in range(HEADS_STEP)], 0)


def unstack_heads(block_t):
    return jnp.concatenate(
        [block_t[:, h * QBLK : (h + 1) * QBLK].T for h in range(HEADS_STEP)], 1
    )


def bias_of(lo, qb):
    key = lax.broadcasted_iota(jnp.int32, (SPAN, QBLK), 0) + qb * QBLK
    query = lax.broadcasted_iota(jnp.int32, (SPAN, QBLK), 1) + (WINDOW + qb * QBLK)
    allowed = (key >= lo) & (key <= query)
    bias = jnp.where(allowed, 0.0, neg_large).astype(F32)
    return jnp.concatenate([bias] * HEADS_STEP, 1)


def attend_block(bias, queries, keys, values):
    scores = mm_nt(keys, queries) * scale + bias
    top = jnp.max(scores, axis=0, keepdims=True)
    raised = jnp.exp(scores - top)
    total = jnp.sum(raised, axis=0, keepdims=True)
    return mm_tn(values, raised.astype(BF)) * (1.0 / total), top + jnp.log(total)


def snake(pos, size_a, size_b):
    if size_b == 1:
        return pos, pos * 0
    down = pos // size_a
    first = 1 - (down + 7) // 8
    q = (pos - size_a) * (1 - first)
    a_up = size_a - 1 - q // (size_b - 1)
    k = q % (size_b - 1)
    odd = a_up % 2
    b_up = odd * (1 + k) + (1 - odd) * (size_b - 1 - k)
    return first * pos + (1 - first) * a_up, (1 - first) * b_up


def snake_place(a, b, size_a, size_b):
    if size_b == 1:
        return a
    moved = (b + size_b - 1) // size_b
    odd = a % 2
    along = odd * (b - 1) + (1 - odd) * (size_b - 1 - b)
    return (1 - moved) * a + moved * (size_a + (size_a - 1 - a) * (size_b - 1) + along)


def kept_slot(a, b, size_a, size_b):
    half = size_a * size_b // 2
    return (1 - b % 2) * half + a * (size_b // 2) + b // 2


def back_kernel(sizes, low_ref, q_ref, kv_ref, branch_ref, lse_ref, down_in, *refs):
    size_a, size_b, size_x = sizes
    weights_in, refs = refs[:3], refs[3:]
    dq_ref, pairs_ref, sum_ref, normed_ref, refs = *refs[:4], refs[4:]
    w_out, w_query, w_kv, do_ref, refs = *refs[:4], refs[4:]
    dkv, down, recv, send, halo_out, halo_in = refs[:6]
    load_sem, send_sem, recv_sem, halo_send, halo_recv = refs[6:]
    chips = size_a * size_b
    n_ctx = chips * 2
    ia, ib, ic, ix = (lax.axis_index(name) for name in ALL)
    own = (ia * size_b + ib) * 2 + ic
    place = snake_place(ia, ib, size_a, size_b)
    tok = q_ref.shape[0]
    halo = WINDOW // tok
    groups = H // HEADS_STEP
    blocks = tok // QBLK * groups
    part = down.shape[0] // chips
    quarter = down.shape[1] // 4
    chains = [(way, sub) for way in range(2) for sub in range(2)]
    last = chips - 2

    loading = pltpu.make_async_copy(down_in, down, load_sem.at[0])
    loading.start()
    weights = [
        pltpu.make_async_copy(src, dst, load_sem.at[1 + n])
        for n, (src, dst) in enumerate(zip(weights_in, (w_out, w_query, w_kv)))
    ]
    for copy in weights:
        copy.start()
    dkv[...] = jnp.zeros_like(dkv)

    def on_ring(step):
        return snake((place + 2 * chips + step) % chips, size_a, size_b)

    def ctx_device(step):
        e = (own + n_ctx + step) % n_ctx
        return e // 2 // size_b, e // 2 % size_b, e % 2, ix

    barrier = pltpu.get_barrier_semaphore()
    for k in range(1, n_ctx):
        pl.semaphore_signal(barrier, inc=1, device_id=ctx_device(k), device_id_type=MESH)
    pl.semaphore_wait(barrier, n_ctx - 1)

    def remote(src, dst, sent, came, device):
        return pltpu.make_async_remote_copy(
            src_ref=src,
            dst_ref=dst,
            send_sem=sent,
            recv_sem=came,
            device_id=device,
            device_id_type=MESH,
        )

    def ring_copy(way, sub, step, parity):
        return remote(
            send.at[way, sub, parity],
            recv.at[way, sub, step],
            send_sem.at[way, sub, parity],
            recv_sem.at[way, sub, step],
            on_ring(1 - 2 * way) + (ic, ix),
        )

    def columns(way, sub):
        return slice((2 * way + sub) * quarter, (2 * way + sub + 1) * quarter)

    def chunk(way, sub, step):
        a, b = on_ring(step * (2 * way - 1))
        rows = pl.ds(pl.multiple_of(kept_slot(a, b, size_a, size_b) * part, part), part)
        return down[rows, columns(way, sub)]

    def advance(step):
        parity = step % 2
        for way, sub in chains:
            value = chunk(way, sub, step + 1).astype(F32)
            ring_copy(way, sub, step - 1, 1 - parity).wait_recv()
            value = value + recv[way, sub, step - 1].astype(F32)

            @pl.when(step >= 2)
            def _():
                ring_copy(way, sub, step - 2, parity).wait_send()

            send[way, sub, parity] = value.astype(BF)
            ring_copy(way, sub, step, parity).start()

    def attend_step(t):
        qb, hg = t // groups, t % groups
        width = HEADS_STEP * HD
        block = pl.ds(pl.multiple_of(qb * QBLK, QBLK), QBLK)
        cols = pl.ds(pl.multiple_of(hg * width, width), width)
        rows = pl.ds(pl.multiple_of(qb * QBLK, QBLK), SPAN)
        keys = kv_ref[rows, :HD]
        values = kv_ref[rows, HD:]
        queries = stack_heads(q_ref[block, cols])
        d_out = stack_heads(do_ref[block, cols])
        scores = mm_nt(keys, queries) * scale + bias_of(low_ref[qb], qb)
        probs = jnp.exp(scores - lse_ref[t])
        d_probs = mm_nt(values, d_out)
        delta = jnp.sum(probs * d_probs, axis=0, keepdims=True)
        d_scores = (probs * (d_probs - delta)).astype(BF)
        dq_ref[block, cols] = unstack_heads(mm_tn(keys, d_scores) * scale).astype(BF)
        dkv[rows, :HD] += mm(d_scores, queries) * scale
        dkv[rows, HD:] += mm(probs.astype(BF), d_out)

    def halo_copy(k):
        sems = (halo_send.at[k - 1], halo_recv.at[k - 1])
        return remote(halo_out.at[k - 1], halo_in.at[k - 1], *sems, ctx_device(-k))

    def both(step, carry):
        advance(step)
        attend_step(2 * step - 2)
        attend_step(2 * step - 1)
        return carry

    def alone(step, carry):
        advance(step)
        return carry

    tile = 512

    def context_step(t, carry):
        at = pl.ds(pl.multiple_of(t * tile, tile), tile)
        do_ref[:, at] = mm_nt(branch_ref[...], w_out[at, :]).astype(BF)
        return carry

    def normed_step(t, carry):
        at = pl.ds(pl.multiple_of(t * tile, tile), tile)
        normed_ref[:, at] = mm_nt(dq_ref[...], w_query[at, :]) + mm_nt(pairs_ref[...], w_kv[at, :])
        return carry

    loading.wait()
    for way, sub in chains:
        send[way, sub, 0] = chunk(way, sub, 1)
        ring_copy(way, sub, 0, 0).start()
    weights[0].wait()
    lax.fori_loop(0, w_out.shape[0] // tile, context_step, 0)
    busy = blocks // 2
    lax.fori_loop(1, busy + 1, both, 0)
    for k in range(1, halo + 1):

        @pl.when(own >= k)
        def _():
            halo_out[k - 1] = dkv[(halo - k) * tok : (halo - k + 1) * tok, :].astype(BF)
            halo_copy(k).start()

    lax.fori_loop(busy + 1, busy + 2, alone, 0)
    for k in range(1, halo + 1):

        @pl.when(own + k < n_ctx)
        def _():
            halo_copy(k).wait_recv()
            dkv[WINDOW:, :] += halo_in[k - 1].astype(F32)

    pairs_ref[...] = dkv[WINDOW:, :].astype(BF)
    for copy in weights[1:]:
        copy.wait()
    lax.fori_loop(0, w_query.shape[0] // tile, normed_step, 0)
    lax.fori_loop(busy + 2, last + 1, alone, 0)
    for way, sub in chains:
        value = chunk(way, sub, chips).astype(F32)
        ring_copy(way, sub, last, last % 2).wait_recv()
        value = value + recv[way, sub, last].astype(F32)
        sum_ref[:, columns(way, sub)] = value.astype(BF)
    for way, sub in chains:
        ring_copy(way, sub, last - 1, (last - 1) % 2).wait_send()
        ring_copy(way, sub, last, last % 2).wait_send()
    for k in range(1, halo + 1):

        @pl.when(own >= k)
        def _():
            halo_copy(k).wait_send()


def attend_back(sizes, queries, window, low, d_branch, lse, down, w_out, w_query, w_kv):
    chips = sizes[0] * sizes[1]
    tok = queries.shape[0]
    halo = WINDOW // tok
    part, width = down.shape[0] // chips, down.shape[1]
    sem = pltpu.SemaphoreType.DMA
    vmem = pl.BlockSpec(memory_space=pltpu.VMEM)
    return pl.pallas_call(
        functools.partial(back_kernel, sizes),
        in_specs=[vmem] * 5 + [pl.BlockSpec(memory_space=pl.ANY)] * 4,
        out_specs=[vmem] * 4,
        out_shape=[
            jax.ShapeDtypeStruct((tok, H * HD), BF),
            jax.ShapeDtypeStruct((tok, 2 * HD), BF),
            jax.ShapeDtypeStruct((part, width), BF),
            jax.ShapeDtypeStruct((tok, width), F32),
        ],
        scratch_shapes=[
            pltpu.VMEM(w_out.shape, BF),
            pltpu.VMEM(w_query.shape, BF),
            pltpu.VMEM(w_kv.shape, BF),
            pltpu.VMEM((tok, H * HD), BF),
            pltpu.VMEM((WINDOW + tok, 2 * HD), F32),
            pltpu.VMEM(down.shape, BF),
            pltpu.VMEM((2, 2, chips - 1, part, width // 4), BF),
            pltpu.VMEM((2, 2, 2, part, width // 4), BF),
            pltpu.VMEM((halo, tok, 2 * HD), BF),
            pltpu.VMEM((halo, tok, 2 * HD), BF),
            sem((4,)),
            sem((2, 2, 2)),
            sem((2, 2, chips - 1)),
            sem((halo,)),
            sem((halo,)),
        ],
        compiler_params=pltpu.CompilerParams(
            collective_id=3, has_side_effects=True, vmem_limit_bytes=60 * 1024 * 1024
        ),
        cost_estimate=pl.CostEstimate(
            flops=10 * tok * H * HD * SPAN, bytes_accessed=100 * 1024 * 1024, transcendentals=0
        ),
        name="attend_back",
    )(low.reshape(tok // QBLK, 1, QBLK), queries, window, d_branch, lse, down, w_out, w_query, w_kv)


class Piece:
    def __init__(self, at, rows, square, shared, part, parts):
        self.at, self.rows, self.square, self.shared = at, rows, square, shared
        self.part, self.parts = part, parts
        self.relays = [0, 1, 2, 3] if square else []
        if shared:
            self.relays += [4, 5, 6, 7, 8] if square else [4]


def fetch_kernel(sizes, pieces, n_in, n_dealt, *refs):
    size_a, size_b, size_x = sizes
    n_ctx = size_a * size_b * 2
    ins, low_ref, refs = refs[:n_in], refs[n_in], refs[n_in + 1 :]
    outs, refs = refs[:n_in], refs[n_in:]
    normed_ref, query_ref, window_out, context_ref, lse_ref, cot_rows, refs = *refs[:6], refs[6:]
    tok_in, w_query, w_kv, gain_in, window, refs = *refs[:5], refs[5:]
    load_sem, halo_send, halo_recv, cot_send, cot_recv, refs = *refs[:5], refs[5:]
    n_weights = n_in - n_dealt - 1
    stages, refs = refs[:n_weights], refs[n_weights:]
    keep_sem, own_sem, deal_send, deal_recv, gain_send, gain_recv = refs[:6]
    x_send, x_recv, relay_send, relay_recv = refs[6:]
    ia, ib, ic, ix = (lax.axis_index(name) for name in ALL)
    own = (ia * size_b + ib) * 2 + ic
    rank = ix * 2 + ic
    pa, pb = ia % 2, ib % 2
    other_a, other_b = ia + 1 - 2 * pa, ib + 1 - 2 * pb
    corner = pa * 2 + pb
    corner_a, corner_b, corner_d = (1 - pa) * 2 + pb, pa * 2 + 1 - pb, 3 - corner

    barrier = pltpu.get_barrier_semaphore()
    greeted = []
    for k in range(1, n_ctx):
        e = (own + k) % n_ctx
        greeted.append((e // 2 // size_b, e // 2 % size_b, e % 2, ix))
    for s in range(1, size_x):
        greeted.append((ia, ib, ic, (ix + s) % size_x))
    for device in greeted:
        pl.semaphore_signal(barrier, inc=1, device_id=device, device_id_type=MESH)
    pl.semaphore_wait(barrier, len(greeted))

    def remote(src, dst, send, recv, device):
        return pltpu.make_async_remote_copy(
            src_ref=src,
            dst_ref=dst,
            send_sem=send,
            recv_sem=recv,
            device_id=device,
            device_id_type=MESH,
        )

    def x_copy(i, s):
        p = pieces[i]
        shard, full = ins[p.at], outs[p.at]
        target = (ix + s) % size_x
        height = shard.shape[0]
        rows, start = region(p, corner, ic)
        if p.shared:
            src = shard.at[pl.ds(start, rows), :]
        else:
            cols = full.shape[1]
            at = pl.multiple_of((target * 2 + ic) * cols, cols)
            src = shard.at[pl.ds(start, rows), pl.ds(at, cols)]
        dst = full.at[pl.ds(pl.multiple_of(ix * height + start, rows), rows), :]
        return remote(src, dst, x_send.at[i, s], x_recv.at[i, s], (ia, ib, ic, target))

    def region(p, which, core):
        owner = which if p.square else 0
        owners = 4 if p.square else 1
        if p.shared:
            owner, owners = owner * 2 + core, owners * 2
        rows = p.rows // (owners * p.parts)
        return rows, pl.multiple_of((owner * p.parts + p.part) * rows, rows)

    def landed(i, s, which, core, half=None):
        p = pieces[i]
        rows, start = region(p, which, core)
        start = start + (ix + size_x - s) % size_x * p.rows
        if half is not None:
            rows = rows // 2
            start = start + half * rows
        return outs[p.at].at[pl.ds(pl.multiple_of(start, rows), rows), :]

    def relay(i, s, kind, incoming=False):
        sem = (relay_send.at[i, s, kind], relay_recv.at[i, s, kind])
        if kind < 4:
            device = (other_a, ib, ic, ix) if kind in (1, 2) else (ia, other_b, ic, ix)
            sent = (
                landed(i, s, corner, ic),
                landed(i, s, corner, ic),
                landed(i, s, corner_b, ic, 0),
                landed(i, s, corner_a, ic, 1),
            )[kind]
            came = (
                landed(i, s, corner_b, ic),
                landed(i, s, corner_a, ic),
                landed(i, s, corner_d, ic, 0),
                landed(i, s, corner_d, ic, 1),
            )[kind]
        else:
            device = (ia, ib, 1 - ic, ix)
            which, half = ((corner, None), (corner_b, None), (corner_a, None), (corner_d, 0), (corner_d, 1))[
                kind - 4
            ]
            sent = landed(i, s, which, ic, half)
            came = landed(i, s, which, 1 - ic, half)
        ref = came if incoming else sent
        return remote(ref, ref, *sem, device)

    rows = ins[0].shape[0] // n_ctx

    def deal_copy(t, k):
        e = (own + k) % n_ctx
        src = ins[t].at[pl.ds(pl.multiple_of(e * rows, rows), rows), :]
        dst = outs[t].at[pl.ds(pl.multiple_of(own * rows, rows), rows), :]
        if k == 0:
            return pltpu.make_async_copy(src, dst, own_sem.at[t])
        device = (e // 2 // size_b, e // 2 % size_b, e % 2, ix)
        return remote(src, dst, deal_send.at[t, k], deal_recv.at[t, k], device)

    g = n_in - 1

    def gain_copy(s):
        if s == 0:
            return pltpu.make_async_copy(ins[g], outs[g].at[ix], own_sem.at[g])
        device = (ia, ib, ic, (ix + s) % size_x)
        return remote(ins[g], outs[g].at[ix], gain_send.at[s], gain_recv.at[s], device)

    def keep_copy(w, out):
        shard, full = ins[w], outs[w]
        stage = stages[w - n_dealt]
        height = shard.shape[0]
        sem = keep_sem.at[w, out]
        if out:
            dst = full.at[pl.ds(pl.multiple_of(ix * height, height), height), :]
            return pltpu.make_async_copy(stage, dst, sem)
        src = shard
        if full.shape[1] != shard.shape[1]:
            cols = full.shape[1]
            src = shard.at[:, pl.ds(pl.multiple_of(rank * cols, cols), cols)]
        return pltpu.make_async_copy(src, stage, sem)

    tok = tok_in.shape[0]
    halo = WINDOW // tok
    at_query, at_kv = n_dealt, n_dealt + 1

    def load(src, dst, n):
        copy = pltpu.make_async_copy(src, dst, load_sem.at[n])
        copy.start()
        copy.wait()

    def core_parts_in(i):
        for s in range(1, size_x):
            for kind in pieces[i].relays:
                if kind >= 4:
                    relay(i, s, kind, True).wait_recv()
        keep_copy(pieces[i].at, 1).wait()

    def halo_copy(k):
        e = own + k
        device = (e // 2 // size_b, e // 2 % size_b, e % 2, ix)
        src = window.at[pl.ds(WINDOW, tok), :]
        dst = window.at[pl.ds((halo - k) * tok, tok), :]
        return remote(src, dst, halo_send.at[k - 1], halo_recv.at[k - 1], device)

    def normalise():
        for k in range(n_ctx):
            deal_copy(0, k).wait()
        for s in range(size_x):
            gain_copy(s).wait()
        load(outs[0], tok_in, 0)
        load(outs[g], gain_in, 1)
        gain = []
        for x in range(size_x):
            values = gain_in[x].astype(F32)
            gain += [values[r : r + 1, :] for r in range(values.shape[0] // 2)]
        values = tok_in[...].astype(F32)
        unit, _ = norm_stats(values)
        normed_ref[...] = (unit * jnp.concatenate(gain, 1)).astype(BF)

    def keys_values():
        core_parts_in(1)
        load(outs[at_kv], w_kv, 2)
        window[WINDOW:, :] = mm(normed_ref[...], w_kv[...]).astype(BF)
        for k in range(1, halo + 1):

            @pl.when(own + k < n_ctx)
            def _():
                halo_copy(k).start()

            @pl.when(own < k)
            def _():
                window[(halo - k) * tok : (halo - k + 1) * tok, :] = jnp.zeros((tok, 2 * HD), BF)

    def project():
        core_parts_in(0)
        load(outs[at_query], w_query, 3)

        def step(t, carry):
            cols = pl.ds(pl.multiple_of(t * 512, 512), 512)
            query_ref[:, cols] = mm(normed_ref[...], w_query[:, cols]).astype(BF)
            return carry

        lax.fori_loop(0, H * HD // 512, step, 0)

    def halo_in():
        for k in range(1, halo + 1):

            @pl.when(own >= k)
            def _():
                halo_copy(k).wait_recv()

    def cot_copy(b):
        sems = (cot_send.at[b], cot_recv.at[b])
        if b % 2:
            src = outs[1] if b == 1 else cot_rows.at[b - 2]
            return remote(src, cot_rows.at[b - 1], *sems, (ia, ib, 1 - ic, ix))
        device = (ia, ib, ic, (ix + b // 2) % size_x)
        return remote(outs[1], cot_rows.at[b - 1], *sems, device)

    def spread_cotangent():
        for k in range(n_ctx):
            deal_copy(1, k).wait()
        for s in range(1, size_x):
            cot_copy(2 * s).start()
        cot_copy(1).start()

    def attend(qb):
        low = low_ref[:, qb * QBLK : (qb + 1) * QBLK]
        bias = bias_of(low, qb)
        keys = window[qb * QBLK : qb * QBLK + SPAN, :HD]
        values = window[qb * QBLK : qb * QBLK + SPAN, HD:]
        rows = slice(qb * QBLK, (qb + 1) * QBLK)

        def step(t, carry):
            width = HEADS_STEP * HD
            cols = pl.ds(pl.multiple_of(t * width, width), width)
            out_t, lse = attend_block(bias, stack_heads(query_ref[rows, cols]), keys, values)
            context_ref[rows, cols] = unstack_heads(out_t).astype(BF)
            lse_ref[qb * (H // HEADS_STEP) + t] = lse
            return carry

        lax.fori_loop(0, H // HEADS_STEP, step, 0)

    blocks = tok // QBLK
    tasks = {2 * size_x - 1: [normalise, keys_values], 2 * size_x: [spread_cotangent, project]}
    for qb in range(blocks):
        task = functools.partial(attend, qb)
        tasks[2 * size_x + 1 + qb] = [halo_in, task] if qb == 0 else [task]

    ahead = 4
    order = [(i, s) for i in range(len(pieces)) for s in range(1, size_x)]
    for k in range(n_ctx):
        deal_copy(0, k).start()
    for s in range(size_x):
        gain_copy(s).start()
    for i, s in order[:ahead]:
        x_copy(i, s).start()
    for t in range(1, n_dealt):
        for k in range(n_ctx):
            deal_copy(t, k).start()
    for w in range(n_dealt, n_dealt + n_weights):
        keep_copy(w, 0).start()

    for n in range(len(order) + 2):
        if n < n_weights:
            keep_copy(n_dealt + n, 0).wait()
            keep_copy(n_dealt + n, 1).start()
        if n < len(order):
            i, s = order[n]
            x_copy(i, s).wait_recv()
            for kind in (0, 1, 4):
                if kind in pieces[i].relays:
                    relay(i, s, kind).start()
            if n + ahead < len(order):
                x_copy(i, s).wait_send()
                x_copy(*order[n + ahead]).start()
        if 1 <= n <= len(order) and pieces[order[n - 1][0]].square:
            i, s = order[n - 1]
            relay(i, s, 0, True).wait_recv()
            relay(i, s, 2).start()
            relay(i, s, 1, True).wait_recv()
            relay(i, s, 3).start()
            if pieces[i].shared:
                relay(i, s, 5).start()
                relay(i, s, 6).start()
        if n >= 2 and pieces[order[n - 2][0]].square:
            i, s = order[n - 2]
            relay(i, s, 2, True).wait_recv()
            relay(i, s, 3, True).wait_recv()
            if pieces[i].shared:
                relay(i, s, 7).start()
                relay(i, s, 8).start()
        for task in tasks.get(n, []):
            task()

    for s in range(1, size_x):
        cot_copy(2 * s).wait_recv()
        cot_copy(2 * s + 1).start()
    window_out[...] = window[...]
    for k in range(1, halo + 1):

        @pl.when(own + k < n_ctx)
        def _():
            halo_copy(k).wait_send()

    for n, (i, s) in enumerate(order):
        if n + ahead >= len(order):
            x_copy(i, s).wait_send()
        for kind in pieces[i].relays:
            relay(i, s, kind).wait_send()
            if kind >= 4 and i > 1:
                relay(i, s, kind, True).wait_recv()
    for b in range(1, 2 * size_x):
        cot_copy(b).wait_send()
        if b % 2:
            cot_copy(b).wait_recv()
    for w in range(n_dealt + 2, n_dealt + n_weights):
        keep_copy(w, 1).wait()


def fetch(sizes, dealt, shared, split, gains, low):
    size_a, size_b, size_x = sizes
    n_ctx = size_a * size_b * 2
    ins = dealt + shared + split + [gains]
    outs = [jax.ShapeDtypeStruct(a.shape, BF) for a in dealt]
    outs += [jax.ShapeDtypeStruct((size_x * a.shape[0], a.shape[1]), BF) for a in shared]
    outs += [
        jax.ShapeDtypeStruct((size_x * a.shape[0], a.shape[1] // (2 * size_x)), BF) for a in split
    ]
    outs.append(jax.ShapeDtypeStruct((size_x,) + gains.shape, BF))
    pieces = []
    first = len(dealt)
    pieces.append(Piece(first, shared[0].shape[0], True, True, 0, 1))
    pieces.append(Piece(first + 1, shared[1].shape[0], False, True, 0, 1))
    for part in range(2):
        for n, a in enumerate(split):
            pieces.append(Piece(first + len(shared) + n, a.shape[0], True, False, part, 2))
    pieces.append(Piece(first + 2, shared[2].shape[0], False, True, 0, 1))
    count = len(pieces)
    tok, width = dealt[0].shape
    sem = pltpu.SemaphoreType.DMA
    vmem = pl.BlockSpec(memory_space=pltpu.VMEM)
    return pl.pallas_call(
        functools.partial(fetch_kernel, sizes, pieces, len(ins), len(dealt)),
        in_specs=[pl.BlockSpec(memory_space=pl.ANY)] * len(ins) + [vmem],
        out_specs=[pl.BlockSpec(memory_space=pl.ANY)] * len(outs) + [vmem] * 5 + [pl.BlockSpec(memory_space=pl.ANY)],
        out_shape=outs
        + [
            jax.ShapeDtypeStruct((tok, width), BF),
            jax.ShapeDtypeStruct((tok, H * HD), BF),
            jax.ShapeDtypeStruct((WINDOW + tok, 2 * HD), BF),
            jax.ShapeDtypeStruct((tok, H * HD), BF),
            jax.ShapeDtypeStruct((tok // QBLK * (H // HEADS_STEP), 1, ROWS), F32),
            jax.ShapeDtypeStruct((2 * size_x - 1, tok, width), BF),
        ],
        scratch_shapes=[
            pltpu.VMEM((tok, width), BF),
            pltpu.VMEM((width, H * HD), BF),
            pltpu.VMEM((width, 2 * HD), BF),
            pltpu.VMEM((size_x,) + gains.shape, BF),
            pltpu.VMEM((WINDOW + tok, 2 * HD), BF),
            sem((4,)),
            sem((WINDOW // tok,)),
            sem((WINDOW // tok,)),
            sem((2 * size_x,)),
            sem((2 * size_x,)),
        ]
        + [
            pltpu.VMEM((a.shape[0], o.shape[1]), BF)
            for a, o in zip(ins[len(dealt) : -1], outs[len(dealt) : -1])
        ]
        + [
            sem((len(ins), 2)),
            sem((len(ins),)),
            sem((len(dealt), n_ctx)),
            sem((len(dealt), n_ctx)),
            sem((size_x,)),
            sem((size_x,)),
            sem((count, size_x)),
            sem((count, size_x)),
            sem((count, size_x, 9)),
            sem((count, size_x, 9)),
        ],
        compiler_params=pltpu.CompilerParams(
            collective_id=1, has_side_effects=True, vmem_limit_bytes=60 * 1024 * 1024
        ),
        cost_estimate=pl.CostEstimate(
            flops=0, bytes_accessed=300 * 1024 * 1024, transcendentals=0
        ),
        name="fetch",
    )(*ins, low)


def mlp_kernel(sizes, own_ref, *refs):
    size_a, size_b, size_x = sizes
    ranks = 2 * size_x
    cots_in, refs = refs[:2], refs[2:]
    weights_in, refs = refs[:3], refs[3:]
    grad_ref, rows_out, dg_out, du_out, part_out, down_out, refs = *refs[:6], refs[6:]
    rows, cot, w_gate, w_up, w_down, hid, dg, du = refs[:8]
    to_core, in_core, to_x, in_x, total, part_stage, down_stage = refs[8:15]
    load_sem, ag_send, ag_recv, core_send, core_recv, x_send, x_recv, out_sem, stage_sem = refs[15:]
    ia, ib, ic, ix = (lax.axis_index(name) for name in ALL)
    hidden_units = w_down.shape[0]
    tok, width = own_ref.shape
    tiles, _, tile = total.shape
    unit = hid.shape[2] // (hid.shape[2] // 512 if hid.shape[2] % 512 == 0 else hid.shape[2] // 256)

    loads = [
        pltpu.make_async_copy(own_ref, rows.at[0], load_sem.at[0]),
        pltpu.make_async_copy(weights_in[0], w_gate, load_sem.at[1]),
        pltpu.make_async_copy(weights_in[1], w_up, load_sem.at[2]),
        pltpu.make_async_copy(
            weights_in[2].at[pl.ds(pl.multiple_of(ic * hidden_units, hidden_units), hidden_units), :],
            w_down,
            load_sem.at[3],
        ),
    ]
    loads.append(pltpu.make_async_copy(cots_in[0], cot.at[0], load_sem.at[4]))
    loads.append(pltpu.make_async_copy(cots_in[1], cot.at[pl.ds(1, ranks - 1)], load_sem.at[5]))
    for copy in loads:
        copy.start()

    partner = (ia, ib, 1 - ic, ix)

    def across(step):
        return ia, ib, ic, (ix + size_x + step) % size_x

    barrier = pltpu.get_barrier_semaphore()
    greeted = [partner] + [across(s) for s in range(1, size_x)]
    for device in greeted:
        pl.semaphore_signal(barrier, inc=1, device_id=device, device_id_type=MESH)
    pl.semaphore_wait(barrier, len(greeted))

    def remote(src, dst, sent, came, device):
        return pltpu.make_async_remote_copy(
            src_ref=src,
            dst_ref=dst,
            send_sem=sent,
            recv_sem=came,
            device_id=device,
            device_id_type=MESH,
        )

    def gather(b):
        if b == 1:
            return remote(own_ref, rows.at[1], ag_send.at[1], ag_recv.at[1], partner)
        if b % 2:
            return remote(rows.at[b - 1], rows.at[b], ag_send.at[b], ag_recv.at[b], partner)
        return remote(own_ref, rows.at[b], ag_send.at[b], ag_recv.at[b], across(b // 2))

    def core_copy(s):
        return remote(to_core.at[s], in_core.at[s], core_send.at[s], core_recv.at[s], partner)

    def x_copy(s, t):
        return remote(
            to_x.at[s, t], in_x.at[s, t], x_send.at[s, t], x_recv.at[s, t], across(-s)
        )

    def results(b):
        to = pl.ds(b * tok, tok)
        return [
            pltpu.make_async_copy(rows.at[b], rows_out.at[to, :], out_sem.at[0, b]),
            pltpu.make_async_copy(dg.at[b], dg_out.at[to, :], out_sem.at[1, b]),
            pltpu.make_async_copy(du.at[b], du_out.at[to, :], out_sem.at[2, b]),
        ]

    def forward(b):
        def step(t, carry):
            units = pl.ds(pl.multiple_of(t * unit, unit), unit)
            gate = mm(rows[b], w_gate[:, units])
            upward = mm(rows[b], w_up[:, units])
            d_hidden = mm_nt(cot[b], w_down[units, :])
            square = gate * gate
            bent = jnp.tanh(root * gate * (1.0 + cubic * square))
            half = 0.5 * (1.0 + bent)
            act = gate * half
            slope = half + 0.5 * gate * (1.0 - bent * bent) * root * (1.0 + 3.0 * cubic * square)
            hid[b, :, units] = (act * upward).astype(BF)
            dg[b, :, units] = (d_hidden * upward * slope).astype(BF)
            du[b, :, units] = (d_hidden * act).astype(BF)
            return carry

        lax.fori_loop(0, hid.shape[2] // unit, step, 0)
        for copy in results(b):
            copy.start()

    def backward(b):
        s, other = b // 2, b % 2
        if not other:
            core_copy(s).wait_recv()

        def step(t, carry):
            at = pl.ds(pl.multiple_of(t * tile, tile), tile)
            value = mm_nt(dg[b], w_gate[at, :]) + mm_nt(du[b], w_up[at, :])
            if other:
                to_core[s, t] = value.astype(BF)
                return carry
            value = value + in_core[s, t].astype(F32)
            if s:
                to_x[s, t] = value.astype(BF)
                x_copy(s, t).start()
            else:
                total[t] = value
            return carry

        lax.fori_loop(0, tiles, step, 0)
        if other:
            core_copy(s).start()

    def part_copy(b):
        return pltpu.make_async_copy(part_stage.at[b % 2], part_out.at[b], stage_sem.at[b % 2])

    def branch(b):
        if b >= 2:
            part_copy(b - 2).wait()

        def step(t, carry):
            at = pl.ds(pl.multiple_of(t * tile, tile), tile)
            part_stage[b % 2, :, at] = mm(hid[b], w_down[:, at]).astype(BF)
            return carry

        lax.fori_loop(0, tiles, step, 0)
        part_copy(b).start()

    depth = down_stage.shape[1]
    strips = hidden_units // depth

    def down_copy(t, slot):
        to = pl.ds(pl.multiple_of(t * depth, depth), depth)
        return pltpu.make_async_copy(down_stage.at[slot], down_out.at[to, :], stage_sem.at[2 + slot])

    def down_step(t, carry):
        slot = t % 2

        @pl.when(t >= 2)
        def _():
            down_copy(t - 2, slot).wait()

        units = pl.ds(pl.multiple_of(t * depth, depth), depth)
        value = mm_tn(hid[0, :, units], cot[0])
        for b in range(1, ranks):
            value = value + mm_tn(hid[b, :, units], cot[b])
        down_stage[slot] = value.astype(BF)
        down_copy(t, slot).start()
        return carry

    gather(1).start()
    for s in range(1, size_x):
        gather(2 * s).start()
    for copy in loads:
        copy.wait()
    forward(0)
    gather(1).wait_recv()
    forward(1)
    backward(1)
    for s in range(1, size_x):
        gather(2 * s).wait_recv()
        gather(2 * s + 1).start()
        forward(2 * s)
        gather(2 * s + 1).wait_recv()
        forward(2 * s + 1)
        backward(2 * s + 1)
        backward(2 * s)
    backward(0)
    lax.fori_loop(0, strips, down_step, 0)
    for b in range(ranks):
        branch(b)
    for s in range(1, size_x):
        for t in range(tiles):
            x_copy(s, t).wait()
    for t in range(tiles):
        value = total[t]
        for s in range(1, size_x):
            value = value + in_x[s, t].astype(F32)
        grad_ref[:, t * tile : (t + 1) * tile] = value
    for b in range(1, ranks):
        gather(b).wait_send()
    for s in range(size_x):
        core_copy(s).wait_send()
    for b in range(ranks):
        for copy in results(b):
            copy.wait()
    part_copy(ranks - 2).wait()
    part_copy(ranks - 1).wait()
    down_copy(strips - 2, (strips - 2) % 2).wait()
    down_copy(strips - 1, (strips - 1) % 2).wait()


def feed_forward(sizes, normed, cot, cot_rows, w_gate, w_up, down_weight):
    ranks = 2 * sizes[2]
    size_x = sizes[2]
    tok, width = normed.shape
    units = w_gate.shape[1]
    tile = 512
    tiles = width // tile
    sem = pltpu.SemaphoreType.DMA
    hbm = pl.BlockSpec(memory_space=pl.ANY)
    return pl.pallas_call(
        functools.partial(mlp_kernel, sizes),
        in_specs=[hbm] * 6,
        out_specs=[pl.BlockSpec(memory_space=pltpu.VMEM)] + [hbm] * 5,
        out_shape=[
            jax.ShapeDtypeStruct((tok, width), F32),
            jax.ShapeDtypeStruct((ranks * tok, width), BF),
            jax.ShapeDtypeStruct((ranks * tok, units), BF),
            jax.ShapeDtypeStruct((ranks * tok, units), BF),
            jax.ShapeDtypeStruct((ranks, tok, width), BF),
            jax.ShapeDtypeStruct((units, width), BF),
        ],
        scratch_shapes=[
            pltpu.VMEM((ranks, tok, width), BF),
            pltpu.VMEM((ranks, tok, width), BF),
            pltpu.VMEM((width, units), BF),
            pltpu.VMEM((width, units), BF),
            pltpu.VMEM((units, width), BF),
            pltpu.VMEM((ranks, tok, units), BF),
            pltpu.VMEM((ranks, tok, units), BF),
            pltpu.VMEM((ranks, tok, units), BF),
            pltpu.VMEM((size_x, tiles, tok, tile), BF),
            pltpu.VMEM((size_x, tiles, tok, tile), BF),
            pltpu.VMEM((size_x, tiles, tok, tile), BF),
            pltpu.VMEM((size_x, tiles, tok, tile), BF),
            pltpu.VMEM((tiles, tok, tile), F32),
            pltpu.VMEM((2, tok, width), BF),
            pltpu.VMEM((2, 256, width), BF),
            sem((6,)),
            sem((ranks,)),
            sem((ranks,)),
            sem((size_x,)),
            sem((size_x,)),
            sem((size_x, tiles)),
            sem((size_x, tiles)),
            sem((3, ranks)),
            sem((4,)),
        ],
        compiler_params=pltpu.CompilerParams(
            collective_id=2, has_side_effects=True, vmem_limit_bytes=62 * 1024 * 1024
        ),
        cost_estimate=pl.CostEstimate(
            flops=14 * ranks * tok * width * units,
            bytes_accessed=60 * 1024 * 1024,
            transcendentals=0,
        ),
        name="feed_forward",
    )(normed, cot, cot_rows, w_gate, w_up, down_weight)


class Job:
    def __init__(self, phase, left, right, rows, cols, by_rank):
        self.phase, self.left, self.right = phase, left, right
        self.rows, self.cols, self.by_rank = rows, cols, by_rank


def grads_kernel(sizes, jobs, *refs):
    size_a, size_b, size_x = sizes
    chips = size_a * size_b
    n_ctx = 2 * chips
    ranks = 2 * size_x
    count = len(jobs)
    ins, refs = refs[:13], refs[13:]
    outs, refs = refs[:count], refs[count:]
    down_out, refs = refs[0], refs[1:]
    dealt, refs = refs[:2], refs[2:]
    gain_out, refs = refs[0], refs[1:]
    held, refs = refs[:8], refs[8:]
    gain_ctx, gain_x, resid_in, part_own, part_core, part_x, down_passed, refs = *refs[:7], refs[7:]
    recv, refs = refs[:count], refs[count:]
    send, refs = refs[:count], refs[count:]
    done, refs = refs[:count], refs[count:]
    load_sem, group_send, group_recv, deal_send, deal_recv, part_sem = refs[:6]
    gain_send, gain_recv, send_sem, recv_sem, done_send, done_recv, own_sem = refs[6:]
    ia, ib, ic, ix = (lax.axis_index(name) for name in ALL)
    own = (ia * size_b + ib) * 2 + ic
    rank = ix * 2 + ic
    place = snake_place(ia, ib, size_a, size_b)

    def on_ring(step):
        return snake((place + 2 * chips + step) % chips, size_a, size_b)

    def member(k):
        return (ic + k) % 2, (ix + k // 2) % size_x

    def ctx_device(k):
        e = (own + k) % n_ctx
        return e // 2 // size_b, e // 2 % size_b, e % 2, ix

    def keeper(row_chunk):
        chip = row_chunk // ranks
        return chip // size_b, chip % size_b, (row_chunk // size_x) % 2, row_chunk % size_x

    kept = rank * chips + kept_slot(ia, ib, size_a, size_b)
    kept_id = keeper(kept)
    flat = own * size_x + ix
    from_rank = flat // chips
    from_slot = flat % chips
    half = chips // 2
    from_id = (
        (from_slot % half) // (size_b // 2),
        ((from_slot % half) % (size_b // 2)) * 2 + 1 - from_slot // half,
        from_rank % 2,
        from_rank // 2,
    )

    def remote(src, dst, sent, came, device):
        return pltpu.make_async_remote_copy(
            src_ref=src,
            dst_ref=dst,
            send_sem=sent,
            recv_sem=came,
            device_id=device,
            device_id_type=MESH,
        )

    loads = [pltpu.make_async_copy(ins[i], held[i], load_sem.at[i]) for i in range(3)]
    for copy in loads:
        copy.start()

    barrier = pltpu.get_barrier_semaphore()
    greeted = [ctx_device(k) for k in range(1, n_ctx)] + [from_id]
    greeted += [(ia, ib) + member(k) for k in range(2, ranks)]
    for device in greeted:
        pl.semaphore_signal(barrier, inc=1, device_id=device, device_id_type=MESH)
    pl.semaphore_wait(barrier, len(greeted))

    passed_on = (3, 5)

    def group_copy(i, k):
        c, x = member(k)
        src, dst = ins[i], held[i].at[k]
        target = x * 2 + c
        if i == 4:
            rows = held[i].shape[1]
            src = src.at[pl.ds(pl.multiple_of(target * rows, rows), rows), :]
        if i == 6:
            cols = held[i].shape[2]
            src = src.at[:, pl.ds(pl.multiple_of(target * cols, cols), cols)]
        if k == 0:
            return pltpu.make_async_copy(src, dst, load_sem.at[i])
        if k % 2 and k > 1 and i in passed_on:
            src, x = held[i].at[k - 1], ix
        return remote(src, dst, group_send.at[i, k], group_recv.at[i, k], (ia, ib, c, x))

    def deal_copy(t, k):
        e = (own + k) % n_ctx
        source = part_own.at[0] if t == 0 else ins[9]
        rows = source.shape[0] // n_ctx
        src = source.at[pl.ds(pl.multiple_of(e * rows, rows), rows), :]
        dst = dealt[t].at[pl.ds(pl.multiple_of(own * rows, rows), rows), :]
        if k == 0:
            return pltpu.make_async_copy(src, dst, load_sem.at[8 + t])
        return remote(src, dst, deal_send.at[t, k], deal_recv.at[t, k], ctx_device(k))

    def part_load(step):
        return pltpu.make_async_copy(ins[8].at[2 * step], part_own.at[step], part_sem.at[step])

    def part_core_copy(step):
        device = (ia, ib, 1 - ic, ix)
        src, dst = ins[8].at[2 * step + 1], part_core.at[step]
        return remote(src, dst, group_send.at[0, step], group_recv.at[0, step], device)

    def part_x_copy(step):
        device = (ia, ib, ic, (ix + size_x - step) % size_x)
        src, dst = part_own.at[step], part_x.at[step - 1]
        return remote(src, dst, group_send.at[1, step], group_recv.at[1, step], device)

    crossing = size_x == 2
    down_sem = (done_send.at[count, 0], done_recv.at[count, 0])
    down_copy = remote(ins[12], down_out, *down_sem, kept_id)
    if crossing:
        straight = kept % size_x == ix
        hop_sem = (done_send.at[count, 1], done_recv.at[count, 1])
        down_hop = remote(ins[12], down_passed, *hop_sem, (ia, ib, ic, 1 - ix))
        passed_id = keeper(((1 - ix) * 2 + ic) * chips + kept_slot(ia, ib, size_a, size_b))
        pass_sem = (done_send.at[count, 2], done_recv.at[count, 0])
        down_pass = remote(down_passed, down_out, *pass_sem, passed_id)

    resid_copy = pltpu.make_async_copy(ins[11], resid_in, load_sem.at[11])

    def gain_copy(k):
        src, dst = ins[10].at[(own + k) % n_ctx], gain_ctx.at[k]
        if k == 0:
            return pltpu.make_async_copy(src, dst, load_sem.at[10])
        return remote(src, dst, deal_send.at[2, k], deal_recv.at[2, k], ctx_device(k))

    def gain_copy_x(s):
        device = (ia, ib, ic, (ix + s) % size_x)
        return remote(gain_x.at[0], gain_x.at[s], gain_send.at[s], gain_recv.at[s], device)

    def ring_copy(j, way, step, parity):
        neighbour = on_ring(1 - 2 * way) + (ic, ix)
        return remote(
            send[j].at[way, parity],
            recv[j].at[way, step],
            send_sem.at[j, way, parity],
            recv_sem.at[j, way, step],
            neighbour,
        )

    def product(j, way, step):
        job = jobs[j]
        a, b = on_ring(step * (2 * way - 1))
        part = job.rows // chips
        cols = slice(way * job.cols // 2, (way + 1) * job.cols // 2)
        left, right = held[job.left], held[job.right]
        if job.phase == 0:
            start = pl.multiple_of((a * size_b + b) * part, part)
            return mm_tn(left[:, pl.ds(start, part)], right[:, cols])
        if job.by_rank:
            start = kept_slot(a, b, size_a, size_b) * part
            if left.shape[1] != job.rows:
                start = start + rank * job.rows
        else:
            start = (a * size_b + b) * part
        rows = pl.ds(pl.multiple_of(start, part), part)
        total = mm(left[0, rows, :], right[0, :, cols])
        for k in range(1, ranks):
            total = total + mm(left[k, rows, :], right[k, :, cols])
        return total

    def deliver(j):
        job = jobs[j]
        if job.by_rank:
            return [remote(done[j], outs[j], done_send.at[j, 0], done_recv.at[j, 0], kept_id)]
        part = job.rows // (chips * ranks)
        copies = []
        for k in range(ranks):
            c, x = member(k)
            start = pl.multiple_of((c * size_x + x) * part, part)
            src, dst = done[j].at[pl.ds(start, part), :], outs[j].at[rank]
            if k == 0:
                copies.append(pltpu.make_async_copy(src, dst, own_sem.at[j]))
            else:
                copies.append(
                    remote(src, dst, done_send.at[j, k], done_recv.at[j, k], (ia, ib, c, x))
                )
        return copies

    def begin(j):
        for way in range(2):
            send[j][way, 0] = product(j, way, 1).astype(BF)
            ring_copy(j, way, 0, 0).start()

    def advance(j, step):
        parity = step % 2
        for way in range(2):
            part = product(j, way, step + 1)
            ring_copy(j, way, step - 1, 1 - parity).wait_recv()
            part = part + recv[j][way, step - 1].astype(F32)

            @pl.when(step >= 2)
            def _():
                ring_copy(j, way, step - 2, parity).wait_send()

            send[j][way, parity] = part.astype(BF)
            ring_copy(j, way, step, parity).start()

    last = chips - 2

    def finish(j):
        cols = jobs[j].cols // 2
        for way in range(2):
            part = product(j, way, chips)
            ring_copy(j, way, last, last % 2).wait_recv()
            part = part + recv[j][way, last].astype(F32)
            done[j][:, way * cols : (way + 1) * cols] = part.astype(BF)
        for copy in deliver(j):
            copy.start()
        for way in range(2):
            ring_copy(j, way, last - 1, (last - 1) % 2).wait_send()
            ring_copy(j, way, last, last % 2).wait_send()

    early = [j for j in range(count) if jobs[j].phase == 0]
    late = [j for j in range(count) if jobs[j].phase == 1]
    lag = 3

    def early_step(step, carry):
        for j in early:
            advance(j, step)
        return carry

    def both_step(step, carry):
        for j in late:
            advance(j, step - lag)
        for j in early:
            advance(j, step)
        return carry

    def late_step(step, carry):
        for j in late:
            advance(j, step)
        return carry

    for copy in loads:
        copy.wait()
    for j in early:
        begin(j)
    for step in range(size_x):
        part_load(step).start()
        part_core_copy(step).start()
    for i in (6, 7, 5, 4, 3):
        for k in range(ranks):
            if not (k % 2 and k > 1 and i in passed_on):
                group_copy(i, k).start()
    resid_copy.start()
    for k in range(n_ctx):
        gain_copy(k).start()
    for k in range(n_ctx):
        deal_copy(1, k).start()
    if crossing:

        @pl.when(straight)
        def _():
            down_copy.start()

        @pl.when(jnp.logical_not(straight))
        def _():
            down_hop.start()

    else:
        down_copy.start()
    lax.fori_loop(1, 2, early_step, 0)
    for step in range(size_x):
        part_load(step).wait()
        part_core_copy(step).wait()
    for step in range(1, size_x):
        summed = part_own[step].astype(F32) + part_core[step].astype(F32)
        part_own[step] = summed.astype(BF)
        part_x_copy(step).start()
    lax.fori_loop(2, lag, early_step, 0)
    if crossing:

        @pl.when(straight)
        def _():
            down_hop.wait_recv()
            down_pass.start()

    for i in reversed(passed_on):
        for k in range(2, ranks, 2):
            group_copy(i, k).wait_recv()
            group_copy(i, k + 1).start()
    for k in range(n_ctx):
        gain_copy(k).wait()
    gain_x[0] = jnp.sum(gain_ctx[...], axis=0)
    for s in range(1, size_x):
        gain_copy_x(s).start()
    lax.fori_loop(lag, lag + 1, early_step, 0)
    for i in range(3, 8):
        for k in range(ranks):
            if k and k % 2 == 0 and i in passed_on:
                group_copy(i, k).wait_send()
            else:
                group_copy(i, k).wait()
    for j in late:
        begin(j)
    resid_copy.wait()
    summed = resid_in[...] + part_own[0].astype(F32) + part_core[0].astype(F32)
    for step in range(1, size_x):
        part_x_copy(step).wait()
        summed = summed + part_x[step - 1].astype(F32)
    part_own[0] = summed.astype(BF)
    for k in range(n_ctx):
        deal_copy(0, k).start()
    lax.fori_loop(lag + 1, last + 1, both_step, 0)
    for j in early:
        finish(j)
    lax.fori_loop(last + 1 - lag, last + 1, late_step, 0)
    for j in late:
        finish(j)
    for s in range(1, size_x):
        gain_copy_x(s).wait()
    gain_out[...] = jnp.sum(gain_x[...], axis=0)
    for t in range(2):
        for k in range(n_ctx):
            deal_copy(t, k).wait()
    down_copy.wait_recv()
    if crossing:

        @pl.when(straight)
        def _():
            down_copy.wait_send()
            down_pass.wait_send()

        @pl.when(jnp.logical_not(straight))
        def _():
            down_hop.wait_send()

    else:
        down_copy.wait_send()
    for j in range(count):
        for copy in deliver(j):
            copy.wait()


def sum_grads(sizes, ins):
    size_a, size_b, size_x = sizes
    chips = size_a * size_b
    ranks = 2 * size_x
    normed_mlp, d_gate, d_upward = ins[:3]
    width = normed_mlp.shape[1]
    tok = ins[5].shape[0]
    part_width = width // ranks
    jobs = [
        Job(0, 0, 1, width, d_gate.shape[1], False),
        Job(0, 0, 2, width, d_upward.shape[1], False),
        Job(1, 3, 6, width, part_width, False),
        Job(1, 4, 5, part_width, width, True),
        Job(1, 3, 7, part_width, 2 * HD, True),
    ]
    held = [pltpu.VMEM(a.shape, BF) for a in ins[:3]]
    held += [
        pltpu.VMEM((ranks,) + shape, BF)
        for shape in (
            (width, tok),
            (part_width, tok),
            (tok, width),
            (tok, part_width),
            (tok, 2 * HD),
        )
    ]
    outs, recv, send, done = [], [], [], []
    flops = 0
    for job in jobs:
        part = job.rows // chips
        if job.by_rank:
            outs.append(jax.ShapeDtypeStruct((part, job.cols), BF))
        else:
            outs.append(jax.ShapeDtypeStruct((ranks, part // ranks, job.cols), BF))
        recv.append(pltpu.VMEM((2, chips - 1, part, job.cols // 2), BF))
        send.append(pltpu.VMEM((2, 2, part, job.cols // 2), BF))
        done.append(pltpu.VMEM((part, job.cols), BF))
        flops += 2 * job.rows * job.cols * normed_mlp.shape[0]
    count = len(jobs)
    outs.append(jax.ShapeDtypeStruct(ins[12].shape, BF))
    outs += [jax.ShapeDtypeStruct((tok, width), BF)] * 2
    gain_shape = ins[10].shape[1:]
    outs.append(jax.ShapeDtypeStruct(gain_shape, F32))
    sem = pltpu.SemaphoreType.DMA
    return pl.pallas_call(
        functools.partial(grads_kernel, sizes, jobs),
        in_specs=[pl.BlockSpec(memory_space=pl.ANY)] * len(ins),
        out_specs=[pl.BlockSpec(memory_space=pl.ANY)] * (count + 3)
        + [pl.BlockSpec(memory_space=pltpu.VMEM)],
        out_shape=outs,
        scratch_shapes=held
        + [
            pltpu.VMEM((2 * chips,) + gain_shape, F32),
            pltpu.VMEM((size_x,) + gain_shape, F32),
            pltpu.VMEM((tok, width), F32),
            pltpu.VMEM((size_x, tok, width), BF),
            pltpu.VMEM((size_x, tok, width), BF),
            pltpu.VMEM((size_x - 1, tok, width), BF),
            pltpu.VMEM(ins[12].shape, BF),
        ]
        + recv
        + send
        + done
        + [
            sem((len(ins),)),
            sem((8, ranks)),
            sem((8, ranks)),
            sem((3, 2 * chips)),
            sem((3, 2 * chips)),
            sem((size_x,)),
            sem((size_x,)),
            sem((size_x,)),
            sem((count, 2, 2)),
            sem((count, 2, chips - 1)),
            sem((count + 1, ranks)),
            sem((count + 1, ranks)),
            sem((count,)),
        ],
        compiler_params=pltpu.CompilerParams(
            collective_id=0, has_side_effects=True, vmem_limit_bytes=63 * 1024 * 1024
        ),
        cost_estimate=pl.CostEstimate(
            flops=flops, bytes_accessed=400 * 1024 * 1024, transcendentals=0
        ),
        name="sum_grads",
    )(*ins)


def norm_stats(values):
    inv = lax.rsqrt(jnp.mean(values * values, axis=-1, keepdims=True) + epsilon)
    return values * inv, inv


def norm_back(unit, inv, gain, grad):
    scaled = grad * gain
    inner = jnp.mean(scaled * unit, axis=-1, keepdims=True)
    return inv * (scaled - unit * inner), jnp.sum(grad * unit, axis=0)


def on_device(
    sizes,
    tokens,
    lengths,
    dealing,
    attn_gain,
    query_weight,
    kv_weight,
    out_weight,
    mlp_gain,
    gate_weight,
    up_weight,
    down_weight,
    cotangent,
):
    size_a, size_b, size_x = sizes
    chips = size_a * size_b
    n_ctx = chips * 2
    ranks = 2 * size_x
    ia, ib, ic, ix = (lax.axis_index(name) for name in ALL)
    chip = ia * size_b + ib
    own = chip * 2 + ic
    flat = own * size_x + ix
    rank = ix * 2 + ic
    tok = tokens.shape[1]
    width = tokens.shape[2]
    piece = tok // n_ctx
    halo = WINDOW // tok

    def pick(array, index, axis=0):
        return lax.dynamic_index_in_dim(array, index, axis, keepdims=False)

    own_deal = pick(dealing[0], own)
    deal = (own_deal[:, None] == jnp.arange(tok, dtype=jnp.int32)[None, :]).astype(BF)

    gains = jnp.stack([attn_gain, mlp_gain]).reshape(-1, 128)
    stream = own * tok + jnp.arange(tok, dtype=jnp.int32)
    ends = jnp.cumsum(lengths[0])
    starts = jnp.max(jnp.where(stream[:, None] >= ends[None, :], ends[None, :], 0), axis=1)
    low = jnp.maximum(starts, stream - (WINDOW - 1)) - (own * tok - WINDOW)
    low = low.astype(jnp.int32)[None, :]
    inputs_low, cot, w_query, w_kv, w_out, w_gate, w_up, gains, *attended = fetch(
        sizes,
        [mm(deal, tokens[0]).astype(BF), mm(deal, cotangent[0]).astype(BF)],
        [query_weight, kv_weight, out_weight],
        [gate_weight, up_weight],
        gains,
        low,
    )
    normed, queries, window, context, lse, cot_rows = attended
    gains = gains.reshape(size_x, 2, -1).astype(F32)
    gain_one = gains[:, 0].reshape(-1)
    gain_two = gains[:, 1].reshape(-1)


    inputs = inputs_low.astype(F32)
    unit_one, inv_one = norm_stats(inputs)
    resid = inputs + mm(context, w_out)

    unit_two, inv_two = norm_stats(resid)
    d_normed_mlp, mlp_rows, d_gate, d_upward, mlp_parts, down_grad = feed_forward(
        sizes, (unit_two * gain_two).astype(BF), cot, cot_rows, w_gate, w_up, down_weight
    )
    d_resid_part, mlp_gain_grad = norm_back(unit_two, inv_two, gain_two, d_normed_mlp)
    d_resid = cot.astype(F32) + d_resid_part
    d_branch = d_resid.astype(BF)

    d_queries, d_pairs, down_sum, d_normed = attend_back(
        sizes, queries, window, low, d_branch, lse, down_grad, w_out, w_query, w_kv
    )
    d_inputs, attn_gain_grad = norm_back(unit_one, inv_one, gain_one, d_normed)
    gain_part = width // (n_ctx * size_x)
    gain_grads = jnp.stack([attn_gain_grad, mlp_gain_grad]).reshape(2, n_ctx, size_x, gain_part)
    gain_grads = gain_grads.transpose(1, 2, 0, 3).reshape(n_ctx, -1)
    gain_grads = jnp.pad(gain_grads, ((0, 0), (0, 1024 - gain_grads.shape[1])))
    sums = sum_grads(
        sizes,
        [
            mlp_rows,
            d_gate,
            d_upward,
            normed.T,
            context.T,
            d_branch,
            d_queries,
            d_pairs,
            mlp_parts,
            (d_resid + d_inputs).astype(BF),
            gain_grads.reshape(n_ctx, 8, 128),
            resid,
            down_sum,
        ],
    )
    gate_grad, up_grad, query_grad = (
        v.transpose(1, 0, 2).reshape(v.shape[1], -1).astype(F32) for v in sums[:3]
    )
    out_grad, kv_grad, down_grad = (v.astype(F32) for v in sums[3:6])
    block_output = mm_tn(deal, sums[6]).astype(BF)
    token_grad = mm_tn(deal, sums[7])
    gain_grads = lax.dynamic_slice(sums[8].reshape(-1), (ix * 2 * gain_part,), (2 * gain_part,))
    attn_gain_grad, mlp_gain_grad = gain_grads[:gain_part], gain_grads[gain_part:]
    return (
        block_output[None],
        token_grad[None],
        attn_gain_grad,
        query_grad,
        kv_grad,
        out_grad,
        mlp_gain_grad,
        gate_grad,
        up_grad,
        down_grad,
    )


def solution(mesh):
    n_ctx, size_x = mesh.shape["ctx"], mesh.shape["fsdp"]
    chips = n_ctx // 2
    size_a = 4 if chips % 4 == 0 else chips
    size_b = chips // size_a
    fine = Mesh(mesh.devices.reshape(size_a, size_b, 2, size_x), ALL)
    rows = P("x", CTX, None)
    split = P("x", None)
    every = P(ALL)
    matrix = P(ALL, None)
    return jax.shard_map(
        functools.partial(on_device, (size_a, size_b, size_x)),
        mesh=fine,
        in_specs=(
            rows,
            split,
            P("x", None, None),
            P("x"),
            split,
            split,
            split,
            P("x"),
            split,
            split,
            split,
            rows,
        ),
        out_specs=(rows, rows, every, matrix, matrix, matrix, every, matrix, matrix, matrix),
        check_vma=False,
    )
```

```python
import functools

import jax
import jax.numpy as jnp
import numpy as np
from jax import lax
from jax.experimental import pallas as pl
from jax.experimental.pallas import tpu as pltpu
from jax.sharding import Mesh
from jax.sharding import PartitionSpec as P

H = 16
HD = 128
WINDOW = 1024
QBLK = 128
HEADS_STEP = 4
SPAN = WINDOW + QBLK
ROWS = HEADS_STEP * QBLK

epsilon = 1e-06
neg_large = -1e30
scale = HD ** (-0.5)
root = (2.0 / np.pi) ** 0.5
cubic = 0.044715
BF = jnp.bfloat16
F32 = jnp.float32
CTX = ("a", "b", "c")
ALL = ("a", "b", "c", "x")
MESH = pl.DeviceIdType.MESH


def mm(left, right):
    return jnp.dot(left, right, preferred_element_type=F32)


def mm_tn(left, right):
    return lax.dot_general(left, right, (((0,), (0,)), ((), ())), preferred_element_type=F32)


def mm_nt(left, right):
    return lax.dot_general(left, right, (((1,), (1,)), ((), ())), preferred_element_type=F32)


def stack_heads(block):
    return jnp.concatenate([block[:, h * HD : (h + 1) * HD] for h in range(HEADS_STEP)], 0)


def unstack_heads(block_t):
    return jnp.concatenate(
        [block_t[:, h * QBLK : (h + 1) * QBLK].T for h in range(HEADS_STEP)], 1
    )


def bias_of(lo, qb):
    key = lax.broadcasted_iota(jnp.int32, (SPAN, QBLK), 0) + qb * QBLK
    query = lax.broadcasted_iota(jnp.int32, (SPAN, QBLK), 1) + (WINDOW + qb * QBLK)
    allowed = (key >= lo) & (key <= query)
    bias = jnp.where(allowed, 0.0, neg_large).astype(F32)
    return jnp.concatenate([bias] * HEADS_STEP, 1)


def attend_block(bias, queries, keys, values):
    scores = mm_nt(keys, queries) * scale + bias
    top = jnp.max(scores, axis=0, keepdims=True)
    raised = jnp.exp(scores - top)
    total = jnp.sum(raised, axis=0, keepdims=True)
    return mm_tn(values, raised.astype(BF)) * (1.0 / total), top + jnp.log(total)


def snake(pos, size_a, size_b):
    if size_b == 1:
        return pos, pos * 0
    down = pos // size_a
    first = 1 - (down + 7) // 8
    q = (pos - size_a) * (1 - first)
    a_up = size_a - 1 - q // (size_b - 1)
    k = q % (size_b - 1)
    odd = a_up % 2
    b_up = odd * (1 + k) + (1 - odd) * (size_b - 1 - k)
    return first * pos + (1 - first) * a_up, (1 - first) * b_up


def snake_place(a, b, size_a, size_b):
    if size_b == 1:
        return a
    moved = (b + size_b - 1) // size_b
    odd = a % 2
    along = odd * (b - 1) + (1 - odd) * (size_b - 1 - b)
    return (1 - moved) * a + moved * (size_a + (size_a - 1 - a) * (size_b - 1) + along)


def kept_slot(a, b, size_a, size_b):
    half = size_a * size_b // 2
    return (1 - b % 2) * half + a * (size_b // 2) + b // 2


def back_kernel(sizes, low_ref, q_ref, kv_ref, branch_ref, lse_ref, down_in, *refs):
    size_a, size_b, size_x = sizes
    weights_in, refs = refs[:3], refs[3:]
    dq_ref, pairs_ref, sum_ref, normed_ref, refs = *refs[:4], refs[4:]
    w_out, w_query, w_kv, do_ref, refs = *refs[:4], refs[4:]
    dkv, down, recv, send, halo_out, halo_in = refs[:6]
    load_sem, send_sem, recv_sem, halo_send, halo_recv = refs[6:]
    chips = size_a * size_b
    n_ctx = chips * 2
    ia, ib, ic, ix = (lax.axis_index(name) for name in ALL)
    own = (ia * size_b + ib) * 2 + ic
    place = snake_place(ia, ib, size_a, size_b)
    tok = q_ref.shape[0]
    halo = WINDOW // tok
    groups = H // HEADS_STEP
    blocks = tok // QBLK * groups
    part = down.shape[0] // chips
    quarter = down.shape[1] // 4
    chains = [(way, sub) for way in range(2) for sub in range(2)]
    last = chips - 2

    loading = pltpu.make_async_copy(down_in, down, load_sem.at[0])
    loading.start()
    weights = [
        pltpu.make_async_copy(src, dst, load_sem.at[1 + n])
        for n, (src, dst) in enumerate(zip(weights_in, (w_out, w_query, w_kv)))
    ]
    for copy in weights:
        copy.start()
    dkv[...] = jnp.zeros_like(dkv)

    def on_ring(step):
        return snake((place + 2 * chips + step) % chips, size_a, size_b)

    def ctx_device(step):
        e = (own + n_ctx + step) % n_ctx
        return e // 2 // size_b, e // 2 % size_b, e % 2, ix

    barrier = pltpu.get_barrier_semaphore()
    for k in range(1, n_ctx):
        pl.semaphore_signal(barrier, inc=1, device_id=ctx_device(k), device_id_type=MESH)
    pl.semaphore_wait(barrier, n_ctx - 1)

    def remote(src, dst, sent, came, device):
        return pltpu.make_async_remote_copy(
            src_ref=src,
            dst_ref=dst,
            send_sem=sent,
            recv_sem=came,
            device_id=device,
            device_id_type=MESH,
        )

    def ring_copy(way, sub, step, parity):
        return remote(
            send.at[way, sub, parity],
            recv.at[way, sub, step],
            send_sem.at[way, sub, parity],
            recv_sem.at[way, sub, step],
            on_ring(1 - 2 * way) + (ic, ix),
        )

    def columns(way, sub):
        return slice((2 * way + sub) * quarter, (2 * way + sub + 1) * quarter)

    def chunk(way, sub, step):
        a, b = on_ring(step * (2 * way - 1))
        rows = pl.ds(pl.multiple_of(kept_slot(a, b, size_a, size_b) * part, part), part)
        return down[rows, columns(way, sub)]

    def advance(step):
        parity = step % 2
        for way, sub in chains:
            value = chunk(way, sub, step + 1).astype(F32)
            ring_copy(way, sub, step - 1, 1 - parity).wait_recv()
            value = value + recv[way, sub, step - 1].astype(F32)

            @pl.when(step >= 2)
            def _():
                ring_copy(way, sub, step - 2, parity).wait_send()

            send[way, sub, parity] = value.astype(BF)
            ring_copy(way, sub, step, parity).start()

    def attend_step(t):
        qb, hg = t // groups, t % groups
        width = HEADS_STEP * HD
        block = pl.ds(pl.multiple_of(qb * QBLK, QBLK), QBLK)
        cols = pl.ds(pl.multiple_of(hg * width, width), width)
        rows = pl.ds(pl.multiple_of(qb * QBLK, QBLK), SPAN)
        keys = kv_ref[rows, :HD]
        values = kv_ref[rows, HD:]
        queries = stack_heads(q_ref[block, cols])
        d_out = stack_heads(do_ref[block, cols])
        scores = mm_nt(keys, queries) * scale + bias_of(low_ref[qb], qb)
        probs = jnp.exp(scores - lse_ref[t])
        d_probs = mm_nt(values, d_out)
        delta = jnp.sum(probs * d_probs, axis=0, keepdims=True)
        d_scores = (probs * (d_probs - delta)).astype(BF)
        dq_ref[block, cols] = unstack_heads(mm_tn(keys, d_scores) * scale).astype(BF)
        dkv[rows, :HD] += mm(d_scores, queries) * scale
        dkv[rows, HD:] += mm(probs.astype(BF), d_out)

    def halo_copy(k):
        sems = (halo_send.at[k - 1], halo_recv.at[k - 1])
        return remote(halo_out.at[k - 1], halo_in.at[k - 1], *sems, ctx_device(-k))

    def both(step, carry):
        advance(step)
        attend_step(2 * step - 2)
        attend_step(2 * step - 1)
        return carry

    def alone(step, carry):
        advance(step)
        return carry

    tile = 512

    def context_step(t, carry):
        at = pl.ds(pl.multiple_of(t * tile, tile), tile)
        do_ref[:, at] = mm_nt(branch_ref[...], w_out[at, :]).astype(BF)
        return carry

    def normed_step(t, carry):
        at = pl.ds(pl.multiple_of(t * tile, tile), tile)
        normed_ref[:, at] = mm_nt(dq_ref[...], w_query[at, :]) + mm_nt(pairs_ref[...], w_kv[at, :])
        return carry

    loading.wait()
    for way, sub in chains:
        send[way, sub, 0] = chunk(way, sub, 1)
        ring_copy(way, sub, 0, 0).start()
    weights[0].wait()
    lax.fori_loop(0, w_out.shape[0] // tile, context_step, 0)
    busy = blocks // 2
    lax.fori_loop(1, busy + 1, both, 0)
    for k in range(1, halo + 1):

        @pl.when(own >= k)
        def _():
            halo_out[k - 1] = dkv[(halo - k) * tok : (halo - k + 1) * tok, :].astype(BF)
            halo_copy(k).start()

    lax.fori_loop(busy + 1, busy + 2, alone, 0)
    for k in range(1, halo + 1):

        @pl.when(own + k < n_ctx)
        def _():
            halo_copy(k).wait_recv()
            dkv[WINDOW:, :] += halo_in[k - 1].astype(F32)

    pairs_ref[...] = dkv[WINDOW:, :].astype(BF)
    for copy in weights[1:]:
        copy.wait()
    lax.fori_loop(0, w_query.shape[0] // tile, normed_step, 0)
    lax.fori_loop(busy + 2, last + 1, alone, 0)
    for way, sub in chains:
        value = chunk(way, sub, chips).astype(F32)
        ring_copy(way, sub, last, last % 2).wait_recv()
        value = value + recv[way, sub, last].astype(F32)
        sum_ref[:, columns(way, sub)] = value.astype(BF)
    for way, sub in chains:
        ring_copy(way, sub, last - 1, (last - 1) % 2).wait_send()
        ring_copy(way, sub, last, last % 2).wait_send()
    for k in range(1, halo + 1):

        @pl.when(own >= k)
        def _():
            halo_copy(k).wait_send()


def attend_back(sizes, queries, window, low, d_branch, lse, down, w_out, w_query, w_kv):
    chips = sizes[0] * sizes[1]
    tok = queries.shape[0]
    halo = WINDOW // tok
    part, width = down.shape[0] // chips, down.shape[1]
    sem = pltpu.SemaphoreType.DMA
    vmem = pl.BlockSpec(memory_space=pltpu.VMEM)
    return pl.pallas_call(
        functools.partial(back_kernel, sizes),
        in_specs=[vmem] * 5 + [pl.BlockSpec(memory_space=pl.ANY)] * 4,
        out_specs=[vmem] * 4,
        out_shape=[
            jax.ShapeDtypeStruct((tok, H * HD), BF),
            jax.ShapeDtypeStruct((tok, 2 * HD), BF),
            jax.ShapeDtypeStruct((part, width), BF),
            jax.ShapeDtypeStruct((tok, width), F32),
        ],
        scratch_shapes=[
            pltpu.VMEM(w_out.shape, BF),
            pltpu.VMEM(w_query.shape, BF),
            pltpu.VMEM(w_kv.shape, BF),
            pltpu.VMEM((tok, H * HD), BF),
            pltpu.VMEM((WINDOW + tok, 2 * HD), F32),
            pltpu.VMEM(down.shape, BF),
            pltpu.VMEM((2, 2, chips - 1, part, width // 4), BF),
            pltpu.VMEM((2, 2, 2, part, width // 4), BF),
            pltpu.VMEM((halo, tok, 2 * HD), BF),
            pltpu.VMEM((halo, tok, 2 * HD), BF),
            sem((4,)),
            sem((2, 2, 2)),
            sem((2, 2, chips - 1)),
            sem((halo,)),
            sem((halo,)),
        ],
        compiler_params=pltpu.CompilerParams(
            collective_id=3, has_side_effects=True, vmem_limit_bytes=60 * 1024 * 1024
        ),
        cost_estimate=pl.CostEstimate(
            flops=10 * tok * H * HD * SPAN, bytes_accessed=100 * 1024 * 1024, transcendentals=0
        ),
        name="attend_back",
    )(low.reshape(tok // QBLK, 1, QBLK), queries, window, d_branch, lse, down, w_out, w_query, w_kv)


class Piece:
    def __init__(self, at, rows, square, shared, part, parts):
        self.at, self.rows, self.square, self.shared = at, rows, square, shared
        self.part, self.parts = part, parts
        self.relays = [0, 1, 2, 3] if square else []
        if shared:
            self.relays += [4, 5, 6, 7, 8] if square else [4]


def fetch_kernel(sizes, pieces, n_in, n_dealt, *refs):
    size_a, size_b, size_x = sizes
    n_ctx = size_a * size_b * 2
    ins, low_ref, refs = refs[:n_in], refs[n_in], refs[n_in + 1 :]
    outs, refs = refs[:n_in], refs[n_in:]
    normed_ref, query_ref, window_out, context_ref, lse_ref, cot_rows, refs = *refs[:6], refs[6:]
    normed_t_ref, context_t_ref, refs = *refs[:2], refs[2:]
    tok_in, w_query, w_kv, gain_in, window, refs = *refs[:5], refs[5:]
    load_sem, halo_send, halo_recv, cot_send, cot_recv, refs = *refs[:5], refs[5:]
    n_weights = n_in - n_dealt - 1
    stages, refs = refs[:n_weights], refs[n_weights:]
    keep_sem, own_sem, deal_send, deal_recv, gain_send, gain_recv = refs[:6]
    x_send, x_recv, relay_send, relay_recv = refs[6:]
    ia, ib, ic, ix = (lax.axis_index(name) for name in ALL)
    own = (ia * size_b + ib) * 2 + ic
    rank = ix * 2 + ic
    pa, pb = ia % 2, ib % 2
    other_a, other_b = ia + 1 - 2 * pa, ib + 1 - 2 * pb
    corner = pa * 2 + pb
    corner_a, corner_b, corner_d = (1 - pa) * 2 + pb, pa * 2 + 1 - pb, 3 - corner

    barrier = pltpu.get_barrier_semaphore()
    greeted = []
    for k in range(1, n_ctx):
        e = (own + k) % n_ctx
        greeted.append((e // 2 // size_b, e // 2 % size_b, e % 2, ix))
    for s in range(1, size_x):
        greeted.append((ia, ib, ic, (ix + s) % size_x))
    for device in greeted:
        pl.semaphore_signal(barrier, inc=1, device_id=device, device_id_type=MESH)
    pl.semaphore_wait(barrier, len(greeted))

    def remote(src, dst, send, recv, device):
        return pltpu.make_async_remote_copy(
            src_ref=src,
            dst_ref=dst,
            send_sem=send,
            recv_sem=recv,
            device_id=device,
            device_id_type=MESH,
        )

    def x_copy(i, s):
        p = pieces[i]
        shard, full = ins[p.at], outs[p.at]
        target = (ix + s) % size_x
        height = shard.shape[0]
        rows, start = region(p, corner, ic)
        if p.shared:
            src = shard.at[pl.ds(start, rows), :]
        else:
            cols = full.shape[1]
            at = pl.multiple_of((target * 2 + ic) * cols, cols)
            src = shard.at[pl.ds(start, rows), pl.ds(at, cols)]
        dst = full.at[pl.ds(pl.multiple_of(ix * height + start, rows), rows), :]
        return remote(src, dst, x_send.at[i, s], x_recv.at[i, s], (ia, ib, ic, target))

    def region(p, which, core):
        owner = which if p.square else 0
        owners = 4 if p.square else 1
        if p.shared:
            owner, owners = owner * 2 + core, owners * 2
        rows = p.rows // (owners * p.parts)
        return rows, pl.multiple_of((owner * p.parts + p.part) * rows, rows)

    def landed(i, s, which, core, half=None):
        p = pieces[i]
        rows, start = region(p, which, core)
        start = start + (ix + size_x - s) % size_x * p.rows
        if half is not None:
            rows = rows // 2
            start = start + half * rows
        return outs[p.at].at[pl.ds(pl.multiple_of(start, rows), rows), :]

    def relay(i, s, kind, incoming=False):
        sem = (relay_send.at[i, s, kind], relay_recv.at[i, s, kind])
        if kind < 4:
            device = (other_a, ib, ic, ix) if kind in (1, 2) else (ia, other_b, ic, ix)
            sent = (
                landed(i, s, corner, ic),
                landed(i, s, corner, ic),
                landed(i, s, corner_b, ic, 0),
                landed(i, s, corner_a, ic, 1),
            )[kind]
            came = (
                landed(i, s, corner_b, ic),
                landed(i, s, corner_a, ic),
                landed(i, s, corner_d, ic, 0),
                landed(i, s, corner_d, ic, 1),
            )[kind]
        else:
            device = (ia, ib, 1 - ic, ix)
            which, half = ((corner, None), (corner_b, None), (corner_a, None), (corner_d, 0), (corner_d, 1))[
                kind - 4
            ]
            sent = landed(i, s, which, ic, half)
            came = landed(i, s, which, 1 - ic, half)
        ref = came if incoming else sent
        return remote(ref, ref, *sem, device)

    rows = ins[0].shape[0] // n_ctx

    def deal_copy(t, k):
        e = (own + k) % n_ctx
        src = ins[t].at[pl.ds(pl.multiple_of(e * rows, rows), rows), :]
        dst = outs[t].at[pl.ds(pl.multiple_of(own * rows, rows), rows), :]
        if k == 0:
            return pltpu.make_async_copy(src, dst, own_sem.at[t])
        device = (e // 2 // size_b, e // 2 % size_b, e % 2, ix)
        return remote(src, dst, deal_send.at[t, k], deal_recv.at[t, k], device)

    g = n_in - 1

    def gain_copy(s):
        if s == 0:
            return pltpu.make_async_copy(ins[g], outs[g].at[ix], own_sem.at[g])
        device = (ia, ib, ic, (ix + s) % size_x)
        return remote(ins[g], outs[g].at[ix], gain_send.at[s], gain_recv.at[s], device)

    def keep_copy(w, out):
        shard, full = ins[w], outs[w]
        stage = stages[w - n_dealt]
        height = shard.shape[0]
        sem = keep_sem.at[w, out]
        if out:
            dst = full.at[pl.ds(pl.multiple_of(ix * height, height), height), :]
            return pltpu.make_async_copy(stage, dst, sem)
        src = shard
        if full.shape[1] != shard.shape[1]:
            cols = full.shape[1]
            src = shard.at[:, pl.ds(pl.multiple_of(rank * cols, cols), cols)]
        return pltpu.make_async_copy(src, stage, sem)

    tok = tok_in.shape[0]
    halo = WINDOW // tok
    at_query, at_kv = n_dealt, n_dealt + 1

    def load(src, dst, n):
        copy = pltpu.make_async_copy(src, dst, load_sem.at[n])
        copy.start()
        copy.wait()

    def core_parts_in(i):
        for s in range(1, size_x):
            for kind in pieces[i].relays:
                if kind >= 4:
                    relay(i, s, kind, True).wait_recv()
        keep_copy(pieces[i].at, 1).wait()

    def halo_copy(k):
        e = own + k
        device = (e // 2 // size_b, e // 2 % size_b, e % 2, ix)
        src = window.at[pl.ds(WINDOW, tok), :]
        dst = window.at[pl.ds((halo - k) * tok, tok), :]
        return remote(src, dst, halo_send.at[k - 1], halo_recv.at[k - 1], device)

    def normalise():
        for k in range(n_ctx):
            deal_copy(0, k).wait()
        for s in range(size_x):
            gain_copy(s).wait()
        load(outs[0], tok_in, 0)
        load(outs[g], gain_in, 1)
        gain = []
        for x in range(size_x):
            values = gain_in[x].astype(F32)
            gain += [values[r : r + 1, :] for r in range(values.shape[0] // 2)]
        values = tok_in[...].astype(F32)
        unit, _ = norm_stats(values)
        normed_ref[...] = (unit * jnp.concatenate(gain, 1)).astype(BF)

    def transpose():
        def step(t, carry):
            at = pl.ds(pl.multiple_of(t * HD, HD), HD)
            normed_t_ref[at, :] = normed_ref[:, at].astype(F32).T.astype(BF)
            return carry

        lax.fori_loop(0, normed_ref.shape[1] // HD, step, 0)

    def keys_values():
        core_parts_in(1)
        load(outs[at_kv], w_kv, 2)
        window[WINDOW:, :] = mm(normed_ref[...], w_kv[...]).astype(BF)
        for k in range(1, halo + 1):

            @pl.when(own + k < n_ctx)
            def _():
                halo_copy(k).start()

            @pl.when(own < k)
            def _():
                window[(halo - k) * tok : (halo - k + 1) * tok, :] = jnp.zeros((tok, 2 * HD), BF)

    def project():
        core_parts_in(0)
        load(outs[at_query], w_query, 3)

        def step(t, carry):
            cols = pl.ds(pl.multiple_of(t * 512, 512), 512)
            query_ref[:, cols] = mm(normed_ref[...], w_query[:, cols]).astype(BF)
            return carry

        lax.fori_loop(0, H * HD // 512, step, 0)

    def halo_in():
        for k in range(1, halo + 1):

            @pl.when(own >= k)
            def _():
                halo_copy(k).wait_recv()

    def cot_copy(b):
        sems = (cot_send.at[b], cot_recv.at[b])
        if b % 2:
            src = outs[1] if b == 1 else cot_rows.at[b - 2]
            return remote(src, cot_rows.at[b - 1], *sems, (ia, ib, 1 - ic, ix))
        device = (ia, ib, ic, (ix + b // 2) % size_x)
        return remote(outs[1], cot_rows.at[b - 1], *sems, device)

    def spread_cotangent():
        for k in range(n_ctx):
            deal_copy(1, k).wait()
        for s in range(1, size_x):
            cot_copy(2 * s).start()
        cot_copy(1).start()

    def attend(qb):
        low = low_ref[:, qb * QBLK : (qb + 1) * QBLK]
        bias = bias_of(low, qb)
        keys = window[qb * QBLK : qb * QBLK + SPAN, :HD]
        values = window[qb * QBLK : qb * QBLK + SPAN, HD:]
        rows = slice(qb * QBLK, (qb + 1) * QBLK)

        def step(t, carry):
            width = HEADS_STEP * HD
            cols = pl.ds(pl.multiple_of(t * width, width), width)
            out_t, lse = attend_block(bias, stack_heads(query_ref[rows, cols]), keys, values)
            context_ref[rows, cols] = unstack_heads(out_t).astype(BF)
            for h in range(HEADS_STEP):
                at = pl.ds(pl.multiple_of((t * HEADS_STEP + h) * HD, HD), HD)
                context_t_ref[at, rows] = out_t[:, h * QBLK : (h + 1) * QBLK].astype(BF)
            lse_ref[qb * (H // HEADS_STEP) + t] = lse
            return carry

        lax.fori_loop(0, H // HEADS_STEP, step, 0)

    blocks = tok // QBLK
    tasks = {2 * size_x - 1: [normalise, keys_values], 2 * size_x: [spread_cotangent, project]}
    for qb in range(blocks):
        task = functools.partial(attend, qb)
        tasks[2 * size_x + 1 + qb] = [halo_in, task] if qb == 0 else [task]

    tasks[2 * size_x + 1 + blocks] = [transpose]
    ahead = 4
    order = [(i, s) for i in range(len(pieces)) for s in range(1, size_x)]
    for k in range(n_ctx):
        deal_copy(0, k).start()
    for s in range(size_x):
        gain_copy(s).start()
    for i, s in order[:ahead]:
        x_copy(i, s).start()
    for t in range(1, n_dealt):
        for k in range(n_ctx):
            deal_copy(t, k).start()
    for w in range(n_dealt, n_dealt + n_weights):
        keep_copy(w, 0).start()

    for n in range(len(order) + 2):
        if n < n_weights:
            keep_copy(n_dealt + n, 0).wait()
            keep_copy(n_dealt + n, 1).start()
        if n < len(order):
            i, s = order[n]
            x_copy(i, s).wait_recv()
            for kind in (0, 1, 4):
                if kind in pieces[i].relays:
                    relay(i, s, kind).start()
            if n + ahead < len(order):
                x_copy(i, s).wait_send()
                x_copy(*order[n + ahead]).start()
        if 1 <= n <= len(order) and pieces[order[n - 1][0]].square:
            i, s = order[n - 1]
            relay(i, s, 0, True).wait_recv()
            relay(i, s, 2).start()
            relay(i, s, 1, True).wait_recv()
            relay(i, s, 3).start()
            if pieces[i].shared:
                relay(i, s, 5).start()
                relay(i, s, 6).start()
        if n >= 2 and pieces[order[n - 2][0]].square:
            i, s = order[n - 2]
            relay(i, s, 2, True).wait_recv()
            relay(i, s, 3, True).wait_recv()
            if pieces[i].shared:
                relay(i, s, 7).start()
                relay(i, s, 8).start()
        for task in tasks.get(n, []):
            task()

    for s in range(1, size_x):
        cot_copy(2 * s).wait_recv()
        cot_copy(2 * s + 1).start()
    window_out[...] = window[...]
    for k in range(1, halo + 1):

        @pl.when(own + k < n_ctx)
        def _():
            halo_copy(k).wait_send()

    for n, (i, s) in enumerate(order):
        if n + ahead >= len(order):
            x_copy(i, s).wait_send()
        for kind in pieces[i].relays:
            relay(i, s, kind).wait_send()
            if kind >= 4 and i > 1:
                relay(i, s, kind, True).wait_recv()
    for b in range(1, 2 * size_x):
        cot_copy(b).wait_send()
        if b % 2:
            cot_copy(b).wait_recv()
    for w in range(n_dealt + 2, n_dealt + n_weights):
        keep_copy(w, 1).wait()


def fetch(sizes, dealt, shared, split, gains, low):
    size_a, size_b, size_x = sizes
    n_ctx = size_a * size_b * 2
    ins = dealt + shared + split + [gains]
    outs = [jax.ShapeDtypeStruct(a.shape, BF) for a in dealt]
    outs += [jax.ShapeDtypeStruct((size_x * a.shape[0], a.shape[1]), BF) for a in shared]
    outs += [
        jax.ShapeDtypeStruct((size_x * a.shape[0], a.shape[1] // (2 * size_x)), BF) for a in split
    ]
    outs.append(jax.ShapeDtypeStruct((size_x,) + gains.shape, BF))
    pieces = []
    first = len(dealt)
    pieces.append(Piece(first, shared[0].shape[0], True, True, 0, 1))
    pieces.append(Piece(first + 1, shared[1].shape[0], False, True, 0, 1))
    for part in range(2):
        for n, a in enumerate(split):
            pieces.append(Piece(first + len(shared) + n, a.shape[0], True, False, part, 2))
    pieces.append(Piece(first + 2, shared[2].shape[0], False, True, 0, 1))
    count = len(pieces)
    tok, width = dealt[0].shape
    sem = pltpu.SemaphoreType.DMA
    vmem = pl.BlockSpec(memory_space=pltpu.VMEM)
    return pl.pallas_call(
        functools.partial(fetch_kernel, sizes, pieces, len(ins), len(dealt)),
        in_specs=[pl.BlockSpec(memory_space=pl.ANY)] * len(ins) + [vmem],
        out_specs=[pl.BlockSpec(memory_space=pl.ANY)] * len(outs) + [vmem] * 5 + [pl.BlockSpec(memory_space=pl.ANY)] + [vmem] * 2,
        out_shape=outs
        + [
            jax.ShapeDtypeStruct((tok, width), BF),
            jax.ShapeDtypeStruct((tok, H * HD), BF),
            jax.ShapeDtypeStruct((WINDOW + tok, 2 * HD), BF),
            jax.ShapeDtypeStruct((tok, H * HD), BF),
            jax.ShapeDtypeStruct((tok // QBLK * (H // HEADS_STEP), 1, ROWS), F32),
            jax.ShapeDtypeStruct((2 * size_x - 1, tok, width), BF),
            jax.ShapeDtypeStruct((width, tok), BF),
            jax.ShapeDtypeStruct((H * HD, tok), BF),
        ],
        scratch_shapes=[
            pltpu.VMEM((tok, width), BF),
            pltpu.VMEM((width, H * HD), BF),
            pltpu.VMEM((width, 2 * HD), BF),
            pltpu.VMEM((size_x,) + gains.shape, BF),
            pltpu.VMEM((WINDOW + tok, 2 * HD), BF),
            sem((4,)),
            sem((WINDOW // tok,)),
            sem((WINDOW // tok,)),
            sem((2 * size_x,)),
            sem((2 * size_x,)),
        ]
        + [
            pltpu.VMEM((a.shape[0], o.shape[1]), BF)
            for a, o in zip(ins[len(dealt) : -1], outs[len(dealt) : -1])
        ]
        + [
            sem((len(ins), 2)),
            sem((len(ins),)),
            sem((len(dealt), n_ctx)),
            sem((len(dealt), n_ctx)),
            sem((size_x,)),
            sem((size_x,)),
            sem((count, size_x)),
            sem((count, size_x)),
            sem((count, size_x, 9)),
            sem((count, size_x, 9)),
        ],
        compiler_params=pltpu.CompilerParams(
            collective_id=1, has_side_effects=True, vmem_limit_bytes=60 * 1024 * 1024
        ),
        cost_estimate=pl.CostEstimate(
            flops=0, bytes_accessed=300 * 1024 * 1024, transcendentals=0
        ),
        name="fetch",
    )(*ins, low)


def mlp_kernel(sizes, own_ref, *refs):
    size_a, size_b, size_x = sizes
    ranks = 2 * size_x
    cots_in, refs = refs[:2], refs[2:]
    weights_in, refs = refs[:3], refs[3:]
    grad_ref, rows_out, dg_out, du_out, part_out, down_out, refs = *refs[:6], refs[6:]
    rows, cot, w_gate, w_up, w_down, hid, dg, du = refs[:8]
    to_core, in_core, to_x, in_x, total, part_stage, down_stage = refs[8:15]
    load_sem, ag_send, ag_recv, core_send, core_recv, x_send, x_recv, out_sem, stage_sem = refs[15:]
    ia, ib, ic, ix = (lax.axis_index(name) for name in ALL)
    hidden_units = w_down.shape[0]
    tok, width = own_ref.shape
    tiles, _, tile = total.shape
    unit = hid.shape[2] // (hid.shape[2] // 512 if hid.shape[2] % 512 == 0 else hid.shape[2] // 256)

    loads = [
        pltpu.make_async_copy(own_ref, rows.at[0], load_sem.at[0]),
        pltpu.make_async_copy(weights_in[0], w_gate, load_sem.at[1]),
        pltpu.make_async_copy(weights_in[1], w_up, load_sem.at[2]),
        pltpu.make_async_copy(
            weights_in[2].at[pl.ds(pl.multiple_of(ic * hidden_units, hidden_units), hidden_units), :],
            w_down,
            load_sem.at[3],
        ),
    ]
    loads.append(pltpu.make_async_copy(cots_in[0], cot.at[0], load_sem.at[4]))
    loads.append(pltpu.make_async_copy(cots_in[1], cot.at[pl.ds(1, ranks - 1)], load_sem.at[5]))
    for copy in loads:
        copy.start()

    partner = (ia, ib, 1 - ic, ix)

    def across(step):
        return ia, ib, ic, (ix + size_x + step) % size_x

    barrier = pltpu.get_barrier_semaphore()
    greeted = [partner] + [across(s) for s in range(1, size_x)]
    for device in greeted:
        pl.semaphore_signal(barrier, inc=1, device_id=device, device_id_type=MESH)
    pl.semaphore_wait(barrier, len(greeted))

    def remote(src, dst, sent, came, device):
        return pltpu.make_async_remote_copy(
            src_ref=src,
            dst_ref=dst,
            send_sem=sent,
            recv_sem=came,
            device_id=device,
            device_id_type=MESH,
        )

    def gather(b):
        if b == 1:
            return remote(own_ref, rows.at[1], ag_send.at[1], ag_recv.at[1], partner)
        if b % 2:
            return remote(rows.at[b - 1], rows.at[b], ag_send.at[b], ag_recv.at[b], partner)
        return remote(own_ref, rows.at[b], ag_send.at[b], ag_recv.at[b], across(b // 2))

    def core_copy(s):
        return remote(to_core.at[s], in_core.at[s], core_send.at[s], core_recv.at[s], partner)

    def x_copy(s, t):
        return remote(
            to_x.at[s, t], in_x.at[s, t], x_send.at[s, t], x_recv.at[s, t], across(-s)
        )

    def results(b):
        to = pl.ds(b * tok, tok)
        return [
            pltpu.make_async_copy(rows.at[b], rows_out.at[to, :], out_sem.at[0, b]),
            pltpu.make_async_copy(dg.at[b], dg_out.at[to, :], out_sem.at[1, b]),
            pltpu.make_async_copy(du.at[b], du_out.at[to, :], out_sem.at[2, b]),
        ]

    def forward(b):
        def step(t, carry):
            units = pl.ds(pl.multiple_of(t * unit, unit), unit)
            gate = mm(rows[b], w_gate[:, units])
            upward = mm(rows[b], w_up[:, units])
            d_hidden = mm_nt(cot[b], w_down[units, :])
            square = gate * gate
            bent = jnp.tanh(root * gate * (1.0 + cubic * square))
            half = 0.5 * (1.0 + bent)
            act = gate * half
            slope = half + 0.5 * gate * (1.0 - bent * bent) * root * (1.0 + 3.0 * cubic * square)
            hid[b, :, units] = (act * upward).astype(BF)
            dg[b, :, units] = (d_hidden * upward * slope).astype(BF)
            du[b, :, units] = (d_hidden * act).astype(BF)
            return carry

        lax.fori_loop(0, hid.shape[2] // unit, step, 0)
        for copy in results(b):
            copy.start()

    def backward(b):
        s, other = b // 2, b % 2
        if not other:
            core_copy(s).wait_recv()

        def step(t, carry):
            at = pl.ds(pl.multiple_of(t * tile, tile), tile)
            value = mm_nt(dg[b], w_gate[at, :]) + mm_nt(du[b], w_up[at, :])
            if other:
                to_core[s, t] = value.astype(BF)
                return carry
            value = value + in_core[s, t].astype(F32)
            if s:
                to_x[s, t] = value.astype(BF)
                x_copy(s, t).start()
            else:
                total[t] = value
            return carry

        lax.fori_loop(0, tiles, step, 0)
        if other:
            core_copy(s).start()

    def part_copy(b):
        return pltpu.make_async_copy(part_stage.at[b % 2], part_out.at[b], stage_sem.at[b % 2])

    def branch(b):
        if b >= 2:
            part_copy(b - 2).wait()

        def step(t, carry):
            at = pl.ds(pl.multiple_of(t * tile, tile), tile)
            part_stage[b % 2, :, at] = mm(hid[b], w_down[:, at]).astype(BF)
            return carry

        lax.fori_loop(0, tiles, step, 0)
        part_copy(b).start()

    depth = down_stage.shape[1]
    strips = hidden_units // depth

    def down_copy(t, slot):
        to = pl.ds(pl.multiple_of(t * depth, depth), depth)
        return pltpu.make_async_copy(down_stage.at[slot], down_out.at[to, :], stage_sem.at[2 + slot])

    def down_step(t, carry):
        slot = t % 2

        @pl.when(t >= 2)
        def _():
            down_copy(t - 2, slot).wait()

        units = pl.ds(pl.multiple_of(t * depth, depth), depth)
        value = mm_tn(hid[0, :, units], cot[0])
        for b in range(1, ranks):
            value = value + mm_tn(hid[b, :, units], cot[b])
        down_stage[slot] = value.astype(BF)
        down_copy(t, slot).start()
        return carry

    gather(1).start()
    for s in range(1, size_x):
        gather(2 * s).start()
    for copy in loads:
        copy.wait()
    forward(0)
    gather(1).wait_recv()
    forward(1)
    backward(1)
    for s in range(1, size_x):
        gather(2 * s).wait_recv()
        gather(2 * s + 1).start()
        forward(2 * s)
        gather(2 * s + 1).wait_recv()
        forward(2 * s + 1)
        backward(2 * s + 1)
        backward(2 * s)
    backward(0)
    lax.fori_loop(0, strips, down_step, 0)
    for b in range(ranks):
        branch(b)
    for s in range(1, size_x):
        for t in range(tiles):
            x_copy(s, t).wait()
    for t in range(tiles):
        value = total[t]
        for s in range(1, size_x):
            value = value + in_x[s, t].astype(F32)
        grad_ref[:, t * tile : (t + 1) * tile] = value
    for b in range(1, ranks):
        gather(b).wait_send()
    for s in range(size_x):
        core_copy(s).wait_send()
    for b in range(ranks):
        for copy in results(b):
            copy.wait()
    part_copy(ranks - 2).wait()
    part_copy(ranks - 1).wait()
    down_copy(strips - 2, (strips - 2) % 2).wait()
    down_copy(strips - 1, (strips - 1) % 2).wait()


def feed_forward(sizes, normed, cot, cot_rows, w_gate, w_up, down_weight):
    ranks = 2 * sizes[2]
    size_x = sizes[2]
    tok, width = normed.shape
    units = w_gate.shape[1]
    tile = 512
    tiles = width // tile
    sem = pltpu.SemaphoreType.DMA
    hbm = pl.BlockSpec(memory_space=pl.ANY)
    return pl.pallas_call(
        functools.partial(mlp_kernel, sizes),
        in_specs=[hbm] * 6,
        out_specs=[pl.BlockSpec(memory_space=pltpu.VMEM)] + [hbm] * 5,
        out_shape=[
            jax.ShapeDtypeStruct((tok, width), F32),
            jax.ShapeDtypeStruct((ranks * tok, width), BF),
            jax.ShapeDtypeStruct((ranks * tok, units), BF),
            jax.ShapeDtypeStruct((ranks * tok, units), BF),
            jax.ShapeDtypeStruct((ranks, tok, width), BF),
            jax.ShapeDtypeStruct((units, width), BF),
        ],
        scratch_shapes=[
            pltpu.VMEM((ranks, tok, width), BF),
            pltpu.VMEM((ranks, tok, width), BF),
            pltpu.VMEM((width, units), BF),
            pltpu.VMEM((width, units), BF),
            pltpu.VMEM((units, width), BF),
            pltpu.VMEM((ranks, tok, units), BF),
            pltpu.VMEM((ranks, tok, units), BF),
            pltpu.VMEM((ranks, tok, units), BF),
            pltpu.VMEM((size_x, tiles, tok, tile), BF),
            pltpu.VMEM((size_x, tiles, tok, tile), BF),
            pltpu.VMEM((size_x, tiles, tok, tile), BF),
            pltpu.VMEM((size_x, tiles, tok, tile), BF),
            pltpu.VMEM((tiles, tok, tile), F32),
            pltpu.VMEM((2, tok, width), BF),
            pltpu.VMEM((2, 256, width), BF),
            sem((6,)),
            sem((ranks,)),
            sem((ranks,)),
            sem((size_x,)),
            sem((size_x,)),
            sem((size_x, tiles)),
            sem((size_x, tiles)),
            sem((3, ranks)),
            sem((4,)),
        ],
        compiler_params=pltpu.CompilerParams(
            collective_id=2, has_side_effects=True, vmem_limit_bytes=62 * 1024 * 1024
        ),
        cost_estimate=pl.CostEstimate(
            flops=14 * ranks * tok * width * units,
            bytes_accessed=60 * 1024 * 1024,
            transcendentals=0,
        ),
        name="feed_forward",
    )(normed, cot, cot_rows, w_gate, w_up, down_weight)


class Job:
    def __init__(self, phase, left, right, rows, cols, by_rank):
        self.phase, self.left, self.right = phase, left, right
        self.rows, self.cols, self.by_rank = rows, cols, by_rank


def grads_kernel(sizes, jobs, *refs):
    size_a, size_b, size_x = sizes
    chips = size_a * size_b
    n_ctx = 2 * chips
    ranks = 2 * size_x
    count = len(jobs)
    ins, refs = refs[:13], refs[13:]
    outs, refs = refs[:count], refs[count:]
    down_out, refs = refs[0], refs[1:]
    dealt, refs = refs[:2], refs[2:]
    gain_out, refs = refs[0], refs[1:]
    held, refs = refs[:8], refs[8:]
    gain_ctx, gain_x, resid_in, part_own, part_core, part_x, down_passed, refs = *refs[:7], refs[7:]
    recv, refs = refs[:count], refs[count:]
    send, refs = refs[:count], refs[count:]
    done, refs = refs[:count], refs[count:]
    load_sem, group_send, group_recv, deal_send, deal_recv, part_sem = refs[:6]
    gain_send, gain_recv, send_sem, recv_sem, done_send, done_recv, own_sem = refs[6:]
    ia, ib, ic, ix = (lax.axis_index(name) for name in ALL)
    own = (ia * size_b + ib) * 2 + ic
    rank = ix * 2 + ic
    place = snake_place(ia, ib, size_a, size_b)

    def on_ring(step):
        return snake((place + 2 * chips + step) % chips, size_a, size_b)

    def member(k):
        return (ic + k) % 2, (ix + k // 2) % size_x

    def ctx_device(k):
        e = (own + k) % n_ctx
        return e // 2 // size_b, e // 2 % size_b, e % 2, ix

    def keeper(row_chunk):
        chip = row_chunk // ranks
        return chip // size_b, chip % size_b, (row_chunk // size_x) % 2, row_chunk % size_x

    kept = rank * chips + kept_slot(ia, ib, size_a, size_b)
    kept_id = keeper(kept)
    flat = own * size_x + ix
    from_rank = flat // chips
    from_slot = flat % chips
    half = chips // 2
    from_id = (
        (from_slot % half) // (size_b // 2),
        ((from_slot % half) % (size_b // 2)) * 2 + 1 - from_slot // half,
        from_rank % 2,
        from_rank // 2,
    )

    def remote(src, dst, sent, came, device):
        return pltpu.make_async_remote_copy(
            src_ref=src,
            dst_ref=dst,
            send_sem=sent,
            recv_sem=came,
            device_id=device,
            device_id_type=MESH,
        )

    loads = [pltpu.make_async_copy(ins[i], held[i], load_sem.at[i]) for i in range(3)]
    for copy in loads:
        copy.start()

    barrier = pltpu.get_barrier_semaphore()
    greeted = [ctx_device(k) for k in range(1, n_ctx)] + [from_id]
    greeted += [(ia, ib) + member(k) for k in range(2, ranks)]
    for device in greeted:
        pl.semaphore_signal(barrier, inc=1, device_id=device, device_id_type=MESH)
    pl.semaphore_wait(barrier, len(greeted))

    passed_on = (3, 5)

    def group_copy(i, k):
        c, x = member(k)
        src, dst = ins[i], held[i].at[k]
        target = x * 2 + c
        if i == 4:
            rows = held[i].shape[1]
            src = src.at[pl.ds(pl.multiple_of(target * rows, rows), rows), :]
        if i == 6:
            cols = held[i].shape[2]
            src = src.at[:, pl.ds(pl.multiple_of(target * cols, cols), cols)]
        if k == 0:
            return pltpu.make_async_copy(src, dst, load_sem.at[i])
        if k % 2 and k > 1 and i in passed_on:
            src, x = held[i].at[k - 1], ix
        return remote(src, dst, group_send.at[i, k], group_recv.at[i, k], (ia, ib, c, x))

    def deal_copy(t, k):
        e = (own + k) % n_ctx
        source = part_own.at[0] if t == 0 else ins[9]
        rows = source.shape[0] // n_ctx
        src = source.at[pl.ds(pl.multiple_of(e * rows, rows), rows), :]
        dst = dealt[t].at[pl.ds(pl.multiple_of(own * rows, rows), rows), :]
        if k == 0:
            return pltpu.make_async_copy(src, dst, load_sem.at[8 + t])
        return remote(src, dst, deal_send.at[t, k], deal_recv.at[t, k], ctx_device(k))

    def part_load(step):
        return pltpu.make_async_copy(ins[8].at[2 * step], part_own.at[step], part_sem.at[step])

    def part_core_copy(step):
        device = (ia, ib, 1 - ic, ix)
        src, dst = ins[8].at[2 * step + 1], part_core.at[step]
        return remote(src, dst, group_send.at[0, step], group_recv.at[0, step], device)

    def part_x_copy(step):
        device = (ia, ib, ic, (ix + size_x - step) % size_x)
        src, dst = part_own.at[step], part_x.at[step - 1]
        return remote(src, dst, group_send.at[1, step], group_recv.at[1, step], device)

    crossing = size_x == 2
    down_sem = (done_send.at[count, 0], done_recv.at[count, 0])
    down_copy = remote(ins[12], down_out, *down_sem, kept_id)
    if crossing:
        straight = kept % size_x == ix
        hop_sem = (done_send.at[count, 1], done_recv.at[count, 1])
        down_hop = remote(ins[12], down_passed, *hop_sem, (ia, ib, ic, 1 - ix))
        passed_id = keeper(((1 - ix) * 2 + ic) * chips + kept_slot(ia, ib, size_a, size_b))
        pass_sem = (done_send.at[count, 2], done_recv.at[count, 0])
        down_pass = remote(down_passed, down_out, *pass_sem, passed_id)

    resid_copy = pltpu.make_async_copy(ins[11], resid_in, load_sem.at[11])

    def gain_copy(k):
        src, dst = ins[10].at[(own + k) % n_ctx], gain_ctx.at[k]
        if k == 0:
            return pltpu.make_async_copy(src, dst, load_sem.at[10])
        return remote(src, dst, deal_send.at[2, k], deal_recv.at[2, k], ctx_device(k))

    def gain_copy_x(s):
        device = (ia, ib, ic, (ix + s) % size_x)
        return remote(gain_x.at[0], gain_x.at[s], gain_send.at[s], gain_recv.at[s], device)

    def ring_copy(j, way, step, parity):
        neighbour = on_ring(1 - 2 * way) + (ic, ix)
        return remote(
            send[j].at[way, parity],
            recv[j].at[way, step],
            send_sem.at[j, way, parity],
            recv_sem.at[j, way, step],
            neighbour,
        )

    def product(j, way, step):
        job = jobs[j]
        a, b = on_ring(step * (2 * way - 1))
        part = job.rows // chips
        cols = slice(way * job.cols // 2, (way + 1) * job.cols // 2)
        left, right = held[job.left], held[job.right]
        if job.phase == 0:
            start = pl.multiple_of((a * size_b + b) * part, part)
            return mm_tn(left[:, pl.ds(start, part)], right[:, cols])
        if job.by_rank:
            start = kept_slot(a, b, size_a, size_b) * part
            if left.shape[1] != job.rows:
                start = start + rank * job.rows
        else:
            start = (a * size_b + b) * part
        rows = pl.ds(pl.multiple_of(start, part), part)
        total = mm(left[0, rows, :], right[0, :, cols])
        for k in range(1, ranks):
            total = total + mm(left[k, rows, :], right[k, :, cols])
        return total

    def deliver(j):
        job = jobs[j]
        if job.by_rank:
            return [remote(done[j], outs[j], done_send.at[j, 0], done_recv.at[j, 0], kept_id)]
        part = job.rows // (chips * ranks)
        copies = []
        for k in range(ranks):
            c, x = member(k)
            start = pl.multiple_of((c * size_x + x) * part, part)
            src, dst = done[j].at[pl.ds(start, part), :], outs[j].at[rank]
            if k == 0:
                copies.append(pltpu.make_async_copy(src, dst, own_sem.at[j]))
            else:
                copies.append(
                    remote(src, dst, done_send.at[j, k], done_recv.at[j, k], (ia, ib, c, x))
                )
        return copies

    def begin(j):
        for way in range(2):
            send[j][way, 0] = product(j, way, 1).astype(BF)
            ring_copy(j, way, 0, 0).start()

    def advance(j, step):
        parity = step % 2
        for way in range(2):
            part = product(j, way, step + 1)
            ring_copy(j, way, step - 1, 1 - parity).wait_recv()
            part = part + recv[j][way, step - 1].astype(F32)

            @pl.when(step >= 2)
            def _():
                ring_copy(j, way, step - 2, parity).wait_send()

            send[j][way, parity] = part.astype(BF)
            ring_copy(j, way, step, parity).start()

    last = chips - 2

    def finish(j):
        cols = jobs[j].cols // 2
        for way in range(2):
            part = product(j, way, chips)
            ring_copy(j, way, last, last % 2).wait_recv()
            part = part + recv[j][way, last].astype(F32)
            done[j][:, way * cols : (way + 1) * cols] = part.astype(BF)
        for copy in deliver(j):
            copy.start()
        for way in range(2):
            ring_copy(j, way, last - 1, (last - 1) % 2).wait_send()
            ring_copy(j, way, last, last % 2).wait_send()

    early = [j for j in range(count) if jobs[j].phase == 0]
    late = [j for j in range(count) if jobs[j].phase == 1]
    lag = 3

    def early_step(step, carry):
        for j in early:
            advance(j, step)
        return carry

    def both_step(step, carry):
        for j in late:
            advance(j, step - lag)
        for j in early:
            advance(j, step)
        return carry

    def late_step(step, carry):
        for j in late:
            advance(j, step)
        return carry

    for copy in loads:
        copy.wait()
    for j in early:
        begin(j)
    for step in range(size_x):
        part_load(step).start()
        part_core_copy(step).start()
    for i in (6, 7, 5, 4, 3):
        for k in range(ranks):
            if not (k % 2 and k > 1 and i in passed_on):
                group_copy(i, k).start()
    resid_copy.start()
    for k in range(n_ctx):
        gain_copy(k).start()
    for k in range(n_ctx):
        deal_copy(1, k).start()
    if crossing:

        @pl.when(straight)
        def _():
            down_copy.start()

        @pl.when(jnp.logical_not(straight))
        def _():
            down_hop.start()

    else:
        down_copy.start()
    lax.fori_loop(1, 2, early_step, 0)
    for step in range(size_x):
        part_load(step).wait()
        part_core_copy(step).wait()
    for step in range(1, size_x):
        summed = part_own[step].astype(F32) + part_core[step].astype(F32)
        part_own[step] = summed.astype(BF)
        part_x_copy(step).start()
    lax.fori_loop(2, lag, early_step, 0)
    if crossing:

        @pl.when(straight)
        def _():
            down_hop.wait_recv()
            down_pass.start()

    for i in reversed(passed_on):
        for k in range(2, ranks, 2):
            group_copy(i, k).wait_recv()
            group_copy(i, k + 1).start()
    for k in range(n_ctx):
        gain_copy(k).wait()
    gain_x[0] = jnp.sum(gain_ctx[...], axis=0)
    for s in range(1, size_x):
        gain_copy_x(s).start()
    lax.fori_loop(lag, lag + 1, early_step, 0)
    for i in range(3, 8):
        for k in range(ranks):
            if k and k % 2 == 0 and i in passed_on:
                group_copy(i, k).wait_send()
            else:
                group_copy(i, k).wait()
    for j in late:
        begin(j)
    resid_copy.wait()
    summed = resid_in[...] + part_own[0].astype(F32) + part_core[0].astype(F32)
    for step in range(1, size_x):
        part_x_copy(step).wait()
        summed = summed + part_x[step - 1].astype(F32)
    part_own[0] = summed.astype(BF)
    for k in range(n_ctx):
        deal_copy(0, k).start()
    lax.fori_loop(lag + 1, last + 1, both_step, 0)
    for j in early:
        finish(j)
    lax.fori_loop(last + 1 - lag, last + 1, late_step, 0)
    for j in late:
        finish(j)
    for s in range(1, size_x):
        gain_copy_x(s).wait()
    gain_out[...] = jnp.sum(gain_x[...], axis=0)
    for t in range(2):
        for k in range(n_ctx):
            deal_copy(t, k).wait()
    down_copy.wait_recv()
    if crossing:

        @pl.when(straight)
        def _():
            down_copy.wait_send()
            down_pass.wait_send()

        @pl.when(jnp.logical_not(straight))
        def _():
            down_hop.wait_send()

    else:
        down_copy.wait_send()
    for j in range(count):
        for copy in deliver(j):
            copy.wait()


def sum_grads(sizes, ins):
    size_a, size_b, size_x = sizes
    chips = size_a * size_b
    ranks = 2 * size_x
    normed_mlp, d_gate, d_upward = ins[:3]
    width = normed_mlp.shape[1]
    tok = ins[5].shape[0]
    part_width = width // ranks
    jobs = [
        Job(0, 0, 1, width, d_gate.shape[1], False),
        Job(0, 0, 2, width, d_upward.shape[1], False),
        Job(1, 3, 6, width, part_width, False),
        Job(1, 4, 5, part_width, width, True),
        Job(1, 3, 7, part_width, 2 * HD, True),
    ]
    held = [pltpu.VMEM(a.shape, BF) for a in ins[:3]]
    held += [
        pltpu.VMEM((ranks,) + shape, BF)
        for shape in (
            (width, tok),
            (part_width, tok),
            (tok, width),
            (tok, part_width),
            (tok, 2 * HD),
        )
    ]
    outs, recv, send, done = [], [], [], []
    flops = 0
    for job in jobs:
        part = job.rows // chips
        if job.by_rank:
            outs.append(jax.ShapeDtypeStruct((part, job.cols), BF))
        else:
            outs.append(jax.ShapeDtypeStruct((ranks, part // ranks, job.cols), BF))
        recv.append(pltpu.VMEM((2, chips - 1, part, job.cols // 2), BF))
        send.append(pltpu.VMEM((2, 2, part, job.cols // 2), BF))
        done.append(pltpu.VMEM((part, job.cols), BF))
        flops += 2 * job.rows * job.cols * normed_mlp.shape[0]
    count = len(jobs)
    outs.append(jax.ShapeDtypeStruct(ins[12].shape, BF))
    outs += [jax.ShapeDtypeStruct((tok, width), BF)] * 2
    gain_shape = ins[10].shape[1:]
    outs.append(jax.ShapeDtypeStruct(gain_shape, F32))
    sem = pltpu.SemaphoreType.DMA
    return pl.pallas_call(
        functools.partial(grads_kernel, sizes, jobs),
        in_specs=[pl.BlockSpec(memory_space=pl.ANY)] * len(ins),
        out_specs=[pl.BlockSpec(memory_space=pl.ANY)] * (count + 3)
        + [pl.BlockSpec(memory_space=pltpu.VMEM)],
        out_shape=outs,
        scratch_shapes=held
        + [
            pltpu.VMEM((2 * chips,) + gain_shape, F32),
            pltpu.VMEM((size_x,) + gain_shape, F32),
            pltpu.VMEM((tok, width), F32),
            pltpu.VMEM((size_x, tok, width), BF),
            pltpu.VMEM((size_x, tok, width), BF),
            pltpu.VMEM((size_x - 1, tok, width), BF),
            pltpu.VMEM(ins[12].shape, BF),
        ]
        + recv
        + send
        + done
        + [
            sem((len(ins),)),
            sem((8, ranks)),
            sem((8, ranks)),
            sem((3, 2 * chips)),
            sem((3, 2 * chips)),
            sem((size_x,)),
            sem((size_x,)),
            sem((size_x,)),
            sem((count, 2, 2)),
            sem((count, 2, chips - 1)),
            sem((count + 1, ranks)),
            sem((count + 1, ranks)),
            sem((count,)),
        ],
        compiler_params=pltpu.CompilerParams(
            collective_id=0, has_side_effects=True, vmem_limit_bytes=63 * 1024 * 1024
        ),
        cost_estimate=pl.CostEstimate(
            flops=flops, bytes_accessed=400 * 1024 * 1024, transcendentals=0
        ),
        name="sum_grads",
    )(*ins)


def norm_stats(values):
    inv = lax.rsqrt(jnp.mean(values * values, axis=-1, keepdims=True) + epsilon)
    return values * inv, inv


def norm_back(unit, inv, gain, grad):
    scaled = grad * gain
    inner = jnp.mean(scaled * unit, axis=-1, keepdims=True)
    return inv * (scaled - unit * inner), jnp.sum(grad * unit, axis=0)


def on_device(
    sizes,
    tokens,
    lengths,
    dealing,
    attn_gain,
    query_weight,
    kv_weight,
    out_weight,
    mlp_gain,
    gate_weight,
    up_weight,
    down_weight,
    cotangent,
):
    size_a, size_b, size_x = sizes
    chips = size_a * size_b
    n_ctx = chips * 2
    ranks = 2 * size_x
    ia, ib, ic, ix = (lax.axis_index(name) for name in ALL)
    chip = ia * size_b + ib
    own = chip * 2 + ic
    flat = own * size_x + ix
    rank = ix * 2 + ic
    tok = tokens.shape[1]
    width = tokens.shape[2]
    piece = tok // n_ctx
    halo = WINDOW // tok

    def pick(array, index, axis=0):
        return lax.dynamic_index_in_dim(array, index, axis, keepdims=False)

    own_deal = pick(dealing[0], own)
    deal = (own_deal[:, None] == jnp.arange(tok, dtype=jnp.int32)[None, :]).astype(BF)

    gains = jnp.stack([attn_gain, mlp_gain]).reshape(-1, 128)
    stream = own * tok + jnp.arange(tok, dtype=jnp.int32)
    ends = jnp.cumsum(lengths[0])
    starts = jnp.max(jnp.where(stream[:, None] >= ends[None, :], ends[None, :], 0), axis=1)
    low = jnp.maximum(starts, stream - (WINDOW - 1)) - (own * tok - WINDOW)
    low = low.astype(jnp.int32)[None, :]
    inputs_low, cot, w_query, w_kv, w_out, w_gate, w_up, gains, *attended = fetch(
        sizes,
        [mm(deal, tokens[0]).astype(BF), mm(deal, cotangent[0]).astype(BF)],
        [query_weight, kv_weight, out_weight],
        [gate_weight, up_weight],
        gains,
        low,
    )
    _, queries, window, context, lse, cot_rows, normed_t, context_t = attended
    gains = gains.reshape(size_x, 2, -1).astype(F32)
    gain_one = gains[:, 0].reshape(-1)
    gain_two = gains[:, 1].reshape(-1)


    inputs = inputs_low.astype(F32)
    unit_one, inv_one = norm_stats(inputs)
    resid = inputs + mm(context, w_out)

    unit_two, inv_two = norm_stats(resid)
    d_normed_mlp, mlp_rows, d_gate, d_upward, mlp_parts, down_grad = feed_forward(
        sizes, (unit_two * gain_two).astype(BF), cot, cot_rows, w_gate, w_up, down_weight
    )
    d_resid_part, mlp_gain_grad = norm_back(unit_two, inv_two, gain_two, d_normed_mlp)
    d_resid = cot.astype(F32) + d_resid_part
    d_branch = d_resid.astype(BF)

    d_queries, d_pairs, down_sum, d_normed = attend_back(
        sizes, queries, window, low, d_branch, lse, down_grad, w_out, w_query, w_kv
    )
    d_inputs, attn_gain_grad = norm_back(unit_one, inv_one, gain_one, d_normed)
    gain_part = width // (n_ctx * size_x)
    gain_grads = jnp.stack([attn_gain_grad, mlp_gain_grad]).reshape(2, n_ctx, size_x, gain_part)
    gain_grads = gain_grads.transpose(1, 2, 0, 3).reshape(n_ctx, -1)
    gain_grads = jnp.pad(gain_grads, ((0, 0), (0, 1024 - gain_grads.shape[1])))
    sums = sum_grads(
        sizes,
        [
            mlp_rows,
            d_gate,
            d_upward,
            normed_t,
            context_t,
            d_branch,
            d_queries,
            d_pairs,
            mlp_parts,
            (d_resid + d_inputs).astype(BF),
            gain_grads.reshape(n_ctx, 8, 128),
            resid,
            down_sum,
        ],
    )
    gate_grad, up_grad, query_grad = (
        v.transpose(1, 0, 2).reshape(v.shape[1], -1).astype(F32) for v in sums[:3]
    )
    out_grad, kv_grad, down_grad = (v.astype(F32) for v in sums[3:6])
    block_output = mm_tn(deal, sums[6]).astype(BF)
    token_grad = mm_tn(deal, sums[7])
    gain_grads = lax.dynamic_slice(sums[8].reshape(-1), (ix * 2 * gain_part,), (2 * gain_part,))
    attn_gain_grad, mlp_gain_grad = gain_grads[:gain_part], gain_grads[gain_part:]
    return (
        block_output[None],
        token_grad[None],
        attn_gain_grad,
        query_grad,
        kv_grad,
        out_grad,
        mlp_gain_grad,
        gate_grad,
        up_grad,
        down_grad,
    )


def solution(mesh):
    n_ctx, size_x = mesh.shape["ctx"], mesh.shape["fsdp"]
    chips = n_ctx // 2
    size_a = 4 if chips % 4 == 0 else chips
    size_b = chips // size_a
    fine = Mesh(mesh.devices.reshape(size_a, size_b, 2, size_x), ALL)
    rows = P("x", CTX, None)
    split = P("x", None)
    every = P(ALL)
    matrix = P(ALL, None)
    return jax.shard_map(
        functools.partial(on_device, (size_a, size_b, size_x)),
        mesh=fine,
        in_specs=(
            rows,
            split,
            P("x", None, None),
            P("x"),
            split,
            split,
            split,
            P("x"),
            split,
            split,
            split,
            rows,
        ),
        out_specs=(rows, rows, every, matrix, matrix, matrix, every, matrix, matrix, matrix),
        check_vma=False,
    )
```

```python
import functools

import jax
import jax.numpy as jnp
import numpy as np
from jax import lax
from jax.experimental import pallas as pl
from jax.experimental.pallas import tpu as pltpu
from jax.sharding import Mesh
from jax.sharding import PartitionSpec as P

H = 16
HD = 128
WINDOW = 1024
QBLK = 128
HEADS_STEP = 4
SPAN = WINDOW + QBLK
ROWS = HEADS_STEP * QBLK

epsilon = 1e-06
neg_large = -1e30
scale = HD ** (-0.5)
root = (2.0 / np.pi) ** 0.5
cubic = 0.044715
BF = jnp.bfloat16
F32 = jnp.float32
CTX = ("a", "b", "c")
ALL = ("a", "b", "c", "x")
MESH = pl.DeviceIdType.MESH


def mm(left, right):
    return jnp.dot(left, right, preferred_element_type=F32)


def mm_tn(left, right):
    return lax.dot_general(left, right, (((0,), (0,)), ((), ())), preferred_element_type=F32)


def mm_nt(left, right):
    return lax.dot_general(left, right, (((1,), (1,)), ((), ())), preferred_element_type=F32)


def stack_heads(block):
    return jnp.concatenate([block[:, h * HD : (h + 1) * HD] for h in range(HEADS_STEP)], 0)


def unstack_heads(block_t):
    return jnp.concatenate(
        [block_t[:, h * QBLK : (h + 1) * QBLK].T for h in range(HEADS_STEP)], 1
    )


def bias_of(lo, qb):
    key = lax.broadcasted_iota(jnp.int32, (SPAN, QBLK), 0) + qb * QBLK
    query = lax.broadcasted_iota(jnp.int32, (SPAN, QBLK), 1) + (WINDOW + qb * QBLK)
    allowed = (key >= lo) & (key <= query)
    bias = jnp.where(allowed, 0.0, neg_large).astype(F32)
    return jnp.concatenate([bias] * HEADS_STEP, 1)


def attend_block(bias, queries, keys, values):
    scores = mm_nt(keys, queries) * scale + bias
    top = jnp.max(scores, axis=0, keepdims=True)
    raised = jnp.exp(scores - top)
    total = jnp.sum(raised, axis=0, keepdims=True)
    return mm_tn(values, raised.astype(BF)) * (1.0 / total), top + jnp.log(total)


def snake(pos, size_a, size_b):
    if size_b == 1:
        return pos, pos * 0
    down = pos // size_a
    first = 1 - (down + 7) // 8
    q = (pos - size_a) * (1 - first)
    a_up = size_a - 1 - q // (size_b - 1)
    k = q % (size_b - 1)
    odd = a_up % 2
    b_up = odd * (1 + k) + (1 - odd) * (size_b - 1 - k)
    return first * pos + (1 - first) * a_up, (1 - first) * b_up


def snake_place(a, b, size_a, size_b):
    if size_b == 1:
        return a
    moved = (b + size_b - 1) // size_b
    odd = a % 2
    along = odd * (b - 1) + (1 - odd) * (size_b - 1 - b)
    return (1 - moved) * a + moved * (size_a + (size_a - 1 - a) * (size_b - 1) + along)


def kept_slot(a, b, size_a, size_b):
    half = size_a * size_b // 2
    return (1 - b % 2) * half + a * (size_b // 2) + b // 2


def back_kernel(sizes, low_ref, q_ref, kv_ref, branch_ref, lse_ref, down_in, *refs):
    size_a, size_b, size_x = sizes
    weights_in, refs = refs[:3], refs[3:]
    dq_ref, pairs_ref, sum_ref, normed_ref, refs = *refs[:4], refs[4:]
    w_out, w_query, w_kv, do_ref, refs = *refs[:4], refs[4:]
    dkv, down, recv, send, halo_out, halo_in = refs[:6]
    load_sem, send_sem, recv_sem, halo_send, halo_recv = refs[6:]
    chips = size_a * size_b
    n_ctx = chips * 2
    ia, ib, ic, ix = (lax.axis_index(name) for name in ALL)
    own = (ia * size_b + ib) * 2 + ic
    place = snake_place(ia, ib, size_a, size_b)
    tok = q_ref.shape[0]
    halo = WINDOW // tok
    groups = H // HEADS_STEP
    blocks = tok // QBLK * groups
    part = down.shape[0] // chips
    quarter = down.shape[1] // 4
    chains = [(way, sub) for way in range(2) for sub in range(2)]
    last = chips - 2

    loading = pltpu.make_async_copy(down_in, down, load_sem.at[0])
    loading.start()
    weights = [
        pltpu.make_async_copy(src, dst, load_sem.at[1 + n])
        for n, (src, dst) in enumerate(zip(weights_in, (w_out, w_query, w_kv)))
    ]
    for copy in weights:
        copy.start()
    dkv[...] = jnp.zeros_like(dkv)

    def on_ring(step):
        return snake((place + 2 * chips + step) % chips, size_a, size_b)

    def ctx_device(step):
        e = (own + n_ctx + step) % n_ctx
        return e // 2 // size_b, e // 2 % size_b, e % 2, ix

    barrier = pltpu.get_barrier_semaphore()
    for k in range(1, n_ctx):
        pl.semaphore_signal(barrier, inc=1, device_id=ctx_device(k), device_id_type=MESH)
    pl.semaphore_wait(barrier, n_ctx - 1)

    def remote(src, dst, sent, came, device):
        return pltpu.make_async_remote_copy(
            src_ref=src,
            dst_ref=dst,
            send_sem=sent,
            recv_sem=came,
            device_id=device,
            device_id_type=MESH,
        )

    def ring_copy(way, sub, step, parity):
        return remote(
            send.at[way, sub, parity],
            recv.at[way, sub, step],
            send_sem.at[way, sub, parity],
            recv_sem.at[way, sub, step],
            on_ring(1 - 2 * way) + (ic, ix),
        )

    def columns(way, sub):
        return slice((2 * way + sub) * quarter, (2 * way + sub + 1) * quarter)

    def chunk(way, sub, step):
        a, b = on_ring(step * (2 * way - 1))
        rows = pl.ds(pl.multiple_of(kept_slot(a, b, size_a, size_b) * part, part), part)
        return down[rows, columns(way, sub)]

    def advance(step):
        parity = step % 2
        for way, sub in chains:
            value = chunk(way, sub, step + 1).astype(F32)
            ring_copy(way, sub, step - 1, 1 - parity).wait_recv()
            value = value + recv[way, sub, step - 1].astype(F32)

            @pl.when(step >= 2)
            def _():
                ring_copy(way, sub, step - 2, parity).wait_send()

            send[way, sub, parity] = value.astype(BF)
            ring_copy(way, sub, step, parity).start()

    def attend_step(t):
        qb, hg = t // groups, t % groups
        width = HEADS_STEP * HD
        block = pl.ds(pl.multiple_of(qb * QBLK, QBLK), QBLK)
        cols = pl.ds(pl.multiple_of(hg * width, width), width)
        rows = pl.ds(pl.multiple_of(qb * QBLK, QBLK), SPAN)
        keys = kv_ref[rows, :HD]
        values = kv_ref[rows, HD:]
        queries = stack_heads(q_ref[block, cols])
        d_out = stack_heads(do_ref[block, cols])
        scores = mm_nt(keys, queries) * scale + bias_of(low_ref[qb], qb)
        probs = jnp.exp(scores - lse_ref[t])
        d_probs = mm_nt(values, d_out)
        delta = jnp.sum(probs * d_probs, axis=0, keepdims=True)
        d_scores = (probs * (d_probs - delta)).astype(BF)
        dq_ref[block, cols] = unstack_heads(mm_tn(keys, d_scores) * scale).astype(BF)
        dkv[rows, :HD] += mm(d_scores, queries) * scale
        dkv[rows, HD:] += mm(probs.astype(BF), d_out)

    def halo_copy(k):
        sems = (halo_send.at[k - 1], halo_recv.at[k - 1])
        return remote(halo_out.at[k - 1], halo_in.at[k - 1], *sems, ctx_device(-k))

    def both(step, carry):
        advance(step)
        attend_step(2 * step - 2)
        attend_step(2 * step - 1)
        return carry

    def alone(step, carry):
        advance(step)
        return carry

    tile = 512

    def context_step(t, carry):
        at = pl.ds(pl.multiple_of(t * tile, tile), tile)
        do_ref[:, at] = mm_nt(branch_ref[...], w_out[at, :]).astype(BF)
        return carry

    def normed_step(t, carry):
        at = pl.ds(pl.multiple_of(t * tile, tile), tile)
        normed_ref[:, at] = mm_nt(dq_ref[...], w_query[at, :]) + mm_nt(pairs_ref[...], w_kv[at, :])
        return carry

    loading.wait()
    for way, sub in chains:
        send[way, sub, 0] = chunk(way, sub, 1)
        ring_copy(way, sub, 0, 0).start()
    weights[0].wait()
    lax.fori_loop(0, w_out.shape[0] // tile, context_step, 0)
    busy = blocks // 2
    lax.fori_loop(1, busy + 1, both, 0)
    for k in range(1, halo + 1):

        @pl.when(own >= k)
        def _():
            halo_out[k - 1] = dkv[(halo - k) * tok : (halo - k + 1) * tok, :].astype(BF)
            halo_copy(k).start()

    lax.fori_loop(busy + 1, busy + 2, alone, 0)
    for k in range(1, halo + 1):

        @pl.when(own + k < n_ctx)
        def _():
            halo_copy(k).wait_recv()
            dkv[WINDOW:, :] += halo_in[k - 1].astype(F32)

    pairs_ref[...] = dkv[WINDOW:, :].astype(BF)
    for copy in weights[1:]:
        copy.wait()
    lax.fori_loop(0, w_query.shape[0] // tile, normed_step, 0)
    lax.fori_loop(busy + 2, last + 1, alone, 0)
    for way, sub in chains:
        value = chunk(way, sub, chips).astype(F32)
        ring_copy(way, sub, last, last % 2).wait_recv()
        value = value + recv[way, sub, last].astype(F32)
        sum_ref[:, columns(way, sub)] = value.astype(BF)
    for way, sub in chains:
        ring_copy(way, sub, last - 1, (last - 1) % 2).wait_send()
        ring_copy(way, sub, last, last % 2).wait_send()
    for k in range(1, halo + 1):

        @pl.when(own >= k)
        def _():
            halo_copy(k).wait_send()


def attend_back(sizes, queries, window, low, d_branch, lse, down, w_out, w_query, w_kv):
    chips = sizes[0] * sizes[1]
    tok = queries.shape[0]
    halo = WINDOW // tok
    part, width = down.shape[0] // chips, down.shape[1]
    sem = pltpu.SemaphoreType.DMA
    vmem = pl.BlockSpec(memory_space=pltpu.VMEM)
    return pl.pallas_call(
        functools.partial(back_kernel, sizes),
        in_specs=[vmem] * 5 + [pl.BlockSpec(memory_space=pl.ANY)] * 4,
        out_specs=[vmem] * 4,
        out_shape=[
            jax.ShapeDtypeStruct((tok, H * HD), BF),
            jax.ShapeDtypeStruct((tok, 2 * HD), BF),
            jax.ShapeDtypeStruct((part, width), BF),
            jax.ShapeDtypeStruct((tok, width), F32),
        ],
        scratch_shapes=[
            pltpu.VMEM(w_out.shape, BF),
            pltpu.VMEM(w_query.shape, BF),
            pltpu.VMEM(w_kv.shape, BF),
            pltpu.VMEM((tok, H * HD), BF),
            pltpu.VMEM((WINDOW + tok, 2 * HD), F32),
            pltpu.VMEM(down.shape, BF),
            pltpu.VMEM((2, 2, chips - 1, part, width // 4), BF),
            pltpu.VMEM((2, 2, 2, part, width // 4), BF),
            pltpu.VMEM((halo, tok, 2 * HD), BF),
            pltpu.VMEM((halo, tok, 2 * HD), BF),
            sem((4,)),
            sem((2, 2, 2)),
            sem((2, 2, chips - 1)),
            sem((halo,)),
            sem((halo,)),
        ],
        compiler_params=pltpu.CompilerParams(
            collective_id=3, has_side_effects=True, vmem_limit_bytes=60 * 1024 * 1024
        ),
        cost_estimate=pl.CostEstimate(
            flops=10 * tok * H * HD * SPAN, bytes_accessed=100 * 1024 * 1024, transcendentals=0
        ),
        name="attend_back",
    )(low.reshape(tok // QBLK, 1, QBLK), queries, window, d_branch, lse, down, w_out, w_query, w_kv)


class Piece:
    def __init__(self, at, rows, square, shared, part, parts):
        self.at, self.rows, self.square, self.shared = at, rows, square, shared
        self.part, self.parts = part, parts
        self.relays = [0, 1, 2, 3] if square else []
        if shared:
            self.relays += [4, 5, 6, 7, 8] if square else [4]


def fetch_kernel(sizes, pieces, n_in, n_dealt, *refs):
    size_a, size_b, size_x = sizes
    n_ctx = size_a * size_b * 2
    ins, low_ref, refs = refs[:n_in], refs[n_in], refs[n_in + 1 :]
    outs, refs = refs[:n_in], refs[n_in:]
    normed_ref, query_ref, window_out, context_ref, lse_ref, cot_rows, refs = *refs[:6], refs[6:]
    normed_t_ref, context_t_ref, refs = *refs[:2], refs[2:]
    tok_in, w_query, w_kv, gain_in, window, refs = *refs[:5], refs[5:]
    load_sem, halo_send, halo_recv, cot_send, cot_recv, refs = *refs[:5], refs[5:]
    n_weights = n_in - n_dealt - 1
    stages, refs = refs[:n_weights], refs[n_weights:]
    keep_sem, own_sem, deal_send, deal_recv, gain_send, gain_recv = refs[:6]
    x_send, x_recv, relay_send, relay_recv = refs[6:]
    ia, ib, ic, ix = (lax.axis_index(name) for name in ALL)
    own = (ia * size_b + ib) * 2 + ic
    rank = ix * 2 + ic
    pa, pb = ia % 2, ib % 2
    other_a, other_b = ia + 1 - 2 * pa, ib + 1 - 2 * pb
    corner = pa * 2 + pb
    corner_a, corner_b, corner_d = (1 - pa) * 2 + pb, pa * 2 + 1 - pb, 3 - corner

    barrier = pltpu.get_barrier_semaphore()
    greeted = []
    for k in range(1, n_ctx):
        e = (own + k) % n_ctx
        greeted.append((e // 2 // size_b, e // 2 % size_b, e % 2, ix))
    for s in range(1, size_x):
        greeted.append((ia, ib, ic, (ix + s) % size_x))
    for device in greeted:
        pl.semaphore_signal(barrier, inc=1, device_id=device, device_id_type=MESH)
    pl.semaphore_wait(barrier, len(greeted))

    def remote(src, dst, send, recv, device):
        return pltpu.make_async_remote_copy(
            src_ref=src,
            dst_ref=dst,
            send_sem=send,
            recv_sem=recv,
            device_id=device,
            device_id_type=MESH,
        )

    def x_copy(i, s):
        p = pieces[i]
        shard, full = ins[p.at], outs[p.at]
        target = (ix + s) % size_x
        height = shard.shape[0]
        rows, start = region(p, corner, ic)
        if p.shared:
            src = shard.at[pl.ds(start, rows), :]
        else:
            cols = full.shape[1]
            at = pl.multiple_of((target * 2 + ic) * cols, cols)
            src = shard.at[pl.ds(start, rows), pl.ds(at, cols)]
        dst = full.at[pl.ds(pl.multiple_of(ix * height + start, rows), rows), :]
        return remote(src, dst, x_send.at[i, s], x_recv.at[i, s], (ia, ib, ic, target))

    def region(p, which, core):
        owner = which if p.square else 0
        owners = 4 if p.square else 1
        if p.shared:
            owner, owners = owner * 2 + core, owners * 2
        rows = p.rows // (owners * p.parts)
        return rows, pl.multiple_of((owner * p.parts + p.part) * rows, rows)

    def landed(i, s, which, core, half=None):
        p = pieces[i]
        rows, start = region(p, which, core)
        start = start + (ix + size_x - s) % size_x * p.rows
        if half is not None:
            rows = rows // 2
            start = start + half * rows
        return outs[p.at].at[pl.ds(pl.multiple_of(start, rows), rows), :]

    def relay(i, s, kind, incoming=False):
        sem = (relay_send.at[i, s, kind], relay_recv.at[i, s, kind])
        if kind < 4:
            device = (other_a, ib, ic, ix) if kind in (1, 2) else (ia, other_b, ic, ix)
            sent = (
                landed(i, s, corner, ic),
                landed(i, s, corner, ic),
                landed(i, s, corner_b, ic, 0),
                landed(i, s, corner_a, ic, 1),
            )[kind]
            came = (
                landed(i, s, corner_b, ic),
                landed(i, s, corner_a, ic),
                landed(i, s, corner_d, ic, 0),
                landed(i, s, corner_d, ic, 1),
            )[kind]
        else:
            device = (ia, ib, 1 - ic, ix)
            which, half = ((corner, None), (corner_b, None), (corner_a, None), (corner_d, 0), (corner_d, 1))[
                kind - 4
            ]
            sent = landed(i, s, which, ic, half)
            came = landed(i, s, which, 1 - ic, half)
        ref = came if incoming else sent
        return remote(ref, ref, *sem, device)

    rows = ins[0].shape[0] // n_ctx

    def deal_copy(t, k):
        e = (own + k) % n_ctx
        src = ins[t].at[pl.ds(pl.multiple_of(e * rows, rows), rows), :]
        dst = outs[t].at[pl.ds(pl.multiple_of(own * rows, rows), rows), :]
        if k == 0:
            return pltpu.make_async_copy(src, dst, own_sem.at[t])
        device = (e // 2 // size_b, e // 2 % size_b, e % 2, ix)
        return remote(src, dst, deal_send.at[t, k], deal_recv.at[t, k], device)

    g = n_in - 1

    def gain_copy(s):
        if s == 0:
            return pltpu.make_async_copy(ins[g], outs[g].at[ix], own_sem.at[g])
        device = (ia, ib, ic, (ix + s) % size_x)
        return remote(ins[g], outs[g].at[ix], gain_send.at[s], gain_recv.at[s], device)

    def keep_copy(w, out):
        shard, full = ins[w], outs[w]
        stage = stages[w - n_dealt]
        height = shard.shape[0]
        sem = keep_sem.at[w, out]
        if out:
            dst = full.at[pl.ds(pl.multiple_of(ix * height, height), height), :]
            return pltpu.make_async_copy(stage, dst, sem)
        src = shard
        if full.shape[1] != shard.shape[1]:
            cols = full.shape[1]
            src = shard.at[:, pl.ds(pl.multiple_of(rank * cols, cols), cols)]
        return pltpu.make_async_copy(src, stage, sem)

    tok = tok_in.shape[0]
    halo = WINDOW // tok
    at_query, at_kv = n_dealt, n_dealt + 1

    def load(src, dst, n):
        copy = pltpu.make_async_copy(src, dst, load_sem.at[n])
        copy.start()
        copy.wait()

    def core_parts_in(i):
        for s in range(1, size_x):
            for kind in pieces[i].relays:
                if kind >= 4:
                    relay(i, s, kind, True).wait_recv()
        keep_copy(pieces[i].at, 1).wait()

    def halo_copy(k):
        e = (own + k) % n_ctx
        device = (e // 2 // size_b, e // 2 % size_b, e % 2, ix)
        src = window.at[pl.ds(WINDOW, tok), :]
        dst = window.at[pl.ds((halo - k) * tok, tok), :]
        return remote(src, dst, halo_send.at[k - 1], halo_recv.at[k - 1], device)

    def normalise():
        for k in range(n_ctx):
            deal_copy(0, k).wait()
        for s in range(size_x):
            gain_copy(s).wait()
        load(outs[0], tok_in, 0)
        load(outs[g], gain_in, 1)
        gain = []
        for x in range(size_x):
            values = gain_in[x].astype(F32)
            gain += [values[r : r + 1, :] for r in range(values.shape[0] // 2)]
        values = tok_in[...].astype(F32)
        unit, _ = norm_stats(values)
        normed_ref[...] = (unit * jnp.concatenate(gain, 1)).astype(BF)

    def transpose():
        def step(t, carry):
            at = pl.ds(pl.multiple_of(t * HD, HD), HD)
            normed_t_ref[at, :] = normed_ref[:, at].astype(F32).T.astype(BF)
            return carry

        lax.fori_loop(0, normed_ref.shape[1] // HD, step, 0)

    def keys_values():
        core_parts_in(1)
        load(outs[at_kv], w_kv, 2)
        window[WINDOW:, :] = mm(normed_ref[...], w_kv[...]).astype(BF)
        for k in range(1, halo + 1):

            @pl.when(own + k < n_ctx)
            def _():
                halo_copy(k).start()

            @pl.when(own < k)
            def _():
                window[(halo - k) * tok : (halo - k + 1) * tok, :] = jnp.zeros((tok, 2 * HD), BF)

    def project():
        core_parts_in(0)
        load(outs[at_query], w_query, 3)

        def step(t, carry):
            cols = pl.ds(pl.multiple_of(t * 512, 512), 512)
            query_ref[:, cols] = mm(normed_ref[...], w_query[:, cols]).astype(BF)
            return carry

        lax.fori_loop(0, H * HD // 512, step, 0)

    def halo_in():
        for k in range(1, halo + 1):

            @pl.when(own >= k)
            def _():
                halo_copy(k).wait_recv()

    def cot_copy(b):
        sems = (cot_send.at[b], cot_recv.at[b])
        if b % 2:
            src = outs[1] if b == 1 else cot_rows.at[b - 2]
            return remote(src, cot_rows.at[b - 1], *sems, (ia, ib, 1 - ic, ix))
        device = (ia, ib, ic, (ix + b // 2) % size_x)
        return remote(outs[1], cot_rows.at[b - 1], *sems, device)

    def spread_cotangent():
        for k in range(n_ctx):
            deal_copy(1, k).wait()
        for s in range(1, size_x):
            cot_copy(2 * s).start()
        cot_copy(1).start()

    def attend(qb):
        low = low_ref[:, qb * QBLK : (qb + 1) * QBLK]
        bias = bias_of(low, qb)
        keys = window[qb * QBLK : qb * QBLK + SPAN, :HD]
        values = window[qb * QBLK : qb * QBLK + SPAN, HD:]
        rows = slice(qb * QBLK, (qb + 1) * QBLK)

        def step(t, carry):
            width = HEADS_STEP * HD
            cols = pl.ds(pl.multiple_of(t * width, width), width)
            out_t, lse = attend_block(bias, stack_heads(query_ref[rows, cols]), keys, values)
            context_ref[rows, cols] = unstack_heads(out_t).astype(BF)
            for h in range(HEADS_STEP):
                at = pl.ds(pl.multiple_of((t * HEADS_STEP + h) * HD, HD), HD)
                context_t_ref[at, rows] = out_t[:, h * QBLK : (h + 1) * QBLK].astype(BF)
            lse_ref[qb * (H // HEADS_STEP) + t] = lse
            return carry

        lax.fori_loop(0, H // HEADS_STEP, step, 0)

    blocks = tok // QBLK
    tasks = {2 * size_x - 1: [normalise, keys_values], 2 * size_x: [spread_cotangent, project]}
    for qb in range(blocks):
        task = functools.partial(attend, qb)
        tasks[2 * size_x + 1 + qb] = [halo_in, task] if qb == 0 else [task]

    tasks[2 * size_x + 1 + blocks] = [transpose]
    ahead = 4
    order = [(i, s) for i in range(len(pieces)) for s in range(1, size_x)]
    for k in range(n_ctx):
        deal_copy(0, k).start()
    for s in range(size_x):
        gain_copy(s).start()
    for i, s in order[:ahead]:
        x_copy(i, s).start()
    for t in range(1, n_dealt):
        for k in range(n_ctx):
            deal_copy(t, k).start()
    for w in range(n_dealt, n_dealt + n_weights):
        keep_copy(w, 0).start()

    for n in range(len(order) + 2):
        if n < n_weights:
            keep_copy(n_dealt + n, 0).wait()
            keep_copy(n_dealt + n, 1).start()
        if n < len(order):
            i, s = order[n]
            x_copy(i, s).wait_recv()
            for kind in (0, 1, 4):
                if kind in pieces[i].relays:
                    relay(i, s, kind).start()
            if n + ahead < len(order):
                x_copy(i, s).wait_send()
                x_copy(*order[n + ahead]).start()
        if 1 <= n <= len(order) and pieces[order[n - 1][0]].square:
            i, s = order[n - 1]
            relay(i, s, 0, True).wait_recv()
            relay(i, s, 2).start()
            relay(i, s, 1, True).wait_recv()
            relay(i, s, 3).start()
            if pieces[i].shared:
                relay(i, s, 5).start()
                relay(i, s, 6).start()
        if n >= 2 and pieces[order[n - 2][0]].square:
            i, s = order[n - 2]
            relay(i, s, 2, True).wait_recv()
            relay(i, s, 3, True).wait_recv()
            if pieces[i].shared:
                relay(i, s, 7).start()
                relay(i, s, 8).start()
        for task in tasks.get(n, []):
            task()

    for s in range(1, size_x):
        cot_copy(2 * s).wait_recv()
        cot_copy(2 * s + 1).start()
    window_out[...] = window[...]
    for k in range(1, halo + 1):

        @pl.when(own + k < n_ctx)
        def _():
            halo_copy(k).wait_send()

    for n, (i, s) in enumerate(order):
        if n + ahead >= len(order):
            x_copy(i, s).wait_send()
        for kind in pieces[i].relays:
            relay(i, s, kind).wait_send()
            if kind >= 4 and i > 1:
                relay(i, s, kind, True).wait_recv()
    for b in range(1, 2 * size_x):
        cot_copy(b).wait_send()
        if b % 2:
            cot_copy(b).wait_recv()
    for w in range(n_dealt + 2, n_dealt + n_weights):
        keep_copy(w, 1).wait()


def fetch(sizes, dealt, shared, split, gains, low):
    size_a, size_b, size_x = sizes
    n_ctx = size_a * size_b * 2
    ins = dealt + shared + split + [gains]
    outs = [jax.ShapeDtypeStruct(a.shape, BF) for a in dealt]
    outs += [jax.ShapeDtypeStruct((size_x * a.shape[0], a.shape[1]), BF) for a in shared]
    outs += [
        jax.ShapeDtypeStruct((size_x * a.shape[0], a.shape[1] // (2 * size_x)), BF) for a in split
    ]
    outs.append(jax.ShapeDtypeStruct((size_x,) + gains.shape, BF))
    pieces = []
    first = len(dealt)
    pieces.append(Piece(first, shared[0].shape[0], True, True, 0, 1))
    pieces.append(Piece(first + 1, shared[1].shape[0], False, True, 0, 1))
    for part in range(2):
        for n, a in enumerate(split):
            pieces.append(Piece(first + len(shared) + n, a.shape[0], True, False, part, 2))
    pieces.append(Piece(first + 2, shared[2].shape[0], False, True, 0, 1))
    count = len(pieces)
    tok, width = dealt[0].shape
    sem = pltpu.SemaphoreType.DMA
    vmem = pl.BlockSpec(memory_space=pltpu.VMEM)
    return pl.pallas_call(
        functools.partial(fetch_kernel, sizes, pieces, len(ins), len(dealt)),
        in_specs=[pl.BlockSpec(memory_space=pl.ANY)] * len(ins) + [vmem],
        out_specs=[pl.BlockSpec(memory_space=pl.ANY)] * len(outs) + [vmem] * 5 + [pl.BlockSpec(memory_space=pl.ANY)] + [vmem] * 2,
        out_shape=outs
        + [
            jax.ShapeDtypeStruct((tok, width), BF),
            jax.ShapeDtypeStruct((tok, H * HD), BF),
            jax.ShapeDtypeStruct((WINDOW + tok, 2 * HD), BF),
            jax.ShapeDtypeStruct((tok, H * HD), BF),
            jax.ShapeDtypeStruct((tok // QBLK * (H // HEADS_STEP), 1, ROWS), F32),
            jax.ShapeDtypeStruct((2 * size_x - 1, tok, width), BF),
            jax.ShapeDtypeStruct((width, tok), BF),
            jax.ShapeDtypeStruct((H * HD, tok), BF),
        ],
        scratch_shapes=[
            pltpu.VMEM((tok, width), BF),
            pltpu.VMEM((width, H * HD), BF),
            pltpu.VMEM((width, 2 * HD), BF),
            pltpu.VMEM((size_x,) + gains.shape, BF),
            pltpu.VMEM((WINDOW + tok, 2 * HD), BF),
            sem((4,)),
            sem((WINDOW // tok,)),
            sem((WINDOW // tok,)),
            sem((2 * size_x,)),
            sem((2 * size_x,)),
        ]
        + [
            pltpu.VMEM((a.shape[0], o.shape[1]), BF)
            for a, o in zip(ins[len(dealt) : -1], outs[len(dealt) : -1])
        ]
        + [
            sem((len(ins), 2)),
            sem((len(ins),)),
            sem((len(dealt), n_ctx)),
            sem((len(dealt), n_ctx)),
            sem((size_x,)),
            sem((size_x,)),
            sem((count, size_x)),
            sem((count, size_x)),
            sem((count, size_x, 9)),
            sem((count, size_x, 9)),
        ],
        compiler_params=pltpu.CompilerParams(
            collective_id=1, has_side_effects=True, vmem_limit_bytes=60 * 1024 * 1024
        ),
        cost_estimate=pl.CostEstimate(
            flops=0, bytes_accessed=300 * 1024 * 1024, transcendentals=0
        ),
        name="fetch",
    )(*ins, low)


def mlp_kernel(sizes, own_ref, *refs):
    size_a, size_b, size_x = sizes
    ranks = 2 * size_x
    cots_in, refs = refs[:2], refs[2:]
    weights_in, refs = refs[:3], refs[3:]
    grad_ref, rows_out, dg_out, du_out, part_out, down_out, refs = *refs[:6], refs[6:]
    rows, cot, w_gate, w_up, w_down, hid, dg, du = refs[:8]
    to_core, in_core, to_x, in_x, total, part_stage, down_stage = refs[8:15]
    load_sem, ag_send, ag_recv, core_send, core_recv, x_send, x_recv, out_sem, stage_sem = refs[15:]
    ia, ib, ic, ix = (lax.axis_index(name) for name in ALL)
    hidden_units = w_down.shape[0]
    tok, width = own_ref.shape
    tiles, _, tile = total.shape
    unit = hid.shape[2] // (hid.shape[2] // 512 if hid.shape[2] % 512 == 0 else hid.shape[2] // 256)

    loads = [
        pltpu.make_async_copy(own_ref, rows.at[0], load_sem.at[0]),
        pltpu.make_async_copy(weights_in[0], w_gate, load_sem.at[1]),
        pltpu.make_async_copy(weights_in[1], w_up, load_sem.at[2]),
        pltpu.make_async_copy(
            weights_in[2].at[pl.ds(pl.multiple_of(ic * hidden_units, hidden_units), hidden_units), :],
            w_down,
            load_sem.at[3],
        ),
    ]
    loads.append(pltpu.make_async_copy(cots_in[0], cot.at[0], load_sem.at[4]))
    loads.append(pltpu.make_async_copy(cots_in[1], cot.at[pl.ds(1, ranks - 1)], load_sem.at[5]))
    for copy in loads:
        copy.start()

    partner = (ia, ib, 1 - ic, ix)

    def across(step):
        return ia, ib, ic, (ix + size_x + step) % size_x

    barrier = pltpu.get_barrier_semaphore()
    greeted = [partner] + [across(s) for s in range(1, size_x)]
    for device in greeted:
        pl.semaphore_signal(barrier, inc=1, device_id=device, device_id_type=MESH)
    pl.semaphore_wait(barrier, len(greeted))

    def remote(src, dst, sent, came, device):
        return pltpu.make_async_remote_copy(
            src_ref=src,
            dst_ref=dst,
            send_sem=sent,
            recv_sem=came,
            device_id=device,
            device_id_type=MESH,
        )

    def gather(b):
        if b == 1:
            return remote(own_ref, rows.at[1], ag_send.at[1], ag_recv.at[1], partner)
        if b % 2:
            return remote(rows.at[b - 1], rows.at[b], ag_send.at[b], ag_recv.at[b], partner)
        return remote(own_ref, rows.at[b], ag_send.at[b], ag_recv.at[b], across(b // 2))

    def core_copy(s):
        return remote(to_core.at[s], in_core.at[s], core_send.at[s], core_recv.at[s], partner)

    def x_copy(s, t):
        return remote(
            to_x.at[s, t], in_x.at[s, t], x_send.at[s, t], x_recv.at[s, t], across(-s)
        )

    def results(b):
        to = pl.ds(b * tok, tok)
        return [
            pltpu.make_async_copy(rows.at[b], rows_out.at[to, :], out_sem.at[0, b]),
            pltpu.make_async_copy(dg.at[b], dg_out.at[to, :], out_sem.at[1, b]),
            pltpu.make_async_copy(du.at[b], du_out.at[to, :], out_sem.at[2, b]),
        ]

    def forward(b):
        def step(t, carry):
            units = pl.ds(pl.multiple_of(t * unit, unit), unit)
            gate = mm(rows[b], w_gate[:, units])
            upward = mm(rows[b], w_up[:, units])
            d_hidden = mm_nt(cot[b], w_down[units, :])
            square = gate * gate
            bent = jnp.tanh(root * gate * (1.0 + cubic * square))
            half = 0.5 * (1.0 + bent)
            act = gate * half
            slope = half + 0.5 * gate * (1.0 - bent * bent) * root * (1.0 + 3.0 * cubic * square)
            hid[b, :, units] = (act * upward).astype(BF)
            dg[b, :, units] = (d_hidden * upward * slope).astype(BF)
            du[b, :, units] = (d_hidden * act).astype(BF)
            return carry

        lax.fori_loop(0, hid.shape[2] // unit, step, 0)
        for copy in results(b):
            copy.start()

    def backward(b):
        s, other = b // 2, b % 2
        if not other:
            core_copy(s).wait_recv()

        def step(t, carry):
            at = pl.ds(pl.multiple_of(t * tile, tile), tile)
            value = mm_nt(dg[b], w_gate[at, :]) + mm_nt(du[b], w_up[at, :])
            if other:
                to_core[s, t] = value.astype(BF)
                return carry
            value = value + in_core[s, t].astype(F32)
            if s:
                to_x[s, t] = value.astype(BF)
                x_copy(s, t).start()
            else:
                total[t] = value
            return carry

        lax.fori_loop(0, tiles, step, 0)
        if other:
            core_copy(s).start()

    def part_copy(b):
        return pltpu.make_async_copy(part_stage.at[b % 2], part_out.at[b], stage_sem.at[b % 2])

    def branch(b):
        if b >= 2:
            part_copy(b - 2).wait()

        def step(t, carry):
            at = pl.ds(pl.multiple_of(t * tile, tile), tile)
            part_stage[b % 2, :, at] = mm(hid[b], w_down[:, at]).astype(BF)
            return carry

        lax.fori_loop(0, tiles, step, 0)
        part_copy(b).start()

    depth = down_stage.shape[1]
    strips = hidden_units // depth

    def down_copy(t, slot):
        to = pl.ds(pl.multiple_of(t * depth, depth), depth)
        return pltpu.make_async_copy(down_stage.at[slot], down_out.at[to, :], stage_sem.at[2 + slot])

    def down_step(t, carry):
        slot = t % 2

        @pl.when(t >= 2)
        def _():
            down_copy(t - 2, slot).wait()

        units = pl.ds(pl.multiple_of(t * depth, depth), depth)
        value = mm_tn(hid[0, :, units], cot[0])
        for b in range(1, ranks):
            value = value + mm_tn(hid[b, :, units], cot[b])
        down_stage[slot] = value.astype(BF)
        down_copy(t, slot).start()
        return carry

    gather(1).start()
    for s in range(1, size_x):
        gather(2 * s).start()
    for copy in loads:
        copy.wait()
    forward(0)
    gather(1).wait_recv()
    forward(1)
    backward(1)
    for s in range(1, size_x):
        gather(2 * s).wait_recv()
        gather(2 * s + 1).start()
        forward(2 * s)
        gather(2 * s + 1).wait_recv()
        forward(2 * s + 1)
        backward(2 * s + 1)
        backward(2 * s)
    backward(0)
    lax.fori_loop(0, strips, down_step, 0)
    for b in range(ranks):
        branch(b)
    for s in range(1, size_x):
        for t in range(tiles):
            x_copy(s, t).wait()
    for t in range(tiles):
        value = total[t]
        for s in range(1, size_x):
            value = value + in_x[s, t].astype(F32)
        grad_ref[:, t * tile : (t + 1) * tile] = value
    for b in range(1, ranks):
        gather(b).wait_send()
    for s in range(size_x):
        core_copy(s).wait_send()
    for b in range(ranks):
        for copy in results(b):
            copy.wait()
    part_copy(ranks - 2).wait()
    part_copy(ranks - 1).wait()
    down_copy(strips - 2, (strips - 2) % 2).wait()
    down_copy(strips - 1, (strips - 1) % 2).wait()


def feed_forward(sizes, normed, cot, cot_rows, w_gate, w_up, down_weight):
    ranks = 2 * sizes[2]
    size_x = sizes[2]
    tok, width = normed.shape
    units = w_gate.shape[1]
    tile = 512
    tiles = width // tile
    sem = pltpu.SemaphoreType.DMA
    hbm = pl.BlockSpec(memory_space=pl.ANY)
    return pl.pallas_call(
        functools.partial(mlp_kernel, sizes),
        in_specs=[hbm] * 6,
        out_specs=[pl.BlockSpec(memory_space=pltpu.VMEM)] + [hbm] * 5,
        out_shape=[
            jax.ShapeDtypeStruct((tok, width), F32),
            jax.ShapeDtypeStruct((ranks * tok, width), BF),
            jax.ShapeDtypeStruct((ranks * tok, units), BF),
            jax.ShapeDtypeStruct((ranks * tok, units), BF),
            jax.ShapeDtypeStruct((ranks, tok, width), BF),
            jax.ShapeDtypeStruct((units, width), BF),
        ],
        scratch_shapes=[
            pltpu.VMEM((ranks, tok, width), BF),
            pltpu.VMEM((ranks, tok, width), BF),
            pltpu.VMEM((width, units), BF),
            pltpu.VMEM((width, units), BF),
            pltpu.VMEM((units, width), BF),
            pltpu.VMEM((ranks, tok, units), BF),
            pltpu.VMEM((ranks, tok, units), BF),
            pltpu.VMEM((ranks, tok, units), BF),
            pltpu.VMEM((size_x, tiles, tok, tile), BF),
            pltpu.VMEM((size_x, tiles, tok, tile), BF),
            pltpu.VMEM((size_x, tiles, tok, tile), BF),
            pltpu.VMEM((size_x, tiles, tok, tile), BF),
            pltpu.VMEM((tiles, tok, tile), F32),
            pltpu.VMEM((2, tok, width), BF),
            pltpu.VMEM((2, 256, width), BF),
            sem((6,)),
            sem((ranks,)),
            sem((ranks,)),
            sem((size_x,)),
            sem((size_x,)),
            sem((size_x, tiles)),
            sem((size_x, tiles)),
            sem((3, ranks)),
            sem((4,)),
        ],
        compiler_params=pltpu.CompilerParams(
            collective_id=2, has_side_effects=True, vmem_limit_bytes=62 * 1024 * 1024
        ),
        cost_estimate=pl.CostEstimate(
            flops=14 * ranks * tok * width * units,
            bytes_accessed=60 * 1024 * 1024,
            transcendentals=0,
        ),
        name="feed_forward",
    )(normed, cot, cot_rows, w_gate, w_up, down_weight)


class Job:
    def __init__(self, phase, left, right, rows, cols, by_rank):
        self.phase, self.left, self.right = phase, left, right
        self.rows, self.cols, self.by_rank = rows, cols, by_rank


def grads_kernel(sizes, jobs, *refs):
    size_a, size_b, size_x = sizes
    chips = size_a * size_b
    n_ctx = 2 * chips
    ranks = 2 * size_x
    count = len(jobs)
    ins, refs = refs[:13], refs[13:]
    outs, refs = refs[:count], refs[count:]
    down_out, refs = refs[0], refs[1:]
    dealt, refs = refs[:2], refs[2:]
    gain_out, refs = refs[0], refs[1:]
    held, refs = refs[:8], refs[8:]
    gain_ctx, gain_x, resid_in, part_own, part_core, part_x, down_passed, refs = *refs[:7], refs[7:]
    recv, refs = refs[:count], refs[count:]
    send, refs = refs[:count], refs[count:]
    done, refs = refs[:count], refs[count:]
    load_sem, group_send, group_recv, deal_send, deal_recv, part_sem = refs[:6]
    gain_send, gain_recv, send_sem, recv_sem, done_send, done_recv, own_sem = refs[6:]
    ia, ib, ic, ix = (lax.axis_index(name) for name in ALL)
    own = (ia * size_b + ib) * 2 + ic
    rank = ix * 2 + ic
    place = snake_place(ia, ib, size_a, size_b)

    def on_ring(step):
        return snake((place + 2 * chips + step) % chips, size_a, size_b)

    def member(k):
        return (ic + k) % 2, (ix + k // 2) % size_x

    def ctx_device(k):
        e = (own + k) % n_ctx
        return e // 2 // size_b, e // 2 % size_b, e % 2, ix

    def keeper(row_chunk):
        chip = row_chunk // ranks
        return chip // size_b, chip % size_b, (row_chunk // size_x) % 2, row_chunk % size_x

    kept = rank * chips + kept_slot(ia, ib, size_a, size_b)
    kept_id = keeper(kept)
    flat = own * size_x + ix
    from_rank = flat // chips
    from_slot = flat % chips
    half = chips // 2
    from_id = (
        (from_slot % half) // (size_b // 2),
        ((from_slot % half) % (size_b // 2)) * 2 + 1 - from_slot // half,
        from_rank % 2,
        from_rank // 2,
    )

    def remote(src, dst, sent, came, device):
        return pltpu.make_async_remote_copy(
            src_ref=src,
            dst_ref=dst,
            send_sem=sent,
            recv_sem=came,
            device_id=device,
            device_id_type=MESH,
        )

    loads = [pltpu.make_async_copy(ins[i], held[i], load_sem.at[i]) for i in range(3)]
    for copy in loads:
        copy.start()

    barrier = pltpu.get_barrier_semaphore()
    greeted = [ctx_device(k) for k in range(1, n_ctx)] + [from_id]
    greeted += [(ia, ib) + member(k) for k in range(2, ranks)]
    for device in greeted:
        pl.semaphore_signal(barrier, inc=1, device_id=device, device_id_type=MESH)
    pl.semaphore_wait(barrier, len(greeted))

    passed_on = (3, 5)

    def group_copy(i, k):
        c, x = member(k)
        src, dst = ins[i], held[i].at[k]
        target = x * 2 + c
        if i == 4:
            rows = held[i].shape[1]
            src = src.at[pl.ds(pl.multiple_of(target * rows, rows), rows), :]
        if i == 6:
            cols = held[i].shape[2]
            src = src.at[:, pl.ds(pl.multiple_of(target * cols, cols), cols)]
        if k == 0:
            return pltpu.make_async_copy(src, dst, load_sem.at[i])
        if k % 2 and k > 1 and i in passed_on:
            src, x = held[i].at[k - 1], ix
        return remote(src, dst, group_send.at[i, k], group_recv.at[i, k], (ia, ib, c, x))

    def deal_copy(t, k):
        e = (own + k) % n_ctx
        source = part_own.at[0] if t == 0 else ins[9]
        rows = source.shape[0] // n_ctx
        src = source.at[pl.ds(pl.multiple_of(e * rows, rows), rows), :]
        dst = dealt[t].at[pl.ds(pl.multiple_of(own * rows, rows), rows), :]
        if k == 0:
            return pltpu.make_async_copy(src, dst, load_sem.at[8 + t])
        return remote(src, dst, deal_send.at[t, k], deal_recv.at[t, k], ctx_device(k))

    def part_load(step):
        return pltpu.make_async_copy(ins[8].at[2 * step], part_own.at[step], part_sem.at[step])

    def part_core_copy(step):
        device = (ia, ib, 1 - ic, ix)
        src, dst = ins[8].at[2 * step + 1], part_core.at[step]
        return remote(src, dst, group_send.at[0, step], group_recv.at[0, step], device)

    def part_x_copy(step):
        device = (ia, ib, ic, (ix + size_x - step) % size_x)
        src, dst = part_own.at[step], part_x.at[step - 1]
        return remote(src, dst, group_send.at[1, step], group_recv.at[1, step], device)

    crossing = size_x == 2
    down_sem = (done_send.at[count, 0], done_recv.at[count, 0])
    down_copy = remote(ins[12], down_out, *down_sem, kept_id)
    if crossing:
        straight = kept % size_x == ix
        hop_sem = (done_send.at[count, 1], done_recv.at[count, 1])
        down_hop = remote(ins[12], down_passed, *hop_sem, (ia, ib, ic, 1 - ix))
        passed_id = keeper(((1 - ix) * 2 + ic) * chips + kept_slot(ia, ib, size_a, size_b))
        pass_sem = (done_send.at[count, 2], done_recv.at[count, 0])
        down_pass = remote(down_passed, down_out, *pass_sem, passed_id)

    resid_copy = pltpu.make_async_copy(ins[11], resid_in, load_sem.at[11])

    def gain_copy(k):
        src, dst = ins[10].at[(own + k) % n_ctx], gain_ctx.at[k]
        if k == 0:
            return pltpu.make_async_copy(src, dst, load_sem.at[10])
        return remote(src, dst, deal_send.at[2, k], deal_recv.at[2, k], ctx_device(k))

    def gain_copy_x(s):
        device = (ia, ib, ic, (ix + s) % size_x)
        return remote(gain_x.at[0], gain_x.at[s], gain_send.at[s], gain_recv.at[s], device)

    def ring_copy(j, way, step, parity):
        neighbour = on_ring(1 - 2 * way) + (ic, ix)
        return remote(
            send[j].at[way, parity],
            recv[j].at[way, step],
            send_sem.at[j, way, parity],
            recv_sem.at[j, way, step],
            neighbour,
        )

    def product(j, way, step):
        job = jobs[j]
        a, b = on_ring(step * (2 * way - 1))
        part = job.rows // chips
        cols = slice(way * job.cols // 2, (way + 1) * job.cols // 2)
        left, right = held[job.left], held[job.right]
        if job.phase == 0:
            start = pl.multiple_of((a * size_b + b) * part, part)
            return mm_tn(left[:, pl.ds(start, part)], right[:, cols])
        if job.by_rank:
            start = kept_slot(a, b, size_a, size_b) * part
            if left.shape[1] != job.rows:
                start = start + rank * job.rows
        else:
            start = (a * size_b + b) * part
        rows = pl.ds(pl.multiple_of(start, part), part)
        total = mm(left[0, rows, :], right[0, :, cols])
        for k in range(1, ranks):
            total = total + mm(left[k, rows, :], right[k, :, cols])
        return total

    def deliver(j):
        job = jobs[j]
        if job.by_rank:
            return [remote(done[j], outs[j], done_send.at[j, 0], done_recv.at[j, 0], kept_id)]
        part = job.rows // (chips * ranks)
        copies = []
        for k in range(ranks):
            c, x = member(k)
            start = pl.multiple_of((c * size_x + x) * part, part)
            src, dst = done[j].at[pl.ds(start, part), :], outs[j].at[rank]
            if k == 0:
                copies.append(pltpu.make_async_copy(src, dst, own_sem.at[j]))
            else:
                copies.append(
                    remote(src, dst, done_send.at[j, k], done_recv.at[j, k], (ia, ib, c, x))
                )
        return copies

    def begin(j):
        for way in range(2):
            send[j][way, 0] = product(j, way, 1).astype(BF)
            ring_copy(j, way, 0, 0).start()

    def advance(j, step):
        parity = step % 2
        for way in range(2):
            part = product(j, way, step + 1)
            ring_copy(j, way, step - 1, 1 - parity).wait_recv()
            part = part + recv[j][way, step - 1].astype(F32)

            @pl.when(step >= 2)
            def _():
                ring_copy(j, way, step - 2, parity).wait_send()

            send[j][way, parity] = part.astype(BF)
            ring_copy(j, way, step, parity).start()

    last = chips - 2

    def finish(j):
        cols = jobs[j].cols // 2
        for way in range(2):
            part = product(j, way, chips)
            ring_copy(j, way, last, last % 2).wait_recv()
            part = part + recv[j][way, last].astype(F32)
            done[j][:, way * cols : (way + 1) * cols] = part.astype(BF)
        for copy in deliver(j):
            copy.start()
        for way in range(2):
            ring_copy(j, way, last - 1, (last - 1) % 2).wait_send()
            ring_copy(j, way, last, last % 2).wait_send()

    early = [j for j in range(count) if jobs[j].phase == 0]
    late = [j for j in range(count) if jobs[j].phase == 1]
    lag = 3

    def early_step(step, carry):
        for j in early:
            advance(j, step)
        return carry

    def both_step(step, carry):
        for j in late:
            advance(j, step - lag)
        for j in early:
            advance(j, step)
        return carry

    def late_step(step, carry):
        for j in late:
            advance(j, step)
        return carry

    for copy in loads:
        copy.wait()
    for j in early:
        begin(j)
    for step in range(size_x):
        part_load(step).start()
        part_core_copy(step).start()
    for i in (6, 7, 5, 4, 3):
        for k in range(ranks):
            if not (k % 2 and k > 1 and i in passed_on):
                group_copy(i, k).start()
    resid_copy.start()
    for k in range(n_ctx):
        gain_copy(k).start()
    for k in range(n_ctx):
        deal_copy(1, k).start()
    if crossing:

        @pl.when(straight)
        def _():
            down_copy.start()

        @pl.when(jnp.logical_not(straight))
        def _():
            down_hop.start()

    else:
        down_copy.start()
    lax.fori_loop(1, 2, early_step, 0)
    for step in range(size_x):
        part_load(step).wait()
        part_core_copy(step).wait()
    for step in range(1, size_x):
        summed = part_own[step].astype(F32) + part_core[step].astype(F32)
        part_own[step] = summed.astype(BF)
        part_x_copy(step).start()
    lax.fori_loop(2, lag, early_step, 0)
    if crossing:

        @pl.when(straight)
        def _():
            down_hop.wait_recv()
            down_pass.start()

    for i in reversed(passed_on):
        for k in range(2, ranks, 2):
            group_copy(i, k).wait_recv()
            group_copy(i, k + 1).start()
    for k in range(n_ctx):
        gain_copy(k).wait()
    gain_x[0] = jnp.sum(gain_ctx[...], axis=0)
    for s in range(1, size_x):
        gain_copy_x(s).start()
    lax.fori_loop(lag, lag + 1, early_step, 0)
    for i in range(3, 8):
        for k in range(ranks):
            if k and k % 2 == 0 and i in passed_on:
                group_copy(i, k).wait_send()
            else:
                group_copy(i, k).wait()
    for j in late:
        begin(j)
    resid_copy.wait()
    summed = resid_in[...] + part_own[0].astype(F32) + part_core[0].astype(F32)
    for step in range(1, size_x):
        part_x_copy(step).wait()
        summed = summed + part_x[step - 1].astype(F32)
    part_own[0] = summed.astype(BF)
    for k in range(n_ctx):
        deal_copy(0, k).start()
    lax.fori_loop(lag + 1, last + 1, both_step, 0)
    for j in early:
        finish(j)
    lax.fori_loop(last + 1 - lag, last + 1, late_step, 0)
    for j in late:
        finish(j)
    for s in range(1, size_x):
        gain_copy_x(s).wait()
    gain_out[...] = jnp.sum(gain_x[...], axis=0)
    for t in range(2):
        for k in range(n_ctx):
            deal_copy(t, k).wait()
    down_copy.wait_recv()
    if crossing:

        @pl.when(straight)
        def _():
            down_copy.wait_send()
            down_pass.wait_send()

        @pl.when(jnp.logical_not(straight))
        def _():
            down_hop.wait_send()

    else:
        down_copy.wait_send()
    for j in range(count):
        for copy in deliver(j):
            copy.wait()


def sum_grads(sizes, ins):
    size_a, size_b, size_x = sizes
    chips = size_a * size_b
    ranks = 2 * size_x
    normed_mlp, d_gate, d_upward = ins[:3]
    width = normed_mlp.shape[1]
    tok = ins[5].shape[0]
    part_width = width // ranks
    jobs = [
        Job(0, 0, 1, width, d_gate.shape[1], False),
        Job(0, 0, 2, width, d_upward.shape[1], False),
        Job(1, 3, 6, width, part_width, False),
        Job(1, 4, 5, part_width, width, True),
        Job(1, 3, 7, part_width, 2 * HD, True),
    ]
    held = [pltpu.VMEM(a.shape, BF) for a in ins[:3]]
    held += [
        pltpu.VMEM((ranks,) + shape, BF)
        for shape in (
            (width, tok),
            (part_width, tok),
            (tok, width),
            (tok, part_width),
            (tok, 2 * HD),
        )
    ]
    outs, recv, send, done = [], [], [], []
    flops = 0
    for job in jobs:
        part = job.rows // chips
        if job.by_rank:
            outs.append(jax.ShapeDtypeStruct((part, job.cols), BF))
        else:
            outs.append(jax.ShapeDtypeStruct((ranks, part // ranks, job.cols), BF))
        recv.append(pltpu.VMEM((2, chips - 1, part, job.cols // 2), BF))
        send.append(pltpu.VMEM((2, 2, part, job.cols // 2), BF))
        done.append(pltpu.VMEM((part, job.cols), BF))
        flops += 2 * job.rows * job.cols * normed_mlp.shape[0]
    count = len(jobs)
    outs.append(jax.ShapeDtypeStruct(ins[12].shape, BF))
    outs += [jax.ShapeDtypeStruct((tok, width), BF)] * 2
    gain_shape = ins[10].shape[1:]
    outs.append(jax.ShapeDtypeStruct(gain_shape, F32))
    sem = pltpu.SemaphoreType.DMA
    return pl.pallas_call(
        functools.partial(grads_kernel, sizes, jobs),
        in_specs=[pl.BlockSpec(memory_space=pl.ANY)] * len(ins),
        out_specs=[pl.BlockSpec(memory_space=pl.ANY)] * (count + 3)
        + [pl.BlockSpec(memory_space=pltpu.VMEM)],
        out_shape=outs,
        scratch_shapes=held
        + [
            pltpu.VMEM((2 * chips,) + gain_shape, F32),
            pltpu.VMEM((size_x,) + gain_shape, F32),
            pltpu.VMEM((tok, width), F32),
            pltpu.VMEM((size_x, tok, width), BF),
            pltpu.VMEM((size_x, tok, width), BF),
            pltpu.VMEM((size_x - 1, tok, width), BF),
            pltpu.VMEM(ins[12].shape, BF),
        ]
        + recv
        + send
        + done
        + [
            sem((len(ins),)),
            sem((8, ranks)),
            sem((8, ranks)),
            sem((3, 2 * chips)),
            sem((3, 2 * chips)),
            sem((size_x,)),
            sem((size_x,)),
            sem((size_x,)),
            sem((count, 2, 2)),
            sem((count, 2, chips - 1)),
            sem((count + 1, ranks)),
            sem((count + 1, ranks)),
            sem((count,)),
        ],
        compiler_params=pltpu.CompilerParams(
            collective_id=0, has_side_effects=True, vmem_limit_bytes=63 * 1024 * 1024
        ),
        cost_estimate=pl.CostEstimate(
            flops=flops, bytes_accessed=400 * 1024 * 1024, transcendentals=0
        ),
        name="sum_grads",
    )(*ins)


def norm_stats(values):
    inv = lax.rsqrt(jnp.mean(values * values, axis=-1, keepdims=True) + epsilon)
    return values * inv, inv


def norm_back(unit, inv, gain, grad):
    scaled = grad * gain
    inner = jnp.mean(scaled * unit, axis=-1, keepdims=True)
    return inv * (scaled - unit * inner), jnp.sum(grad * unit, axis=0)


def on_device(
    sizes,
    tokens,
    lengths,
    dealing,
    attn_gain,
    query_weight,
    kv_weight,
    out_weight,
    mlp_gain,
    gate_weight,
    up_weight,
    down_weight,
    cotangent,
):
    size_a, size_b, size_x = sizes
    chips = size_a * size_b
    n_ctx = chips * 2
    ranks = 2 * size_x
    ia, ib, ic, ix = (lax.axis_index(name) for name in ALL)
    chip = ia * size_b + ib
    own = chip * 2 + ic
    flat = own * size_x + ix
    rank = ix * 2 + ic
    tok = tokens.shape[1]
    width = tokens.shape[2]
    piece = tok // n_ctx
    halo = WINDOW // tok

    def pick(array, index, axis=0):
        return lax.dynamic_index_in_dim(array, index, axis, keepdims=False)

    own_deal = pick(dealing[0], own)
    deal = (own_deal[:, None] == jnp.arange(tok, dtype=jnp.int32)[None, :]).astype(BF)

    gains = jnp.stack([attn_gain, mlp_gain]).reshape(-1, 128)
    stream = own * tok + jnp.arange(tok, dtype=jnp.int32)
    ends = jnp.cumsum(lengths[0])
    starts = jnp.max(jnp.where(stream[:, None] >= ends[None, :], ends[None, :], 0), axis=1)
    low = jnp.maximum(starts, stream - (WINDOW - 1)) - (own * tok - WINDOW)
    low = low.astype(jnp.int32)[None, :]
    inputs_low, cot, w_query, w_kv, w_out, w_gate, w_up, gains, *attended = fetch(
        sizes,
        [mm(deal, tokens[0]).astype(BF), mm(deal, cotangent[0]).astype(BF)],
        [query_weight, kv_weight, out_weight],
        [gate_weight, up_weight],
        gains,
        low,
    )
    _, queries, window, context, lse, cot_rows, normed_t, context_t = attended
    gains = gains.reshape(size_x, 2, -1).astype(F32)
    gain_one = gains[:, 0].reshape(-1)
    gain_two = gains[:, 1].reshape(-1)


    inputs = inputs_low.astype(F32)
    unit_one, inv_one = norm_stats(inputs)
    resid = inputs + mm(context, w_out)

    unit_two, inv_two = norm_stats(resid)
    d_normed_mlp, mlp_rows, d_gate, d_upward, mlp_parts, down_grad = feed_forward(
        sizes, (unit_two * gain_two).astype(BF), cot, cot_rows, w_gate, w_up, down_weight
    )
    d_resid_part, mlp_gain_grad = norm_back(unit_two, inv_two, gain_two, d_normed_mlp)
    d_resid = cot.astype(F32) + d_resid_part
    d_branch = d_resid.astype(BF)

    d_queries, d_pairs, down_sum, d_normed = attend_back(
        sizes, queries, window, low, d_branch, lse, down_grad, w_out, w_query, w_kv
    )
    d_inputs, attn_gain_grad = norm_back(unit_one, inv_one, gain_one, d_normed)
    gain_part = width // (n_ctx * size_x)
    gain_grads = jnp.stack([attn_gain_grad, mlp_gain_grad]).reshape(2, n_ctx, size_x, gain_part)
    gain_grads = gain_grads.transpose(1, 2, 0, 3).reshape(n_ctx, -1)
    gain_grads = jnp.pad(gain_grads, ((0, 0), (0, 1024 - gain_grads.shape[1])))
    sums = sum_grads(
        sizes,
        [
            mlp_rows,
            d_gate,
            d_upward,
            normed_t,
            context_t,
            d_branch,
            d_queries,
            d_pairs,
            mlp_parts,
            (d_resid + d_inputs).astype(BF),
            gain_grads.reshape(n_ctx, 8, 128),
            resid,
            down_sum,
        ],
    )
    gate_grad, up_grad, query_grad = (
        v.transpose(1, 0, 2).reshape(v.shape[1], -1).astype(F32) for v in sums[:3]
    )
    out_grad, kv_grad, down_grad = (v.astype(F32) for v in sums[3:6])
    block_output = mm_tn(deal, sums[6]).astype(BF)
    token_grad = mm_tn(deal, sums[7])
    gain_grads = lax.dynamic_slice(sums[8].reshape(-1), (ix * 2 * gain_part,), (2 * gain_part,))
    attn_gain_grad, mlp_gain_grad = gain_grads[:gain_part], gain_grads[gain_part:]
    return (
        block_output[None],
        token_grad[None],
        attn_gain_grad,
        query_grad,
        kv_grad,
        out_grad,
        mlp_gain_grad,
        gate_grad,
        up_grad,
        down_grad,
    )


def solution(mesh):
    n_ctx, size_x = mesh.shape["ctx"], mesh.shape["fsdp"]
    chips = n_ctx // 2
    size_a = 4 if chips % 4 == 0 else chips
    size_b = chips // size_a
    fine = Mesh(mesh.devices.reshape(size_a, size_b, 2, size_x), ALL)
    rows = P("x", CTX, None)
    split = P("x", None)
    every = P(ALL)
    matrix = P(ALL, None)
    return jax.shard_map(
        functools.partial(on_device, (size_a, size_b, size_x)),
        mesh=fine,
        in_specs=(
            rows,
            split,
            P("x", None, None),
            P("x"),
            split,
            split,
            split,
            P("x"),
            split,
            split,
            split,
            rows,
        ),
        out_specs=(rows, rows, every, matrix, matrix, matrix, every, matrix, matrix, matrix),
        check_vma=False,
    )
```
